32 devices in a mesh: dp: 8 (over y, x, core), seq: 4 (over z).
Axes of the slice: x: 2, y: 2, z: 4, core: 2. Of those that a mesh axis runs over, the one named last changes fastest.
Arguments:
- tokens: bfloat16 [8, 1024, 2048], P('dp', 'seq'), may hold values from -6 to 6
- cotangent: bfloat16 [8, 1024, 2048], P('dp', 'seq'), may hold values from -6 to 6
- norm_gain: bfloat16 [2048], P(('dp', 'seq')), may hold values from 0.5 to 1.5
- in_weight: bfloat16 [2048, 8192], P(('dp', 'seq')), may hold values from -0.125 to 0.125
- conv_weight: bfloat16 [4096, 4], P(('dp', 'seq')), may hold values from -3 to 3
- conv_bias: bfloat16 [4096], P(('dp', 'seq')), may hold values from -3 to 3
- select_weight: bfloat16 [4096, 160], P(('dp', 'seq')), may hold values from -0.09375 to 0.09375
- beta_weight: bfloat16 [4096, 128], P(('dp', 'seq')), may hold values from -0.5 to 0.5
- beta_bias: bfloat16 [4096], P(('dp', 'seq')), may hold values from -8 to 0
- skip_gain: bfloat16 [4096], P(('dp', 'seq')), may hold values from 0.25 to 1.5
- out_weight: bfloat16 [4096, 2048], P(('dp', 'seq')), may hold values from -0.09375 to 0.09375
Outputs:
- result: bfloat16 [8, 1024, 2048], P('dp', 'seq')
- input_grad: bfloat16 [8, 1024, 2048], P('dp', 'seq')
- norm_gain_grad: float32 [2048], P(('dp', 'seq'))
- in_weight_grad: float32 [2048, 8192], P(('dp', 'seq'))
- conv_weight_grad: float32 [4096, 4], P(('dp', 'seq'))
- conv_bias_grad: float32 [4096], P(('dp', 'seq'))
- select_weight_grad: float32 [4096, 160], P(('dp', 'seq'))
- beta_weight_grad: float32 [4096, 128], P(('dp', 'seq'))
- beta_bias_grad: float32 [4096], P(('dp', 'seq'))
- skip_gain_grad: float32 [4096], P(('dp', 'seq'))
- out_weight_grad: float32 [4096, 2048], P(('dp', 'seq'))
The draws below stay inside these ranges and needn't reach their ends.
All inputs are finite; a program needn't handle non-finite values.
Results may differ from the reference program's by a relative error of at most 0.012.
Values may be sent and summed in bfloat16 or wider, within the bound.
A program may use at most 320 MiB of HBM per device.

```python
import math
import jax
import jax.numpy as jnp
from jax import lax

D = 2048
INNER = 4096
STATE = 16
RANK = 128
CONV = 4
SEQS = 8
LENGTH = 1024


def block_levels(stream_key, shape, cuts, low, largest):
    factor_of = 1.0
    for axis_at, shards_of in cuts:
        draws = jax.random.uniform(jax.random.fold_in(jax.random.fold_in(stream_key, 6), axis_at), (shards_of,), jnp.float32, low / len(cuts), largest / len(cuts))
        factor_of = factor_of * jnp.repeat(jnp.exp(draws), shape[axis_at] // shards_of).reshape((-1,) + (1,) * (len(shape) - 1 - axis_at))
    return factor_of


def scatter_about(key, shape, deviation, limit, split=(), dtype=jnp.bfloat16):
    drawn = jax.random.normal(key, shape, jnp.float32) * deviation
    if len(split) > 0:
        drawn = block_levels(key, shape, split, -0.22, 0.18) * drawn
    return jnp.clip(drawn, min=-limit, max=limit).astype(dtype)


def setup_inputs(seed: int = 0) -> dict:
    key_of = jax.random.split(jax.random.key(seed), 12)
    return {
        "tokens": scatter_about(key_of[0], (SEQS, LENGTH, D), 1.0, 6.0, ((0, 8), (1, 4))),
        "cotangent": scatter_about(key_of[1], (SEQS, LENGTH, D), 1.0, 6.0, ((0, 8), (1, 4))),
        "norm_gain": jnp.clip(1.0 + 0.1 * jax.random.normal(key_of[2], (D,), jnp.float32), 0.5, 1.5).astype(jnp.bfloat16),
        "in_weight": scatter_about(key_of[3], (D, 2 * INNER), D ** -0.5, 0.125, ((0, 32),)),
        "conv_weight": scatter_about(key_of[4], (INNER, CONV), CONV ** -0.5, 3.0, ((0, 32),)),
        "conv_bias": scatter_about(key_of[5], (INNER,), 0.5, 3.0, ((0, 32),)),
        "select_weight": scatter_about(key_of[6], (INNER, RANK + 2 * STATE), INNER ** -0.5, 0.09375, ((0, 32),)),
        "beta_weight": scatter_about(key_of[7], (INNER, RANK), RANK ** -0.5, 0.5, ((0, 32),)),
        "beta_bias": jnp.clip(-8.0 + 8.0 * jax.random.uniform(key_of[8], (INNER,), jnp.float32) ** block_levels(key_of[8], (INNER,), ((0, 32),), -0.2, 0.2), -8.0, 0.0).astype(jnp.bfloat16),
        "skip_gain": jnp.clip(0.25 + 1.25 * jax.random.uniform(key_of[9], (INNER,), jnp.float32) ** block_levels(key_of[9], (INNER,), ((0, 32),), -0.2, 0.2), 0.25, 1.5).astype(jnp.bfloat16),
        "out_weight": scatter_about(key_of[10], (INNER, D), INNER ** -0.5, 0.09375, ((0, 32),)),
    }


@jax.custom_vjp
def low(v):
    return lax.optimization_barrier(v.astype(jnp.bfloat16)).astype(jnp.float32)

@jax.custom_vjp
def low_back(v):
    return v

def low_keep(v):
    return (low(v), None)

def low_pass(kept, grad):
    return (grad,)

def back_keep(v):
    return (v, None)

def back_low(kept, grad):
    return (low(grad),)
low.defvjp(low_keep, low_pass)
low_back.defvjp(back_keep, back_low)

def product(left, right):
    return jnp.dot(left, right, precision=lax.Precision.HIGHEST, preferred_element_type=jnp.float32)

def scan_states(rates, keys, queries, values):
    length, inner = rates.shape
    width = keys.shape[1]
    span = math.gcd(64, length)
    count = length // span

    def step(carry, row):
        rate, key, query, value = row
        decay = 1.0 - rate[None, :] * (key * key)[:, None]
        carry = decay * carry + key[:, None] * (rate * value)[None, :]
        return (carry, lax.optimization_barrier(jnp.sum(carry * query[:, None], axis=0)))

    def block(carry, rows):
        return lax.scan(step, carry, rows)
    rows = (rates.reshape(count, span, inner), keys.reshape(count, span, width), queries.reshape(count, span, width), values.reshape(count, span, inner))
    final, emitted = lax.scan(jax.checkpoint(block), jnp.zeros((width, inner), jnp.float32), rows)
    return emitted.reshape(length, inner)

def forward_one(sequence, norm_gain, in_weight, conv_weight, conv_bias, select_weight, beta_weight, beta_bias, skip_gain, out_weight):
    length = sequence.shape[0]
    inner = conv_weight.shape[0]
    width = conv_weight.shape[1]
    rank = beta_weight.shape[1]
    states = (select_weight.shape[1] - rank) // 2
    scale = lax.rsqrt(lax.optimization_barrier(jnp.mean(sequence * sequence, axis=-1, keepdims=True)) + 1e-05)
    normed = low(sequence * scale * norm_gain)
    mixed = low_back(product(normed, in_weight))
    conv_in = low(mixed[:, :inner])
    gate_in = mixed[:, inner:]
    padded = jnp.concatenate([jnp.zeros((width - 1, inner), jnp.float32), conv_in], axis=0)
    conv_sum = conv_bias + padded[0:length] * conv_weight[:, 0]
    for offset in range(1, width):
        conv_sum = conv_sum + padded[offset:offset + length] * conv_weight[:, offset]
    values = low(jax.nn.silu(conv_sum))
    projected = low_back(product(values, select_weight))
    lowrank = low(projected[:, :rank])
    keys = projected[:, rank:rank + states]
    queries = projected[:, rank + states:]
    beta = jax.nn.sigmoid(low_back(product(lowrank, beta_weight.T)) + beta_bias)
    rates = beta / (1.0 + beta * lax.optimization_barrier(jnp.sum(keys * keys, axis=-1, keepdims=True)))
    outputs = scan_states(rates, keys, queries, values)
    gated = low((outputs + skip_gain * values) * jax.nn.silu(gate_in))
    return sequence + product(gated, out_weight)

def reference(tokens, cotangent, norm_gain, in_weight, conv_weight, conv_bias, select_weight, beta_weight, beta_bias, skip_gain, out_weight):
    params = tuple((p.astype(jnp.float32) for p in (norm_gain, in_weight, conv_weight, conv_bias, select_weight, beta_weight, beta_bias, skip_gain, out_weight)))
    inputs = tokens.astype(jnp.float32)
    cotangents = cotangent.astype(jnp.float32)

    def per_sequence(totals, pair):
        sequence, cot_rows = pair
        output, pullback = jax.vjp(forward_one, sequence, *params)
        grads = pullback(cot_rows)
        totals = tuple((total + grad for total, grad in zip(totals, grads[1:])))
        return (totals, (output, grads[0]))
    start = tuple((jnp.zeros_like(p) for p in params))
    totals, (outputs, in_grads) = lax.scan(per_sequence, start, (inputs, cotangents))
    return (outputs.astype(jnp.bfloat16), in_grads.astype(jnp.bfloat16), totals[0], totals[1], totals[2], totals[3], totals[4], totals[5], totals[6], totals[7], totals[8])
```

```python
import jax
import jax.numpy as jnp
from jax import lax
from jax.experimental import pallas as pl
from jax.experimental.pallas import tpu as pltpu
from jax.sharding import PartitionSpec as P

LANE = 128


def sigmoid(v):
    return 1.0 / (1.0 + jnp.exp(-v))


def by_eights(value):
    return value.reshape(value.shape[0] // 8, 8, value.shape[1])


def as_rows(value):
    return value.reshape(value.shape[0] * 8, value.shape[2])


def spread_columns(row_ref, key_ref, query_ref, rows, states):
    lane = lax.broadcasted_iota(jnp.int32, (states, LANE), 1)
    entry = lax.broadcasted_iota(jnp.int32, (states, LANE), 0)
    pick_key = lane == entry
    pick_query = lane == entry + states

    def body(group, carry):
        for offset in range(8):
            t = group * 8 + offset
            row = jnp.broadcast_to(row_ref[group, offset : offset + 1, :], (states, LANE))
            at = pl.multiple_of(t * states, states)
            key = jnp.sum(jnp.where(pick_key, row, 0.0), axis=1, keepdims=True)
            query = jnp.sum(jnp.where(pick_query, row, 0.0), axis=1, keepdims=True)
            key_ref[pl.ds(at, states), :] = jnp.broadcast_to(key, (states, LANE))
            query_ref[pl.ds(at, states), :] = jnp.broadcast_to(query, (states, LANE))
        return carry

    lax.fori_loop(0, rows // 8, body, 0)


def step_sizes(low_ref, kq_ref, weight_ref, bias_ref, states):
    pre = lax.dot_general(
        low_ref[...], weight_ref[...], (((1,), (1,)), ((), ())), preferred_element_type=jnp.float32
    )
    beta = sigmoid(pre + bias_ref[...])
    lane = lax.broadcasted_iota(jnp.int32, kq_ref.shape, 1)
    keys = jnp.where(lane < states, kq_ref[...], 0.0)
    square = jnp.sum(keys * keys, axis=1, keepdims=True)
    return beta, 1.0 / (1.0 + beta * square)


def forward_body(
    states, low_ref, kq_ref, values_ref, gate_ref, weight_ref, bias_ref, skip_ref,
    gated_ref, mixed_ref, history_ref, final_ref,
    state_ref, key_ref, query_ref, rate_ref, input_ref, out_ref, row_ref,
):
    rows, channels = values_ref.shape
    tiles = channels // LANE
    per_group = min(4, tiles)

    @pl.when(pl.program_id(0) == 0)
    def _():
        state_ref[...] = jnp.zeros_like(state_ref)

    beta, inverse = step_sizes(low_ref, kq_ref, weight_ref, bias_ref, states)
    rates = beta * inverse
    rate_ref[...] = by_eights(rates)
    input_ref[...] = by_eights(rates * values_ref[...].astype(jnp.float32))
    row_ref[...] = by_eights(kq_ref[...])
    spread_columns(row_ref, key_ref, query_ref, rows, states)

    for first in range(0, tiles, per_group):
        columns = [slice((first + j) * LANE, (first + j + 1) * LANE) for j in range(per_group)]

        def body(group, carry):
            carry = list(carry)
            for offset in range(8):
                t = group * 8 + offset
                at = pl.multiple_of(t * states, states)
                key = key_ref[pl.ds(at, states), :]
                query = query_ref[pl.ds(at, states), :]
                square = key * key
                for j, cols in enumerate(columns):
                    history_ref[pl.ds(at, states), cols] = carry[j].astype(jnp.bfloat16)
                    rate = rate_ref[group, offset : offset + 1, cols]
                    fed = input_ref[group, offset : offset + 1, cols]
                    carry[j] = (1.0 - rate * square) * carry[j] + key * fed
                    out_ref[group, offset : offset + 1, cols] = jnp.sum(query * carry[j], axis=0, keepdims=True)
            return tuple(carry)

        done = lax.fori_loop(0, rows // 8, body, tuple(state_ref[:, cols] for cols in columns))
        for cols, state in zip(columns, done):
            state_ref[:, cols] = state

    mixed = as_rows(out_ref[...]) + skip_ref[...] * values_ref[...].astype(jnp.float32)
    gate = gate_ref[...]
    mixed_ref[...] = mixed
    gated_ref[...] = (mixed * gate * sigmoid(gate)).astype(jnp.bfloat16)

    @pl.when(pl.program_id(0) == pl.num_programs(0) - 1)
    def _():
        final_ref[...] = state_ref[...]


def forward_scan(low, kq, values, gate, weight, bias, skip, states):
    length, channels = values.shape
    rank = low.shape[1]
    rows = min(128, length)
    blocks = length // rows
    by_row = lambda width: pl.BlockSpec((rows, width), lambda i: (i, 0))
    whole = lambda a: pl.BlockSpec(a.shape, lambda i: (0, 0))
    return pl.pallas_call(
        lambda *refs: forward_body(states, *refs),
        grid=(blocks,),
        in_specs=[by_row(rank), by_row(LANE), by_row(channels), by_row(channels), whole(weight), whole(bias), whole(skip)],
        out_specs=[
            by_row(channels),
            by_row(channels),
            pl.BlockSpec((rows * states, channels), lambda i: (i, 0)),
            pl.BlockSpec((states, channels), lambda i: (0, 0)),
        ],
        out_shape=[
            jax.ShapeDtypeStruct((length, channels), jnp.bfloat16),
            jax.ShapeDtypeStruct((length, channels), jnp.float32),
            jax.ShapeDtypeStruct((length * states, channels), jnp.bfloat16),
            jax.ShapeDtypeStruct((states, channels), jnp.float32),
        ],
        scratch_shapes=[
            pltpu.VMEM((states, channels), jnp.float32),
            pltpu.VMEM((rows * states, LANE), jnp.float32),
            pltpu.VMEM((rows * states, LANE), jnp.float32),
            pltpu.VMEM((rows // 8, 8, channels), jnp.float32),
            pltpu.VMEM((rows // 8, 8, channels), jnp.float32),
            pltpu.VMEM((rows // 8, 8, channels), jnp.float32),
            pltpu.VMEM((rows // 8, 8, LANE), jnp.float32),
        ],
        compiler_params=pltpu.CompilerParams(vmem_limit_bytes=48 * 1024 * 1024),
        cost_estimate=pl.CostEstimate(flops=14 * length * states * channels, bytes_accessed=2 * length * states * channels, transcendentals=0),
    )(low, kq, values, gate, weight, bias, skip)


def backward_body(
    states, low_ref, kq_ref, values_ref, gate_ref, mixed_ref, dgated_ref, history_ref, final_ref, weight_ref, bias_ref, skip_ref,
    dgate_ref, dpre_ref, dvalues_ref, dlow_ref, dkq_ref, bias_grad_ref, skip_grad_ref,
    grad_ref, state_ref, key_ref, query_ref, rate_ref, do_ref, values32_ref, fed_ref, kept_ref, part_key_ref, part_query_ref, row_ref, placed_ref,
):
    rows, channels = values_ref.shape
    tiles = channels // LANE
    per_group = min(4, tiles)

    @pl.when(pl.program_id(0) == 0)
    def _():
        grad_ref[...] = jnp.zeros_like(grad_ref)
        state_ref[...] = final_ref[...]
        bias_grad_ref[...] = jnp.zeros_like(bias_grad_ref)
        skip_grad_ref[...] = jnp.zeros_like(skip_grad_ref)

    beta, inverse = step_sizes(low_ref, kq_ref, weight_ref, bias_ref, states)
    rate_ref[...] = by_eights(beta * inverse)
    values = values_ref[...].astype(jnp.float32)
    values32_ref[...] = by_eights(values)
    gate = gate_ref[...]
    dgated = dgated_ref[...].astype(jnp.float32)
    s = sigmoid(gate)
    do = dgated * (gate * s)
    do_ref[...] = by_eights(do)
    dgate_ref[...] = (dgated * mixed_ref[...] * (s + gate * s * (1.0 - s))).astype(jnp.bfloat16)
    skip_grad_ref[...] += jnp.sum(do * values, axis=0, keepdims=True)
    row_ref[...] = by_eights(kq_ref[...])
    spread_columns(row_ref, key_ref, query_ref, rows, states)

    for first in range(0, tiles, per_group):
        columns = [slice((first + j) * LANE, (first + j + 1) * LANE) for j in range(per_group)]

        def body(step, carry):
            grads, lates = list(carry[0]), list(carry[1])
            group = rows // 8 - 1 - step
            for offset in reversed(range(8)):
                t = group * 8 + offset
                at = pl.multiple_of(t * states, states)
                key = key_ref[pl.ds(at, states), :]
                query = query_ref[pl.ds(at, states), :]
                sum_key = None
                sum_query = None
                for j, cols in enumerate(columns):
                    rate = rate_ref[group, offset : offset + 1, cols]
                    out_grad = do_ref[group, offset : offset + 1, cols]
                    value = values32_ref[group, offset : offset + 1, cols]
                    before = history_ref[pl.ds(at, states), cols].astype(jnp.float32)
                    grad = grads[j] + query * out_grad
                    scaled = rate * grad
                    by_key = key * scaled
                    kept = scaled * before
                    fed_ref[group, offset : offset + 1, cols] = jnp.sum(by_key, axis=0, keepdims=True)
                    kept_ref[group, offset : offset + 1, cols] = jnp.sum(key * (key * kept), axis=0, keepdims=True)
                    term_key = value * scaled - 2.0 * (key * kept)
                    term_query = lates[j] * out_grad
                    sum_key = term_key if sum_key is None else sum_key + term_key
                    sum_query = term_query if sum_query is None else sum_query + term_query
                    grads[j] = grad - key * by_key
                    lates[j] = before
                if first == 0:
                    part_key_ref[pl.ds(at, states), :] = sum_key
                    part_query_ref[pl.ds(at, states), :] = sum_query
                else:
                    part_key_ref[pl.ds(at, states), :] += sum_key
                    part_query_ref[pl.ds(at, states), :] += sum_query
            return (tuple(grads), tuple(lates))

        start = (tuple(grad_ref[:, cols] for cols in columns), tuple(state_ref[:, cols] for cols in columns))
        grads, lates = lax.fori_loop(0, rows // 8, body, start)
        for cols, grad, late in zip(columns, grads, lates):
            grad_ref[:, cols] = grad
            state_ref[:, cols] = late

    fed = as_rows(fed_ref[...])
    dvalues_ref[...] = fed + skip_ref[...] * as_rows(do_ref[...])
    scaled = as_rows(values32_ref[...]) * fed - as_rows(kept_ref[...])
    beta, inverse = step_sizes(low_ref, kq_ref, weight_ref, bias_ref, states)
    dpre = scaled * (1.0 - beta) * inverse
    bias_grad_ref[...] += jnp.sum(dpre, axis=0, keepdims=True)
    dpre_low = dpre.astype(jnp.bfloat16)
    dpre_ref[...] = dpre_low
    dlow_ref[...] = jnp.dot(dpre_low, weight_ref[...], preferred_element_type=jnp.float32)
    through = -2.0 * jnp.sum(scaled * beta * inverse, axis=1, keepdims=True)

    lane = lax.broadcasted_iota(jnp.int32, (states, LANE), 1)
    entry = lax.broadcasted_iota(jnp.int32, (states, LANE), 0)

    def gather(group, carry):
        for offset in range(8):
            t = group * 8 + offset
            at = pl.multiple_of(t * states, states)
            key = jnp.sum(part_key_ref[pl.ds(at, states), :], axis=1, keepdims=True)
            query = jnp.sum(part_query_ref[pl.ds(at, states), :], axis=1, keepdims=True)
            placed = jnp.where(lane == entry, key, 0.0) + jnp.where(lane == entry + states, query, 0.0)
            placed_ref[group, offset : offset + 1, :] = jnp.sum(placed, axis=0, keepdims=True)
        return carry

    lax.fori_loop(0, rows // 8, gather, 0)
    lanes = lax.broadcasted_iota(jnp.int32, kq_ref.shape, 1)
    dkq_ref[...] = as_rows(placed_ref[...]) + jnp.where(lanes < states, kq_ref[...] * through, 0.0)


def backward_scan(low, kq, values, gate, mixed, dgated, history, final, weight, bias, skip, states):
    length, channels = values.shape
    rank = low.shape[1]
    rows = min(128, length)
    blocks = length // rows
    by_row = lambda width: pl.BlockSpec((rows, width), lambda i: (blocks - 1 - i, 0))
    whole = lambda a: pl.BlockSpec(a.shape, lambda i: (0, 0))
    total = pl.BlockSpec((1, channels), lambda i: (0, 0))
    wide = pltpu.VMEM((rows // 8, 8, channels), jnp.float32)
    spread = pltpu.VMEM((rows * states, LANE), jnp.float32)
    return pl.pallas_call(
        lambda *refs: backward_body(states, *refs),
        grid=(blocks,),
        in_specs=[
            by_row(rank), by_row(LANE), by_row(channels), by_row(channels), by_row(channels), by_row(channels),
            pl.BlockSpec((rows * states, channels), lambda i: (blocks - 1 - i, 0)),
            whole(final), whole(weight), whole(bias), whole(skip),
        ],
        out_specs=[by_row(channels), by_row(channels), by_row(channels), by_row(rank), by_row(LANE), total, total],
        out_shape=[
            jax.ShapeDtypeStruct((length, channels), jnp.bfloat16),
            jax.ShapeDtypeStruct((length, channels), jnp.bfloat16),
            jax.ShapeDtypeStruct((length, channels), jnp.float32),
            jax.ShapeDtypeStruct((length, rank), jnp.float32),
            jax.ShapeDtypeStruct((length, LANE), jnp.float32),
            jax.ShapeDtypeStruct((1, channels), jnp.float32),
            jax.ShapeDtypeStruct((1, channels), jnp.float32),
        ],
        scratch_shapes=[
            pltpu.VMEM((states, channels), jnp.float32),
            pltpu.VMEM((states, channels), jnp.float32),
            spread, spread, wide, wide, wide, wide, wide, spread, spread,
            pltpu.VMEM((rows // 8, 8, LANE), jnp.float32), pltpu.VMEM((rows // 8, 8, LANE), jnp.float32),
        ],
        compiler_params=pltpu.CompilerParams(vmem_limit_bytes=56 * 1024 * 1024),
        cost_estimate=pl.CostEstimate(flops=30 * length * states * channels, bytes_accessed=2 * length * states * channels, transcendentals=0),
    )(low, kq, values, gate, mixed, dgated, history, final, weight, bias, skip)


def contract(left, right, left_dim, right_dim):
    return lax.dot_general(
        left, right, (((left_dim,), (right_dim,)), ((), ())), preferred_element_type=jnp.float32
    )


def gathered(shard, axis):
    return lax.all_gather(shard, axis, axis=0, tiled=True)


def scattered(total, axis):
    return lax.psum_scatter(total, axis, scatter_dimension=0, tiled=True)


def summed_rows(partial, axis):
    size = lax.axis_size(axis)
    parts = partial.astype(jnp.bfloat16).reshape((size, partial.shape[0] // size) + partial.shape[1:])
    parts = lax.all_to_all(parts, axis, 0, 0)
    return jnp.sum(parts.astype(jnp.float32), axis=0)


def later(rows, by):
    if by == 0:
        return rows
    return jnp.pad(rows, ((by, 0), (0, 0)))[: rows.shape[0]]


def sooner(rows, by):
    if by == 0:
        return rows
    return jnp.pad(rows, ((0, by), (0, 0)))[by:]


def local(
    tokens,
    cotangent,
    norm_gain,
    in_weight,
    conv_weight,
    conv_bias,
    select_weight,
    beta_weight,
    beta_bias,
    skip_gain,
    out_weight,
):
    parts, dps = lax.axis_size("seq"), lax.axis_size("dp")
    rows, width = tokens.shape[1:]
    block = conv_weight.shape[0]
    channels = block * dps
    taps = conv_weight.shape[1]
    rank = beta_weight.shape[1]
    states = (select_weight.shape[1] - rank) // 2
    own = in_weight.shape[0]

    gain = gathered(norm_gain, ("dp", "seq")).astype(jnp.float32)
    flat = tokens.reshape(rows, width).astype(jnp.float32)
    scale = lax.rsqrt(jnp.mean(flat * flat, axis=-1, keepdims=True) + 1e-05)
    normed = gathered((flat * scale * gain).astype(jnp.bfloat16), "seq")
    spread = in_weight.reshape(own, 2, dps, parts, block).transpose(3, 0, 1, 2, 4).reshape(parts, own, 2 * channels)
    in_w = gathered(lax.all_to_all(spread, "seq", 0, 0).reshape(parts * own, 2 * channels), "dp")
    conv_w = gathered(conv_weight, "dp").astype(jnp.float32)
    conv_b = gathered(conv_bias, "dp").astype(jnp.float32)
    select_w = gathered(select_weight, "dp")
    beta_w = gathered(beta_weight, "dp")
    beta_b = gathered(beta_bias, "dp").astype(jnp.float32).reshape(1, channels)
    skip = gathered(skip_gain, "dp").astype(jnp.float32).reshape(1, channels)
    out_w = gathered(out_weight, "dp")
    cot = gathered(cotangent.reshape(rows, width), "seq")

    conv_in = jnp.dot(normed, in_w[:, :channels], preferred_element_type=jnp.float32).astype(jnp.bfloat16)
    gate = jnp.dot(normed, in_w[:, channels:], preferred_element_type=jnp.float32)
    conv_wide = conv_in.astype(jnp.float32)
    conv_sum = conv_b
    for tap in range(taps):
        conv_sum = conv_sum + later(conv_wide, taps - 1 - tap) * conv_w[:, tap]
    values = jax.nn.silu(conv_sum).astype(jnp.bfloat16)
    projected = lax.psum(jnp.dot(values, select_w, preferred_element_type=jnp.float32), "seq")
    low = projected[:, :rank].astype(jnp.bfloat16)
    kq = jnp.pad(projected[:, rank:], ((0, 0), (0, LANE - 2 * states)))

    gated, mixed, history, final = forward_scan(low, kq, values, gate, beta_w, beta_b, skip, states)
    result_part = jnp.dot(gated, out_w, preferred_element_type=jnp.float32)
    result = (flat + summed_rows(result_part, "seq")).astype(jnp.bfloat16)
    out_grad = summed_rows(contract(gated, cot, 0, 0), "dp")
    dgated = contract(cot, out_w, 1, 1)
    dgate, dpre_low, dvalues, dlow, dkq, bias_grad, skip_grad = backward_scan(
        low, kq, values, gate, mixed, dgated, history, final, beta_w, beta_b, skip, states
    )
    dprojected = lax.psum(jnp.concatenate([dlow, dkq[:, : 2 * states]], axis=1), "seq").astype(jnp.bfloat16)
    beta_grad = scattered(contract(dpre_low, low, 0, 0), "dp")
    select_grad = scattered(contract(values, dprojected, 0, 0), "dp")
    dvalues = contract(dprojected, select_w, 1, 1) + dvalues
    s = jax.nn.sigmoid(conv_sum)
    dconv = dvalues * (s + conv_sum * s * (1.0 - s))
    conv_w_grad = jnp.stack(
        [jnp.sum(dconv * later(conv_wide, taps - 1 - tap), axis=0) for tap in range(taps)], axis=1
    )
    conv_b_grad = jnp.sum(dconv, axis=0)
    dconv_in = 0.0
    for tap in range(taps):
        dconv_in = dconv_in + sooner(dconv, taps - 1 - tap) * conv_w[:, tap]
    dmixed = jnp.concatenate([dconv_in.astype(jnp.bfloat16), dgate], axis=1)
    in_grad = summed_rows(contract(normed, dmixed, 0, 0), "dp").astype(jnp.bfloat16)
    in_grad = lax.all_to_all(in_grad.reshape(parts, own, 2 * channels), "seq", 0, 0)
    in_grad = in_grad.reshape(parts, own, 2, dps, block).transpose(1, 2, 3, 0, 4).reshape(own, 2 * parts * channels)
    dnormed = summed_rows(contract(dmixed, in_w, 1, 1), "seq")
    v = dnormed * gain
    du = scale * v - flat * (scale * scale * scale) * jnp.mean(flat * v, axis=-1, keepdims=True)
    input_grad = (cotangent.reshape(rows, width).astype(jnp.float32) + du).astype(jnp.bfloat16)
    gain_grad = scattered(jnp.sum(dnormed * flat * scale, axis=0), ("dp", "seq"))
    rows_grad = scattered(
        jnp.concatenate(
            [conv_w_grad, conv_b_grad[:, None], bias_grad.reshape(channels, 1), skip_grad.reshape(channels, 1)], axis=1
        ),
        "dp",
    )
    return (
        result.reshape(tokens.shape),
        input_grad.reshape(tokens.shape),
        gain_grad,
        in_grad.astype(jnp.float32),
        rows_grad[:, :taps],
        rows_grad[:, taps],
        select_grad,
        beta_grad,
        rows_grad[:, taps + 1],
        rows_grad[:, taps + 2],
        out_grad,
    )


def solution(mesh):
    split = P(("dp", "seq"))
    rows = P("dp", "seq", None)
    return jax.shard_map(
        local,
        mesh=mesh,
        in_specs=(rows, rows) + (split,) * 9,
        out_specs=(rows, rows) + (split,) * 9,
        check_vma=False,
    )
```

```python
import jax
import jax.numpy as jnp
from jax import lax
from jax.experimental import pallas as pl
from jax.experimental.pallas import tpu as pltpu
from jax.sharding import PartitionSpec as P

LANE = 128


def sigmoid(v):
    return 1.0 / (1.0 + jnp.exp(-v))


def by_eights(value):
    return value.reshape(value.shape[0] // 8, 8, value.shape[1])


def as_rows(value):
    return value.reshape(value.shape[0] * 8, value.shape[2])


def spread_columns(row_ref, key_ref, query_ref, rows, states):
    lane = lax.broadcasted_iota(jnp.int32, (states, LANE), 1)
    entry = lax.broadcasted_iota(jnp.int32, (states, LANE), 0)
    pick_key = lane == entry
    pick_query = lane == entry + states

    def body(group, carry):
        for offset in range(8):
            t = group * 8 + offset
            row = jnp.broadcast_to(row_ref[group, offset : offset + 1, :], (states, LANE))
            at = pl.multiple_of(t * states, states)
            key = jnp.sum(jnp.where(pick_key, row, 0.0), axis=1, keepdims=True)
            query = jnp.sum(jnp.where(pick_query, row, 0.0), axis=1, keepdims=True)
            key_ref[pl.ds(at, states), :] = jnp.broadcast_to(key, (states, LANE))
            query_ref[pl.ds(at, states), :] = jnp.broadcast_to(query, (states, LANE))
        return carry

    lax.fori_loop(0, rows // 8, body, 0)


def step_sizes(low_ref, kq_ref, weight_ref, bias_ref, states):
    pre = lax.dot_general(
        low_ref[...], weight_ref[...], (((1,), (1,)), ((), ())), preferred_element_type=jnp.float32
    )
    beta = sigmoid(pre + bias_ref[...])
    lane = lax.broadcasted_iota(jnp.int32, kq_ref.shape, 1)
    keys = jnp.where(lane < states, kq_ref[...], 0.0)
    square = jnp.sum(keys * keys, axis=1, keepdims=True)
    return beta, 1.0 / (1.0 + beta * square)


def forward_body(
    states, low_ref, kq_ref, values_ref, gate_ref, weight_ref, bias_ref, skip_ref,
    gated_ref, mixed_ref, history_ref, final_ref,
    state_ref, key_ref, query_ref, rate_ref, input_ref, out_ref, row_ref,
):
    rows, channels = values_ref.shape
    tiles = channels // LANE
    per_group = min(4, tiles)

    @pl.when(pl.program_id(0) == 0)
    def _():
        state_ref[...] = jnp.zeros_like(state_ref)

    beta, inverse = step_sizes(low_ref, kq_ref, weight_ref, bias_ref, states)
    rates = beta * inverse
    rate_ref[...] = by_eights(rates)
    input_ref[...] = by_eights(rates * values_ref[...].astype(jnp.float32))
    row_ref[...] = by_eights(kq_ref[...])
    spread_columns(row_ref, key_ref, query_ref, rows, states)

    for first in range(0, tiles, per_group):
        columns = [slice((first + j) * LANE, (first + j + 1) * LANE) for j in range(per_group)]

        def body(group, carry):
            carry = list(carry)
            for offset in range(8):
                t = group * 8 + offset
                at = pl.multiple_of(t * states, states)
                key = key_ref[pl.ds(at, states), :]
                query = query_ref[pl.ds(at, states), :]
                square = key * key
                for j, cols in enumerate(columns):
                    history_ref[pl.ds(at, states), cols] = carry[j].astype(jnp.bfloat16)
                    rate = rate_ref[group, offset : offset + 1, cols]
                    fed = input_ref[group, offset : offset + 1, cols]
                    carry[j] = (1.0 - rate * square) * carry[j] + key * fed
                    out_ref[group, offset : offset + 1, cols] = jnp.sum(query * carry[j], axis=0, keepdims=True)
            return tuple(carry)

        done = lax.fori_loop(0, rows // 8, body, tuple(state_ref[:, cols] for cols in columns))
        for cols, state in zip(columns, done):
            state_ref[:, cols] = state

    mixed = as_rows(out_ref[...]) + skip_ref[...] * values_ref[...].astype(jnp.float32)
    gate = gate_ref[...]
    mixed_ref[...] = mixed
    gated_ref[...] = (mixed * gate * sigmoid(gate)).astype(jnp.bfloat16)

    @pl.when(pl.program_id(0) == pl.num_programs(0) - 1)
    def _():
        final_ref[...] = state_ref[...]


def forward_scan(low, kq, values, gate, weight, bias, skip, states):
    length, channels = values.shape
    rank = low.shape[1]
    rows = min(128, length)
    blocks = length // rows
    by_row = lambda width: pl.BlockSpec((rows, width), lambda i: (i, 0))
    whole = lambda a: pl.BlockSpec(a.shape, lambda i: (0, 0))
    return pl.pallas_call(
        lambda *refs: forward_body(states, *refs),
        grid=(blocks,),
        in_specs=[by_row(rank), by_row(LANE), by_row(channels), by_row(channels), whole(weight), whole(bias), whole(skip)],
        out_specs=[
            by_row(channels),
            by_row(channels),
            pl.BlockSpec((rows * states, channels), lambda i: (i, 0)),
            pl.BlockSpec((states, channels), lambda i: (0, 0)),
        ],
        out_shape=[
            jax.ShapeDtypeStruct((length, channels), jnp.bfloat16),
            jax.ShapeDtypeStruct((length, channels), jnp.float32),
            jax.ShapeDtypeStruct((length * states, channels), jnp.bfloat16),
            jax.ShapeDtypeStruct((states, channels), jnp.float32),
        ],
        scratch_shapes=[
            pltpu.VMEM((states, channels), jnp.float32),
            pltpu.VMEM((rows * states, LANE), jnp.float32),
            pltpu.VMEM((rows * states, LANE), jnp.float32),
            pltpu.VMEM((rows // 8, 8, channels), jnp.float32),
            pltpu.VMEM((rows // 8, 8, channels), jnp.float32),
            pltpu.VMEM((rows // 8, 8, channels), jnp.float32),
            pltpu.VMEM((rows // 8, 8, LANE), jnp.float32),
        ],
        compiler_params=pltpu.CompilerParams(vmem_limit_bytes=48 * 1024 * 1024),
        cost_estimate=pl.CostEstimate(flops=14 * length * states * channels, bytes_accessed=2 * length * states * channels, transcendentals=0),
    )(low, kq, values, gate, weight, bias, skip)


def backward_body(
    states, low_ref, kq_ref, values_ref, gate_ref, mixed_ref, dgated_ref, history_ref, final_ref, weight_ref, bias_ref, skip_ref,
    dgate_ref, dpre_ref, dvalues_ref, dlow_ref, dkq_ref, bias_grad_ref, skip_grad_ref,
    grad_ref, state_ref, key_ref, query_ref, rate_ref, do_ref, values32_ref, fed_ref, kept_ref, part_key_ref, part_query_ref, row_ref, placed_ref,
):
    rows, channels = values_ref.shape
    tiles = channels // LANE
    per_group = min(4, tiles)

    @pl.when(pl.program_id(0) == 0)
    def _():
        grad_ref[...] = jnp.zeros_like(grad_ref)
        state_ref[...] = final_ref[...]
        bias_grad_ref[...] = jnp.zeros_like(bias_grad_ref)
        skip_grad_ref[...] = jnp.zeros_like(skip_grad_ref)

    beta, inverse = step_sizes(low_ref, kq_ref, weight_ref, bias_ref, states)
    rate_ref[...] = by_eights(beta * inverse)
    values = values_ref[...].astype(jnp.float32)
    values32_ref[...] = by_eights(values)
    gate = gate_ref[...]
    dgated = dgated_ref[...].astype(jnp.float32)
    s = sigmoid(gate)
    do = dgated * (gate * s)
    do_ref[...] = by_eights(do)
    dgate_ref[...] = (dgated * mixed_ref[...] * (s + gate * s * (1.0 - s))).astype(jnp.bfloat16)
    skip_grad_ref[...] += jnp.sum(do * values, axis=0, keepdims=True)
    row_ref[...] = by_eights(kq_ref[...])
    spread_columns(row_ref, key_ref, query_ref, rows, states)

    for first in range(0, tiles, per_group):
        columns = [slice((first + j) * LANE, (first + j + 1) * LANE) for j in range(per_group)]

        def body(step, carry):
            grads, lates = list(carry[0]), list(carry[1])
            group = rows // 8 - 1 - step
            for offset in reversed(range(8)):
                t = group * 8 + offset
                at = pl.multiple_of(t * states, states)
                key = key_ref[pl.ds(at, states), :]
                query = query_ref[pl.ds(at, states), :]
                sum_key = None
                sum_query = None
                for j, cols in enumerate(columns):
                    rate = rate_ref[group, offset : offset + 1, cols]
                    out_grad = do_ref[group, offset : offset + 1, cols]
                    value = values32_ref[group, offset : offset + 1, cols]
                    before = history_ref[pl.ds(at, states), cols].astype(jnp.float32)
                    grad = grads[j] + query * out_grad
                    scaled = rate * grad
                    by_key = key * scaled
                    kept = scaled * before
                    fed_ref[group, offset : offset + 1, cols] = jnp.sum(by_key, axis=0, keepdims=True)
                    kept_ref[group, offset : offset + 1, cols] = jnp.sum(key * (key * kept), axis=0, keepdims=True)
                    term_key = value * scaled - 2.0 * (key * kept)
                    term_query = lates[j] * out_grad
                    sum_key = term_key if sum_key is None else sum_key + term_key
                    sum_query = term_query if sum_query is None else sum_query + term_query
                    grads[j] = grad - key * by_key
                    lates[j] = before
                if first == 0:
                    part_key_ref[pl.ds(at, states), :] = sum_key
                    part_query_ref[pl.ds(at, states), :] = sum_query
                else:
                    part_key_ref[pl.ds(at, states), :] += sum_key
                    part_query_ref[pl.ds(at, states), :] += sum_query
            return (tuple(grads), tuple(lates))

        start = (tuple(grad_ref[:, cols] for cols in columns), tuple(state_ref[:, cols] for cols in columns))
        grads, lates = lax.fori_loop(0, rows // 8, body, start)
        for cols, grad, late in zip(columns, grads, lates):
            grad_ref[:, cols] = grad
            state_ref[:, cols] = late

    fed = as_rows(fed_ref[...])
    dvalues_ref[...] = fed + skip_ref[...] * as_rows(do_ref[...])
    scaled = as_rows(values32_ref[...]) * fed - as_rows(kept_ref[...])
    beta, inverse = step_sizes(low_ref, kq_ref, weight_ref, bias_ref, states)
    dpre = scaled * (1.0 - beta) * inverse
    bias_grad_ref[...] += jnp.sum(dpre, axis=0, keepdims=True)
    dpre_low = dpre.astype(jnp.bfloat16)
    dpre_ref[...] = dpre_low
    dlow_ref[...] = jnp.dot(dpre_low, weight_ref[...], preferred_element_type=jnp.float32)
    through = -2.0 * jnp.sum(scaled * beta * inverse, axis=1, keepdims=True)

    lane = lax.broadcasted_iota(jnp.int32, (states, LANE), 1)
    entry = lax.broadcasted_iota(jnp.int32, (states, LANE), 0)

    def gather(group, carry):
        for offset in range(8):
            t = group * 8 + offset
            at = pl.multiple_of(t * states, states)
            key = jnp.sum(part_key_ref[pl.ds(at, states), :], axis=1, keepdims=True)
            query = jnp.sum(part_query_ref[pl.ds(at, states), :], axis=1, keepdims=True)
            placed = jnp.where(lane == entry, key, 0.0) + jnp.where(lane == entry + states, query, 0.0)
            placed_ref[group, offset : offset + 1, :] = jnp.sum(placed, axis=0, keepdims=True)
        return carry

    lax.fori_loop(0, rows // 8, gather, 0)
    lanes = lax.broadcasted_iota(jnp.int32, kq_ref.shape, 1)
    dkq_ref[...] = as_rows(placed_ref[...]) + jnp.where(lanes < states, kq_ref[...] * through, 0.0)


def backward_scan(low, kq, values, gate, mixed, dgated, history, final, weight, bias, skip, states):
    length, channels = values.shape
    rank = low.shape[1]
    rows = min(128, length)
    blocks = length // rows
    by_row = lambda width: pl.BlockSpec((rows, width), lambda i: (blocks - 1 - i, 0))
    whole = lambda a: pl.BlockSpec(a.shape, lambda i: (0, 0))
    total = pl.BlockSpec((1, channels), lambda i: (0, 0))
    wide = pltpu.VMEM((rows // 8, 8, channels), jnp.float32)
    spread = pltpu.VMEM((rows * states, LANE), jnp.float32)
    return pl.pallas_call(
        lambda *refs: backward_body(states, *refs),
        grid=(blocks,),
        in_specs=[
            by_row(rank), by_row(LANE), by_row(channels), by_row(channels), by_row(channels), by_row(channels),
            pl.BlockSpec((rows * states, channels), lambda i: (blocks - 1 - i, 0)),
            whole(final), whole(weight), whole(bias), whole(skip),
        ],
        out_specs=[by_row(channels), by_row(channels), by_row(channels), by_row(rank), by_row(LANE), total, total],
        out_shape=[
            jax.ShapeDtypeStruct((length, channels), jnp.bfloat16),
            jax.ShapeDtypeStruct((length, channels), jnp.bfloat16),
            jax.ShapeDtypeStruct((length, channels), jnp.float32),
            jax.ShapeDtypeStruct((length, rank), jnp.float32),
            jax.ShapeDtypeStruct((length, LANE), jnp.float32),
            jax.ShapeDtypeStruct((1, channels), jnp.float32),
            jax.ShapeDtypeStruct((1, channels), jnp.float32),
        ],
        scratch_shapes=[
            pltpu.VMEM((states, channels), jnp.float32),
            pltpu.VMEM((states, channels), jnp.float32),
            spread, spread, wide, wide, wide, wide, wide, spread, spread,
            pltpu.VMEM((rows // 8, 8, LANE), jnp.float32), pltpu.VMEM((rows // 8, 8, LANE), jnp.float32),
        ],
        compiler_params=pltpu.CompilerParams(vmem_limit_bytes=56 * 1024 * 1024),
        cost_estimate=pl.CostEstimate(flops=30 * length * states * channels, bytes_accessed=2 * length * states * channels, transcendentals=0),
    )(low, kq, values, gate, mixed, dgated, history, final, weight, bias, skip)


MESH = pl.DeviceIdType.MESH
GAIN_ROWS = 16


def plane_mates(d):
    core, x, y = lax.rem(d, 2), lax.rem(d // 2, 2), d // 4
    return d + 1 - 2 * core, d + 2 - 4 * x, d + 4 - 8 * y


def start_body(
    parts, block,
    tokens_ref, spread_ref, extra_ref, gain_ref,
    normed_out, weight_out, conv_ref, gate_ref, extra_out,
    tokens_all, normed_all, weight_all, extra_all,
    near_send, near_recv, plane_send, plane_recv, gain_send, gain_recv, line_send, line_recv, local_sem,
):
    d, s = lax.axis_index("dp"), lax.axis_index("seq")
    sib, xm, ym = plane_mates(d)
    own = spread_ref.shape[1]
    rows, width = tokens_ref.shape
    small = extra_ref.shape[0]
    channels = conv_ref.shape[1]
    chunk = rows // 4

    barrier = pltpu.get_barrier_semaphore()
    for mate in (sib, xm, ym):
        pl.semaphore_signal(barrier, inc=1, device_id=(mate, s), device_id_type=MESH)
    for k in range(1, parts):
        pl.semaphore_signal(barrier, inc=1, device_id=(d, lax.rem(s + k, parts)), device_id_type=MESH)
    pl.semaphore_wait(barrier, 3 + parts - 1)

    def remote(src, dst, send, recv, to):
        return pltpu.make_async_remote_copy(
            src_ref=src, dst_ref=dst, send_sem=send, recv_sem=recv, device_id=to, device_id_type=MESH
        )

    def weight_rows(owner, source):
        return weight_all.at[pl.ds(pl.multiple_of((owner * parts + source) * own, own), own), :]

    def extra_rows(owner):
        return extra_all.at[owner]

    def gain_rows(source):
        return extra_all.at[d, pl.ds(pl.multiple_of(small + source * GAIN_ROWS, GAIN_ROWS), GAIN_ROWS), pl.ds(0, LANE)]

    near = []
    for k in range(1, parts):
        to = (d, lax.rem(s + k, parts))
        near.append(remote(spread_ref.at[to[1]], weight_rows(d, s), near_send.at[k], near_recv.at[k], to))
        near.append(remote(gain_ref, gain_rows(s), gain_send.at[k], gain_recv.at[k], to))
    for copy in near:
        copy.start()
    mine = [
        pltpu.make_async_copy(spread_ref.at[s], weight_rows(d, s), local_sem.at[0]),
        pltpu.make_async_copy(gain_ref, gain_rows(s), local_sem.at[1]),
        pltpu.make_async_copy(extra_ref, extra_all.at[d, pl.ds(0, small), :], local_sem.at[2]),
        pltpu.make_async_copy(tokens_ref, tokens_all.at[pl.ds(pl.multiple_of(s * rows, rows), rows), :], local_sem.at[3]),
    ]
    for copy in mine:
        copy.start()

    def token_rows(part, c):
        return tokens_all.at[pl.ds(pl.multiple_of(part * rows + c * chunk, chunk), chunk), :]

    def token_copy(way, distance, c):
        part = s - way * (distance - 1)
        src = tokens_ref.at[pl.ds(c * chunk, chunk), :] if distance == 1 else token_rows(part, c)
        side = 0 if way == 1 else 1
        return remote(
            src, token_rows(part, c), line_send.at[side, distance, c], line_recv.at[side, distance, c], (d, s + way)
        )

    def can_send(way, distance):
        reach = s + 1 < parts if way == 1 else s >= 1
        came = s - (distance - 1) >= 0 if way == 1 else s + (distance - 1) < parts
        return jnp.logical_and(reach, came)

    def arrives(way, distance):
        return s >= distance if way == 1 else s + distance < parts

    def send_tokens(distance, c):
        for way in (1, -1):
            @pl.when(can_send(way, distance))
            def _():
                token_copy(way, distance, c).start()

    def sent_tokens(distance, c):
        for way in (1, -1):
            @pl.when(can_send(way, distance))
            def _():
                token_copy(way, distance, c).wait_send()

    def take_tokens(distance, c):
        for way in (1, -1):
            @pl.when(arrives(way, distance))
            def _():
                part = s - way * distance
                side = 0 if way == 1 else 1
                remote(
                    token_rows(part, c), token_rows(part, c), line_send.at[side, distance, c],
                    line_recv.at[side, distance, c], (d, s),
                ).wait_recv()

    units = parts + 1

    def unit(owner, k):
        return extra_rows(owner) if k == parts else weight_rows(owner, lax.rem(s - k + parts, parts))

    kinds = {"own": (d, 0), "x": (xm, 2), "y": (ym, 4)}

    def plane_copy(owner, k, rel, kind, to):
        return remote(unit(owner, k), unit(owner, k), plane_send.at[kind, k], plane_recv.at[rel, k], (to, s))

    diag = xm + ym - d
    sib_of = lambda mate: mate + sib - d

    def route(k):
        steps = [
            (0, d, 1, 0, sib), (0, d, 2, 1, xm), (0, d, 4, 2, ym),
            (2, xm, 3, 3, sib), (4, ym, 5, 5, sib), (6, diag, 7, 7, sib),
        ]
        steps.append((2, xm, 6, 4, ym) if k % 2 == 0 else (4, ym, 6, 6, xm))
        return steps

    def pass_on(stage, k):
        for at, owner, rel, kind, to in route(k):
            if at == stage:
                plane_copy(owner, k, rel, kind, to).start()

    owners = {1: sib, 2: xm, 3: sib_of(xm), 4: ym, 5: sib_of(ym), 6: diag, 7: sib_of(diag)}

    def take(rel, k):
        plane_copy(owners[rel], k, rel, 0, d).wait_recv()

    for c in range(4):
        send_tokens(1, c)
    mine[0].wait()
    pass_on(0, 0)
    for k in range(1, parts):
        near_wait = remote(
            spread_ref.at[s], weight_rows(d, lax.rem(s - k + parts, parts)), near_send.at[k], near_recv.at[k], (d, s)
        )
        near_wait.wait_recv()
        pass_on(0, k)
    mine[1].wait()
    mine[2].wait()
    for k in range(1, parts):
        remote(gain_ref, gain_rows(lax.rem(s - k + parts, parts)), gain_send.at[k], gain_recv.at[k], (d, s)).wait_recv()
    pass_on(0, parts)
    for k in range(units):
        take(2, k)
        pass_on(2, k)
        take(4, k)
        pass_on(4, k)
        if k < 4:
            take_tokens(1, k)
            send_tokens(2, k)
    for k in range(units):
        take(6, k)
        pass_on(6, k)
        if k < 4:
            take_tokens(2, k)
            send_tokens(3, k)
    for rel in (1, 3, 5, 7):
        for k in range(units):
            take(rel, k)
    mine[3].wait()
    weight_copy = pltpu.make_async_copy(weight_all, weight_out, local_sem.at[4])
    weight_copy.start()
    extra_out[...] = extra_all[...]

    lane = lax.broadcasted_iota(jnp.int32, (1, LANE), 1)
    pieces = []
    for owner in range(extra_all.shape[0]):
        for source in range(0, parts, 2):
            row = small + source * GAIN_ROWS
            even = extra_all[owner, row : row + GAIN_ROWS, 0:LANE].astype(jnp.float32)[0:1]
            odd = extra_all[owner, row + GAIN_ROWS : row + 2 * GAIN_ROWS, 0:LANE].astype(jnp.float32)[0:1]
            pieces.append(jnp.where(lane < own, even, odd))
    gain = jnp.concatenate(pieces, axis=1)

    tile = min(512, channels)

    def work(part):
        for c in range(4):
            at = pl.ds(pl.multiple_of(part * rows + c * chunk, chunk), chunk)
            flat = tokens_all[at, :].astype(jnp.float32)
            scale = lax.rsqrt(jnp.mean(flat * flat, axis=-1, keepdims=True) + 1e-05)
            normed_all[at, :] = (flat * scale * gain).astype(jnp.bfloat16)
        at = pl.ds(pl.multiple_of(part * rows, rows), rows)

        def columns(n, carry):
            left = pl.multiple_of(n * tile, tile)
            right = pl.multiple_of(channels + n * tile, tile)
            conv_ref[at, pl.ds(left, tile)] = jnp.dot(
                normed_all[at, :], weight_all[:, pl.ds(left, tile)], preferred_element_type=jnp.float32
            ).astype(jnp.bfloat16)
            gate_ref[at, pl.ds(left, tile)] = jnp.dot(
                normed_all[at, :], weight_all[:, pl.ds(right, tile)], preferred_element_type=jnp.float32
            )
            return carry

        lax.fori_loop(0, channels // tile, columns, 0)

    def work_at(low, high):
        def each(part, carry):
            away = jnp.abs(part - s)

            @pl.when(jnp.logical_and(away >= low, away <= high))
            def _():
                work(part)

            return carry

        lax.fori_loop(0, parts, each, 0)

    work_at(0, 2)
    for c in range(4):
        take_tokens(3, c)
    work_at(3, 3)
    normed_copy = pltpu.make_async_copy(normed_all, normed_out, local_sem.at[5])
    normed_copy.start()

    for copy in near:
        copy.wait_send()
    for k in range(units):
        for at, owner, rel, kind, to in route(k):
            plane_copy(owner, k, rel, kind, to).wait_send()
    for distance in range(1, parts):
        for c in range(4):
            sent_tokens(distance, c)
    weight_copy.wait()
    normed_copy.wait()


def start(tokens, spread, extra, gain, dps):
    parts, own, both = spread.shape
    rows, width = tokens.shape
    small, lanes = extra.shape
    any_space = pl.BlockSpec(memory_space=pl.ANY)
    vmem = pl.BlockSpec(memory_space=pltpu.VMEM)
    tall = small + parts * GAIN_ROWS
    dma = pltpu.SemaphoreType.DMA
    return pl.pallas_call(
        lambda *refs: start_body(parts, own, *refs),
        out_shape=[
            jax.ShapeDtypeStruct((parts * rows, width), jnp.bfloat16),
            jax.ShapeDtypeStruct((dps * parts * own, both), jnp.bfloat16),
            jax.ShapeDtypeStruct((parts * rows, both // 2), jnp.bfloat16),
            jax.ShapeDtypeStruct((parts * rows, both // 2), jnp.float32),
            jax.ShapeDtypeStruct((dps, tall, lanes), jnp.bfloat16),
        ],
        in_specs=[vmem, vmem, vmem, vmem],
        out_specs=[any_space, any_space, vmem, vmem, vmem],
        scratch_shapes=[
            pltpu.VMEM((parts * rows, width), jnp.bfloat16),
            pltpu.VMEM((parts * rows, width), jnp.bfloat16),
            pltpu.VMEM((dps * parts * own, both), jnp.bfloat16),
            pltpu.VMEM((dps, tall, lanes), jnp.bfloat16),
            dma((parts,)), dma((parts,)),
            dma((8, parts + 1)), dma((8, parts + 1)),
            dma((parts,)), dma((parts,)),
            dma((2, parts, 4)), dma((2, parts, 4)),
            dma((6,)),
        ],
        compiler_params=pltpu.CompilerParams(
            collective_id=1, has_side_effects=True, vmem_limit_bytes=56 * 1024 * 1024
        ),
        cost_estimate=pl.CostEstimate(
            flops=2 * parts * rows * width * both, bytes_accessed=40 * 1024 * 1024, transcendentals=0
        ),
    )(tokens, spread, extra, gain)


def contract(left, right, left_dim, right_dim):
    return lax.dot_general(
        left, right, (((left_dim,), (right_dim,)), ((), ())), preferred_element_type=jnp.float32
    )


def gathered(shard, axis):
    return lax.all_gather(shard, axis, axis=0, tiled=True)


def scattered(total, axis):
    return lax.psum_scatter(total, axis, scatter_dimension=0, tiled=True)


def summed_rows(partial, axis):
    size = lax.axis_size(axis)
    parts = partial.astype(jnp.bfloat16).reshape((size, partial.shape[0] // size) + partial.shape[1:])
    parts = lax.all_to_all(parts, axis, 0, 0)
    return jnp.sum(parts.astype(jnp.float32), axis=0)


def later(rows, by):
    if by == 0:
        return rows
    return jnp.pad(rows, ((by, 0), (0, 0)))[: rows.shape[0]]


def sooner(rows, by):
    if by == 0:
        return rows
    return jnp.pad(rows, ((0, by), (0, 0)))[by:]


def local(
    tokens,
    cotangent,
    norm_gain,
    in_weight,
    conv_weight,
    conv_bias,
    select_weight,
    beta_weight,
    beta_bias,
    skip_gain,
    out_weight,
):
    parts, dps = lax.axis_size("seq"), lax.axis_size("dp")
    rows, width = tokens.shape[1:]
    block = conv_weight.shape[0]
    channels = block * dps
    taps = conv_weight.shape[1]
    rank = beta_weight.shape[1]
    states = (select_weight.shape[1] - rank) // 2
    own = in_weight.shape[0]

    flat = tokens.reshape(rows, width).astype(jnp.float32)
    scale = lax.rsqrt(jnp.mean(flat * flat, axis=-1, keepdims=True) + 1e-05)
    spread = in_weight.reshape(own, 2, dps, parts, block).transpose(3, 0, 1, 2, 4).reshape(parts, own, 2 * channels)
    vectors = jnp.concatenate(
        [conv_weight, conv_bias[:, None], beta_bias[:, None], skip_gain[:, None]], axis=1
    )
    wide = -(-select_weight.shape[1] // LANE) * LANE
    small = jnp.concatenate(
        [
            jnp.pad(select_weight, ((0, 0), (0, wide - select_weight.shape[1]))),
            beta_weight,
            jnp.pad(vectors, ((0, 0), (0, LANE - vectors.shape[1]))),
        ],
        axis=1,
    )
    if (dps, parts, 2 * own) == (8, 4, LANE):
        doubled = jnp.broadcast_to(jnp.tile(norm_gain.reshape(1, own), (1, 2)), (GAIN_ROWS, LANE))
        normed, in_w, conv_in, gate, extra = start(tokens.reshape(rows, width), spread, small, doubled, dps)
        smalls = extra[:, :block].reshape(channels, small.shape[1])
        gain = extra[:, block:, :own].reshape(dps * parts, GAIN_ROWS, own)[:, 0].reshape(width)
    else:
        gain = gathered(norm_gain, ("dp", "seq"))
        normed = gathered((flat * scale * gain.astype(jnp.float32)).astype(jnp.bfloat16), "seq")
        in_w = gathered(lax.all_to_all(spread, "seq", 0, 0).reshape(parts * own, 2 * channels), "dp")
        smalls = gathered(small, "dp")
        conv_in = jnp.dot(normed, in_w[:, :channels], preferred_element_type=jnp.float32).astype(jnp.bfloat16)
        gate = jnp.dot(normed, in_w[:, channels:], preferred_element_type=jnp.float32)
    gain = gain.astype(jnp.float32)
    select_w = smalls[:, : select_weight.shape[1]]
    beta_w = smalls[:, wide : wide + rank]
    vectors = smalls[:, wide + rank :].astype(jnp.float32)
    conv_w, conv_b = vectors[:, :taps], vectors[:, taps]
    beta_b, skip = vectors[:, taps + 1].reshape(1, channels), vectors[:, taps + 2].reshape(1, channels)
    out_shard, cot_shard, conv_in = lax.optimization_barrier((out_weight, cotangent.reshape(rows, width), conv_in))
    out_w = gathered(out_shard, "dp")
    cot = gathered(cot_shard, "seq")

    conv_wide = conv_in.astype(jnp.float32)
    conv_sum = conv_b
    for tap in range(taps):
        conv_sum = conv_sum + later(conv_wide, taps - 1 - tap) * conv_w[:, tap]
    values = jax.nn.silu(conv_sum).astype(jnp.bfloat16)
    projected = lax.psum(jnp.dot(values, select_w, preferred_element_type=jnp.float32), "seq")
    low = projected[:, :rank].astype(jnp.bfloat16)
    kq = jnp.pad(projected[:, rank:], ((0, 0), (0, LANE - 2 * states)))

    gated, mixed, history, final = forward_scan(low, kq, values, gate, beta_w, beta_b, skip, states)
    result_part = jnp.dot(gated, out_w, preferred_element_type=jnp.float32)
    result = (flat + summed_rows(result_part, "seq")).astype(jnp.bfloat16)
    out_grad = summed_rows(contract(gated, cot, 0, 0), "dp")
    dgated = contract(cot, out_w, 1, 1)
    dgate, dpre_low, dvalues, dlow, dkq, bias_grad, skip_grad = backward_scan(
        low, kq, values, gate, mixed, dgated, history, final, beta_w, beta_b, skip, states
    )
    dprojected = lax.psum(jnp.concatenate([dlow, dkq[:, : 2 * states]], axis=1), "seq").astype(jnp.bfloat16)
    beta_grad = scattered(contract(dpre_low, low, 0, 0), "dp")
    select_grad = scattered(contract(values, dprojected, 0, 0), "dp")
    dvalues = contract(dprojected, select_w, 1, 1) + dvalues
    s = jax.nn.sigmoid(conv_sum)
    dconv = dvalues * (s + conv_sum * s * (1.0 - s))
    conv_w_grad = jnp.stack(
        [jnp.sum(dconv * later(conv_wide, taps - 1 - tap), axis=0) for tap in range(taps)], axis=1
    )
    conv_b_grad = jnp.sum(dconv, axis=0)
    dconv_in = 0.0
    for tap in range(taps):
        dconv_in = dconv_in + sooner(dconv, taps - 1 - tap) * conv_w[:, tap]
    dmixed = jnp.concatenate([dconv_in.astype(jnp.bfloat16), dgate], axis=1)
    in_grad = summed_rows(contract(normed, dmixed, 0, 0), "dp").astype(jnp.bfloat16)
    in_grad = lax.all_to_all(in_grad.reshape(parts, own, 2 * channels), "seq", 0, 0)
    in_grad = in_grad.reshape(parts, own, 2, dps, block).transpose(1, 2, 3, 0, 4).reshape(own, 2 * parts * channels)
    dnormed = summed_rows(contract(dmixed, in_w, 1, 1), "seq")
    v = dnormed * gain
    du = scale * v - flat * (scale * scale * scale) * jnp.mean(flat * v, axis=-1, keepdims=True)
    input_grad = (cotangent.reshape(rows, width).astype(jnp.float32) + du).astype(jnp.bfloat16)
    gain_grad = scattered(jnp.sum(dnormed * flat * scale, axis=0), ("dp", "seq"))
    rows_grad = scattered(
        jnp.concatenate(
            [conv_w_grad, conv_b_grad[:, None], bias_grad.reshape(channels, 1), skip_grad.reshape(channels, 1)], axis=1
        ),
        "dp",
    )
    return (
        result.reshape(tokens.shape),
        input_grad.reshape(tokens.shape),
        gain_grad,
        in_grad.astype(jnp.float32),
        rows_grad[:, :taps],
        rows_grad[:, taps],
        select_grad,
        beta_grad,
        rows_grad[:, taps + 1],
        rows_grad[:, taps + 2],
        out_grad,
    )


def solution(mesh):
    split = P(("dp", "seq"))
    rows = P("dp", "seq", None)
    return jax.shard_map(
        local,
        mesh=mesh,
        in_specs=(rows, rows) + (split,) * 9,
        out_specs=(rows, rows) + (split,) * 9,
        check_vma=False,
    )
```

```python
import jax
import jax.numpy as jnp
from jax import lax
from jax.experimental import pallas as pl
from jax.experimental.pallas import tpu as pltpu
from jax.sharding import PartitionSpec as P

LANE = 128


def sigmoid(v):
    return 1.0 / (1.0 + jnp.exp(-v))


def by_eights(value):
    return value.reshape(value.shape[0] // 8, 8, value.shape[1])


def as_rows(value):
    return value.reshape(value.shape[0] * 8, value.shape[2])


def spread_columns(row_ref, key_ref, query_ref, rows, states):
    lane = lax.broadcasted_iota(jnp.int32, (states, LANE), 1)
    entry = lax.broadcasted_iota(jnp.int32, (states, LANE), 0)
    pick_key = lane == entry
    pick_query = lane == entry + states

    def body(group, carry):
        for offset in range(8):
            t = group * 8 + offset
            row = jnp.broadcast_to(row_ref[group, offset : offset + 1, :], (states, LANE))
            at = pl.multiple_of(t * states, states)
            key = jnp.sum(jnp.where(pick_key, row, 0.0), axis=1, keepdims=True)
            query = jnp.sum(jnp.where(pick_query, row, 0.0), axis=1, keepdims=True)
            key_ref[pl.ds(at, states), :] = jnp.broadcast_to(key, (states, LANE))
            query_ref[pl.ds(at, states), :] = jnp.broadcast_to(query, (states, LANE))
        return carry

    lax.fori_loop(0, rows // 8, body, 0)


def step_sizes(low_ref, kq_ref, weight_ref, bias_ref, states):
    pre = lax.dot_general(
        low_ref[...], weight_ref[...], (((1,), (1,)), ((), ())), preferred_element_type=jnp.float32
    )
    beta = sigmoid(pre + bias_ref[...])
    lane = lax.broadcasted_iota(jnp.int32, kq_ref.shape, 1)
    keys = jnp.where(lane < states, kq_ref[...], 0.0)
    square = jnp.sum(keys * keys, axis=1, keepdims=True)
    return beta, 1.0 / (1.0 + beta * square)


def forward_body(
    states, low_ref, kq_ref, values_ref, gate_ref, weight_ref, bias_ref, skip_ref,
    gated_ref, mixed_ref, history_ref, final_ref,
    state_ref, key_ref, query_ref, rate_ref, input_ref, out_ref, row_ref,
):
    rows, channels = values_ref.shape
    tiles = channels // LANE
    per_group = min(4, tiles)

    @pl.when(pl.program_id(0) == 0)
    def _():
        state_ref[...] = jnp.zeros_like(state_ref)

    beta, inverse = step_sizes(low_ref, kq_ref, weight_ref, bias_ref, states)
    rates = beta * inverse
    rate_ref[...] = by_eights(rates)
    input_ref[...] = by_eights(rates * values_ref[...].astype(jnp.float32))
    row_ref[...] = by_eights(kq_ref[...])
    spread_columns(row_ref, key_ref, query_ref, rows, states)

    for first in range(0, tiles, per_group):
        columns = [slice((first + j) * LANE, (first + j + 1) * LANE) for j in range(per_group)]

        def body(group, carry):
            carry = list(carry)
            for offset in range(8):
                t = group * 8 + offset
                at = pl.multiple_of(t * states, states)
                key = key_ref[pl.ds(at, states), :]
                query = query_ref[pl.ds(at, states), :]
                square = key * key
                for j, cols in enumerate(columns):
                    history_ref[pl.ds(at, states), cols] = carry[j].astype(jnp.bfloat16)
                    rate = rate_ref[group, offset : offset + 1, cols]
                    fed = input_ref[group, offset : offset + 1, cols]
                    carry[j] = (1.0 - rate * square) * carry[j] + key * fed
                    out_ref[group, offset : offset + 1, cols] = jnp.sum(query * carry[j], axis=0, keepdims=True)
            return tuple(carry)

        done = lax.fori_loop(0, rows // 8, body, tuple(state_ref[:, cols] for cols in columns))
        for cols, state in zip(columns, done):
            state_ref[:, cols] = state

    mixed = as_rows(out_ref[...]) + skip_ref[...] * values_ref[...].astype(jnp.float32)
    gate = gate_ref[...]
    mixed_ref[...] = mixed
    gated_ref[...] = (mixed * gate * sigmoid(gate)).astype(jnp.bfloat16)

    @pl.when(pl.program_id(0) == pl.num_programs(0) - 1)
    def _():
        final_ref[...] = state_ref[...]


def forward_scan(low, kq, values, gate, weight, bias, skip, states):
    length, channels = values.shape
    rank = low.shape[1]
    rows = min(128, length)
    blocks = length // rows
    by_row = lambda width: pl.BlockSpec((rows, width), lambda i: (i, 0))
    whole = lambda a: pl.BlockSpec(a.shape, lambda i: (0, 0))
    return pl.pallas_call(
        lambda *refs: forward_body(states, *refs),
        grid=(blocks,),
        in_specs=[by_row(rank), by_row(LANE), by_row(channels), by_row(channels), whole(weight), whole(bias), whole(skip)],
        out_specs=[
            by_row(channels),
            by_row(channels),
            pl.BlockSpec((rows * states, channels), lambda i: (i, 0)),
            pl.BlockSpec((states, channels), lambda i: (0, 0)),
        ],
        out_shape=[
            jax.ShapeDtypeStruct((length, channels), jnp.bfloat16),
            jax.ShapeDtypeStruct((length, channels), jnp.float32),
            jax.ShapeDtypeStruct((length * states, channels), jnp.bfloat16),
            jax.ShapeDtypeStruct((states, channels), jnp.float32),
        ],
        scratch_shapes=[
            pltpu.VMEM((states, channels), jnp.float32),
            pltpu.VMEM((rows * states, LANE), jnp.float32),
            pltpu.VMEM((rows * states, LANE), jnp.float32),
            pltpu.VMEM((rows // 8, 8, channels), jnp.float32),
            pltpu.VMEM((rows // 8, 8, channels), jnp.float32),
            pltpu.VMEM((rows // 8, 8, channels), jnp.float32),
            pltpu.VMEM((rows // 8, 8, LANE), jnp.float32),
        ],
        compiler_params=pltpu.CompilerParams(vmem_limit_bytes=48 * 1024 * 1024),
        cost_estimate=pl.CostEstimate(flops=14 * length * states * channels, bytes_accessed=2 * length * states * channels, transcendentals=0),
    )(low, kq, values, gate, weight, bias, skip)


def backward_body(
    states, links, low_ref, kq_ref, values_ref, gate_ref, mixed_ref, dgated_ref, history_ref, final_ref, weight_ref, bias_ref, skip_ref,
    result_ref, out_ref, dgate_ref, dpre_ref, dvalues_ref, dlow_ref, dkq_ref, bias_grad_ref, skip_grad_ref, result_came, out_came,
    grad_ref, state_ref, key_ref, query_ref, rate_ref, do_ref, values32_ref, fed_ref, kept_ref, part_key_ref, part_query_ref, row_ref, placed_ref, *sems,
):
    rows, channels = values_ref.shape
    tiles = channels // LANE
    per_group = min(4, tiles)
    copies = links(result_ref, out_ref, result_came, out_came, *sems)

    @pl.when(pl.program_id(0) == 0)
    def _():
        grad_ref[...] = jnp.zeros_like(grad_ref)
        state_ref[...] = final_ref[...]
        bias_grad_ref[...] = jnp.zeros_like(bias_grad_ref)
        skip_grad_ref[...] = jnp.zeros_like(skip_grad_ref)
        for copy in copies:
            copy.start()

    beta, inverse = step_sizes(low_ref, kq_ref, weight_ref, bias_ref, states)
    rate_ref[...] = by_eights(beta * inverse)
    values = values_ref[...].astype(jnp.float32)
    values32_ref[...] = by_eights(values)
    gate = gate_ref[...]
    dgated = dgated_ref[...].astype(jnp.float32)
    s = sigmoid(gate)
    do = dgated * (gate * s)
    do_ref[...] = by_eights(do)
    dgate_ref[...] = (dgated * mixed_ref[...] * (s + gate * s * (1.0 - s))).astype(jnp.bfloat16)
    skip_grad_ref[...] += jnp.sum(do * values, axis=0, keepdims=True)
    row_ref[...] = by_eights(kq_ref[...])
    spread_columns(row_ref, key_ref, query_ref, rows, states)

    for first in range(0, tiles, per_group):
        columns = [slice((first + j) * LANE, (first + j + 1) * LANE) for j in range(per_group)]

        def body(step, carry):
            grads, lates = list(carry[0]), list(carry[1])
            group = rows // 8 - 1 - step
            for offset in reversed(range(8)):
                t = group * 8 + offset
                at = pl.multiple_of(t * states, states)
                key = key_ref[pl.ds(at, states), :]
                query = query_ref[pl.ds(at, states), :]
                sum_key = None
                sum_query = None
                for j, cols in enumerate(columns):
                    rate = rate_ref[group, offset : offset + 1, cols]
                    out_grad = do_ref[group, offset : offset + 1, cols]
                    value = values32_ref[group, offset : offset + 1, cols]
                    before = history_ref[pl.ds(at, states), cols].astype(jnp.float32)
                    grad = grads[j] + query * out_grad
                    scaled = rate * grad
                    by_key = key * scaled
                    kept = scaled * before
                    fed_ref[group, offset : offset + 1, cols] = jnp.sum(by_key, axis=0, keepdims=True)
                    kept_ref[group, offset : offset + 1, cols] = jnp.sum(key * (key * kept), axis=0, keepdims=True)
                    term_key = value * scaled - 2.0 * (key * kept)
                    term_query = lates[j] * out_grad
                    sum_key = term_key if sum_key is None else sum_key + term_key
                    sum_query = term_query if sum_query is None else sum_query + term_query
                    grads[j] = grad - key * by_key
                    lates[j] = before
                if first == 0:
                    part_key_ref[pl.ds(at, states), :] = sum_key
                    part_query_ref[pl.ds(at, states), :] = sum_query
                else:
                    part_key_ref[pl.ds(at, states), :] += sum_key
                    part_query_ref[pl.ds(at, states), :] += sum_query
            return (tuple(grads), tuple(lates))

        start = (tuple(grad_ref[:, cols] for cols in columns), tuple(state_ref[:, cols] for cols in columns))
        grads, lates = lax.fori_loop(0, rows // 8, body, start)
        for cols, grad, late in zip(columns, grads, lates):
            grad_ref[:, cols] = grad
            state_ref[:, cols] = late

    fed = as_rows(fed_ref[...])
    dvalues_ref[...] = fed + skip_ref[...] * as_rows(do_ref[...])
    scaled = as_rows(values32_ref[...]) * fed - as_rows(kept_ref[...])
    beta, inverse = step_sizes(low_ref, kq_ref, weight_ref, bias_ref, states)
    dpre = scaled * (1.0 - beta) * inverse
    bias_grad_ref[...] += jnp.sum(dpre, axis=0, keepdims=True)
    dpre_low = dpre.astype(jnp.bfloat16)
    dpre_ref[...] = dpre_low
    dlow_ref[...] = jnp.dot(dpre_low, weight_ref[...], preferred_element_type=jnp.float32)
    through = -2.0 * jnp.sum(scaled * beta * inverse, axis=1, keepdims=True)

    lane = lax.broadcasted_iota(jnp.int32, (states, LANE), 1)
    entry = lax.broadcasted_iota(jnp.int32, (states, LANE), 0)

    def gather(group, carry):
        for offset in range(8):
            t = group * 8 + offset
            at = pl.multiple_of(t * states, states)
            key = jnp.sum(part_key_ref[pl.ds(at, states), :], axis=1, keepdims=True)
            query = jnp.sum(part_query_ref[pl.ds(at, states), :], axis=1, keepdims=True)
            placed = jnp.where(lane == entry, key, 0.0) + jnp.where(lane == entry + states, query, 0.0)
            placed_ref[group, offset : offset + 1, :] = jnp.sum(placed, axis=0, keepdims=True)
        return carry

    lax.fori_loop(0, rows // 8, gather, 0)
    lanes = lax.broadcasted_iota(jnp.int32, kq_ref.shape, 1)
    dkq_ref[...] = as_rows(placed_ref[...]) + jnp.where(lanes < states, kq_ref[...] * through, 0.0)

    @pl.when(pl.program_id(0) == pl.num_programs(0) - 1)
    def _():
        for copy in copies:
            copy.wait_recv()
        for copy in copies:
            copy.wait_send()


def exchange(parts, dps, result_ref, out_ref, result_came, out_came, result_send, result_recv, out_send, out_recv):
    d, s = lax.axis_index("dp"), lax.axis_index("seq")

    @pl.when(pl.program_id(0) == 0)
    def _():
        barrier = pltpu.get_barrier_semaphore()
        for k in range(1, parts):
            pl.semaphore_signal(barrier, inc=1, device_id=(d, lax.rem(s + k, parts)), device_id_type=MESH)
        for k in range(1, dps):
            pl.semaphore_signal(barrier, inc=1, device_id=(lax.rem(d + k, dps), s), device_id_type=MESH)
        pl.semaphore_wait(barrier, parts + dps - 2)

    copies = []
    for k in range(1, parts):
        to = lax.rem(s + k, parts)
        copies.append(
            pltpu.make_async_remote_copy(
                src_ref=result_ref.at[to], dst_ref=result_came.at[k - 1], send_sem=result_send.at[k - 1],
                recv_sem=result_recv.at[k - 1], device_id=(d, to), device_id_type=MESH,
            )
        )
    for k in range(1, dps):
        to = lax.rem(d + k, dps)
        copies.append(
            pltpu.make_async_remote_copy(
                src_ref=out_ref.at[to], dst_ref=out_came.at[k - 1], send_sem=out_send.at[k - 1],
                recv_sem=out_recv.at[k - 1], device_id=(to, s), device_id_type=MESH,
            )
        )
    return copies


def backward_scan(low, kq, values, gate, mixed, dgated, history, final, weight, bias, skip, result_part, out_part, states):
    length, channels = values.shape
    rank = low.shape[1]
    rows = min(128, length)
    blocks = length // rows
    by_row = lambda width: pl.BlockSpec((rows, width), lambda i: (blocks - 1 - i, 0))
    whole = lambda a: pl.BlockSpec(a.shape, lambda i: (0, 0))
    total = pl.BlockSpec((1, channels), lambda i: (0, 0))
    wide = pltpu.VMEM((rows // 8, 8, channels), jnp.float32)
    spread = pltpu.VMEM((rows * states, LANE), jnp.float32)
    anywhere = pl.BlockSpec(memory_space=pl.ANY)
    dma = pltpu.SemaphoreType.DMA
    parts, dps = result_part.shape[0], out_part.shape[0]
    links = lambda *refs: exchange(parts, dps, *refs)
    return pl.pallas_call(
        lambda *refs: backward_body(states, links, *refs),
        grid=(blocks,),
        in_specs=[
            by_row(rank), by_row(LANE), by_row(channels), by_row(channels), by_row(channels), by_row(channels),
            pl.BlockSpec((rows * states, channels), lambda i: (blocks - 1 - i, 0)),
            whole(final), whole(weight), whole(bias), whole(skip), anywhere, anywhere,
        ],
        out_specs=[by_row(channels), by_row(channels), by_row(channels), by_row(rank), by_row(LANE), total, total, anywhere, anywhere],
        out_shape=[
            jax.ShapeDtypeStruct((length, channels), jnp.bfloat16),
            jax.ShapeDtypeStruct((length, channels), jnp.bfloat16),
            jax.ShapeDtypeStruct((length, channels), jnp.float32),
            jax.ShapeDtypeStruct((length, rank), jnp.float32),
            jax.ShapeDtypeStruct((length, LANE), jnp.float32),
            jax.ShapeDtypeStruct((1, channels), jnp.float32),
            jax.ShapeDtypeStruct((1, channels), jnp.float32),
            jax.ShapeDtypeStruct((parts - 1,) + result_part.shape[1:], jnp.bfloat16),
            jax.ShapeDtypeStruct((dps - 1,) + out_part.shape[1:], jnp.bfloat16),
        ],
        scratch_shapes=[
            pltpu.VMEM((states, channels), jnp.float32),
            pltpu.VMEM((states, channels), jnp.float32),
            spread, spread, wide, wide, wide, wide, wide, spread, spread,
            pltpu.VMEM((rows // 8, 8, LANE), jnp.float32), pltpu.VMEM((rows // 8, 8, LANE), jnp.float32),
            dma((parts - 1,)), dma((parts - 1,)), dma((dps - 1,)), dma((dps - 1,)),
        ],
        compiler_params=pltpu.CompilerParams(collective_id=3, has_side_effects=True, vmem_limit_bytes=56 * 1024 * 1024),
        cost_estimate=pl.CostEstimate(flops=30 * length * states * channels, bytes_accessed=2 * length * states * channels, transcendentals=0),
    )(low, kq, values, gate, mixed, dgated, history, final, weight, bias, skip, result_part, out_part)


MESH = pl.DeviceIdType.MESH
GAIN_ROWS = 16


def plane_mates(d):
    core, x, y = lax.rem(d, 2), lax.rem(d // 2, 2), d // 4
    return d + 1 - 2 * core, d + 2 - 4 * x, d + 4 - 8 * y


def start_body(
    parts, block,
    tokens_ref, spread_ref, extra_ref, gain_ref,
    normed_out, weight_out, conv_ref, gate_ref, extra_out,
    tokens_all, normed_all, weight_all, extra_all,
    near_send, near_recv, plane_send, plane_recv, gain_send, gain_recv, line_send, line_recv, local_sem,
):
    d, s = lax.axis_index("dp"), lax.axis_index("seq")
    sib, xm, ym = plane_mates(d)
    own = spread_ref.shape[1]
    rows, width = tokens_ref.shape
    small = extra_ref.shape[0]
    channels = conv_ref.shape[1]
    chunk = rows // 4

    barrier = pltpu.get_barrier_semaphore()
    for mate in (sib, xm, ym):
        pl.semaphore_signal(barrier, inc=1, device_id=(mate, s), device_id_type=MESH)
    for k in range(1, parts):
        pl.semaphore_signal(barrier, inc=1, device_id=(d, lax.rem(s + k, parts)), device_id_type=MESH)
    pl.semaphore_wait(barrier, 3 + parts - 1)

    def remote(src, dst, send, recv, to):
        return pltpu.make_async_remote_copy(
            src_ref=src, dst_ref=dst, send_sem=send, recv_sem=recv, device_id=to, device_id_type=MESH
        )

    def weight_rows(owner, source):
        return weight_all.at[pl.ds(pl.multiple_of((owner * parts + source) * own, own), own), :]

    def extra_rows(owner):
        return extra_all.at[owner]

    def gain_rows(source):
        return extra_all.at[d, pl.ds(pl.multiple_of(small + source * GAIN_ROWS, GAIN_ROWS), GAIN_ROWS), pl.ds(0, LANE)]

    near = []
    for k in range(1, parts):
        to = (d, lax.rem(s + k, parts))
        near.append(remote(spread_ref.at[to[1]], weight_rows(d, s), near_send.at[k], near_recv.at[k], to))
        near.append(remote(gain_ref, gain_rows(s), gain_send.at[k], gain_recv.at[k], to))
    for copy in near:
        copy.start()
    mine = [
        pltpu.make_async_copy(spread_ref.at[s], weight_rows(d, s), local_sem.at[0]),
        pltpu.make_async_copy(gain_ref, gain_rows(s), local_sem.at[1]),
        pltpu.make_async_copy(extra_ref, extra_all.at[d, pl.ds(0, small), :], local_sem.at[2]),
        pltpu.make_async_copy(tokens_ref, tokens_all.at[pl.ds(pl.multiple_of(s * rows, rows), rows), :], local_sem.at[3]),
    ]
    for copy in mine:
        copy.start()

    def token_rows(part, c):
        return tokens_all.at[pl.ds(pl.multiple_of(part * rows + c * chunk, chunk), chunk), :]

    def token_copy(way, distance, c):
        part = s - way * (distance - 1)
        src = tokens_ref.at[pl.ds(c * chunk, chunk), :] if distance == 1 else token_rows(part, c)
        side = 0 if way == 1 else 1
        return remote(
            src, token_rows(part, c), line_send.at[side, distance, c], line_recv.at[side, distance, c], (d, s + way)
        )

    def can_send(way, distance):
        reach = s + 1 < parts if way == 1 else s >= 1
        came = s - (distance - 1) >= 0 if way == 1 else s + (distance - 1) < parts
        return jnp.logical_and(reach, came)

    def arrives(way, distance):
        return s >= distance if way == 1 else s + distance < parts

    def send_tokens(distance, c):
        for way in (1, -1):
            @pl.when(can_send(way, distance))
            def _():
                token_copy(way, distance, c).start()

    def sent_tokens(distance, c):
        for way in (1, -1):
            @pl.when(can_send(way, distance))
            def _():
                token_copy(way, distance, c).wait_send()

    def take_tokens(distance, c):
        for way in (1, -1):
            @pl.when(arrives(way, distance))
            def _():
                part = s - way * distance
                side = 0 if way == 1 else 1
                remote(
                    token_rows(part, c), token_rows(part, c), line_send.at[side, distance, c],
                    line_recv.at[side, distance, c], (d, s),
                ).wait_recv()

    units = parts + 1

    def unit(owner, k):
        return extra_rows(owner) if k == parts else weight_rows(owner, lax.rem(s - k + parts, parts))

    kinds = {"own": (d, 0), "x": (xm, 2), "y": (ym, 4)}

    def plane_copy(owner, k, rel, kind, to):
        return remote(unit(owner, k), unit(owner, k), plane_send.at[kind, k], plane_recv.at[rel, k], (to, s))

    diag = xm + ym - d
    sib_of = lambda mate: mate + sib - d

    def route(k):
        steps = [
            (0, d, 1, 0, sib), (0, d, 2, 1, xm), (0, d, 4, 2, ym),
            (2, xm, 3, 3, sib), (4, ym, 5, 5, sib), (6, diag, 7, 7, sib),
        ]
        steps.append((2, xm, 6, 4, ym) if k % 2 == 0 else (4, ym, 6, 6, xm))
        return steps

    def pass_on(stage, k):
        for at, owner, rel, kind, to in route(k):
            if at == stage:
                plane_copy(owner, k, rel, kind, to).start()

    owners = {1: sib, 2: xm, 3: sib_of(xm), 4: ym, 5: sib_of(ym), 6: diag, 7: sib_of(diag)}

    def take(rel, k):
        plane_copy(owners[rel], k, rel, 0, d).wait_recv()

    for c in range(4):
        send_tokens(1, c)
    mine[0].wait()
    pass_on(0, 0)
    for k in range(1, parts):
        near_wait = remote(
            spread_ref.at[s], weight_rows(d, lax.rem(s - k + parts, parts)), near_send.at[k], near_recv.at[k], (d, s)
        )
        near_wait.wait_recv()
        pass_on(0, k)
    mine[1].wait()
    mine[2].wait()
    for k in range(1, parts):
        remote(gain_ref, gain_rows(lax.rem(s - k + parts, parts)), gain_send.at[k], gain_recv.at[k], (d, s)).wait_recv()
    pass_on(0, parts)
    for k in range(units):
        take(2, k)
        pass_on(2, k)
        take(4, k)
        pass_on(4, k)
        if k < 4:
            take_tokens(1, k)
            send_tokens(2, k)
    for k in range(units):
        take(6, k)
        pass_on(6, k)
        if k < 4:
            take_tokens(2, k)
            send_tokens(3, k)
    for rel in (1, 3, 5, 7):
        for k in range(units):
            take(rel, k)
    mine[3].wait()
    weight_copy = pltpu.make_async_copy(weight_all, weight_out, local_sem.at[4])
    weight_copy.start()
    extra_out[...] = extra_all[...]

    lane = lax.broadcasted_iota(jnp.int32, (1, LANE), 1)
    pieces = []
    for owner in range(extra_all.shape[0]):
        for source in range(0, parts, 2):
            row = small + source * GAIN_ROWS
            even = extra_all[owner, row : row + GAIN_ROWS, 0:LANE].astype(jnp.float32)[0:1]
            odd = extra_all[owner, row + GAIN_ROWS : row + 2 * GAIN_ROWS, 0:LANE].astype(jnp.float32)[0:1]
            pieces.append(jnp.where(lane < own, even, odd))
    gain = jnp.concatenate(pieces, axis=1)

    tile = min(512, channels)

    def work(part):
        for c in range(4):
            at = pl.ds(pl.multiple_of(part * rows + c * chunk, chunk), chunk)
            flat = tokens_all[at, :].astype(jnp.float32)
            scale = lax.rsqrt(jnp.mean(flat * flat, axis=-1, keepdims=True) + 1e-05)
            normed_all[at, :] = (flat * scale * gain).astype(jnp.bfloat16)
        at = pl.ds(pl.multiple_of(part * rows, rows), rows)

        def columns(n, carry):
            left = pl.multiple_of(n * tile, tile)
            right = pl.multiple_of(channels + n * tile, tile)
            conv_ref[at, pl.ds(left, tile)] = jnp.dot(
                normed_all[at, :], weight_all[:, pl.ds(left, tile)], preferred_element_type=jnp.float32
            ).astype(jnp.bfloat16)
            gate_ref[at, pl.ds(left, tile)] = jnp.dot(
                normed_all[at, :], weight_all[:, pl.ds(right, tile)], preferred_element_type=jnp.float32
            )
            return carry

        lax.fori_loop(0, channels // tile, columns, 0)

    def work_at(low, high):
        def each(part, carry):
            away = jnp.abs(part - s)

            @pl.when(jnp.logical_and(away >= low, away <= high))
            def _():
                work(part)

            return carry

        lax.fori_loop(0, parts, each, 0)

    work_at(0, 2)
    for c in range(4):
        take_tokens(3, c)
    work_at(3, 3)
    normed_copy = pltpu.make_async_copy(normed_all, normed_out, local_sem.at[5])
    normed_copy.start()

    for copy in near:
        copy.wait_send()
    for k in range(units):
        for at, owner, rel, kind, to in route(k):
            plane_copy(owner, k, rel, kind, to).wait_send()
    for distance in range(1, parts):
        for c in range(4):
            sent_tokens(distance, c)
    weight_copy.wait()
    normed_copy.wait()


def start(tokens, spread, extra, gain, dps):
    parts, own, both = spread.shape
    rows, width = tokens.shape
    small, lanes = extra.shape
    any_space = pl.BlockSpec(memory_space=pl.ANY)
    vmem = pl.BlockSpec(memory_space=pltpu.VMEM)
    tall = small + parts * GAIN_ROWS
    dma = pltpu.SemaphoreType.DMA
    return pl.pallas_call(
        lambda *refs: start_body(parts, own, *refs),
        out_shape=[
            jax.ShapeDtypeStruct((parts * rows, width), jnp.bfloat16),
            jax.ShapeDtypeStruct((dps * parts * own, both), jnp.bfloat16),
            jax.ShapeDtypeStruct((parts * rows, both // 2), jnp.bfloat16),
            jax.ShapeDtypeStruct((parts * rows, both // 2), jnp.float32),
            jax.ShapeDtypeStruct((dps, tall, lanes), jnp.bfloat16),
        ],
        in_specs=[vmem, vmem, vmem, vmem],
        out_specs=[any_space, any_space, vmem, vmem, vmem],
        scratch_shapes=[
            pltpu.VMEM((parts * rows, width), jnp.bfloat16),
            pltpu.VMEM((parts * rows, width), jnp.bfloat16),
            pltpu.VMEM((dps * parts * own, both), jnp.bfloat16),
            pltpu.VMEM((dps, tall, lanes), jnp.bfloat16),
            dma((parts,)), dma((parts,)),
            dma((8, parts + 1)), dma((8, parts + 1)),
            dma((parts,)), dma((parts,)),
            dma((2, parts, 4)), dma((2, parts, 4)),
            dma((6,)),
        ],
        compiler_params=pltpu.CompilerParams(
            collective_id=1, has_side_effects=True, vmem_limit_bytes=56 * 1024 * 1024
        ),
        cost_estimate=pl.CostEstimate(
            flops=2 * parts * rows * width * both, bytes_accessed=40 * 1024 * 1024, transcendentals=0
        ),
    )(tokens, spread, extra, gain)


def end_body(
    parts, block,
    dmixed_ref, normed_ref, weight_ref, tokens_ref, cot_ref, gain_ref, shard_ref, small_ref,
    input_grad_ref, in_grad_ref, gain_grad_ref, small_grad_ref,
    dn, dn_recv, sib_send, sib_recv, q_send, q_recv, total, z_send, z_recv,
    small_sib_send, small_sib_recv, small_q_send, small_q_recv,
    line_send, line_recv, pair_send, pair_recv, cross_send, cross_recv, near_send, near_recv,
):
    d, s = lax.axis_index("dp"), lax.axis_index("seq")
    sib, xm, ym = plane_mates(d)
    diag = xm + ym - d
    own, both = shard_ref.shape[0], dmixed_ref.shape[1]
    rows, width = tokens_ref.shape
    chunk = rows // 4
    tall = parts * own
    tile = min(512, both)

    barrier = pltpu.get_barrier_semaphore()
    for mate in (sib, xm, ym, diag):
        pl.semaphore_signal(barrier, inc=1, device_id=(mate, s), device_id_type=MESH)
    for k in range(1, parts):
        pl.semaphore_signal(barrier, inc=1, device_id=(d, lax.rem(s + k, parts)), device_id_type=MESH)
    pl.semaphore_wait(barrier, 4 + parts - 1)

    def remote(src, dst, send, recv, to):
        return pltpu.make_async_remote_copy(
            src_ref=src, dst_ref=dst, send_sem=send, recv_sem=recv, device_id=to, device_id_type=MESH
        )

    def dn_rows(part, c):
        return pl.ds(pl.multiple_of(part * rows + c * chunk, chunk), chunk)

    def slot(way, left, part, c):
        at = parts if way == -1 and left == 0 else part
        return dn_recv.at[at, pl.ds(c * chunk, chunk), :]

    def line_copy(way, steps, c):
        side = 0 if way == 1 else 1
        part = s + way * steps
        return remote(
            dn.at[dn_rows(part, c), :], slot(way, steps - 1, part, c), line_send.at[side, steps, c],
            line_recv.at[side, steps - 1, c], (d, s + way),
        )

    def valid(way, steps):
        return s + steps < parts if way == 1 else s >= steps

    def upstream(way):
        return s >= 1 if way == 1 else s + 1 < parts

    def line_wait(way, left, c):
        side = 0 if way == 1 else 1
        place = slot(way, left, s + way * left, c)
        remote(place, place, line_send.at[side, left, c], line_recv.at[side, left, c], (d, s)).wait_recv()

    def pass_line(steps, c):
        for way in (1, -1):
            @pl.when(valid(way, steps))
            def _():
                if steps < parts - 1:
                    @pl.when(upstream(way))
                    def _():
                        line_wait(way, steps, c)
                        mine = dn_rows(s + way * steps, c)
                        came = dn_recv[s + way * steps, c * chunk : (c + 1) * chunk, :]
                        dn[mine, :] = (dn[mine, :].astype(jnp.float32) + came.astype(jnp.float32)).astype(jnp.bfloat16)

                line_copy(way, steps, c).start()

    def dn_part(part):
        at = pl.ds(pl.multiple_of(part * rows, rows), rows)

        def columns(n, carry):
            cols = pl.ds(pl.multiple_of(n * tile, tile), tile)
            dn[at, cols] = lax.dot_general(
                dmixed_ref[at, :], weight_ref[cols, :], (((1,), (1,)), ((), ())), preferred_element_type=jnp.float32
            ).astype(jnp.bfloat16)
            return carry

        lax.fori_loop(0, width // tile, columns, 0)

    def each_part(part, carry):
        dn_part(part)
        return carry

    lax.fori_loop(0, parts, each_part, 0)
    for c in range(4):
        pass_line(parts - 1, c)

    def grad_block(owner, store):
        left = pl.ds(pl.multiple_of(owner * tall, tall), tall)

        def columns(n, carry):
            cols = pl.ds(pl.multiple_of(n * tile, tile), tile)
            store(
                cols,
                lax.dot_general(
                    normed_ref[:, left], dmixed_ref[:, cols], (((0,), (0,)), ((), ())),
                    preferred_element_type=jnp.float32,
                ),
            )
            return carry

        lax.fori_loop(0, both // tile, columns, 0)

    mates = (diag, xm, ym, d)
    sib_of = lambda mate: mate + sib - d

    def pair_copy(r):
        return remote(sib_send.at[r], sib_recv.at[r], pair_send.at[0, r], pair_recv.at[0, r], (sib, s))

    def pair_copy_small(r):
        return remote(small_sib_send.at[r], small_sib_recv.at[r], pair_send.at[1, r], pair_recv.at[1, r], (sib, s))

    def cross_copy(r):
        return remote(q_send.at[r], q_recv.at[r], cross_send.at[0, r], cross_recv.at[0, r], (mates[r], s))

    def cross_copy_small(r):
        return remote(small_q_send.at[r], small_q_recv.at[r], cross_send.at[1, r], cross_recv.at[1, r], (mates[r], s))

    for r in range(4):
        def store_pair(cols, value):
            sib_send[r, :, cols] = value.astype(jnp.bfloat16)

        grad_block(sib_of(mates[r]), store_pair)
        pair_copy(r).start()
        small_sib_send[r] = small_ref[sib_of(mates[r])].astype(jnp.bfloat16)
        pair_copy_small(r).start()
        if parts > 2:
            pass_line(parts - 2, r)
    for r in range(4):
        pair_copy(r).wait_recv()
        pair_copy_small(r).wait_recv()
        both_small = small_ref[mates[r]] + small_sib_recv[r].astype(jnp.float32)
        if r < 3:
            def store_cross(cols, value):
                q_send[r, :, cols] = (value + sib_recv[r, :, cols].astype(jnp.float32)).astype(jnp.bfloat16)

            grad_block(mates[r], store_cross)
            cross_copy(r).start()
            small_q_send[r] = both_small.astype(jnp.bfloat16)
            cross_copy_small(r).start()
        else:
            def store_total(cols, value):
                total[:, cols] = value + sib_recv[r, :, cols].astype(jnp.float32)

            grad_block(mates[r], store_total)
            small_grad_ref[...] = both_small
        if parts > 3:
            pass_line(parts - 3, r)

    for r in range(3):
        cross_copy(r).wait_recv()
        cross_copy_small(r).wait_recv()
        total[...] += q_recv[r].astype(jnp.float32)
        small_grad_ref[...] += small_q_recv[r].astype(jnp.float32)
    z_send[...] = total[...].astype(jnp.bfloat16)

    def near_copy(k):
        to = lax.rem(s + k, parts)
        return remote(
            z_send.at[pl.ds(pl.multiple_of(to * own, own), own), :], z_recv.at[k], near_send.at[k], near_recv.at[k], (d, to)
        )

    for k in range(1, parts):
        near_copy(k).start()

    for c in range(4):
        mine = dn_rows(s, c)
        dn_total = dn[mine, :].astype(jnp.float32)
        for way in (1, -1):
            @pl.when(upstream(way))
            def _():
                line_wait(way, 0, c)

        at = pl.ds(c * chunk, chunk)
        low = jnp.where(upstream(1), dn_recv[s, at, :].astype(jnp.float32), 0.0)
        high = jnp.where(upstream(-1), dn_recv[parts, at, :].astype(jnp.float32), 0.0)
        v = (dn_total + low + high) * gain_ref[...]
        flat = tokens_ref[at, :].astype(jnp.float32)
        scale = lax.rsqrt(jnp.mean(flat * flat, axis=-1, keepdims=True) + 1e-05)
        du = scale * v - flat * (scale * scale * scale) * jnp.mean(flat * v, axis=-1, keepdims=True)
        input_grad_ref[at, :] = (cot_ref[at, :].astype(jnp.float32) + du).astype(jnp.bfloat16)

    channel_blocks = both // block
    gain_total = jnp.zeros((own, block), jnp.float32)
    for k in range(parts):
        source = lax.rem(s - k + parts, parts)
        if k > 0:
            near_copy(k).wait_recv()
        for j in range(channel_blocks):
            cols = slice(j * block, (j + 1) * block)
            if k == 0:
                piece = z_send[pl.ds(pl.multiple_of(s * own, own), own), cols]
            else:
                piece = z_recv[k, :, cols]
            piece = piece.astype(jnp.float32)
            to = pl.ds(pl.multiple_of((j * parts + source) * block, block), block)
            in_grad_ref[:, to] = piece
            gain_total = gain_total + piece * shard_ref[:, to].astype(jnp.float32)
    gain_grad_ref[...] = jnp.broadcast_to(jnp.sum(gain_total, axis=1, keepdims=True), gain_grad_ref.shape)

    for r in range(4):
        pair_copy(r).wait_send()
        pair_copy_small(r).wait_send()
    for r in range(3):
        cross_copy(r).wait_send()
        cross_copy_small(r).wait_send()
    for k in range(1, parts):
        near_copy(k).wait_send()
    for steps in range(1, parts):
        for c in range(4):
            for way in (1, -1):
                @pl.when(valid(way, steps))
                def _():
                    line_copy(way, steps, c).wait_send()


def end(dmixed, normed, weight, tokens, cotangent, gain, shard, small, parts, block):
    both = dmixed.shape[1]
    rows, width = tokens.shape
    own = shard.shape[0]
    dps, _, lanes = small.shape
    tall = parts * own
    vmem = pl.BlockSpec(memory_space=pltpu.VMEM)
    dma = pltpu.SemaphoreType.DMA
    low = jnp.bfloat16
    return pl.pallas_call(
        lambda *refs: end_body(parts, block, *refs),
        out_shape=[
            jax.ShapeDtypeStruct((rows, width), low),
            jax.ShapeDtypeStruct((own, parts * both), jnp.float32),
            jax.ShapeDtypeStruct((own, LANE), jnp.float32),
            jax.ShapeDtypeStruct((block, lanes), jnp.float32),
        ],
        in_specs=[vmem] * 8,
        out_specs=[vmem] * 4,
        scratch_shapes=[
            pltpu.VMEM((parts * rows, width), low),
            pltpu.VMEM((parts + 1, rows, width), low),
            pltpu.VMEM((4, tall, both), low), pltpu.VMEM((4, tall, both), low),
            pltpu.VMEM((3, tall, both), low), pltpu.VMEM((3, tall, both), low),
            pltpu.VMEM((tall, both), jnp.float32),
            pltpu.VMEM((tall, both), low), pltpu.VMEM((parts, own, both), low),
            pltpu.VMEM((4, block, lanes), low), pltpu.VMEM((4, block, lanes), low),
            pltpu.VMEM((3, block, lanes), low), pltpu.VMEM((3, block, lanes), low),
            dma((2, parts, 4)), dma((2, parts, 4)),
            dma((2, 4)), dma((2, 4)), dma((2, 3)), dma((2, 3)), dma((parts,)), dma((parts,)),
        ],
        compiler_params=pltpu.CompilerParams(
            collective_id=2, has_side_effects=True, vmem_limit_bytes=60 * 1024 * 1024
        ),
        cost_estimate=pl.CostEstimate(
            flops=4 * parts * rows * width * both, bytes_accessed=30 * 1024 * 1024, transcendentals=0
        ),
    )(dmixed, normed, weight, tokens, cotangent, gain, shard, small)


def contract(left, right, left_dim, right_dim):
    return lax.dot_general(
        left, right, (((left_dim,), (right_dim,)), ((), ())), preferred_element_type=jnp.float32
    )


def gathered(shard, axis):
    return lax.all_gather(shard, axis, axis=0, tiled=True)


def scattered(total, axis):
    return lax.psum_scatter(total, axis, scatter_dimension=0, tiled=True)


def summed_rows(partial, axis):
    size = lax.axis_size(axis)
    parts = partial.astype(jnp.bfloat16).reshape((size, partial.shape[0] // size) + partial.shape[1:])
    parts = lax.all_to_all(parts, axis, 0, 0)
    return jnp.sum(parts.astype(jnp.float32), axis=0)


def later(rows, by):
    if by == 0:
        return rows
    return jnp.pad(rows, ((by, 0), (0, 0)))[: rows.shape[0]]


def sooner(rows, by):
    if by == 0:
        return rows
    return jnp.pad(rows, ((0, by), (0, 0)))[by:]


def local(
    tokens,
    cotangent,
    norm_gain,
    in_weight,
    conv_weight,
    conv_bias,
    select_weight,
    beta_weight,
    beta_bias,
    skip_gain,
    out_weight,
):
    parts, dps = lax.axis_size("seq"), lax.axis_size("dp")
    rows, width = tokens.shape[1:]
    block = conv_weight.shape[0]
    channels = block * dps
    taps = conv_weight.shape[1]
    rank = beta_weight.shape[1]
    states = (select_weight.shape[1] - rank) // 2
    own = in_weight.shape[0]

    flat = tokens.reshape(rows, width).astype(jnp.float32)
    scale = lax.rsqrt(jnp.mean(flat * flat, axis=-1, keepdims=True) + 1e-05)
    spread = in_weight.reshape(own, 2, dps, parts, block).transpose(3, 0, 1, 2, 4).reshape(parts, own, 2 * channels)
    vectors = jnp.concatenate(
        [conv_weight, conv_bias[:, None], beta_bias[:, None], skip_gain[:, None]], axis=1
    )
    wide = -(-select_weight.shape[1] // LANE) * LANE
    small = jnp.concatenate(
        [
            jnp.pad(select_weight, ((0, 0), (0, wide - select_weight.shape[1]))),
            beta_weight,
            jnp.pad(vectors, ((0, 0), (0, LANE - vectors.shape[1]))),
        ],
        axis=1,
    )
    if (dps, parts, 2 * own) == (8, 4, LANE):
        doubled = jnp.broadcast_to(jnp.tile(norm_gain.reshape(1, own), (1, 2)), (GAIN_ROWS, LANE))
        normed, in_w, conv_in, gate, extra = start(tokens.reshape(rows, width), spread, small, doubled, dps)
        smalls = extra[:, :block].reshape(channels, small.shape[1])
        gain = extra[:, block:, :own].reshape(dps * parts, GAIN_ROWS, own)[:, 0].reshape(width)
    else:
        gain = gathered(norm_gain, ("dp", "seq"))
        normed = gathered((flat * scale * gain.astype(jnp.float32)).astype(jnp.bfloat16), "seq")
        in_w = gathered(lax.all_to_all(spread, "seq", 0, 0).reshape(parts * own, 2 * channels), "dp")
        smalls = gathered(small, "dp")
        conv_in = jnp.dot(normed, in_w[:, :channels], preferred_element_type=jnp.float32).astype(jnp.bfloat16)
        gate = jnp.dot(normed, in_w[:, channels:], preferred_element_type=jnp.float32)
    gain = gain.astype(jnp.float32)
    select_w = smalls[:, : select_weight.shape[1]]
    beta_w = smalls[:, wide : wide + rank]
    vectors = smalls[:, wide + rank :].astype(jnp.float32)
    conv_w, conv_b = vectors[:, :taps], vectors[:, taps]
    beta_b, skip = vectors[:, taps + 1].reshape(1, channels), vectors[:, taps + 2].reshape(1, channels)
    out_shard, cot_shard, conv_in = lax.optimization_barrier((out_weight, cotangent.reshape(rows, width), conv_in))
    out_w = gathered(out_shard, "dp")
    cot = gathered(cot_shard, "seq")

    conv_wide = conv_in.astype(jnp.float32)
    conv_sum = conv_b
    for tap in range(taps):
        conv_sum = conv_sum + later(conv_wide, taps - 1 - tap) * conv_w[:, tap]
    values = jax.nn.silu(conv_sum).astype(jnp.bfloat16)
    projected = lax.psum(jnp.dot(values, select_w, preferred_element_type=jnp.float32), "seq")
    low = projected[:, :rank].astype(jnp.bfloat16)
    kq = jnp.pad(projected[:, rank:], ((0, 0), (0, LANE - 2 * states)))

    gated, mixed, history, final = forward_scan(low, kq, values, gate, beta_w, beta_b, skip, states)
    result_part = jnp.dot(gated, out_w, preferred_element_type=jnp.float32).astype(jnp.bfloat16)
    result_part = result_part.reshape(parts, rows, width)
    out_part = contract(gated, cot, 0, 0).astype(jnp.bfloat16).reshape(dps, block, width)
    dgated = contract(cot, out_w, 1, 1)
    dgate, dpre_low, dvalues, dlow, dkq, bias_grad, skip_grad, result_came, out_came = backward_scan(
        low, kq, values, gate, mixed, dgated, history, final, beta_w, beta_b, skip, result_part, out_part, states
    )
    part_here = lax.dynamic_index_in_dim(result_part, lax.axis_index("seq"), 0, False).astype(jnp.float32)
    result = (flat + (part_here + jnp.sum(result_came.astype(jnp.float32), axis=0))).astype(jnp.bfloat16)
    out_here = lax.dynamic_index_in_dim(out_part, lax.axis_index("dp"), 0, False).astype(jnp.float32)
    out_grad = out_here + jnp.sum(out_came.astype(jnp.float32), axis=0)
    dprojected = lax.psum(jnp.concatenate([dlow, dkq[:, : 2 * states]], axis=1), "seq").astype(jnp.bfloat16)
    beta_grad = contract(dpre_low, low, 0, 0)
    select_grad = contract(values, dprojected, 0, 0)
    dvalues = contract(dprojected, select_w, 1, 1) + dvalues
    s = jax.nn.sigmoid(conv_sum)
    dconv = dvalues * (s + conv_sum * s * (1.0 - s))
    conv_w_grad = jnp.stack(
        [jnp.sum(dconv * later(conv_wide, taps - 1 - tap), axis=0) for tap in range(taps)], axis=1
    )
    conv_b_grad = jnp.sum(dconv, axis=0)
    dconv_in = 0.0
    for tap in range(taps):
        dconv_in = dconv_in + sooner(dconv, taps - 1 - tap) * conv_w[:, tap]
    dmixed = jnp.concatenate([dconv_in.astype(jnp.bfloat16), dgate], axis=1)
    vector_grads = jnp.concatenate(
        [conv_w_grad, conv_b_grad[:, None], bias_grad.reshape(channels, 1), skip_grad.reshape(channels, 1)], axis=1
    )
    small_grads = jnp.concatenate(
        [
            jnp.pad(select_grad, ((0, 0), (0, wide - select_grad.shape[1]))),
            beta_grad,
            jnp.pad(vector_grads, ((0, 0), (0, LANE - vector_grads.shape[1]))),
        ],
        axis=1,
    ).reshape(dps, block, wide + rank + LANE)
    cot_here = cotangent.reshape(rows, width)
    if (dps, parts, 2 * own) == (8, 4, LANE):
        input_grad, in_grad, gain_sums, small_grads = end(
            dmixed, normed, in_w, tokens.reshape(rows, width), cot_here, gain.reshape(1, width), in_weight, small_grads,
            parts, block,
        )
        gain_sums = gain_sums[:, 0]
    else:
        in_grad = summed_rows(contract(normed, dmixed, 0, 0), "dp").astype(jnp.bfloat16)
        in_grad = lax.all_to_all(in_grad.reshape(parts, own, 2 * channels), "seq", 0, 0).astype(jnp.float32)
        in_grad = in_grad.reshape(parts, own, 2, dps, block).transpose(1, 2, 3, 0, 4).reshape(own, 2 * parts * channels)
        gain_sums = jnp.sum(in_grad * in_weight.astype(jnp.float32), axis=1)
        v = summed_rows(contract(dmixed, in_w, 1, 1), "seq") * gain
        du = scale * v - flat * (scale * scale * scale) * jnp.mean(flat * v, axis=-1, keepdims=True)
        input_grad = (cot_here.astype(jnp.float32) + du).astype(jnp.bfloat16)
        small_grads = jnp.sum(lax.all_to_all(small_grads, "dp", 0, 0), axis=0)
    rows_grad = small_grads[:, wide + rank :]
    return (
        result.reshape(tokens.shape),
        input_grad.reshape(tokens.shape),
        gain_sums / norm_gain.astype(jnp.float32),
        in_grad,
        rows_grad[:, :taps],
        rows_grad[:, taps],
        small_grads[:, : select_weight.shape[1]],
        small_grads[:, wide : wide + rank],
        rows_grad[:, taps + 1],
        rows_grad[:, taps + 2],
        out_grad,
    )


def solution(mesh):
    split = P(("dp", "seq"))
    rows = P("dp", "seq", None)
    return jax.shard_map(
        local,
        mesh=mesh,
        in_specs=(rows, rows) + (split,) * 9,
        out_specs=(rows, rows) + (split,) * 9,
        check_vma=False,
    )
```

```python
import jax
import jax.numpy as jnp
from jax import lax
from jax.experimental import pallas as pl
from jax.experimental.pallas import tpu as pltpu
from jax.sharding import PartitionSpec as P

LANE = 128


def sigmoid(v):
    return 1.0 / (1.0 + jnp.exp(-v))


def by_eights(value):
    return value.reshape(value.shape[0] // 8, 8, value.shape[1])


def as_rows(value):
    return value.reshape(value.shape[0] * 8, value.shape[2])


def spread_columns(row_ref, key_ref, query_ref, rows, states):
    lane = lax.broadcasted_iota(jnp.int32, (states, LANE), 1)
    entry = lax.broadcasted_iota(jnp.int32, (states, LANE), 0)
    pick_key = lane == entry
    pick_query = lane == entry + states

    def body(group, carry):
        for offset in range(8):
            t = group * 8 + offset
            row = jnp.broadcast_to(row_ref[group, offset : offset + 1, :], (states, LANE))
            at = pl.multiple_of(t * states, states)
            key = jnp.sum(jnp.where(pick_key, row, 0.0), axis=1, keepdims=True)
            query = jnp.sum(jnp.where(pick_query, row, 0.0), axis=1, keepdims=True)
            key_ref[pl.ds(at, states), :] = jnp.broadcast_to(key, (states, LANE))
            query_ref[pl.ds(at, states), :] = jnp.broadcast_to(query, (states, LANE))
        return carry

    lax.fori_loop(0, rows // 8, body, 0)


def step_sizes(low, kq, weight_ref, bias_ref, states):
    pre = lax.dot_general(
        low, weight_ref[...], (((1,), (1,)), ((), ())), preferred_element_type=jnp.float32
    )
    beta = sigmoid(pre + bias_ref[...])
    lane = lax.broadcasted_iota(jnp.int32, kq.shape, 1)
    keys = jnp.where(lane < states, kq, 0.0)
    square = jnp.sum(keys * keys, axis=1, keepdims=True)
    return beta, 1.0 / (1.0 + beta * square)


def forward_rows(states, rows, channels, history_ref, state_ref, key_ref, query_ref, rate_ref, input_ref, out_ref):
    tiles = channels // LANE
    per_group = min(4, tiles)
    for first in range(0, tiles, per_group):
        columns = [slice((first + j) * LANE, (first + j + 1) * LANE) for j in range(per_group)]

        def body(group, carry):
            carry = list(carry)
            for offset in range(8):
                t = group * 8 + offset
                at = pl.multiple_of(t * states, states)
                key = key_ref[pl.ds(at, states), :]
                query = query_ref[pl.ds(at, states), :]
                square = key * key
                for j, cols in enumerate(columns):
                    history_ref[pl.ds(at, states), cols] = carry[j].astype(jnp.bfloat16)
                    rate = rate_ref[group, offset : offset + 1, cols]
                    fed = input_ref[group, offset : offset + 1, cols]
                    carry[j] = (1.0 - rate * square) * carry[j] + key * fed
                    out_ref[group, offset : offset + 1, cols] = jnp.sum(query * carry[j], axis=0, keepdims=True)
            return tuple(carry)

        done = lax.fori_loop(0, rows // 8, body, tuple(state_ref[:, cols] for cols in columns))
        for cols, state in zip(columns, done):
            state_ref[:, cols] = state


def forward_body(
    states, low_ref, kq_ref, values_ref, gate_ref, weight_ref, bias_ref, skip_ref,
    gated_ref, mixed_ref, history_ref, final_ref,
    state_ref, key_ref, query_ref, rate_ref, input_ref, out_ref, row_ref,
):
    rows, channels = values_ref.shape

    @pl.when(pl.program_id(0) == 0)
    def _():
        state_ref[...] = jnp.zeros_like(state_ref)

    beta, inverse = step_sizes(low_ref[...], kq_ref[...], weight_ref, bias_ref, states)
    rates = beta * inverse
    rate_ref[...] = by_eights(rates)
    input_ref[...] = by_eights(rates * values_ref[...].astype(jnp.float32))
    row_ref[...] = by_eights(kq_ref[...])
    spread_columns(row_ref, key_ref, query_ref, rows, states)

    forward_rows(states, rows, channels, history_ref, state_ref, key_ref, query_ref, rate_ref, input_ref, out_ref)
    mixed = as_rows(out_ref[...]) + skip_ref[...] * values_ref[...].astype(jnp.float32)
    gate = gate_ref[...]
    mixed_ref[...] = mixed
    gated_ref[...] = (mixed * gate * sigmoid(gate)).astype(jnp.bfloat16)

    @pl.when(pl.program_id(0) == pl.num_programs(0) - 1)
    def _():
        final_ref[...] = state_ref[...]


def forward_scan(low, kq, values, gate, weight, bias, skip, states):
    length, channels = values.shape
    rank = low.shape[1]
    rows = min(128, length)
    blocks = length // rows
    by_row = lambda width: pl.BlockSpec((rows, width), lambda i: (i, 0))
    whole = lambda a: pl.BlockSpec(a.shape, lambda i: (0, 0))
    return pl.pallas_call(
        lambda *refs: forward_body(states, *refs),
        grid=(blocks,),
        in_specs=[by_row(rank), by_row(LANE), by_row(channels), by_row(channels), whole(weight), whole(bias), whole(skip)],
        out_specs=[
            by_row(channels),
            by_row(channels),
            pl.BlockSpec((rows * states, channels), lambda i: (i, 0)),
            pl.BlockSpec((states, channels), lambda i: (0, 0)),
        ],
        out_shape=[
            jax.ShapeDtypeStruct((length, channels), jnp.bfloat16),
            jax.ShapeDtypeStruct((length, channels), jnp.float32),
            jax.ShapeDtypeStruct((length * states, channels), jnp.bfloat16),
            jax.ShapeDtypeStruct((states, channels), jnp.float32),
        ],
        scratch_shapes=[
            pltpu.VMEM((states, channels), jnp.float32),
            pltpu.VMEM((rows * states, LANE), jnp.float32),
            pltpu.VMEM((rows * states, LANE), jnp.float32),
            pltpu.VMEM((rows // 8, 8, channels), jnp.float32),
            pltpu.VMEM((rows // 8, 8, channels), jnp.float32),
            pltpu.VMEM((rows // 8, 8, channels), jnp.float32),
            pltpu.VMEM((rows // 8, 8, LANE), jnp.float32),
        ],
        compiler_params=pltpu.CompilerParams(vmem_limit_bytes=48 * 1024 * 1024),
        cost_estimate=pl.CostEstimate(flops=14 * length * states * channels, bytes_accessed=2 * length * states * channels, transcendentals=0),
    )(low, kq, values, gate, weight, bias, skip)


def backward_body(
    states, links, low_ref, kq_ref, values_ref, gate_ref, mixed_ref, dgated_ref, history_ref, final_ref, weight_ref, bias_ref, skip_ref,
    result_ref, out_ref, dgate_ref, dpre_ref, dvalues_ref, dlow_ref, dkq_ref, bias_grad_ref, skip_grad_ref, result_came, out_came,
    grad_ref, state_ref, key_ref, query_ref, rate_ref, do_ref, values32_ref, fed_ref, kept_ref, part_key_ref, part_query_ref, row_ref, placed_ref, *sems,
):
    rows, channels = values_ref.shape
    tiles = channels // LANE
    per_group = min(4, tiles)
    copies = links(result_ref, out_ref, result_came, out_came, *sems)

    @pl.when(pl.program_id(0) == 0)
    def _():
        grad_ref[...] = jnp.zeros_like(grad_ref)
        state_ref[...] = final_ref[...]
        bias_grad_ref[...] = jnp.zeros_like(bias_grad_ref)
        skip_grad_ref[...] = jnp.zeros_like(skip_grad_ref)
        for copy in copies:
            copy.start()

    beta, inverse = step_sizes(low_ref[...], kq_ref[...], weight_ref, bias_ref, states)
    rate_ref[...] = by_eights(beta * inverse)
    values = values_ref[...].astype(jnp.float32)
    values32_ref[...] = by_eights(values)
    gate = gate_ref[...]
    dgated = dgated_ref[...].astype(jnp.float32)
    s = sigmoid(gate)
    do = dgated * (gate * s)
    do_ref[...] = by_eights(do)
    dgate_ref[...] = (dgated * mixed_ref[...] * (s + gate * s * (1.0 - s))).astype(jnp.bfloat16)
    skip_grad_ref[...] += jnp.sum(do * values, axis=0, keepdims=True)
    row_ref[...] = by_eights(kq_ref[...])
    spread_columns(row_ref, key_ref, query_ref, rows, states)

    for first in range(0, tiles, per_group):
        columns = [slice((first + j) * LANE, (first + j + 1) * LANE) for j in range(per_group)]

        def body(step, carry):
            grads, lates = list(carry[0]), list(carry[1])
            group = rows // 8 - 1 - step
            for offset in reversed(range(8)):
                t = group * 8 + offset
                at = pl.multiple_of(t * states, states)
                key = key_ref[pl.ds(at, states), :]
                query = query_ref[pl.ds(at, states), :]
                sum_key = None
                sum_query = None
                for j, cols in enumerate(columns):
                    rate = rate_ref[group, offset : offset + 1, cols]
                    out_grad = do_ref[group, offset : offset + 1, cols]
                    value = values32_ref[group, offset : offset + 1, cols]
                    before = history_ref[pl.ds(at, states), cols].astype(jnp.float32)
                    grad = grads[j] + query * out_grad
                    scaled = rate * grad
                    by_key = key * scaled
                    kept = scaled * before
                    fed_ref[group, offset : offset + 1, cols] = jnp.sum(by_key, axis=0, keepdims=True)
                    kept_ref[group, offset : offset + 1, cols] = jnp.sum(key * (key * kept), axis=0, keepdims=True)
                    term_key = value * scaled - 2.0 * (key * kept)
                    term_query = lates[j] * out_grad
                    sum_key = term_key if sum_key is None else sum_key + term_key
                    sum_query = term_query if sum_query is None else sum_query + term_query
                    grads[j] = grad - key * by_key
                    lates[j] = before
                if first == 0:
                    part_key_ref[pl.ds(at, states), :] = sum_key
                    part_query_ref[pl.ds(at, states), :] = sum_query
                else:
                    part_key_ref[pl.ds(at, states), :] += sum_key
                    part_query_ref[pl.ds(at, states), :] += sum_query
            return (tuple(grads), tuple(lates))

        start = (tuple(grad_ref[:, cols] for cols in columns), tuple(state_ref[:, cols] for cols in columns))
        grads, lates = lax.fori_loop(0, rows // 8, body, start)
        for cols, grad, late in zip(columns, grads, lates):
            grad_ref[:, cols] = grad
            state_ref[:, cols] = late

    fed = as_rows(fed_ref[...])
    dvalues_ref[...] = fed + skip_ref[...] * as_rows(do_ref[...])
    scaled = as_rows(values32_ref[...]) * fed - as_rows(kept_ref[...])
    beta, inverse = step_sizes(low_ref[...], kq_ref[...], weight_ref, bias_ref, states)
    dpre = scaled * (1.0 - beta) * inverse
    bias_grad_ref[...] += jnp.sum(dpre, axis=0, keepdims=True)
    dpre_low = dpre.astype(jnp.bfloat16)
    dpre_ref[...] = dpre_low
    dlow_ref[...] = jnp.dot(dpre_low, weight_ref[...], preferred_element_type=jnp.float32)
    through = -2.0 * jnp.sum(scaled * beta * inverse, axis=1, keepdims=True)

    lane = lax.broadcasted_iota(jnp.int32, (states, LANE), 1)
    entry = lax.broadcasted_iota(jnp.int32, (states, LANE), 0)

    def gather(group, carry):
        for offset in range(8):
            t = group * 8 + offset
            at = pl.multiple_of(t * states, states)
            key = jnp.sum(part_key_ref[pl.ds(at, states), :], axis=1, keepdims=True)
            query = jnp.sum(part_query_ref[pl.ds(at, states), :], axis=1, keepdims=True)
            placed = jnp.where(lane == entry, key, 0.0) + jnp.where(lane == entry + states, query, 0.0)
            placed_ref[group, offset : offset + 1, :] = jnp.sum(placed, axis=0, keepdims=True)
        return carry

    lax.fori_loop(0, rows // 8, gather, 0)
    lanes = lax.broadcasted_iota(jnp.int32, kq_ref.shape, 1)
    dkq_ref[...] = as_rows(placed_ref[...]) + jnp.where(lanes < states, kq_ref[...] * through, 0.0)

    @pl.when(pl.program_id(0) == pl.num_programs(0) - 1)
    def _():
        for copy in copies:
            copy.wait_recv()
        for copy in copies:
            copy.wait_send()


def exchange(parts, dps, result_ref, out_ref, result_came, out_came, result_send, result_recv, out_send, out_recv):
    d, s = lax.axis_index("dp"), lax.axis_index("seq")

    @pl.when(pl.program_id(0) == 0)
    def _():
        barrier = pltpu.get_barrier_semaphore()
        for k in range(1, parts):
            pl.semaphore_signal(barrier, inc=1, device_id=(d, lax.rem(s + k, parts)), device_id_type=MESH)
        for k in range(1, dps):
            pl.semaphore_signal(barrier, inc=1, device_id=(lax.rem(d + k, dps), s), device_id_type=MESH)
        pl.semaphore_wait(barrier, parts + dps - 2)

    copies = []
    for k in range(1, parts):
        to = lax.rem(s + k, parts)
        copies.append(
            pltpu.make_async_remote_copy(
                src_ref=result_ref.at[to], dst_ref=result_came.at[k - 1], send_sem=result_send.at[k - 1],
                recv_sem=result_recv.at[k - 1], device_id=(d, to), device_id_type=MESH,
            )
        )
    for k in range(1, dps):
        to = lax.rem(d + k, dps)
        copies.append(
            pltpu.make_async_remote_copy(
                src_ref=out_ref.at[to], dst_ref=out_came.at[k - 1], send_sem=out_send.at[k - 1],
                recv_sem=out_recv.at[k - 1], device_id=(to, s), device_id_type=MESH,
            )
        )
    return copies


def backward_scan(low, kq, values, gate, mixed, dgated, history, final, weight, bias, skip, result_part, out_part, states):
    length, channels = values.shape
    rank = low.shape[1]
    rows = min(128, length)
    blocks = length // rows
    by_row = lambda width: pl.BlockSpec((rows, width), lambda i: (blocks - 1 - i, 0))
    whole = lambda a: pl.BlockSpec(a.shape, lambda i: (0, 0))
    total = pl.BlockSpec((1, channels), lambda i: (0, 0))
    wide = pltpu.VMEM((rows // 8, 8, channels), jnp.float32)
    spread = pltpu.VMEM((rows * states, LANE), jnp.float32)
    anywhere = pl.BlockSpec(memory_space=pl.ANY)
    dma = pltpu.SemaphoreType.DMA
    parts, dps = result_part.shape[0], out_part.shape[0]
    links = lambda *refs: exchange(parts, dps, *refs)
    return pl.pallas_call(
        lambda *refs: backward_body(states, links, *refs),
        grid=(blocks,),
        in_specs=[
            by_row(rank), by_row(LANE), by_row(channels), by_row(channels), by_row(channels), by_row(channels),
            pl.BlockSpec((rows * states, channels), lambda i: (blocks - 1 - i, 0)),
            whole(final), whole(weight), whole(bias), whole(skip), anywhere, anywhere,
        ],
        out_specs=[by_row(channels), by_row(channels), by_row(channels), by_row(rank), by_row(LANE), total, total, anywhere, anywhere],
        out_shape=[
            jax.ShapeDtypeStruct((length, channels), jnp.bfloat16),
            jax.ShapeDtypeStruct((length, channels), jnp.bfloat16),
            jax.ShapeDtypeStruct((length, channels), jnp.float32),
            jax.ShapeDtypeStruct((length, rank), jnp.float32),
            jax.ShapeDtypeStruct((length, LANE), jnp.float32),
            jax.ShapeDtypeStruct((1, channels), jnp.float32),
            jax.ShapeDtypeStruct((1, channels), jnp.float32),
            jax.ShapeDtypeStruct((parts - 1,) + result_part.shape[1:], jnp.bfloat16),
            jax.ShapeDtypeStruct((dps - 1,) + out_part.shape[1:], jnp.bfloat16),
        ],
        scratch_shapes=[
            pltpu.VMEM((states, channels), jnp.float32),
            pltpu.VMEM((states, channels), jnp.float32),
            spread, spread, wide, wide, wide, wide, wide, spread, spread,
            pltpu.VMEM((rows // 8, 8, LANE), jnp.float32), pltpu.VMEM((rows // 8, 8, LANE), jnp.float32),
            dma((parts - 1,)), dma((parts - 1,)), dma((dps - 1,)), dma((dps - 1,)),
        ],
        compiler_params=pltpu.CompilerParams(collective_id=3, has_side_effects=True, vmem_limit_bytes=56 * 1024 * 1024),
        cost_estimate=pl.CostEstimate(flops=30 * length * states * channels, bytes_accessed=2 * length * states * channels, transcendentals=0),
    )(low, kq, values, gate, mixed, dgated, history, final, weight, bias, skip, result_part, out_part)


MESH = pl.DeviceIdType.MESH
GAIN_ROWS = 16


def plane_mates(d):
    core, x, y = lax.rem(d, 2), lax.rem(d // 2, 2), d // 4
    return d + 1 - 2 * core, d + 2 - 4 * x, d + 4 - 8 * y


def start_body(
    parts, block,
    tokens_ref, spread_ref, extra_ref, gain_ref,
    normed_out, weight_out, conv_ref, gate_ref, extra_out,
    tokens_all, normed_all, weight_all, extra_all,
    near_send, near_recv, plane_send, plane_recv, gain_send, gain_recv, line_send, line_recv, local_sem,
):
    d, s = lax.axis_index("dp"), lax.axis_index("seq")
    sib, xm, ym = plane_mates(d)
    own = spread_ref.shape[1]
    rows, width = tokens_ref.shape
    small = extra_ref.shape[0]
    channels = conv_ref.shape[1]
    chunk = rows // 4

    barrier = pltpu.get_barrier_semaphore()
    for mate in (sib, xm, ym):
        pl.semaphore_signal(barrier, inc=1, device_id=(mate, s), device_id_type=MESH)
    for k in range(1, parts):
        pl.semaphore_signal(barrier, inc=1, device_id=(d, lax.rem(s + k, parts)), device_id_type=MESH)
    pl.semaphore_wait(barrier, 3 + parts - 1)

    def remote(src, dst, send, recv, to):
        return pltpu.make_async_remote_copy(
            src_ref=src, dst_ref=dst, send_sem=send, recv_sem=recv, device_id=to, device_id_type=MESH
        )

    def weight_rows(owner, source):
        return weight_all.at[pl.ds(pl.multiple_of((owner * parts + source) * own, own), own), :]

    def extra_rows(owner):
        return extra_all.at[owner]

    def gain_rows(source):
        return extra_all.at[d, pl.ds(pl.multiple_of(small + source * GAIN_ROWS, GAIN_ROWS), GAIN_ROWS), pl.ds(0, LANE)]

    near = []
    for k in range(1, parts):
        to = (d, lax.rem(s + k, parts))
        near.append(remote(spread_ref.at[to[1]], weight_rows(d, s), near_send.at[k], near_recv.at[k], to))
        near.append(remote(gain_ref, gain_rows(s), gain_send.at[k], gain_recv.at[k], to))
    for copy in near:
        copy.start()
    mine = [
        pltpu.make_async_copy(spread_ref.at[s], weight_rows(d, s), local_sem.at[0]),
        pltpu.make_async_copy(gain_ref, gain_rows(s), local_sem.at[1]),
        pltpu.make_async_copy(extra_ref, extra_all.at[d, pl.ds(0, small), :], local_sem.at[2]),
        pltpu.make_async_copy(tokens_ref, tokens_all.at[pl.ds(pl.multiple_of(s * rows, rows), rows), :], local_sem.at[3]),
    ]
    for copy in mine:
        copy.start()

    def token_rows(part, c):
        return tokens_all.at[pl.ds(pl.multiple_of(part * rows + c * chunk, chunk), chunk), :]

    def token_copy(way, distance, c):
        part = s - way * (distance - 1)
        src = tokens_ref.at[pl.ds(c * chunk, chunk), :] if distance == 1 else token_rows(part, c)
        side = 0 if way == 1 else 1
        return remote(
            src, token_rows(part, c), line_send.at[side, distance, c], line_recv.at[side, distance, c], (d, s + way)
        )

    def can_send(way, distance):
        reach = s + 1 < parts if way == 1 else s >= 1
        came = s - (distance - 1) >= 0 if way == 1 else s + (distance - 1) < parts
        return jnp.logical_and(reach, came)

    def arrives(way, distance):
        return s >= distance if way == 1 else s + distance < parts

    def send_tokens(distance, c):
        for way in (1, -1):
            @pl.when(can_send(way, distance))
            def _():
                token_copy(way, distance, c).start()

    def sent_tokens(distance, c):
        for way in (1, -1):
            @pl.when(can_send(way, distance))
            def _():
                token_copy(way, distance, c).wait_send()

    def take_tokens(distance, c):
        for way in (1, -1):
            @pl.when(arrives(way, distance))
            def _():
                part = s - way * distance
                side = 0 if way == 1 else 1
                remote(
                    token_rows(part, c), token_rows(part, c), line_send.at[side, distance, c],
                    line_recv.at[side, distance, c], (d, s),
                ).wait_recv()

    units = parts + 1

    def unit(owner, k):
        return extra_rows(owner) if k == parts else weight_rows(owner, lax.rem(s - k + parts, parts))

    kinds = {"own": (d, 0), "x": (xm, 2), "y": (ym, 4)}

    def plane_copy(owner, k, rel, kind, to):
        return remote(unit(owner, k), unit(owner, k), plane_send.at[kind, k], plane_recv.at[rel, k], (to, s))

    diag = xm + ym - d
    sib_of = lambda mate: mate + sib - d

    def route(k):
        steps = [
            (0, d, 1, 0, sib), (0, d, 2, 1, xm), (0, d, 4, 2, ym),
            (2, xm, 3, 3, sib), (4, ym, 5, 5, sib), (6, diag, 7, 7, sib),
        ]
        steps.append((2, xm, 6, 4, ym) if k % 2 == 0 else (4, ym, 6, 6, xm))
        return steps

    def pass_on(stage, k):
        for at, owner, rel, kind, to in route(k):
            if at == stage:
                plane_copy(owner, k, rel, kind, to).start()

    owners = {1: sib, 2: xm, 3: sib_of(xm), 4: ym, 5: sib_of(ym), 6: diag, 7: sib_of(diag)}

    def take(rel, k):
        plane_copy(owners[rel], k, rel, 0, d).wait_recv()

    for c in range(4):
        send_tokens(1, c)
    mine[0].wait()
    pass_on(0, 0)
    for k in range(1, parts):
        near_wait = remote(
            spread_ref.at[s], weight_rows(d, lax.rem(s - k + parts, parts)), near_send.at[k], near_recv.at[k], (d, s)
        )
        near_wait.wait_recv()
        pass_on(0, k)
    mine[1].wait()
    mine[2].wait()
    for k in range(1, parts):
        remote(gain_ref, gain_rows(lax.rem(s - k + parts, parts)), gain_send.at[k], gain_recv.at[k], (d, s)).wait_recv()
    pass_on(0, parts)
    for k in range(units):
        take(2, k)
        pass_on(2, k)
        take(4, k)
        pass_on(4, k)
        if k < 4:
            take_tokens(1, k)
            send_tokens(2, k)
    for k in range(units):
        take(6, k)
        pass_on(6, k)
        if k < 4:
            take_tokens(2, k)
            send_tokens(3, k)
    for rel in (1, 3, 5, 7):
        for k in range(units):
            take(rel, k)
    mine[3].wait()
    weight_copy = pltpu.make_async_copy(weight_all, weight_out, local_sem.at[4])
    weight_copy.start()
    extra_out[...] = extra_all[...]

    lane = lax.broadcasted_iota(jnp.int32, (1, LANE), 1)
    pieces = []
    for owner in range(extra_all.shape[0]):
        for source in range(0, parts, 2):
            row = small + source * GAIN_ROWS
            even = extra_all[owner, row : row + GAIN_ROWS, 0:LANE].astype(jnp.float32)[0:1]
            odd = extra_all[owner, row + GAIN_ROWS : row + 2 * GAIN_ROWS, 0:LANE].astype(jnp.float32)[0:1]
            pieces.append(jnp.where(lane < own, even, odd))
    gain = jnp.concatenate(pieces, axis=1)

    tile = min(512, channels)

    def work(part):
        for c in range(4):
            at = pl.ds(pl.multiple_of(part * rows + c * chunk, chunk), chunk)
            flat = tokens_all[at, :].astype(jnp.float32)
            scale = lax.rsqrt(jnp.mean(flat * flat, axis=-1, keepdims=True) + 1e-05)
            normed_all[at, :] = (flat * scale * gain).astype(jnp.bfloat16)
        at = pl.ds(pl.multiple_of(part * rows, rows), rows)

        def columns(n, carry):
            left = pl.multiple_of(n * tile, tile)
            right = pl.multiple_of(channels + n * tile, tile)
            conv_ref[at, pl.ds(left, tile)] = jnp.dot(
                normed_all[at, :], weight_all[:, pl.ds(left, tile)], preferred_element_type=jnp.float32
            ).astype(jnp.bfloat16)
            gate_ref[at, pl.ds(left, tile)] = jnp.dot(
                normed_all[at, :], weight_all[:, pl.ds(right, tile)], preferred_element_type=jnp.float32
            )
            return carry

        lax.fori_loop(0, channels // tile, columns, 0)

    def work_at(low, high):
        def each(part, carry):
            away = jnp.abs(part - s)

            @pl.when(jnp.logical_and(away >= low, away <= high))
            def _():
                work(part)

            return carry

        lax.fori_loop(0, parts, each, 0)

    work_at(0, 2)
    for c in range(4):
        take_tokens(3, c)
    work_at(3, 3)
    normed_copy = pltpu.make_async_copy(normed_all, normed_out, local_sem.at[5])
    normed_copy.start()

    for copy in near:
        copy.wait_send()
    for k in range(units):
        for at, owner, rel, kind, to in route(k):
            plane_copy(owner, k, rel, kind, to).wait_send()
    for distance in range(1, parts):
        for c in range(4):
            sent_tokens(distance, c)
    weight_copy.wait()
    normed_copy.wait()


def start(tokens, spread, extra, gain, dps):
    parts, own, both = spread.shape
    rows, width = tokens.shape
    small, lanes = extra.shape
    any_space = pl.BlockSpec(memory_space=pl.ANY)
    vmem = pl.BlockSpec(memory_space=pltpu.VMEM)
    tall = small + parts * GAIN_ROWS
    dma = pltpu.SemaphoreType.DMA
    return pl.pallas_call(
        lambda *refs: start_body(parts, own, *refs),
        out_shape=[
            jax.ShapeDtypeStruct((parts * rows, width), jnp.bfloat16),
            jax.ShapeDtypeStruct((dps * parts * own, both), jnp.bfloat16),
            jax.ShapeDtypeStruct((parts * rows, both // 2), jnp.bfloat16),
            jax.ShapeDtypeStruct((parts * rows, both // 2), jnp.float32),
            jax.ShapeDtypeStruct((dps, tall, lanes), jnp.bfloat16),
        ],
        in_specs=[vmem, vmem, vmem, vmem],
        out_specs=[any_space, any_space, vmem, vmem, vmem],
        scratch_shapes=[
            pltpu.VMEM((parts * rows, width), jnp.bfloat16),
            pltpu.VMEM((parts * rows, width), jnp.bfloat16),
            pltpu.VMEM((dps * parts * own, both), jnp.bfloat16),
            pltpu.VMEM((dps, tall, lanes), jnp.bfloat16),
            dma((parts,)), dma((parts,)),
            dma((8, parts + 1)), dma((8, parts + 1)),
            dma((parts,)), dma((parts,)),
            dma((2, parts, 4)), dma((2, parts, 4)),
            dma((6,)),
        ],
        compiler_params=pltpu.CompilerParams(
            collective_id=1, has_side_effects=True, vmem_limit_bytes=56 * 1024 * 1024
        ),
        cost_estimate=pl.CostEstimate(
            flops=2 * parts * rows * width * both, bytes_accessed=40 * 1024 * 1024, transcendentals=0
        ),
    )(tokens, spread, extra, gain)


def end_body(
    parts, block,
    dmixed_ref, normed_ref, weight_ref, tokens_ref, cot_ref, gain_ref, shard_ref, small_ref,
    input_grad_ref, in_grad_ref, gain_grad_ref, small_grad_ref,
    dn, dn_recv, sib_send, sib_recv, q_send, q_recv, total, z_send, z_recv,
    small_sib_send, small_sib_recv, small_q_send, small_q_recv,
    line_send, line_recv, pair_send, pair_recv, cross_send, cross_recv, near_send, near_recv,
):
    d, s = lax.axis_index("dp"), lax.axis_index("seq")
    sib, xm, ym = plane_mates(d)
    diag = xm + ym - d
    own, both = shard_ref.shape[0], dmixed_ref.shape[1]
    rows, width = tokens_ref.shape
    chunk = rows // 4
    tall = parts * own
    tile = min(512, both)

    barrier = pltpu.get_barrier_semaphore()
    for mate in (sib, xm, ym, diag):
        pl.semaphore_signal(barrier, inc=1, device_id=(mate, s), device_id_type=MESH)
    for k in range(1, parts):
        pl.semaphore_signal(barrier, inc=1, device_id=(d, lax.rem(s + k, parts)), device_id_type=MESH)
    pl.semaphore_wait(barrier, 4 + parts - 1)

    def remote(src, dst, send, recv, to):
        return pltpu.make_async_remote_copy(
            src_ref=src, dst_ref=dst, send_sem=send, recv_sem=recv, device_id=to, device_id_type=MESH
        )

    def dn_rows(part, c):
        return pl.ds(pl.multiple_of(part * rows + c * chunk, chunk), chunk)

    def slot(way, left, part, c):
        at = parts if way == -1 and left == 0 else part
        return dn_recv.at[at, pl.ds(c * chunk, chunk), :]

    def line_copy(way, steps, c):
        side = 0 if way == 1 else 1
        part = s + way * steps
        return remote(
            dn.at[dn_rows(part, c), :], slot(way, steps - 1, part, c), line_send.at[side, steps, c],
            line_recv.at[side, steps - 1, c], (d, s + way),
        )

    def valid(way, steps):
        return s + steps < parts if way == 1 else s >= steps

    def upstream(way):
        return s >= 1 if way == 1 else s + 1 < parts

    def line_wait(way, left, c):
        side = 0 if way == 1 else 1
        place = slot(way, left, s + way * left, c)
        remote(place, place, line_send.at[side, left, c], line_recv.at[side, left, c], (d, s)).wait_recv()

    def pass_line(steps, c):
        for way in (1, -1):
            @pl.when(valid(way, steps))
            def _():
                if steps < parts - 1:
                    @pl.when(upstream(way))
                    def _():
                        line_wait(way, steps, c)
                        mine = dn_rows(s + way * steps, c)
                        came = dn_recv[s + way * steps, c * chunk : (c + 1) * chunk, :]
                        dn[mine, :] = (dn[mine, :].astype(jnp.float32) + came.astype(jnp.float32)).astype(jnp.bfloat16)

                line_copy(way, steps, c).start()

    def dn_part(part):
        at = pl.ds(pl.multiple_of(part * rows, rows), rows)

        def columns(n, carry):
            cols = pl.ds(pl.multiple_of(n * tile, tile), tile)
            dn[at, cols] = lax.dot_general(
                dmixed_ref[at, :], weight_ref[cols, :], (((1,), (1,)), ((), ())), preferred_element_type=jnp.float32
            ).astype(jnp.bfloat16)
            return carry

        lax.fori_loop(0, width // tile, columns, 0)

    def each_part(part, carry):
        dn_part(part)
        return carry

    lax.fori_loop(0, parts, each_part, 0)
    for c in range(4):
        pass_line(parts - 1, c)

    def grad_block(owner, store):
        left = pl.ds(pl.multiple_of(owner * tall, tall), tall)

        def columns(n, carry):
            cols = pl.ds(pl.multiple_of(n * tile, tile), tile)
            store(
                cols,
                lax.dot_general(
                    normed_ref[:, left], dmixed_ref[:, cols], (((0,), (0,)), ((), ())),
                    preferred_element_type=jnp.float32,
                ),
            )
            return carry

        lax.fori_loop(0, both // tile, columns, 0)

    mates = (diag, xm, ym, d)
    sib_of = lambda mate: mate + sib - d

    def pair_copy(r):
        return remote(sib_send.at[r], sib_recv.at[r], pair_send.at[0, r], pair_recv.at[0, r], (sib, s))

    def pair_copy_small(r):
        return remote(small_sib_send.at[r], small_sib_recv.at[r], pair_send.at[1, r], pair_recv.at[1, r], (sib, s))

    def cross_copy(r):
        return remote(q_send.at[r], q_recv.at[r], cross_send.at[0, r], cross_recv.at[0, r], (mates[r], s))

    def cross_copy_small(r):
        return remote(small_q_send.at[r], small_q_recv.at[r], cross_send.at[1, r], cross_recv.at[1, r], (mates[r], s))

    for r in range(4):
        def store_pair(cols, value):
            sib_send[r, :, cols] = value.astype(jnp.bfloat16)

        grad_block(sib_of(mates[r]), store_pair)
        pair_copy(r).start()
        small_sib_send[r] = small_ref[sib_of(mates[r])].astype(jnp.bfloat16)
        pair_copy_small(r).start()
        if parts > 2:
            pass_line(parts - 2, r)
    for r in range(4):
        pair_copy(r).wait_recv()
        pair_copy_small(r).wait_recv()
        both_small = small_ref[mates[r]] + small_sib_recv[r].astype(jnp.float32)
        if r < 3:
            def store_cross(cols, value):
                q_send[r, :, cols] = (value + sib_recv[r, :, cols].astype(jnp.float32)).astype(jnp.bfloat16)

            grad_block(mates[r], store_cross)
            cross_copy(r).start()
            small_q_send[r] = both_small.astype(jnp.bfloat16)
            cross_copy_small(r).start()
        else:
            def store_total(cols, value):
                total[:, cols] = value + sib_recv[r, :, cols].astype(jnp.float32)

            grad_block(mates[r], store_total)
            small_grad_ref[...] = both_small
        if parts > 3:
            pass_line(parts - 3, r)

    for r in range(3):
        cross_copy(r).wait_recv()
        cross_copy_small(r).wait_recv()
        total[...] += q_recv[r].astype(jnp.float32)
        small_grad_ref[...] += small_q_recv[r].astype(jnp.float32)
    z_send[...] = total[...].astype(jnp.bfloat16)

    def near_copy(k):
        to = lax.rem(s + k, parts)
        return remote(
            z_send.at[pl.ds(pl.multiple_of(to * own, own), own), :], z_recv.at[k], near_send.at[k], near_recv.at[k], (d, to)
        )

    for k in range(1, parts):
        near_copy(k).start()

    for c in range(4):
        mine = dn_rows(s, c)
        dn_total = dn[mine, :].astype(jnp.float32)
        for way in (1, -1):
            @pl.when(upstream(way))
            def _():
                line_wait(way, 0, c)

        at = pl.ds(c * chunk, chunk)
        low = jnp.where(upstream(1), dn_recv[s, at, :].astype(jnp.float32), 0.0)
        high = jnp.where(upstream(-1), dn_recv[parts, at, :].astype(jnp.float32), 0.0)
        v = (dn_total + low + high) * gain_ref[...]
        flat = tokens_ref[at, :].astype(jnp.float32)
        scale = lax.rsqrt(jnp.mean(flat * flat, axis=-1, keepdims=True) + 1e-05)
        du = scale * v - flat * (scale * scale * scale) * jnp.mean(flat * v, axis=-1, keepdims=True)
        input_grad_ref[at, :] = (cot_ref[at, :].astype(jnp.float32) + du).astype(jnp.bfloat16)

    channel_blocks = both // block
    gain_total = jnp.zeros((own, block), jnp.float32)
    for k in range(parts):
        source = lax.rem(s - k + parts, parts)
        if k > 0:
            near_copy(k).wait_recv()
        for j in range(channel_blocks):
            cols = slice(j * block, (j + 1) * block)
            if k == 0:
                piece = z_send[pl.ds(pl.multiple_of(s * own, own), own), cols]
            else:
                piece = z_recv[k, :, cols]
            piece = piece.astype(jnp.float32)
            to = pl.ds(pl.multiple_of((j * parts + source) * block, block), block)
            in_grad_ref[:, to] = piece
            gain_total = gain_total + piece * shard_ref[:, to].astype(jnp.float32)
    gain_grad_ref[...] = jnp.broadcast_to(jnp.sum(gain_total, axis=1, keepdims=True), gain_grad_ref.shape)

    for r in range(4):
        pair_copy(r).wait_send()
        pair_copy_small(r).wait_send()
    for r in range(3):
        cross_copy(r).wait_send()
        cross_copy_small(r).wait_send()
    for k in range(1, parts):
        near_copy(k).wait_send()
    for steps in range(1, parts):
        for c in range(4):
            for way in (1, -1):
                @pl.when(valid(way, steps))
                def _():
                    line_copy(way, steps, c).wait_send()


def end(dmixed, normed, weight, tokens, cotangent, gain, shard, small, parts, block):
    both = dmixed.shape[1]
    rows, width = tokens.shape
    own = shard.shape[0]
    dps, _, lanes = small.shape
    tall = parts * own
    vmem = pl.BlockSpec(memory_space=pltpu.VMEM)
    dma = pltpu.SemaphoreType.DMA
    low = jnp.bfloat16
    return pl.pallas_call(
        lambda *refs: end_body(parts, block, *refs),
        out_shape=[
            jax.ShapeDtypeStruct((rows, width), low),
            jax.ShapeDtypeStruct((own, parts * both), jnp.float32),
            jax.ShapeDtypeStruct((own, LANE), jnp.float32),
            jax.ShapeDtypeStruct((block, lanes), jnp.float32),
        ],
        in_specs=[vmem] * 8,
        out_specs=[vmem] * 4,
        scratch_shapes=[
            pltpu.VMEM((parts * rows, width), low),
            pltpu.VMEM((parts + 1, rows, width), low),
            pltpu.VMEM((4, tall, both), low), pltpu.VMEM((4, tall, both), low),
            pltpu.VMEM((3, tall, both), low), pltpu.VMEM((3, tall, both), low),
            pltpu.VMEM((tall, both), jnp.float32),
            pltpu.VMEM((tall, both), low), pltpu.VMEM((parts, own, both), low),
            pltpu.VMEM((4, block, lanes), low), pltpu.VMEM((4, block, lanes), low),
            pltpu.VMEM((3, block, lanes), low), pltpu.VMEM((3, block, lanes), low),
            dma((2, parts, 4)), dma((2, parts, 4)),
            dma((2, 4)), dma((2, 4)), dma((2, 3)), dma((2, 3)), dma((parts,)), dma((parts,)),
        ],
        compiler_params=pltpu.CompilerParams(
            collective_id=2, has_side_effects=True, vmem_limit_bytes=60 * 1024 * 1024
        ),
        cost_estimate=pl.CostEstimate(
            flops=4 * parts * rows * width * both, bytes_accessed=30 * 1024 * 1024, transcendentals=0
        ),
    )(dmixed, normed, weight, tokens, cotangent, gain, shard, small)


def linked_forward_body(
    states, parts, dps, taps,
    conv_in_ref, gate_ref, select_ref, conv_w_ref, conv_b_ref, weight_ref, bias_ref, skip_ref, out_shard, cot_shard,
    gated_ref, mixed_ref, history_ref, final_ref, values_ref, low_ref, kq_ref, out_all, cot_all,
    state_ref, key_ref, query_ref, rate_ref, input_ref, out_ref, row_ref,
    part_low, part_kq, came_low, came_kq, sum_low, sum_kq,
    rs_send, rs_recv, ag_send, ag_recv, out_send, out_recv, line_send, line_recv, local_sem,
):
    d, s = lax.axis_index("dp"), lax.axis_index("seq")
    step = pl.program_id(0)
    length, channels = values_ref.shape
    rows = gate_ref.shape[0]
    span = length // parts
    block = out_shard.shape[0]
    chunk = span // 4
    packed = LANE // (2 * states)
    short = span // packed

    def remote(src, dst, send, recv, to):
        return pltpu.make_async_remote_copy(
            src_ref=src, dst_ref=dst, send_sem=send, recv_sem=recv, device_id=to, device_id_type=MESH
        )

    def out_rows(owner):
        return out_all.at[pl.ds(pl.multiple_of(owner * block, block), block), :]

    out_copies = []
    for k in range(1, dps):
        out_copies.append(
            remote(out_shard, out_rows(d), out_send.at[k - 1], out_recv.at[k - 1], (lax.rem(d + k, dps), s))
        )

    def cot_rows(part, c):
        return cot_all.at[pl.ds(pl.multiple_of(part * span + c * chunk, chunk), chunk), :]

    def cot_copy(way, distance, c):
        part = s - way * (distance - 1)
        src = cot_shard.at[pl.ds(c * chunk, chunk), :] if distance == 1 else cot_rows(part, c)
        side = 0 if way == 1 else 1
        return remote(
            src, cot_rows(part, c), line_send.at[side, distance, c], line_recv.at[side, distance, c], (d, s + way)
        )

    def can_send(way, distance):
        reach = s + 1 < parts if way == 1 else s >= 1
        came = s - (distance - 1) >= 0 if way == 1 else s + (distance - 1) < parts
        return jnp.logical_and(reach, came)

    def send_cot(distance, c):
        for way in (1, -1):
            @pl.when(can_send(way, distance))
            def _():
                cot_copy(way, distance, c).start()

    def sent_cot(distance, c):
        for way in (1, -1):
            @pl.when(can_send(way, distance))
            def _():
                cot_copy(way, distance, c).wait_send()

    def take_cot(distance, c):
        for way in (1, -1):
            @pl.when(s >= distance if way == 1 else s + distance < parts)
            def _():
                part = s - way * distance
                side = 0 if way == 1 else 1
                remote(
                    cot_rows(part, c), cot_rows(part, c), line_send.at[side, distance, c],
                    line_recv.at[side, distance, c], (d, s),
                ).wait_recv()

    def own_copies():
        return (
            pltpu.make_async_copy(out_shard, out_rows(d), local_sem.at[0]),
            pltpu.make_async_copy(
                cot_shard, cot_all.at[pl.ds(pl.multiple_of(s * span, span), span), :], local_sem.at[1]
            ),
        )

    @pl.when(step == 0)
    def _():
        barrier = pltpu.get_barrier_semaphore()
        for k in range(1, parts):
            pl.semaphore_signal(barrier, inc=1, device_id=(d, lax.rem(s + k, parts)), device_id_type=MESH)
        for k in range(1, dps):
            pl.semaphore_signal(barrier, inc=1, device_id=(lax.rem(d + k, dps), s), device_id_type=MESH)
        pl.semaphore_wait(barrier, parts + dps - 2)
        state_ref[...] = jnp.zeros_like(state_ref)
        for copy in out_copies:
            copy.start()
        for copy in own_copies():
            copy.start()
        for c in range(4):
            send_cot(1, c)

    def rs_copies(k):
        at = lax.rem(s + k, parts)
        return (
            remote(part_low.at[at], came_low.at[k - 1], rs_send.at[0, k - 1], rs_recv.at[0, k - 1], (d, at)),
            remote(part_kq.at[at], came_kq.at[k - 1], rs_send.at[1, k - 1], rs_recv.at[1, k - 1], (d, at)),
        )

    def ag_copies(k):
        to = lax.rem(s + k, parts)
        return (
            remote(sum_low.at[s], sum_low.at[s], ag_send.at[0, k - 1], ag_recv.at[0, k - 1], (d, to)),
            remote(sum_kq.at[s], sum_kq.at[s], ag_send.at[1, k - 1], ag_recv.at[1, k - 1], (d, to)),
        )

    def ag_taken(k, part):
        return (
            remote(sum_low.at[part], sum_low.at[part], ag_send.at[0, k - 1], ag_recv.at[0, k - 1], (d, s)),
            remote(sum_kq.at[part], sum_kq.at[part], ag_send.at[1, k - 1], ag_recv.at[1, k - 1], (d, s)),
        )

    def convolve(part):
        start = pl.multiple_of(part * span, span)
        before = pl.multiple_of(jnp.maximum(start - 16, 0), 16)
        wide = min(256, channels)
        for left in range(0, channels, wide):
            cols = slice(left, left + wide)
            head = conv_in_ref[pl.ds(before, 16), cols].astype(jnp.float32)
            head = jnp.where(part == 0, 0.0, head)
            body = jnp.concatenate([head, conv_in_ref[pl.ds(start, span), cols].astype(jnp.float32)], axis=0)
            total = conv_b_ref[:, cols]
            for tap in range(taps):
                by = taps - 1 - tap
                total = total + body[16 - by : 16 - by + span] * conv_w_ref[tap : tap + 1, cols]
            values_ref[pl.ds(start, span), cols] = (total * sigmoid(total)).astype(jnp.bfloat16)
        projected = jnp.dot(values_ref[pl.ds(start, span), :], select_ref[...], preferred_element_type=jnp.float32)
        part_low[part] = projected[:, :LANE]
        pack = projected[:short, LANE:]
        for g in range(1, packed):
            pack = pack + pltpu.roll(projected[g * short : (g + 1) * short, LANE:], g * 2 * states, 1)
        part_kq[part] = pack

    @pl.when(step < parts - 1)
    def _():
        convolve(lax.rem(s + 1 + step, parts))

    for k in range(1, parts):
        @pl.when(step == k - 1)
        def _():
            for copy in rs_copies(k):
                copy.start()

    @pl.when(step == parts - 1)
    def _():
        convolve(s)
        low = part_low[s]
        kq = part_kq[s]
        for k in range(1, parts):
            for copy in rs_copies(k):
                copy.wait_recv()
            low = low + came_low[k - 1]
            kq = kq + came_kq[k - 1]
        sum_low[s] = low.astype(jnp.bfloat16)
        sum_kq[s] = kq
        for k in range(1, parts):
            for copy in ag_copies(k):
                copy.start()

    per_part = span // rows
    at_block = step - parts

    def unpack(part):
        start = pl.multiple_of(part * span, span)
        low_ref[pl.ds(start, span), :] = sum_low[part]
        pack = sum_kq[part]
        lane = lax.broadcasted_iota(jnp.int32, pack.shape, 1)
        for g in range(packed):
            turned = pack if g == 0 else pltpu.roll(pack, LANE - g * 2 * states, 1)
            kq_ref[pl.ds(pl.multiple_of(start + g * short, short), short), :] = jnp.where(lane < 2 * states, turned, 0.0)

    for part in range(parts):
        @pl.when(at_block == part * per_part)
        def _():
            for k in range(1, parts):
                @pl.when(lax.rem(s - k + parts, parts) == part)
                def _():
                    for copy in ag_taken(k, part):
                        copy.wait_recv()

            unpack(part)

    plan = {0: ((1, 0), (1, 1)), 1: ((1, 2), (1, 3)), 2: ((2, 0),), 3: ((2, 1),), 4: ((2, 2),), 5: ((2, 3),)}
    for at, moves in plan.items():
        @pl.when(at_block == at)
        def _():
            for distance, c in moves:
                take_cot(distance, c)
                send_cot(distance + 1, c)

    @pl.when(at_block >= 0)
    def _():
        here = pl.ds(pl.multiple_of(at_block * rows, rows), rows)
        kq = kq_ref[here, :]
        values = values_ref[here, :].astype(jnp.float32)
        beta, inverse = step_sizes(low_ref[here, :], kq, weight_ref, bias_ref, states)
        rates = beta * inverse
        rate_ref[...] = by_eights(rates)
        input_ref[...] = by_eights(rates * values)
        row_ref[...] = by_eights(kq)
        spread_columns(row_ref, key_ref, query_ref, rows, states)
        forward_rows(states, rows, channels, history_ref, state_ref, key_ref, query_ref, rate_ref, input_ref, out_ref)
        mixed = as_rows(out_ref[...]) + skip_ref[...] * values
        gate = gate_ref[...]
        mixed_ref[...] = mixed
        gated_ref[...] = (mixed * gate * sigmoid(gate)).astype(jnp.bfloat16)

    @pl.when(step == pl.num_programs(0) - 1)
    def _():
        final_ref[...] = state_ref[...]
        for c in range(4):
            take_cot(parts - 1, c)
        for copy in own_copies():
            copy.wait()
        for copy in out_copies:
            copy.wait_recv()
        for copy in out_copies:
            copy.wait_send()
        for distance in range(1, parts):
            for c in range(4):
                sent_cot(distance, c)
        for k in range(1, parts):
            for copy in rs_copies(k) + ag_copies(k):
                copy.wait_send()


def linked_forward(conv_in, gate, select, conv_w, conv_b, weight, bias, skip, out_shard, cot_shard, parts, dps, states):
    length, channels = conv_in.shape
    taps = conv_w.shape[0]
    block, width = out_shard.shape
    span = length // parts
    rows = min(128, span)
    blocks = length // rows
    short = span // (LANE // (2 * states))
    at = lambda i: jnp.maximum(i - parts, 0)
    by_row = lambda size: pl.BlockSpec((rows, size), lambda i: (at(i), 0))
    whole = lambda a: pl.BlockSpec(a.shape, lambda i: (0, 0))
    kept = lambda *shape: pl.BlockSpec(shape, lambda i: (0, 0))
    anywhere = pl.BlockSpec(memory_space=pl.ANY)
    dma = pltpu.SemaphoreType.DMA
    f32, low = jnp.float32, jnp.bfloat16
    eights = pltpu.VMEM((rows // 8, 8, channels), f32)
    return pl.pallas_call(
        lambda *refs: linked_forward_body(states, parts, dps, taps, *refs),
        grid=(parts + blocks,),
        in_specs=[
            whole(conv_in), by_row(channels), whole(select), whole(conv_w), whole(conv_b), whole(weight), whole(bias),
            whole(skip), anywhere, anywhere,
        ],
        out_specs=[
            by_row(channels), by_row(channels), pl.BlockSpec((rows * states, channels), lambda i: (at(i), 0)),
            kept(states, channels), kept(length, channels), kept(length, LANE), kept(length, LANE), anywhere, anywhere,
        ],
        out_shape=[
            jax.ShapeDtypeStruct((length, channels), low),
            jax.ShapeDtypeStruct((length, channels), f32),
            jax.ShapeDtypeStruct((length * states, channels), low),
            jax.ShapeDtypeStruct((states, channels), f32),
            jax.ShapeDtypeStruct((length, channels), low),
            jax.ShapeDtypeStruct((length, LANE), low),
            jax.ShapeDtypeStruct((length, LANE), f32),
            jax.ShapeDtypeStruct((dps * block, width), low),
            jax.ShapeDtypeStruct((length, width), low),
        ],
        scratch_shapes=[
            pltpu.VMEM((states, channels), f32),
            pltpu.VMEM((rows * states, LANE), f32), pltpu.VMEM((rows * states, LANE), f32),
            eights, eights, eights, pltpu.VMEM((rows // 8, 8, LANE), f32),
            pltpu.VMEM((parts, span, LANE), f32), pltpu.VMEM((parts, short, LANE), f32),
            pltpu.VMEM((parts - 1, span, LANE), f32), pltpu.VMEM((parts - 1, short, LANE), f32),
            pltpu.VMEM((parts, span, LANE), low), pltpu.VMEM((parts, short, LANE), f32),
            dma((2, parts - 1)), dma((2, parts - 1)), dma((2, parts - 1)), dma((2, parts - 1)),
            dma((dps - 1,)), dma((dps - 1,)), dma((2, parts, 4)), dma((2, parts, 4)), dma((2,)),
        ],
        compiler_params=pltpu.CompilerParams(
            collective_id=4, has_side_effects=True, vmem_limit_bytes=56 * 1024 * 1024
        ),
        cost_estimate=pl.CostEstimate(
            flops=14 * length * states * channels, bytes_accessed=2 * length * states * channels, transcendentals=0
        ),
    )(conv_in, gate, select, conv_w, conv_b, weight, bias, skip, out_shard, cot_shard)


def contract(left, right, left_dim, right_dim):
    return lax.dot_general(
        left, right, (((left_dim,), (right_dim,)), ((), ())), preferred_element_type=jnp.float32
    )


def gathered(shard, axis):
    return lax.all_gather(shard, axis, axis=0, tiled=True)


def scattered(total, axis):
    return lax.psum_scatter(total, axis, scatter_dimension=0, tiled=True)


def summed_rows(partial, axis):
    size = lax.axis_size(axis)
    parts = partial.astype(jnp.bfloat16).reshape((size, partial.shape[0] // size) + partial.shape[1:])
    parts = lax.all_to_all(parts, axis, 0, 0)
    return jnp.sum(parts.astype(jnp.float32), axis=0)


def later(rows, by):
    if by == 0:
        return rows
    return jnp.pad(rows, ((by, 0), (0, 0)))[: rows.shape[0]]


def sooner(rows, by):
    if by == 0:
        return rows
    return jnp.pad(rows, ((0, by), (0, 0)))[by:]


def local(
    tokens,
    cotangent,
    norm_gain,
    in_weight,
    conv_weight,
    conv_bias,
    select_weight,
    beta_weight,
    beta_bias,
    skip_gain,
    out_weight,
):
    parts, dps = lax.axis_size("seq"), lax.axis_size("dp")
    rows, width = tokens.shape[1:]
    block = conv_weight.shape[0]
    channels = block * dps
    taps = conv_weight.shape[1]
    rank = beta_weight.shape[1]
    states = (select_weight.shape[1] - rank) // 2
    own = in_weight.shape[0]

    flat = tokens.reshape(rows, width).astype(jnp.float32)
    scale = lax.rsqrt(jnp.mean(flat * flat, axis=-1, keepdims=True) + 1e-05)
    spread = in_weight.reshape(own, 2, dps, parts, block).transpose(3, 0, 1, 2, 4).reshape(parts, own, 2 * channels)
    vectors = jnp.concatenate(
        [conv_weight, conv_bias[:, None], beta_bias[:, None], skip_gain[:, None]], axis=1
    )
    wide = -(-select_weight.shape[1] // LANE) * LANE
    small = jnp.concatenate(
        [
            jnp.pad(select_weight, ((0, 0), (0, wide - select_weight.shape[1]))),
            beta_weight,
            jnp.pad(vectors, ((0, 0), (0, LANE - vectors.shape[1]))),
        ],
        axis=1,
    )
    small_slice = (dps, parts, 2 * own, rank) == (8, 4, LANE, LANE)
    if small_slice:
        doubled = jnp.broadcast_to(jnp.tile(norm_gain.reshape(1, own), (1, 2)), (GAIN_ROWS, LANE))
        normed, in_w, conv_in, gate, extra = start(tokens.reshape(rows, width), spread, small, doubled, dps)
        smalls = extra[:, :block].reshape(channels, small.shape[1])
        gain = extra[:, block:, :own].reshape(dps * parts, GAIN_ROWS, own)[:, 0].reshape(width)
    else:
        gain = gathered(norm_gain, ("dp", "seq"))
        normed = gathered((flat * scale * gain.astype(jnp.float32)).astype(jnp.bfloat16), "seq")
        in_w = gathered(lax.all_to_all(spread, "seq", 0, 0).reshape(parts * own, 2 * channels), "dp")
        smalls = gathered(small, "dp")
        conv_in = jnp.dot(normed, in_w[:, :channels], preferred_element_type=jnp.float32).astype(jnp.bfloat16)
        gate = jnp.dot(normed, in_w[:, channels:], preferred_element_type=jnp.float32)
    gain = gain.astype(jnp.float32)
    select_w = smalls[:, : select_weight.shape[1]]
    beta_w = smalls[:, wide : wide + rank]
    vectors = smalls[:, wide + rank :].astype(jnp.float32)
    conv_w, conv_b = vectors[:, :taps], vectors[:, taps]
    beta_b, skip = vectors[:, taps + 1].reshape(1, channels), vectors[:, taps + 2].reshape(1, channels)
    cot_here = cotangent.reshape(rows, width)
    conv_wide = conv_in.astype(jnp.float32)
    conv_sum = conv_b
    for tap in range(taps):
        conv_sum = conv_sum + later(conv_wide, taps - 1 - tap) * conv_w[:, tap]
    if small_slice:
        gated, mixed, history, final, values, low, kq, out_w, cot = linked_forward(
            conv_in, gate, smalls[:, :wide], conv_w.T, conv_b.reshape(1, channels), beta_w, beta_b, skip, out_weight,
            cot_here, parts, dps, states,
        )
    else:
        out_w = gathered(out_weight, "dp")
        cot = gathered(cot_here, "seq")
        values = jax.nn.silu(conv_sum).astype(jnp.bfloat16)
        projected = lax.psum(jnp.dot(values, select_w, preferred_element_type=jnp.float32), "seq")
        low = projected[:, :rank].astype(jnp.bfloat16)
        kq = jnp.pad(projected[:, rank:], ((0, 0), (0, LANE - 2 * states)))
        gated, mixed, history, final = forward_scan(low, kq, values, gate, beta_w, beta_b, skip, states)
    result_part = jnp.dot(gated, out_w, preferred_element_type=jnp.float32).astype(jnp.bfloat16)
    result_part = result_part.reshape(parts, rows, width)
    out_part = contract(gated, cot, 0, 0).astype(jnp.bfloat16).reshape(dps, block, width)
    dgated = contract(cot, out_w, 1, 1)
    dgate, dpre_low, dvalues, dlow, dkq, bias_grad, skip_grad, result_came, out_came = backward_scan(
        low, kq, values, gate, mixed, dgated, history, final, beta_w, beta_b, skip, result_part, out_part, states
    )
    part_here = lax.dynamic_index_in_dim(result_part, lax.axis_index("seq"), 0, False).astype(jnp.float32)
    result = (flat + (part_here + jnp.sum(result_came.astype(jnp.float32), axis=0))).astype(jnp.bfloat16)
    out_here = lax.dynamic_index_in_dim(out_part, lax.axis_index("dp"), 0, False).astype(jnp.float32)
    out_grad = out_here + jnp.sum(out_came.astype(jnp.float32), axis=0)
    dprojected = lax.psum(jnp.concatenate([dlow, dkq[:, : 2 * states]], axis=1), "seq").astype(jnp.bfloat16)
    beta_grad = contract(dpre_low, low, 0, 0)
    select_grad = contract(values, dprojected, 0, 0)
    dvalues = contract(dprojected, select_w, 1, 1) + dvalues
    s = jax.nn.sigmoid(conv_sum)
    dconv = dvalues * (s + conv_sum * s * (1.0 - s))
    conv_w_grad = jnp.stack(
        [jnp.sum(dconv * later(conv_wide, taps - 1 - tap), axis=0) for tap in range(taps)], axis=1
    )
    conv_b_grad = jnp.sum(dconv, axis=0)
    dconv_in = 0.0
    for tap in range(taps):
        dconv_in = dconv_in + sooner(dconv, taps - 1 - tap) * conv_w[:, tap]
    dmixed = jnp.concatenate([dconv_in.astype(jnp.bfloat16), dgate], axis=1)
    vector_grads = jnp.concatenate(
        [conv_w_grad, conv_b_grad[:, None], bias_grad.reshape(channels, 1), skip_grad.reshape(channels, 1)], axis=1
    )
    small_grads = jnp.concatenate(
        [
            jnp.pad(select_grad, ((0, 0), (0, wide - select_grad.shape[1]))),
            beta_grad,
            jnp.pad(vector_grads, ((0, 0), (0, LANE - vector_grads.shape[1]))),
        ],
        axis=1,
    ).reshape(dps, block, wide + rank + LANE)
    if small_slice:
        input_grad, in_grad, gain_sums, small_grads = end(
            dmixed, normed, in_w, tokens.reshape(rows, width), cot_here, gain.reshape(1, width), in_weight, small_grads,
            parts, block,
        )
        gain_sums = gain_sums[:, 0]
    else:
        in_grad = summed_rows(contract(normed, dmixed, 0, 0), "dp").astype(jnp.bfloat16)
        in_grad = lax.all_to_all(in_grad.reshape(parts, own, 2 * channels), "seq", 0, 0).astype(jnp.float32)
        in_grad = in_grad.reshape(parts, own, 2, dps, block).transpose(1, 2, 3, 0, 4).reshape(own, 2 * parts * channels)
        gain_sums = jnp.sum(in_grad * in_weight.astype(jnp.float32), axis=1)
        v = summed_rows(contract(dmixed, in_w, 1, 1), "seq") * gain
        du = scale * v - flat * (scale * scale * scale) * jnp.mean(flat * v, axis=-1, keepdims=True)
        input_grad = (cot_here.astype(jnp.float32) + du).astype(jnp.bfloat16)
        small_grads = jnp.sum(lax.all_to_all(small_grads, "dp", 0, 0), axis=0)
    rows_grad = small_grads[:, wide + rank :]
    return (
        result.reshape(tokens.shape),
        input_grad.reshape(tokens.shape),
        gain_sums / norm_gain.astype(jnp.float32),
        in_grad,
        rows_grad[:, :taps],
        rows_grad[:, taps],
        small_grads[:, : select_weight.shape[1]],
        small_grads[:, wide : wide + rank],
        rows_grad[:, taps + 1],
        rows_grad[:, taps + 2],
        out_grad,
    )


def solution(mesh):
    split = P(("dp", "seq"))
    rows = P("dp", "seq", None)
    return jax.shard_map(
        local,
        mesh=mesh,
        in_specs=(rows, rows) + (split,) * 9,
        out_specs=(rows, rows) + (split,) * 9,
        check_vma=False,
    )
```

```python
import jax
import jax.numpy as jnp
from jax import lax
from jax.experimental import pallas as pl
from jax.experimental.pallas import tpu as pltpu
from jax.sharding import PartitionSpec as P

LANE = 128
PER_GROUP = 4


def sigmoid(v):
    return 1.0 / (1.0 + jnp.exp(-v))


def by_eights(value):
    return value.reshape(value.shape[0] // 8, 8, value.shape[1])


def as_rows(value):
    return value.reshape(value.shape[0] * 8, value.shape[2])


def spread_columns(kq, row_ref, pick_ref, key_ref, query_ref, states):
    rows = kq.shape[0]
    high = kq.astype(jnp.bfloat16).astype(jnp.float32)
    rest = kq - high
    middle = rest.astype(jnp.bfloat16).astype(jnp.float32)
    row_ref[...] = by_eights(high + pltpu.roll(middle, 2 * states, 1) + pltpu.roll(rest - middle, 4 * states, 1))
    lane = lax.broadcasted_iota(jnp.int32, (states, LANE), 1)
    entry = lax.broadcasted_iota(jnp.int32, (states, LANE), 0)
    pick = lax.rem(lane, states) == entry

    def body(group, carry):
        for offset in range(8):
            at = pl.multiple_of((group * 8 + offset) * states, states)
            row = jnp.broadcast_to(row_ref[group, offset : offset + 1, :], (states, LANE))
            pick_ref[pl.ds(at, states), :] = jnp.where(pick, row, 0.0).astype(jnp.bfloat16)
        return carry

    lax.fori_loop(0, rows // 8, body, 0)
    term = lax.broadcasted_iota(jnp.int32, (LANE, 2 * LANE), 0)
    side = lax.broadcasted_iota(jnp.int32, (LANE, 2 * LANE), 1)
    is_query = lax.rem(term, 2 * states) >= states
    halves = jnp.where(is_query == (side >= LANE), 1.0, 0.0).astype(jnp.bfloat16)
    both = jnp.dot(pick_ref[...], halves, preferred_element_type=jnp.float32)
    key_ref[...] = both[:, :LANE]
    query_ref[...] = both[:, LANE:]


def sum_eights(half_ref, first):
    total = half_ref[pl.ds(first, 8, stride=8), :]
    for n in range(1, 8):
        total = total + half_ref[pl.ds(first + n, 8, stride=8), :]
    return total


def step_sizes(low, kq, weight_ref, bias_ref, states):
    pre = lax.dot_general(
        low, weight_ref[...], (((1,), (1,)), ((), ())), preferred_element_type=jnp.float32
    )
    beta = sigmoid(pre + bias_ref[...])
    lane = lax.broadcasted_iota(jnp.int32, kq.shape, 1)
    keys = jnp.where(lane < states, kq, 0.0)
    square = jnp.sum(keys * keys, axis=1, keepdims=True)
    return beta, 1.0 / (1.0 + beta * square)


def forward_rows(states, rows, channels, history_ref, state_ref, key_ref, query_ref, rate_ref, input_ref, out_ref, half_ref):
    tiles = channels // LANE
    per_group = min(8, tiles)
    for first in range(0, tiles, per_group):
        columns = [slice((first + j) * LANE, (first + j + 1) * LANE) for j in range(per_group)]

        def body(group, carry):
            carry = list(carry)
            for offset in range(8):
                t = group * 8 + offset
                at = pl.multiple_of(t * states, states)
                key = key_ref[pl.ds(at, states), :]
                query = query_ref[pl.ds(at, states), :]
                square = key * key
                for j, cols in enumerate(columns):
                    history_ref[pl.ds(at, states), cols] = carry[j].astype(jnp.bfloat16)
                    rate = rate_ref[group, offset : offset + 1, cols]
                    fed = input_ref[group, offset : offset + 1, cols]
                    carry[j] = (1.0 - rate * square) * carry[j] + key * fed
                    read = query * carry[j]
                    half_ref[j * 64 + offset * 8 : j * 64 + offset * 8 + 8, :] = read[0:8] + read[8:16]
            for j, cols in enumerate(columns):
                out_ref[group, :, cols] = sum_eights(half_ref, j * 64)
            return tuple(carry)

        done = lax.fori_loop(0, rows // 8, body, tuple(state_ref[:, cols] for cols in columns))
        for cols, state in zip(columns, done):
            state_ref[:, cols] = state


def forward_body(
    states, low_ref, kq_ref, values_ref, gate_ref, weight_ref, bias_ref, skip_ref,
    gated_ref, mixed_ref, history_ref, final_ref,
    state_ref, key_ref, query_ref, rate_ref, input_ref, out_ref, row_ref, pick_ref, half_ref,
):
    rows, channels = values_ref.shape

    @pl.when(pl.program_id(0) == 0)
    def _():
        state_ref[...] = jnp.zeros_like(state_ref)

    beta, inverse = step_sizes(low_ref[...], kq_ref[...], weight_ref, bias_ref, states)
    rates = beta * inverse
    rate_ref[...] = by_eights(rates)
    input_ref[...] = by_eights(rates * values_ref[...].astype(jnp.float32))
    spread_columns(kq_ref[...], row_ref, pick_ref, key_ref, query_ref, states)

    forward_rows(states, rows, channels, history_ref, state_ref, key_ref, query_ref, rate_ref, input_ref, out_ref, half_ref)
    mixed = as_rows(out_ref[...]) + skip_ref[...] * values_ref[...].astype(jnp.float32)
    gate = gate_ref[...]
    mixed_ref[...] = mixed
    gated_ref[...] = (mixed * gate * sigmoid(gate)).astype(jnp.bfloat16)

    @pl.when(pl.program_id(0) == pl.num_programs(0) - 1)
    def _():
        final_ref[...] = state_ref[...]


def forward_scan(low, kq, values, gate, weight, bias, skip, states):
    length, channels = values.shape
    rank = low.shape[1]
    rows = min(128, length)
    blocks = length // rows
    by_row = lambda width: pl.BlockSpec((rows, width), lambda i: (i, 0))
    whole = lambda a: pl.BlockSpec(a.shape, lambda i: (0, 0))
    return pl.pallas_call(
        lambda *refs: forward_body(states, *refs),
        grid=(blocks,),
        in_specs=[by_row(rank), by_row(LANE), by_row(channels), by_row(channels), whole(weight), whole(bias), whole(skip)],
        out_specs=[
            by_row(channels),
            by_row(channels),
            pl.BlockSpec((rows * states, channels), lambda i: (i, 0)),
            pl.BlockSpec((states, channels), lambda i: (0, 0)),
        ],
        out_shape=[
            jax.ShapeDtypeStruct((length, channels), jnp.bfloat16),
            jax.ShapeDtypeStruct((length, channels), jnp.float32),
            jax.ShapeDtypeStruct((length * states, channels), jnp.bfloat16),
            jax.ShapeDtypeStruct((states, channels), jnp.float32),
        ],
        scratch_shapes=[
            pltpu.VMEM((states, channels), jnp.float32),
            pltpu.VMEM((rows * states, LANE), jnp.float32),
            pltpu.VMEM((rows * states, LANE), jnp.float32),
            pltpu.VMEM((rows // 8, 8, channels), jnp.float32),
            pltpu.VMEM((rows // 8, 8, channels), jnp.float32),
            pltpu.VMEM((rows // 8, 8, channels), jnp.float32),
            pltpu.VMEM((rows // 8, 8, LANE), jnp.float32), pltpu.VMEM((rows * states, LANE), jnp.bfloat16),
            pltpu.VMEM((channels // LANE * 64, LANE), jnp.float32),
        ],
        compiler_params=pltpu.CompilerParams(vmem_limit_bytes=48 * 1024 * 1024),
        cost_estimate=pl.CostEstimate(flops=14 * length * states * channels, bytes_accessed=2 * length * states * channels, transcendentals=0),
    )(low, kq, values, gate, weight, bias, skip)


def backward_rows(
    states, rows, channels, history_ref, grad_ref, state_ref, key_ref, query_ref, rate_ref, do_ref, values32_ref,
    fed_ref, kept_ref, part_key_ref, part_query_ref, half_ref,
):
    tiles = channels // LANE
    per_group = min(PER_GROUP, tiles)
    for first in range(0, tiles, per_group):
        columns = [slice((first + j) * LANE, (first + j + 1) * LANE) for j in range(per_group)]

        def body(step, carry):
            grads, lates = list(carry[0]), list(carry[1])
            group = rows // 8 - 1 - step
            for offset in reversed(range(8)):
                t = group * 8 + offset
                at = pl.multiple_of(t * states, states)
                key = key_ref[pl.ds(at, states), :]
                query = query_ref[pl.ds(at, states), :]
                sum_key = None
                sum_query = None
                for j, cols in enumerate(columns):
                    rate = rate_ref[group, offset : offset + 1, cols]
                    out_grad = do_ref[group, offset : offset + 1, cols]
                    value = values32_ref[group, offset : offset + 1, cols]
                    before = history_ref[pl.ds(at, states), cols].astype(jnp.float32)
                    grad = grads[j] + query * out_grad
                    scaled = rate * grad
                    by_key = key * scaled
                    kept = scaled * before
                    kept = key * kept
                    twice = key * kept
                    at_fed = j * 64 + offset * 8
                    at_kept = (per_group + j) * 64 + offset * 8
                    half_ref[at_fed : at_fed + 8, :] = by_key[0:8] + by_key[8:16]
                    half_ref[at_kept : at_kept + 8, :] = twice[0:8] + twice[8:16]
                    term_key = value * scaled - 2.0 * kept
                    term_query = lates[j] * out_grad
                    sum_key = term_key if sum_key is None else sum_key + term_key
                    sum_query = term_query if sum_query is None else sum_query + term_query
                    grads[j] = grad - key * by_key
                    lates[j] = before
                if first == 0:
                    part_key_ref[pl.ds(at, states), :] = sum_key
                    part_query_ref[pl.ds(at, states), :] = sum_query
                else:
                    part_key_ref[pl.ds(at, states), :] += sum_key
                    part_query_ref[pl.ds(at, states), :] += sum_query
            for j, cols in enumerate(columns):
                fed_ref[group, :, cols] = sum_eights(half_ref, j * 64)
                kept_ref[group, :, cols] = sum_eights(half_ref, (per_group + j) * 64)
            return (tuple(grads), tuple(lates))

        start = (tuple(grad_ref[:, cols] for cols in columns), tuple(state_ref[:, cols] for cols in columns))
        grads, lates = lax.fori_loop(0, rows // 8, body, start)
        for cols, grad, late in zip(columns, grads, lates):
            grad_ref[:, cols] = grad
            state_ref[:, cols] = late


def lane_sums(part_ref, wide_ref, states):
    part = part_ref[...]
    high = part.astype(jnp.bfloat16)
    wide_ref[:, :LANE] = high
    wide_ref[:, LANE:] = (part - high.astype(jnp.float32)).astype(jnp.bfloat16)
    ones = jnp.ones((2 * LANE, LANE), jnp.bfloat16)
    part_ref[...] = jnp.dot(wide_ref[...], ones, preferred_element_type=jnp.float32)


def gather_columns(part_key_ref, part_query_ref, wide_ref, placed_ref, rows, states):
    lane_sums(part_key_ref, wide_ref, states)
    lane_sums(part_query_ref, wide_ref, states)
    lane = lax.broadcasted_iota(jnp.int32, (8, LANE), 1)

    def body(group, carry):
        total = jnp.zeros((8, LANE), jnp.float32)
        for n in range(states):
            at = group * 8 * states + n
            total = jnp.where(lane == n, part_key_ref[pl.ds(at, 8, stride=states), :], total)
            total = jnp.where(lane == n + states, part_query_ref[pl.ds(at, 8, stride=states), :], total)
        placed_ref[group] = total
        return carry

    lax.fori_loop(0, rows // 8, body, 0)


def backward_body(
    states, links, low_ref, kq_ref, values_ref, gate_ref, mixed_ref, dgated_ref, history_ref, final_ref, weight_ref, bias_ref, skip_ref,
    result_ref, out_ref, dgate_ref, dpre_ref, dvalues_ref, dlow_ref, dkq_ref, bias_grad_ref, skip_grad_ref, result_came, out_came,
    grad_ref, state_ref, key_ref, query_ref, rate_ref, do_ref, values32_ref, fed_ref, kept_ref, part_key_ref, part_query_ref, row_ref, placed_ref,
    pick_ref, wide_ref, half_ref, *sems,
):
    rows, channels = values_ref.shape
    copies = links(result_ref, out_ref, result_came, out_came, *sems)

    @pl.when(pl.program_id(0) == 0)
    def _():
        grad_ref[...] = jnp.zeros_like(grad_ref)
        state_ref[...] = final_ref[...]
        bias_grad_ref[...] = jnp.zeros_like(bias_grad_ref)
        skip_grad_ref[...] = jnp.zeros_like(skip_grad_ref)
        for copy in copies:
            copy.start()

    beta, inverse = step_sizes(low_ref[...], kq_ref[...], weight_ref, bias_ref, states)
    rate_ref[...] = by_eights(beta * inverse)
    values = values_ref[...].astype(jnp.float32)
    values32_ref[...] = by_eights(values)
    gate = gate_ref[...]
    dgated = dgated_ref[...].astype(jnp.float32)
    s = sigmoid(gate)
    do = dgated * (gate * s)
    do_ref[...] = by_eights(do)
    dgate_ref[...] = (dgated * mixed_ref[...] * (s + gate * s * (1.0 - s))).astype(jnp.bfloat16)
    skip_grad_ref[...] += jnp.sum(do * values, axis=0, keepdims=True)
    spread_columns(kq_ref[...], row_ref, pick_ref, key_ref, query_ref, states)

    backward_rows(
        states, rows, channels, history_ref, grad_ref, state_ref, key_ref, query_ref, rate_ref, do_ref, values32_ref,
        fed_ref, kept_ref, part_key_ref, part_query_ref, half_ref,
    )
    fed = as_rows(fed_ref[...])
    dvalues_ref[...] = fed + skip_ref[...] * as_rows(do_ref[...])
    scaled = as_rows(values32_ref[...]) * fed - as_rows(kept_ref[...])
    beta, inverse = step_sizes(low_ref[...], kq_ref[...], weight_ref, bias_ref, states)
    dpre = scaled * (1.0 - beta) * inverse
    bias_grad_ref[...] += jnp.sum(dpre, axis=0, keepdims=True)
    dpre_low = dpre.astype(jnp.bfloat16)
    dpre_ref[...] = dpre_low
    dlow_ref[...] = jnp.dot(dpre_low, weight_ref[...], preferred_element_type=jnp.float32)
    through = -2.0 * jnp.sum(scaled * beta * inverse, axis=1, keepdims=True)

    gather_columns(part_key_ref, part_query_ref, wide_ref, placed_ref, rows, states)
    lanes = lax.broadcasted_iota(jnp.int32, kq_ref.shape, 1)
    dkq_ref[...] = as_rows(placed_ref[...]) + jnp.where(lanes < states, kq_ref[...] * through, 0.0)

    @pl.when(pl.program_id(0) == pl.num_programs(0) - 1)
    def _():
        for copy in copies:
            copy.wait_recv()
        for copy in copies:
            copy.wait_send()


def exchange(parts, dps, result_ref, out_ref, result_came, out_came, result_send, result_recv, out_send, out_recv):
    d, s = lax.axis_index("dp"), lax.axis_index("seq")

    @pl.when(pl.program_id(0) == 0)
    def _():
        barrier = pltpu.get_barrier_semaphore()
        for k in range(1, parts):
            pl.semaphore_signal(barrier, inc=1, device_id=(d, lax.rem(s + k, parts)), device_id_type=MESH)
        for k in range(1, dps):
            pl.semaphore_signal(barrier, inc=1, device_id=(lax.rem(d + k, dps), s), device_id_type=MESH)
        pl.semaphore_wait(barrier, parts + dps - 2)

    copies = []
    for k in range(1, parts):
        to = lax.rem(s + k, parts)
        copies.append(
            pltpu.make_async_remote_copy(
                src_ref=result_ref.at[to], dst_ref=result_came.at[k - 1], send_sem=result_send.at[k - 1],
                recv_sem=result_recv.at[k - 1], device_id=(d, to), device_id_type=MESH,
            )
        )
    for k in range(1, dps):
        to = lax.rem(d + k, dps)
        copies.append(
            pltpu.make_async_remote_copy(
                src_ref=out_ref.at[to], dst_ref=out_came.at[k - 1], send_sem=out_send.at[k - 1],
                recv_sem=out_recv.at[k - 1], device_id=(to, s), device_id_type=MESH,
            )
        )
    return copies


def backward_scan(low, kq, values, gate, mixed, dgated, history, final, weight, bias, skip, result_part, out_part, states):
    length, channels = values.shape
    rank = low.shape[1]
    rows = min(128, length)
    blocks = length // rows
    by_row = lambda width: pl.BlockSpec((rows, width), lambda i: (blocks - 1 - i, 0))
    whole = lambda a: pl.BlockSpec(a.shape, lambda i: (0, 0))
    total = pl.BlockSpec((1, channels), lambda i: (0, 0))
    wide = pltpu.VMEM((rows // 8, 8, channels), jnp.float32)
    spread = pltpu.VMEM((rows * states, LANE), jnp.float32)
    anywhere = pl.BlockSpec(memory_space=pl.ANY)
    dma = pltpu.SemaphoreType.DMA
    parts, dps = result_part.shape[0], out_part.shape[0]
    links = lambda *refs: exchange(parts, dps, *refs)
    return pl.pallas_call(
        lambda *refs: backward_body(states, links, *refs),
        grid=(blocks,),
        in_specs=[
            by_row(rank), by_row(LANE), by_row(channels), by_row(channels), by_row(channels), by_row(channels),
            pl.BlockSpec((rows * states, channels), lambda i: (blocks - 1 - i, 0)),
            whole(final), whole(weight), whole(bias), whole(skip), anywhere, anywhere,
        ],
        out_specs=[by_row(channels), by_row(channels), by_row(channels), by_row(rank), by_row(LANE), total, total, anywhere, anywhere],
        out_shape=[
            jax.ShapeDtypeStruct((length, channels), jnp.bfloat16),
            jax.ShapeDtypeStruct((length, channels), jnp.bfloat16),
            jax.ShapeDtypeStruct((length, channels), jnp.float32),
            jax.ShapeDtypeStruct((length, rank), jnp.float32),
            jax.ShapeDtypeStruct((length, LANE), jnp.float32),
            jax.ShapeDtypeStruct((1, channels), jnp.float32),
            jax.ShapeDtypeStruct((1, channels), jnp.float32),
            jax.ShapeDtypeStruct((parts - 1,) + result_part.shape[1:], jnp.bfloat16),
            jax.ShapeDtypeStruct((dps - 1,) + out_part.shape[1:], jnp.bfloat16),
        ],
        scratch_shapes=[
            pltpu.VMEM((states, channels), jnp.float32),
            pltpu.VMEM((states, channels), jnp.float32),
            spread, spread, wide, wide, wide, wide, wide, spread, spread,
            pltpu.VMEM((rows // 8, 8, LANE), jnp.float32), pltpu.VMEM((rows // 8, 8, LANE), jnp.float32),
            pltpu.VMEM((rows * states, LANE), jnp.bfloat16), pltpu.VMEM((rows * states, 2 * LANE), jnp.bfloat16),
            pltpu.VMEM((2 * channels // LANE * 64, LANE), jnp.float32),
            dma((parts - 1,)), dma((parts - 1,)), dma((dps - 1,)), dma((dps - 1,)),
        ],
        compiler_params=pltpu.CompilerParams(collective_id=3, has_side_effects=True, vmem_limit_bytes=56 * 1024 * 1024),
        cost_estimate=pl.CostEstimate(flops=30 * length * states * channels, bytes_accessed=2 * length * states * channels, transcendentals=0),
    )(low, kq, values, gate, mixed, dgated, history, final, weight, bias, skip, result_part, out_part)


MESH = pl.DeviceIdType.MESH
GAIN_ROWS = 16


def plane_mates(d):
    core, x, y = lax.rem(d, 2), lax.rem(d // 2, 2), d // 4
    return d + 1 - 2 * core, d + 2 - 4 * x, d + 4 - 8 * y


def start_body(
    parts, block,
    tokens_ref, spread_ref, extra_ref, gain_ref,
    normed_out, weight_out, conv_ref, gate_ref, extra_out,
    tokens_all, normed_all, weight_all, extra_all,
    near_send, near_recv, plane_send, plane_recv, gain_send, gain_recv, line_send, line_recv, local_sem,
):
    d, s = lax.axis_index("dp"), lax.axis_index("seq")
    sib, xm, ym = plane_mates(d)
    own = spread_ref.shape[1]
    rows, width = tokens_ref.shape
    small = extra_ref.shape[0]
    channels = conv_ref.shape[1]
    chunk = rows // 4

    barrier = pltpu.get_barrier_semaphore()
    for mate in (sib, xm, ym):
        pl.semaphore_signal(barrier, inc=1, device_id=(mate, s), device_id_type=MESH)
    for k in range(1, parts):
        pl.semaphore_signal(barrier, inc=1, device_id=(d, lax.rem(s + k, parts)), device_id_type=MESH)
    pl.semaphore_wait(barrier, 3 + parts - 1)

    def remote(src, dst, send, recv, to):
        return pltpu.make_async_remote_copy(
            src_ref=src, dst_ref=dst, send_sem=send, recv_sem=recv, device_id=to, device_id_type=MESH
        )

    def weight_rows(owner, source):
        return weight_all.at[pl.ds(pl.multiple_of((owner * parts + source) * own, own), own), :]

    def extra_rows(owner):
        return extra_all.at[owner]

    def gain_rows(source):
        return extra_all.at[d, pl.ds(pl.multiple_of(small + source * GAIN_ROWS, GAIN_ROWS), GAIN_ROWS), pl.ds(0, LANE)]

    near = []
    for k in range(1, parts):
        to = (d, lax.rem(s + k, parts))
        near.append(remote(spread_ref.at[to[1]], weight_rows(d, s), near_send.at[k], near_recv.at[k], to))
        near.append(remote(gain_ref, gain_rows(s), gain_send.at[k], gain_recv.at[k], to))
    for copy in near:
        copy.start()
    mine = [
        pltpu.make_async_copy(spread_ref.at[s], weight_rows(d, s), local_sem.at[0]),
        pltpu.make_async_copy(gain_ref, gain_rows(s), local_sem.at[1]),
        pltpu.make_async_copy(extra_ref, extra_all.at[d, pl.ds(0, small), :], local_sem.at[2]),
        pltpu.make_async_copy(tokens_ref, tokens_all.at[pl.ds(pl.multiple_of(s * rows, rows), rows), :], local_sem.at[3]),
    ]
    for copy in mine:
        copy.start()

    def token_rows(part, c):
        return tokens_all.at[pl.ds(pl.multiple_of(part * rows + c * chunk, chunk), chunk), :]

    def token_copy(way, distance, c):
        part = s - way * (distance - 1)
        src = tokens_ref.at[pl.ds(c * chunk, chunk), :] if distance == 1 else token_rows(part, c)
        side = 0 if way == 1 else 1
        return remote(
            src, token_rows(part, c), line_send.at[side, distance, c], line_recv.at[side, distance, c], (d, s + way)
        )

    def can_send(way, distance):
        reach = s + 1 < parts if way == 1 else s >= 1
        came = s - (distance - 1) >= 0 if way == 1 else s + (distance - 1) < parts
        return jnp.logical_and(reach, came)

    def arrives(way, distance):
        return s >= distance if way == 1 else s + distance < parts

    def send_tokens(distance, c):
        for way in (1, -1):
            @pl.when(can_send(way, distance))
            def _():
                token_copy(way, distance, c).start()

    def sent_tokens(distance, c):
        for way in (1, -1):
            @pl.when(can_send(way, distance))
            def _():
                token_copy(way, distance, c).wait_send()

    def take_tokens(distance, c):
        for way in (1, -1):
            @pl.when(arrives(way, distance))
            def _():
                part = s - way * distance
                side = 0 if way == 1 else 1
                remote(
                    token_rows(part, c), token_rows(part, c), line_send.at[side, distance, c],
                    line_recv.at[side, distance, c], (d, s),
                ).wait_recv()

    units = parts + 1

    def unit(owner, k):
        return extra_rows(owner) if k == parts else weight_rows(owner, lax.rem(s - k + parts, parts))

    kinds = {"own": (d, 0), "x": (xm, 2), "y": (ym, 4)}

    def plane_copy(owner, k, rel, kind, to):
        return remote(unit(owner, k), unit(owner, k), plane_send.at[kind, k], plane_recv.at[rel, k], (to, s))

    diag = xm + ym - d
    sib_of = lambda mate: mate + sib - d

    def route(k):
        steps = [
            (0, d, 1, 0, sib), (0, d, 2, 1, xm), (0, d, 4, 2, ym),
            (2, xm, 3, 3, sib), (4, ym, 5, 5, sib), (6, diag, 7, 7, sib),
        ]
        steps.append((2, xm, 6, 4, ym) if k % 2 == 0 else (4, ym, 6, 6, xm))
        return steps

    def pass_on(stage, k):
        for at, owner, rel, kind, to in route(k):
            if at == stage:
                plane_copy(owner, k, rel, kind, to).start()

    owners = {1: sib, 2: xm, 3: sib_of(xm), 4: ym, 5: sib_of(ym), 6: diag, 7: sib_of(diag)}

    def take(rel, k):
        plane_copy(owners[rel], k, rel, 0, d).wait_recv()

    for c in range(4):
        send_tokens(1, c)
    mine[0].wait()
    pass_on(0, 0)
    for k in range(1, parts):
        near_wait = remote(
            spread_ref.at[s], weight_rows(d, lax.rem(s - k + parts, parts)), near_send.at[k], near_recv.at[k], (d, s)
        )
        near_wait.wait_recv()
        pass_on(0, k)
    mine[1].wait()
    mine[2].wait()
    for k in range(1, parts):
        remote(gain_ref, gain_rows(lax.rem(s - k + parts, parts)), gain_send.at[k], gain_recv.at[k], (d, s)).wait_recv()
    pass_on(0, parts)
    for k in range(units):
        take(2, k)
        pass_on(2, k)
        take(4, k)
        pass_on(4, k)
        if k < 4:
            take_tokens(1, k)
            send_tokens(2, k)
    for k in range(units):
        take(6, k)
        pass_on(6, k)
        if k < 4:
            take_tokens(2, k)
            send_tokens(3, k)
    for rel in (1, 3, 5, 7):
        for k in range(units):
            take(rel, k)
    mine[3].wait()
    weight_copy = pltpu.make_async_copy(weight_all, weight_out, local_sem.at[4])
    weight_copy.start()
    extra_out[...] = extra_all[...]

    lane = lax.broadcasted_iota(jnp.int32, (1, LANE), 1)
    pieces = []
    for owner in range(extra_all.shape[0]):
        for source in range(0, parts, 2):
            row = small + source * GAIN_ROWS
            even = extra_all[owner, row : row + GAIN_ROWS, 0:LANE].astype(jnp.float32)[0:1]
            odd = extra_all[owner, row + GAIN_ROWS : row + 2 * GAIN_ROWS, 0:LANE].astype(jnp.float32)[0:1]
            pieces.append(jnp.where(lane < own, even, odd))
    gain = jnp.concatenate(pieces, axis=1)

    tile = min(512, channels)

    def work(part):
        for c in range(4):
            at = pl.ds(pl.multiple_of(part * rows + c * chunk, chunk), chunk)
            flat = tokens_all[at, :].astype(jnp.float32)
            scale = lax.rsqrt(jnp.mean(flat * flat, axis=-1, keepdims=True) + 1e-05)
            normed_all[at, :] = (flat * scale * gain).astype(jnp.bfloat16)
        at = pl.ds(pl.multiple_of(part * rows, rows), rows)

        def columns(n, carry):
            left = pl.multiple_of(n * tile, tile)
            right = pl.multiple_of(channels + n * tile, tile)
            conv_ref[at, pl.ds(left, tile)] = jnp.dot(
                normed_all[at, :], weight_all[:, pl.ds(left, tile)], preferred_element_type=jnp.float32
            ).astype(jnp.bfloat16)
            gate_ref[at, pl.ds(left, tile)] = jnp.dot(
                normed_all[at, :], weight_all[:, pl.ds(right, tile)], preferred_element_type=jnp.float32
            )
            return carry

        lax.fori_loop(0, channels // tile, columns, 0)

    def work_at(low, high):
        def each(part, carry):
            away = jnp.abs(part - s)

            @pl.when(jnp.logical_and(away >= low, away <= high))
            def _():
                work(part)

            return carry

        lax.fori_loop(0, parts, each, 0)

    work_at(0, 2)
    for c in range(4):
        take_tokens(3, c)
    work_at(3, 3)
    normed_copy = pltpu.make_async_copy(normed_all, normed_out, local_sem.at[5])
    normed_copy.start()

    for copy in near:
        copy.wait_send()
    for k in range(units):
        for at, owner, rel, kind, to in route(k):
            plane_copy(owner, k, rel, kind, to).wait_send()
    for distance in range(1, parts):
        for c in range(4):
            sent_tokens(distance, c)
    weight_copy.wait()
    normed_copy.wait()


def start(tokens, spread, extra, gain, dps):
    parts, own, both = spread.shape
    rows, width = tokens.shape
    small, lanes = extra.shape
    any_space = pl.BlockSpec(memory_space=pl.ANY)
    vmem = pl.BlockSpec(memory_space=pltpu.VMEM)
    tall = small + parts * GAIN_ROWS
    dma = pltpu.SemaphoreType.DMA
    return pl.pallas_call(
        lambda *refs: start_body(parts, own, *refs),
        out_shape=[
            jax.ShapeDtypeStruct((parts * rows, width), jnp.bfloat16),
            jax.ShapeDtypeStruct((dps * parts * own, both), jnp.bfloat16),
            jax.ShapeDtypeStruct((parts * rows, both // 2), jnp.bfloat16),
            jax.ShapeDtypeStruct((parts * rows, both // 2), jnp.float32),
            jax.ShapeDtypeStruct((dps, tall, lanes), jnp.bfloat16),
        ],
        in_specs=[vmem, vmem, vmem, vmem],
        out_specs=[any_space, any_space, vmem, vmem, vmem],
        scratch_shapes=[
            pltpu.VMEM((parts * rows, width), jnp.bfloat16),
            pltpu.VMEM((parts * rows, width), jnp.bfloat16),
            pltpu.VMEM((dps * parts * own, both), jnp.bfloat16),
            pltpu.VMEM((dps, tall, lanes), jnp.bfloat16),
            dma((parts,)), dma((parts,)),
            dma((8, parts + 1)), dma((8, parts + 1)),
            dma((parts,)), dma((parts,)),
            dma((2, parts, 4)), dma((2, parts, 4)),
            dma((6,)),
        ],
        compiler_params=pltpu.CompilerParams(
            collective_id=1, has_side_effects=True, vmem_limit_bytes=56 * 1024 * 1024
        ),
        cost_estimate=pl.CostEstimate(
            flops=2 * parts * rows * width * both, bytes_accessed=40 * 1024 * 1024, transcendentals=0
        ),
    )(tokens, spread, extra, gain)


def line_sums(parts, rows, terms, came, send, recv):
    d, s = lax.axis_index("dp"), lax.axis_index("seq")
    chunk = rows // 4

    def own_rows(part, c):
        return pl.ds(pl.multiple_of(part * rows + c * chunk, chunk), chunk)

    def slot(way, left, part, c):
        at = parts if way == -1 and left == 0 else part
        return came.at[at, pl.ds(c * chunk, chunk), :]

    def copy_of(way, steps, c):
        side = 0 if way == 1 else 1
        part = s + way * steps
        return pltpu.make_async_remote_copy(
            src_ref=terms.at[own_rows(part, c), :], dst_ref=slot(way, steps - 1, part, c),
            send_sem=send.at[side, steps, c], recv_sem=recv.at[side, steps - 1, c],
            device_id=(d, s + way), device_id_type=MESH,
        )

    def valid(way, steps):
        return s + steps < parts if way == 1 else s >= steps

    def upstream(way):
        return s >= 1 if way == 1 else s + 1 < parts

    def taken(way, left, c):
        side = 0 if way == 1 else 1
        place = slot(way, left, s + way * left, c)
        pltpu.make_async_remote_copy(
            src_ref=place, dst_ref=place, send_sem=send.at[side, left, c], recv_sem=recv.at[side, left, c],
            device_id=(d, s), device_id_type=MESH,
        ).wait_recv()

    def pass_on(steps, c):
        for way in (1, -1):
            @pl.when(valid(way, steps))
            def _():
                if steps < parts - 1:
                    @pl.when(upstream(way))
                    def _():
                        taken(way, steps, c)
                        mine = own_rows(s + way * steps, c)
                        more = came[s + way * steps, c * chunk : (c + 1) * chunk, :]
                        terms[mine, :] = (terms[mine, :].astype(jnp.float32) + more.astype(jnp.float32)).astype(jnp.bfloat16)

                copy_of(way, steps, c).start()

    def total(c):
        for way in (1, -1):
            @pl.when(upstream(way))
            def _():
                taken(way, 0, c)

        at = pl.ds(c * chunk, chunk)
        low = jnp.where(upstream(1), came[s, at, :].astype(jnp.float32), 0.0)
        high = jnp.where(upstream(-1), came[parts, at, :].astype(jnp.float32), 0.0)
        return terms[own_rows(s, c), :].astype(jnp.float32) + low + high

    def sent():
        for steps in range(1, parts):
            for c in range(4):
                for way in (1, -1):
                    @pl.when(valid(way, steps))
                    def _():
                        copy_of(way, steps, c).wait_send()

    return pass_on, total, sent


def end_body(
    parts, block,
    dmixed_ref, normed_ref, weight_ref, tokens_ref, cot_ref, gain_ref, shard_ref, small_ref,
    input_grad_ref, in_grad_ref, gain_grad_ref, small_grad_ref,
    dn, dn_recv, sib_send, sib_recv, q_send, q_recv, total, z_send, z_recv,
    small_sib_send, small_sib_recv, small_q_send, small_q_recv,
    line_send, line_recv, pair_send, pair_recv, cross_send, cross_recv, near_send, near_recv,
):
    d, s = lax.axis_index("dp"), lax.axis_index("seq")
    sib, xm, ym = plane_mates(d)
    diag = xm + ym - d
    own, both = shard_ref.shape[0], dmixed_ref.shape[1]
    rows, width = tokens_ref.shape
    chunk = rows // 4
    tall = parts * own
    tile = min(512, both)

    barrier = pltpu.get_barrier_semaphore()
    for mate in (sib, xm, ym, diag):
        pl.semaphore_signal(barrier, inc=1, device_id=(mate, s), device_id_type=MESH)
    for k in range(1, parts):
        pl.semaphore_signal(barrier, inc=1, device_id=(d, lax.rem(s + k, parts)), device_id_type=MESH)
    pl.semaphore_wait(barrier, 4 + parts - 1)

    def remote(src, dst, send, recv, to):
        return pltpu.make_async_remote_copy(
            src_ref=src, dst_ref=dst, send_sem=send, recv_sem=recv, device_id=to, device_id_type=MESH
        )

    pass_line, line_total, line_sent = line_sums(parts, rows, dn, dn_recv, line_send, line_recv)

    def dn_part(part):
        at = pl.ds(pl.multiple_of(part * rows, rows), rows)

        def columns(n, carry):
            cols = pl.ds(pl.multiple_of(n * tile, tile), tile)
            dn[at, cols] = lax.dot_general(
                dmixed_ref[at, :], weight_ref[cols, :], (((1,), (1,)), ((), ())), preferred_element_type=jnp.float32
            ).astype(jnp.bfloat16)
            return carry

        lax.fori_loop(0, width // tile, columns, 0)

    def each_part(part, carry):
        dn_part(part)
        return carry

    lax.fori_loop(0, parts, each_part, 0)
    for c in range(4):
        pass_line(parts - 1, c)

    def grad_block(owner, store):
        left = pl.ds(pl.multiple_of(owner * tall, tall), tall)

        def columns(n, carry):
            cols = pl.ds(pl.multiple_of(n * tile, tile), tile)
            store(
                cols,
                lax.dot_general(
                    normed_ref[:, left], dmixed_ref[:, cols], (((0,), (0,)), ((), ())),
                    preferred_element_type=jnp.float32,
                ),
            )
            return carry

        lax.fori_loop(0, both // tile, columns, 0)

    mates = (diag, xm, ym, d)
    sib_of = lambda mate: mate + sib - d

    def pair_copy(r):
        return remote(sib_send.at[r], sib_recv.at[r], pair_send.at[0, r], pair_recv.at[0, r], (sib, s))

    def pair_copy_small(r):
        return remote(small_sib_send.at[r], small_sib_recv.at[r], pair_send.at[1, r], pair_recv.at[1, r], (sib, s))

    def cross_copy(r):
        return remote(q_send.at[r], q_recv.at[r], cross_send.at[0, r], cross_recv.at[0, r], (mates[r], s))

    def cross_copy_small(r):
        return remote(small_q_send.at[r], small_q_recv.at[r], cross_send.at[1, r], cross_recv.at[1, r], (mates[r], s))

    for r in range(4):
        def store_pair(cols, value):
            sib_send[r, :, cols] = value.astype(jnp.bfloat16)

        grad_block(sib_of(mates[r]), store_pair)
        pair_copy(r).start()
        small_sib_send[r] = small_ref[sib_of(mates[r])].astype(jnp.bfloat16)
        pair_copy_small(r).start()
        if parts > 2:
            pass_line(parts - 2, r)
    for r in range(4):
        pair_copy(r).wait_recv()
        pair_copy_small(r).wait_recv()
        both_small = small_ref[mates[r]] + small_sib_recv[r].astype(jnp.float32)
        if r < 3:
            def store_cross(cols, value):
                q_send[r, :, cols] = (value + sib_recv[r, :, cols].astype(jnp.float32)).astype(jnp.bfloat16)

            grad_block(mates[r], store_cross)
            cross_copy(r).start()
            small_q_send[r] = both_small.astype(jnp.bfloat16)
            cross_copy_small(r).start()
        else:
            def store_total(cols, value):
                total[:, cols] = value + sib_recv[r, :, cols].astype(jnp.float32)

            grad_block(mates[r], store_total)
            small_grad_ref[...] = both_small
        if parts > 3:
            pass_line(parts - 3, r)

    for r in range(3):
        cross_copy(r).wait_recv()
        cross_copy_small(r).wait_recv()
        total[...] += q_recv[r].astype(jnp.float32)
        small_grad_ref[...] += small_q_recv[r].astype(jnp.float32)
    z_send[...] = total[...].astype(jnp.bfloat16)

    def near_copy(k):
        to = lax.rem(s + k, parts)
        return remote(
            z_send.at[pl.ds(pl.multiple_of(to * own, own), own), :], z_recv.at[k], near_send.at[k], near_recv.at[k], (d, to)
        )

    for k in range(1, parts):
        near_copy(k).start()

    for c in range(4):
        at = pl.ds(c * chunk, chunk)
        v = line_total(c) * gain_ref[...]
        flat = tokens_ref[at, :].astype(jnp.float32)
        scale = lax.rsqrt(jnp.mean(flat * flat, axis=-1, keepdims=True) + 1e-05)
        du = scale * v - flat * (scale * scale * scale) * jnp.mean(flat * v, axis=-1, keepdims=True)
        input_grad_ref[at, :] = (cot_ref[at, :].astype(jnp.float32) + du).astype(jnp.bfloat16)

    channel_blocks = both // block
    gain_total = jnp.zeros((own, block), jnp.float32)
    for k in range(parts):
        source = lax.rem(s - k + parts, parts)
        if k > 0:
            near_copy(k).wait_recv()
        for j in range(channel_blocks):
            cols = slice(j * block, (j + 1) * block)
            if k == 0:
                piece = z_send[pl.ds(pl.multiple_of(s * own, own), own), cols]
            else:
                piece = z_recv[k, :, cols]
            piece = piece.astype(jnp.float32)
            to = pl.ds(pl.multiple_of((j * parts + source) * block, block), block)
            in_grad_ref[:, to] = piece
            gain_total = gain_total + piece * shard_ref[:, to].astype(jnp.float32)
    gain_grad_ref[...] = jnp.broadcast_to(jnp.sum(gain_total, axis=1, keepdims=True), gain_grad_ref.shape)

    for r in range(4):
        pair_copy(r).wait_send()
        pair_copy_small(r).wait_send()
    for r in range(3):
        cross_copy(r).wait_send()
        cross_copy_small(r).wait_send()
    for k in range(1, parts):
        near_copy(k).wait_send()
    line_sent()


def end(dmixed, normed, weight, tokens, cotangent, gain, shard, small, parts, block):
    both = dmixed.shape[1]
    rows, width = tokens.shape
    own = shard.shape[0]
    dps, _, lanes = small.shape
    tall = parts * own
    vmem = pl.BlockSpec(memory_space=pltpu.VMEM)
    dma = pltpu.SemaphoreType.DMA
    low = jnp.bfloat16
    return pl.pallas_call(
        lambda *refs: end_body(parts, block, *refs),
        out_shape=[
            jax.ShapeDtypeStruct((rows, width), low),
            jax.ShapeDtypeStruct((own, parts * both), jnp.float32),
            jax.ShapeDtypeStruct((own, LANE), jnp.float32),
            jax.ShapeDtypeStruct((block, lanes), jnp.float32),
        ],
        in_specs=[vmem] * 8,
        out_specs=[vmem] * 4,
        scratch_shapes=[
            pltpu.VMEM((parts * rows, width), low),
            pltpu.VMEM((parts + 1, rows, width), low),
            pltpu.VMEM((4, tall, both), low), pltpu.VMEM((4, tall, both), low),
            pltpu.VMEM((3, tall, both), low), pltpu.VMEM((3, tall, both), low),
            pltpu.VMEM((tall, both), jnp.float32),
            pltpu.VMEM((tall, both), low), pltpu.VMEM((parts, own, both), low),
            pltpu.VMEM((4, block, lanes), low), pltpu.VMEM((4, block, lanes), low),
            pltpu.VMEM((3, block, lanes), low), pltpu.VMEM((3, block, lanes), low),
            dma((2, parts, 4)), dma((2, parts, 4)),
            dma((2, 4)), dma((2, 4)), dma((2, 3)), dma((2, 3)), dma((parts,)), dma((parts,)),
        ],
        compiler_params=pltpu.CompilerParams(
            collective_id=2, has_side_effects=True, vmem_limit_bytes=60 * 1024 * 1024
        ),
        cost_estimate=pl.CostEstimate(
            flops=4 * parts * rows * width * both, bytes_accessed=30 * 1024 * 1024, transcendentals=0
        ),
    )(dmixed, normed, weight, tokens, cotangent, gain, shard, small)


def linked_forward_body(
    states, parts, dps, taps,
    conv_in_ref, gate_ref, select_ref, conv_w_ref, conv_b_ref, weight_ref, bias_ref, skip_ref, out_shard, cot_shard,
    gated_ref, mixed_ref, history_ref, final_ref, values_ref, low_ref, kq_ref, out_all, cot_all,
    state_ref, key_ref, query_ref, rate_ref, input_ref, out_ref, row_ref, pick_ref, half_ref,
    part_low, part_kq, came_low, came_kq, sum_low, sum_kq,
    rs_send, rs_recv, ag_send, ag_recv, out_send, out_recv, line_send, line_recv, local_sem,
):
    d, s = lax.axis_index("dp"), lax.axis_index("seq")
    step = pl.program_id(0)
    length, channels = values_ref.shape
    rows = gate_ref.shape[0]
    span = length // parts
    block = out_shard.shape[0]
    chunk = span // 4
    packed = LANE // (2 * states)
    short = span // packed

    def remote(src, dst, send, recv, to):
        return pltpu.make_async_remote_copy(
            src_ref=src, dst_ref=dst, send_sem=send, recv_sem=recv, device_id=to, device_id_type=MESH
        )

    def out_rows(owner):
        return out_all.at[pl.ds(pl.multiple_of(owner * block, block), block), :]

    out_copies = []
    for k in range(1, dps):
        out_copies.append(
            remote(out_shard, out_rows(d), out_send.at[k - 1], out_recv.at[k - 1], (lax.rem(d + k, dps), s))
        )

    def cot_rows(part, c):
        return cot_all.at[pl.ds(pl.multiple_of(part * span + c * chunk, chunk), chunk), :]

    def cot_copy(way, distance, c):
        part = s - way * (distance - 1)
        src = cot_shard.at[pl.ds(c * chunk, chunk), :] if distance == 1 else cot_rows(part, c)
        side = 0 if way == 1 else 1
        return remote(
            src, cot_rows(part, c), line_send.at[side, distance, c], line_recv.at[side, distance, c], (d, s + way)
        )

    def can_send(way, distance):
        reach = s + 1 < parts if way == 1 else s >= 1
        came = s - (distance - 1) >= 0 if way == 1 else s + (distance - 1) < parts
        return jnp.logical_and(reach, came)

    def send_cot(distance, c):
        for way in (1, -1):
            @pl.when(can_send(way, distance))
            def _():
                cot_copy(way, distance, c).start()

    def sent_cot(distance, c):
        for way in (1, -1):
            @pl.when(can_send(way, distance))
            def _():
                cot_copy(way, distance, c).wait_send()

    def take_cot(distance, c):
        for way in (1, -1):
            @pl.when(s >= distance if way == 1 else s + distance < parts)
            def _():
                part = s - way * distance
                side = 0 if way == 1 else 1
                remote(
                    cot_rows(part, c), cot_rows(part, c), line_send.at[side, distance, c],
                    line_recv.at[side, distance, c], (d, s),
                ).wait_recv()

    def own_copies():
        return (
            pltpu.make_async_copy(out_shard, out_rows(d), local_sem.at[0]),
            pltpu.make_async_copy(
                cot_shard, cot_all.at[pl.ds(pl.multiple_of(s * span, span), span), :], local_sem.at[1]
            ),
        )

    @pl.when(step == 0)
    def _():
        barrier = pltpu.get_barrier_semaphore()
        for k in range(1, parts):
            pl.semaphore_signal(barrier, inc=1, device_id=(d, lax.rem(s + k, parts)), device_id_type=MESH)
        for k in range(1, dps):
            pl.semaphore_signal(barrier, inc=1, device_id=(lax.rem(d + k, dps), s), device_id_type=MESH)
        pl.semaphore_wait(barrier, parts + dps - 2)
        state_ref[...] = jnp.zeros_like(state_ref)
        for copy in out_copies:
            copy.start()
        for copy in own_copies():
            copy.start()
        for c in range(2):
            send_cot(1, c)

    def rs_copies(k):
        at = lax.rem(s + k, parts)
        return (
            remote(part_low.at[at], came_low.at[k - 1], rs_send.at[0, k - 1], rs_recv.at[0, k - 1], (d, at)),
            remote(part_kq.at[at], came_kq.at[k - 1], rs_send.at[1, k - 1], rs_recv.at[1, k - 1], (d, at)),
        )

    def ag_copies(k):
        to = lax.rem(s + k, parts)
        return (
            remote(sum_low.at[s], sum_low.at[s], ag_send.at[0, k - 1], ag_recv.at[0, k - 1], (d, to)),
            remote(sum_kq.at[s], sum_kq.at[s], ag_send.at[1, k - 1], ag_recv.at[1, k - 1], (d, to)),
        )

    def ag_taken(k, part):
        return (
            remote(sum_low.at[part], sum_low.at[part], ag_send.at[0, k - 1], ag_recv.at[0, k - 1], (d, s)),
            remote(sum_kq.at[part], sum_kq.at[part], ag_send.at[1, k - 1], ag_recv.at[1, k - 1], (d, s)),
        )

    def convolve(part):
        start = pl.multiple_of(part * span, span)
        before = pl.multiple_of(jnp.maximum(start - 16, 0), 16)
        wide = min(256, channels)
        for left in range(0, channels, wide):
            cols = slice(left, left + wide)
            head = conv_in_ref[pl.ds(before, 16), cols].astype(jnp.float32)
            head = jnp.where(part == 0, 0.0, head)
            body = jnp.concatenate([head, conv_in_ref[pl.ds(start, span), cols].astype(jnp.float32)], axis=0)
            total = conv_b_ref[:, cols]
            for tap in range(taps):
                by = taps - 1 - tap
                total = total + body[16 - by : 16 - by + span] * conv_w_ref[tap : tap + 1, cols]
            values_ref[pl.ds(start, span), cols] = (total * sigmoid(total)).astype(jnp.bfloat16)
        projected = jnp.dot(values_ref[pl.ds(start, span), :], select_ref[...], preferred_element_type=jnp.float32)
        part_low[part] = projected[:, :LANE]
        pack = projected[:short, LANE:]
        for g in range(1, packed):
            pack = pack + pltpu.roll(projected[g * short : (g + 1) * short, LANE:], g * 2 * states, 1)
        part_kq[part] = pack

    @pl.when(step < parts - 1)
    def _():
        convolve(lax.rem(s + 1 + step, parts))

    for k in range(1, parts):
        @pl.when(step == k - 1)
        def _():
            for copy in rs_copies(k):
                copy.start()

    @pl.when(step == parts - 1)
    def _():
        convolve(s)
        low = part_low[s]
        kq = part_kq[s]
        for k in range(1, parts):
            for copy in rs_copies(k):
                copy.wait_recv()
            low = low + came_low[k - 1]
            kq = kq + came_kq[k - 1]
        sum_low[s] = low.astype(jnp.bfloat16)
        sum_kq[s] = kq
        for k in range(1, parts):
            for copy in ag_copies(k):
                copy.start()
        for c in range(2, 4):
            send_cot(1, c)

    per_part = span // rows
    at_block = step - parts

    def unpack(part):
        start = pl.multiple_of(part * span, span)
        low_ref[pl.ds(start, span), :] = sum_low[part]
        pack = sum_kq[part]
        lane = lax.broadcasted_iota(jnp.int32, pack.shape, 1)
        for g in range(packed):
            turned = pack if g == 0 else pltpu.roll(pack, LANE - g * 2 * states, 1)
            kq_ref[pl.ds(pl.multiple_of(start + g * short, short), short), :] = jnp.where(lane < 2 * states, turned, 0.0)

    for part in range(parts):
        @pl.when(at_block == part * per_part)
        def _():
            for k in range(1, parts):
                @pl.when(lax.rem(s - k + parts, parts) == part)
                def _():
                    for copy in ag_taken(k, part):
                        copy.wait_recv()

            unpack(part)

    plan = {0: ((1, 0), (1, 1)), 1: ((1, 2), (1, 3)), 2: ((2, 0), (2, 1)), 3: ((2, 2),), 4: ((2, 3),)}
    for at, moves in plan.items():
        @pl.when(at_block == at)
        def _():
            for distance, c in moves:
                take_cot(distance, c)
                send_cot(distance + 1, c)

    @pl.when(at_block >= 0)
    def _():
        here = pl.ds(pl.multiple_of(at_block * rows, rows), rows)
        kq = kq_ref[here, :]
        values = values_ref[here, :].astype(jnp.float32)
        beta, inverse = step_sizes(low_ref[here, :], kq, weight_ref, bias_ref, states)
        rates = beta * inverse
        rate_ref[...] = by_eights(rates)
        input_ref[...] = by_eights(rates * values)
        spread_columns(kq, row_ref, pick_ref, key_ref, query_ref, states)
        forward_rows(states, rows, channels, history_ref, state_ref, key_ref, query_ref, rate_ref, input_ref, out_ref, half_ref)
        mixed = as_rows(out_ref[...]) + skip_ref[...] * values
        gate = gate_ref[...]
        mixed_ref[...] = mixed
        gated_ref[...] = (mixed * gate * sigmoid(gate)).astype(jnp.bfloat16)

    @pl.when(step == pl.num_programs(0) - 1)
    def _():
        final_ref[...] = state_ref[...]
        for c in range(4):
            take_cot(parts - 1, c)
        for copy in own_copies():
            copy.wait()
        for copy in out_copies:
            copy.wait_recv()
        for copy in out_copies:
            copy.wait_send()
        for distance in range(1, parts):
            for c in range(4):
                sent_cot(distance, c)
        for k in range(1, parts):
            for copy in rs_copies(k) + ag_copies(k):
                copy.wait_send()


def linked_forward(conv_in, gate, select, conv_w, conv_b, weight, bias, skip, out_shard, cot_shard, parts, dps, states):
    length, channels = conv_in.shape
    taps = conv_w.shape[0]
    block, width = out_shard.shape
    span = length // parts
    rows = min(128, span)
    blocks = length // rows
    short = span // (LANE // (2 * states))
    at = lambda i: jnp.maximum(i - parts, 0)
    by_row = lambda size: pl.BlockSpec((rows, size), lambda i: (at(i), 0))
    whole = lambda a: pl.BlockSpec(a.shape, lambda i: (0, 0))
    kept = lambda *shape: pl.BlockSpec(shape, lambda i: (0, 0))
    anywhere = pl.BlockSpec(memory_space=pl.ANY)
    dma = pltpu.SemaphoreType.DMA
    f32, low = jnp.float32, jnp.bfloat16
    eights = pltpu.VMEM((rows // 8, 8, channels), f32)
    return pl.pallas_call(
        lambda *refs: linked_forward_body(states, parts, dps, taps, *refs),
        grid=(parts + blocks,),
        in_specs=[
            whole(conv_in), by_row(channels), whole(select), whole(conv_w), whole(conv_b), whole(weight), whole(bias),
            whole(skip), anywhere, anywhere,
        ],
        out_specs=[
            by_row(channels), by_row(channels), pl.BlockSpec((rows * states, channels), lambda i: (at(i), 0)),
            kept(states, channels), kept(length, channels), kept(length, LANE), kept(length, LANE), anywhere, anywhere,
        ],
        out_shape=[
            jax.ShapeDtypeStruct((length, channels), low),
            jax.ShapeDtypeStruct((length, channels), f32),
            jax.ShapeDtypeStruct((length * states, channels), low),
            jax.ShapeDtypeStruct((states, channels), f32),
            jax.ShapeDtypeStruct((length, channels), low),
            jax.ShapeDtypeStruct((length, LANE), low),
            jax.ShapeDtypeStruct((length, LANE), f32),
            jax.ShapeDtypeStruct((dps * block, width), low),
            jax.ShapeDtypeStruct((length, width), low),
        ],
        scratch_shapes=[
            pltpu.VMEM((states, channels), f32),
            pltpu.VMEM((rows * states, LANE), f32), pltpu.VMEM((rows * states, LANE), f32),
            eights, eights, eights, pltpu.VMEM((rows // 8, 8, LANE), f32),
            pltpu.VMEM((rows * states, LANE), low), pltpu.VMEM((channels // LANE * 64, LANE), f32),
            pltpu.VMEM((parts, span, LANE), f32), pltpu.VMEM((parts, short, LANE), f32),
            pltpu.VMEM((parts - 1, span, LANE), f32), pltpu.VMEM((parts - 1, short, LANE), f32),
            pltpu.VMEM((parts, span, LANE), low), pltpu.VMEM((parts, short, LANE), f32),
            dma((2, parts - 1)), dma((2, parts - 1)), dma((2, parts - 1)), dma((2, parts - 1)),
            dma((dps - 1,)), dma((dps - 1,)), dma((2, parts, 4)), dma((2, parts, 4)), dma((2,)),
        ],
        compiler_params=pltpu.CompilerParams(
            collective_id=4, has_side_effects=True, vmem_limit_bytes=56 * 1024 * 1024
        ),
        cost_estimate=pl.CostEstimate(
            flops=14 * length * states * channels, bytes_accessed=2 * length * states * channels, transcendentals=0
        ),
    )(conv_in, gate, select, conv_w, conv_b, weight, bias, skip, out_shard, cot_shard)


def linked_backward_body(
    states, parts, dps, taps,
    low_ref, kq_ref, gate_ref, mixed_ref, dgated_ref, history_ref, final_ref, weight_ref, bias_ref, skip_ref,
    values_ref, conv_in_ref, select_ref, conv_w_ref, conv_b_ref, tokens_ref, part_ref, out_ref,
    dmixed_ref, small_ref, result_ref, out_came,
    grad_ref, state_ref, key_ref, query_ref, rate_ref, do_ref, values32_ref, fed_ref, kept_ref, part_key_ref,
    part_query_ref, row_ref, placed_ref, pick_ref, wide_ref, half_ref,
    dvalues_ref, dproj_ref, next_ref, vector_ref, part_low, part_kq, came_low, came_kq, sum_low, sum_kq,
    rs_send, rs_recv, ag_send, ag_recv, result_came, line_send, line_recv, out_send, out_recv,
):
    d, s = lax.axis_index("dp"), lax.axis_index("seq")
    step = pl.program_id(0)
    rows, channels = gate_ref.shape
    length = values_ref.shape[0]
    blocks = length // rows
    span = length // parts
    per_part = span // rows
    packed = LANE // (2 * states)
    short = span // packed
    sel = select_ref.shape[1]

    def remote(src, dst, send, recv, to):
        return pltpu.make_async_remote_copy(
            src_ref=src, dst_ref=dst, send_sem=send, recv_sem=recv, device_id=to, device_id_type=MESH
        )

    copies = []
    for k in range(1, dps):
        to = lax.rem(d + k, dps)
        copies.append(remote(out_ref.at[to], out_came.at[k - 1], out_send.at[k - 1], out_recv.at[k - 1], (to, s)))
    pass_line, line_total, line_sent = line_sums(parts, span, part_ref, result_came, line_send, line_recv)

    @pl.when(step == 0)
    def _():
        barrier = pltpu.get_barrier_semaphore()
        for k in range(1, parts):
            pl.semaphore_signal(barrier, inc=1, device_id=(d, lax.rem(s + k, parts)), device_id_type=MESH)
        for k in range(1, dps):
            pl.semaphore_signal(barrier, inc=1, device_id=(lax.rem(d + k, dps), s), device_id_type=MESH)
        pl.semaphore_wait(barrier, parts + dps - 2)
        grad_ref[...] = jnp.zeros_like(grad_ref)
        state_ref[...] = final_ref[...]
        next_ref[...] = jnp.zeros_like(next_ref)
        vector_ref[...] = jnp.zeros_like(vector_ref)
        small_ref[...] = jnp.zeros_like(small_ref)
        for copy in copies:
            copy.start()

    def rs_copies(k):
        at = lax.rem(s + k, parts)
        return (
            remote(part_low.at[at], came_low.at[k - 1], rs_send.at[0, k - 1], rs_recv.at[0, k - 1], (d, at)),
            remote(part_kq.at[at], came_kq.at[k - 1], rs_send.at[1, k - 1], rs_recv.at[1, k - 1], (d, at)),
        )

    def ag_copies(k):
        to = lax.rem(s + k, parts)
        return (
            remote(sum_low.at[s], sum_low.at[s], ag_send.at[0, k - 1], ag_recv.at[0, k - 1], (d, to)),
            remote(sum_kq.at[s], sum_kq.at[s], ag_send.at[1, k - 1], ag_recv.at[1, k - 1], (d, to)),
        )

    def ag_taken(k, part):
        return (
            remote(sum_low.at[part], sum_low.at[part], ag_send.at[0, k - 1], ag_recv.at[0, k - 1], (d, s)),
            remote(sum_kq.at[part], sum_kq.at[part], ag_send.at[1, k - 1], ag_recv.at[1, k - 1], (d, s)),
        )

    def add_up():
        low = part_low[s].astype(jnp.float32)
        kq = part_kq[s]
        for k in range(1, parts):
            for copy in rs_copies(k):
                copy.wait_recv()
            low = low + came_low[k - 1].astype(jnp.float32)
            kq = kq + came_kq[k - 1]
        sum_low[s] = low.astype(jnp.bfloat16)
        sum_kq[s] = kq.astype(jnp.bfloat16)
        for k in range(1, parts):
            for copy in ag_copies(k):
                copy.start()

    def conv_back(part):
        for k in range(1, parts):
            @pl.when(lax.rem(s - k + parts, parts) == part)
            def _():
                for copy in ag_taken(k, part):
                    copy.wait_recv()

        here = pl.ds(pl.multiple_of(part * span, span), span)
        before = pl.multiple_of(jnp.maximum(part * span - 16, 0), 16)
        dproj_ref[:, :LANE] = sum_low[part]
        pack = sum_kq[part].astype(jnp.float32)
        lane = lax.broadcasted_iota(jnp.int32, pack.shape, 1)
        for g in range(packed):
            turned = pack if g == 0 else pltpu.roll(pack, LANE - g * 2 * states, 1)
            dproj_ref[g * short : (g + 1) * short, LANE:] = jnp.where(lane < 2 * states, turned, 0.0).astype(jnp.bfloat16)
        wide = min(256, channels)
        for left in range(0, channels, wide):
            cols = slice(left, left + wide)
            small_ref[cols, :sel] += lax.dot_general(
                values_ref[here, cols], dproj_ref[...], (((0,), (0,)), ((), ())), preferred_element_type=jnp.float32
            )
            head = conv_in_ref[pl.ds(before, 16), cols].astype(jnp.float32)
            head = jnp.where(part == 0, 0.0, head)
            body = jnp.concatenate([head, conv_in_ref[here, cols].astype(jnp.float32)], axis=0)
            total = conv_b_ref[:, cols]
            for tap in range(taps):
                by = taps - 1 - tap
                total = total + body[16 - by : 16 - by + span] * conv_w_ref[tap : tap + 1, cols]
            sg = sigmoid(total)
            dvalues = dvalues_ref[here, cols] + lax.dot_general(
                dproj_ref[...], select_ref[cols, :], (((1,), (1,)), ((), ())), preferred_element_type=jnp.float32
            )
            dconv = dvalues * (sg + total * sg * (1.0 - sg))
            vector_ref[taps : taps + 1, cols] += jnp.sum(dconv, axis=0, keepdims=True)
            after = jnp.concatenate([dconv, next_ref[:, cols]], axis=0)
            dconv_in = jnp.zeros_like(dconv)
            for tap in range(taps):
                by = taps - 1 - tap
                shifted = body[16 - by : 16 - by + span]
                vector_ref[tap : tap + 1, cols] += jnp.sum(dconv * shifted, axis=0, keepdims=True)
                dconv_in = dconv_in + after[by : by + span] * conv_w_ref[tap : tap + 1, cols]
            next_ref[:, cols] = dconv[0:8]
            dmixed_ref[here, cols] = dconv_in.astype(jnp.bfloat16)

    plan = (((3, 0), (3, 1)), ((3, 2), (3, 3), (2, 0)), ((2, 1), (2, 2)), ((2, 3), (1, 0)), ((1, 1),), ((1, 2),), ((1, 3),))
    for at_step, moves in enumerate(plan):
        @pl.when(step == at_step)
        def _():
            for steps, c in moves:
                pass_line(steps, c)

    for part in range(parts):
        ends = (parts - part) * per_part - 1
        sums = ends + (2 if part > 0 else 1)

        @pl.when(jnp.logical_and(step == sums, s == part))
        def _():
            add_up()

        @pl.when(step == sums + 1)
        def _():
            conv_back(part)

    @pl.when(step < blocks)
    def _():
        block = blocks - 1 - step
        here = pl.ds(pl.multiple_of(block * rows, rows), rows)
        low, kq = low_ref[...], kq_ref[...]
        beta, inverse = step_sizes(low, kq, weight_ref, bias_ref, states)
        rate_ref[...] = by_eights(beta * inverse)
        values = values_ref[here, :].astype(jnp.float32)
        values32_ref[...] = by_eights(values)
        gate = gate_ref[...]
        dgated = dgated_ref[...].astype(jnp.float32)
        sg = sigmoid(gate)
        do = dgated * (gate * sg)
        do_ref[...] = by_eights(do)
        dmixed_ref[here, channels:] = (dgated * mixed_ref[...] * (sg + gate * sg * (1.0 - sg))).astype(jnp.bfloat16)
        vector_ref[taps + 2 : taps + 3, :] += jnp.sum(do * values, axis=0, keepdims=True)
        spread_columns(kq, row_ref, pick_ref, key_ref, query_ref, states)
        backward_rows(
            states, rows, channels, history_ref, grad_ref, state_ref, key_ref, query_ref, rate_ref, do_ref, values32_ref,
            fed_ref, kept_ref, part_key_ref, part_query_ref, half_ref,
        )
        fed = as_rows(fed_ref[...])
        dvalues_ref[here, :] = fed + skip_ref[...] * as_rows(do_ref[...])
        scaled = as_rows(values32_ref[...]) * fed - as_rows(kept_ref[...])
        beta, inverse = step_sizes(low, kq, weight_ref, bias_ref, states)
        dpre = scaled * (1.0 - beta) * inverse
        vector_ref[taps + 1 : taps + 2, :] += jnp.sum(dpre, axis=0, keepdims=True)
        dpre_low = dpre.astype(jnp.bfloat16)
        small_ref[:, sel : sel + LANE] += lax.dot_general(
            dpre_low, low, (((0,), (0,)), ((), ())), preferred_element_type=jnp.float32
        )
        through = -2.0 * jnp.sum(scaled * beta * inverse, axis=1, keepdims=True)
        gather_columns(part_key_ref, part_query_ref, wide_ref, placed_ref, rows, states)
        lanes = lax.broadcasted_iota(jnp.int32, kq.shape, 1)
        dkq = as_rows(placed_ref[...]) + jnp.where(lanes < states, kq * through, 0.0)
        part = block // per_part
        within = lax.rem(block, per_part)
        part_low[part, pl.ds(pl.multiple_of(within * rows, rows), rows), :] = jnp.dot(
            dpre_low, weight_ref[...], preferred_element_type=jnp.float32
        ).astype(jnp.bfloat16)
        for g in range(packed):
            first = g * short - within * rows

            @pl.when(jnp.logical_and(first >= 0, first < rows))
            def _():
                for w in range(per_part):
                    if w * rows <= g * short < (w + 1) * rows:
                        lo = g * short - w * rows
                        piece = dkq[lo : lo + short]
                        piece = piece if g == 0 else pltpu.roll(piece, g * 2 * states, 1)
                        if g == (per_part - 1) * rows // short:
                            part_kq[part] = piece
                        else:
                            part_kq[part] += piece

        @pl.when(within == 0)
        def _():
            for k in range(1, parts):
                @pl.when(lax.rem(s + k, parts) == part)
                def _():
                    for copy in rs_copies(k):
                        copy.start()

    @pl.when(step == pl.num_programs(0) - 1)
    def _():
        small_ref[:, sel + LANE :] = jnp.transpose(vector_ref[...])
        chunk = span // 4
        for c in range(4):
            at = pl.ds(c * chunk, chunk)
            result_ref[at, :] = (tokens_ref[at, :].astype(jnp.float32) + line_total(c)).astype(jnp.bfloat16)
        line_sent()
        for copy in copies:
            copy.wait_recv()
        for copy in copies:
            copy.wait_send()
        for k in range(1, parts):
            for copy in rs_copies(k) + ag_copies(k):
                copy.wait_send()


def linked_backward(
    low, kq, gate, mixed, dgated, history, final, weight, bias, skip, values, conv_in, select, conv_w, conv_b, tokens,
    result_part, out_part, parts, states,
):
    length, channels = values.shape
    dps = out_part.shape[0]
    width = tokens.shape[1]
    taps, sel = conv_w.shape[0], select.shape[1]
    span = length // parts
    rows = min(128, span)
    blocks = length // rows
    short = span // (LANE // (2 * states))
    at = lambda i: jnp.maximum(blocks - 1 - i, 0)
    by_row = lambda size: pl.BlockSpec((rows, size), lambda i: (at(i), 0))
    whole = lambda a: pl.BlockSpec(a.shape, lambda i: (0, 0))
    kept = lambda *shape: pl.BlockSpec(shape, lambda i: (0, 0))
    anywhere = pl.BlockSpec(memory_space=pl.ANY)
    dma = pltpu.SemaphoreType.DMA
    f32, bf16 = jnp.float32, jnp.bfloat16
    wide = pltpu.VMEM((rows // 8, 8, channels), f32)
    eights = pltpu.VMEM((rows // 8, 8, LANE), f32)
    spread = pltpu.VMEM((rows * states, LANE), f32)
    return pl.pallas_call(
        lambda *refs: linked_backward_body(states, parts, dps, taps, *refs),
        grid=(blocks + 2,),
        in_specs=[
            by_row(LANE), by_row(LANE), by_row(channels), by_row(channels), by_row(channels),
            pl.BlockSpec((rows * states, channels), lambda i: (at(i), 0)),
            whole(final), whole(weight), whole(bias), whole(skip), whole(values), whole(conv_in), whole(select),
            whole(conv_w), whole(conv_b), whole(tokens), whole(result_part), anywhere,
        ],
        out_specs=[kept(length, 2 * channels), kept(channels, sel + 2 * LANE), kept(span, width), anywhere],
        out_shape=[
            jax.ShapeDtypeStruct((length, 2 * channels), bf16),
            jax.ShapeDtypeStruct((channels, sel + 2 * LANE), f32),
            jax.ShapeDtypeStruct((span, width), bf16),
            jax.ShapeDtypeStruct((dps - 1,) + out_part.shape[1:], bf16),
        ],
        scratch_shapes=[
            pltpu.VMEM((states, channels), f32), pltpu.VMEM((states, channels), f32),
            spread, spread, wide, wide, wide, wide, wide, spread, spread, eights, eights,
            pltpu.VMEM((rows * states, LANE), bf16), pltpu.VMEM((rows * states, 2 * LANE), bf16),
            pltpu.VMEM((2 * channels // LANE * 64, LANE), f32),
            pltpu.VMEM((length, channels), f32), pltpu.VMEM((span, sel), bf16), pltpu.VMEM((8, channels), f32),
            pltpu.VMEM((LANE, channels), f32),
            pltpu.VMEM((parts, span, LANE), bf16), pltpu.VMEM((parts, short, LANE), f32),
            pltpu.VMEM((parts - 1, span, LANE), bf16), pltpu.VMEM((parts - 1, short, LANE), f32),
            pltpu.VMEM((parts, span, LANE), bf16), pltpu.VMEM((parts, short, LANE), bf16),
            dma((2, parts - 1)), dma((2, parts - 1)), dma((2, parts - 1)), dma((2, parts - 1)),
            pltpu.VMEM((parts + 1, span, width), bf16), dma((2, parts, 4)), dma((2, parts, 4)),
            dma((dps - 1,)), dma((dps - 1,)),
        ],
        compiler_params=pltpu.CompilerParams(
            collective_id=5, has_side_effects=True, vmem_limit_bytes=60 * 1024 * 1024
        ),
        cost_estimate=pl.CostEstimate(
            flops=30 * length * states * channels, bytes_accessed=2 * length * states * channels, transcendentals=0
        ),
    )(low, kq, gate, mixed, dgated, history, final, weight, bias, skip, values, conv_in, select, conv_w, conv_b, tokens, result_part, out_part)


def contract(left, right, left_dim, right_dim):
    return lax.dot_general(
        left, right, (((left_dim,), (right_dim,)), ((), ())), preferred_element_type=jnp.float32
    )


def gathered(shard, axis):
    return lax.all_gather(shard, axis, axis=0, tiled=True)


def scattered(total, axis):
    return lax.psum_scatter(total, axis, scatter_dimension=0, tiled=True)


def summed_rows(partial, axis):
    size = lax.axis_size(axis)
    parts = partial.astype(jnp.bfloat16).reshape((size, partial.shape[0] // size) + partial.shape[1:])
    parts = lax.all_to_all(parts, axis, 0, 0)
    return jnp.sum(parts.astype(jnp.float32), axis=0)


def later(rows, by):
    if by == 0:
        return rows
    return jnp.pad(rows, ((by, 0), (0, 0)))[: rows.shape[0]]


def sooner(rows, by):
    if by == 0:
        return rows
    return jnp.pad(rows, ((0, by), (0, 0)))[by:]


def local(
    tokens,
    cotangent,
    norm_gain,
    in_weight,
    conv_weight,
    conv_bias,
    select_weight,
    beta_weight,
    beta_bias,
    skip_gain,
    out_weight,
):
    parts, dps = lax.axis_size("seq"), lax.axis_size("dp")
    rows, width = tokens.shape[1:]
    block = conv_weight.shape[0]
    channels = block * dps
    taps = conv_weight.shape[1]
    rank = beta_weight.shape[1]
    states = (select_weight.shape[1] - rank) // 2
    own = in_weight.shape[0]

    flat = tokens.reshape(rows, width).astype(jnp.float32)
    scale = lax.rsqrt(jnp.mean(flat * flat, axis=-1, keepdims=True) + 1e-05)
    spread = in_weight.reshape(own, 2, dps, parts, block).transpose(3, 0, 1, 2, 4).reshape(parts, own, 2 * channels)
    vectors = jnp.concatenate(
        [conv_weight, conv_bias[:, None], beta_bias[:, None], skip_gain[:, None]], axis=1
    )
    wide = -(-select_weight.shape[1] // LANE) * LANE
    small = jnp.concatenate(
        [
            jnp.pad(select_weight, ((0, 0), (0, wide - select_weight.shape[1]))),
            beta_weight,
            jnp.pad(vectors, ((0, 0), (0, LANE - vectors.shape[1]))),
        ],
        axis=1,
    )
    small_slice = (dps, parts, 2 * own, rank) == (8, 4, LANE, LANE)
    if small_slice:
        doubled = jnp.broadcast_to(jnp.tile(norm_gain.reshape(1, own), (1, 2)), (GAIN_ROWS, LANE))
        normed, in_w, conv_in, gate, extra = start(tokens.reshape(rows, width), spread, small, doubled, dps)
        smalls = extra[:, :block].reshape(channels, small.shape[1])
        gain = extra[:, block:, :own].reshape(dps * parts, GAIN_ROWS, own)[:, 0].reshape(width)
    else:
        gain = gathered(norm_gain, ("dp", "seq"))
        normed = gathered((flat * scale * gain.astype(jnp.float32)).astype(jnp.bfloat16), "seq")
        in_w = gathered(lax.all_to_all(spread, "seq", 0, 0).reshape(parts * own, 2 * channels), "dp")
        smalls = gathered(small, "dp")
        conv_in = jnp.dot(normed, in_w[:, :channels], preferred_element_type=jnp.float32).astype(jnp.bfloat16)
        gate = jnp.dot(normed, in_w[:, channels:], preferred_element_type=jnp.float32)
    gain = gain.astype(jnp.float32)
    select_w = smalls[:, : select_weight.shape[1]]
    beta_w = smalls[:, wide : wide + rank]
    vectors = smalls[:, wide + rank :].astype(jnp.float32)
    conv_w, conv_b = vectors[:, :taps], vectors[:, taps]
    beta_b, skip = vectors[:, taps + 1].reshape(1, channels), vectors[:, taps + 2].reshape(1, channels)
    cot_here = cotangent.reshape(rows, width)
    if small_slice:
        gated, mixed, history, final, values, low, kq, out_w, cot = linked_forward(
            conv_in, gate, smalls[:, :wide], conv_w.T, conv_b.reshape(1, channels), beta_w, beta_b, skip, out_weight,
            cot_here, parts, dps, states,
        )
    else:
        conv_wide = conv_in.astype(jnp.float32)
        conv_sum = conv_b
        for tap in range(taps):
            conv_sum = conv_sum + later(conv_wide, taps - 1 - tap) * conv_w[:, tap]
        out_w = gathered(out_weight, "dp")
        cot = gathered(cot_here, "seq")
        values = jax.nn.silu(conv_sum).astype(jnp.bfloat16)
        projected = lax.psum(jnp.dot(values, select_w, preferred_element_type=jnp.float32), "seq")
        low = projected[:, :rank].astype(jnp.bfloat16)
        kq = jnp.pad(projected[:, rank:], ((0, 0), (0, LANE - 2 * states)))
        gated, mixed, history, final = forward_scan(low, kq, values, gate, beta_w, beta_b, skip, states)
    result_part = jnp.dot(gated, out_w, preferred_element_type=jnp.float32).astype(jnp.bfloat16)
    out_part = contract(gated, cot, 0, 0).astype(jnp.bfloat16).reshape(dps, block, width)
    dgated = contract(cot, out_w, 1, 1)
    if small_slice:
        dmixed, small_grads, result, out_came = linked_backward(
            low, kq, gate, mixed, dgated, history, final, beta_w, beta_b, skip, values, conv_in, smalls[:, :wide], conv_w.T,
            conv_b.reshape(1, channels), tokens.reshape(rows, width), result_part, out_part, parts, states,
        )
        small_grads = small_grads.reshape(dps, block, wide + rank + LANE)
    else:
        result_part = result_part.reshape(parts, rows, width)
        dgate, dpre_low, dvalues, dlow, dkq, bias_grad, skip_grad, result_came, out_came = backward_scan(
            low, kq, values, gate, mixed, dgated, history, final, beta_w, beta_b, skip, result_part, out_part, states
        )
        part_here = lax.dynamic_index_in_dim(result_part, lax.axis_index("seq"), 0, False).astype(jnp.float32)
        result = (flat + (part_here + jnp.sum(result_came.astype(jnp.float32), axis=0))).astype(jnp.bfloat16)
        dprojected = lax.psum(jnp.concatenate([dlow, dkq[:, : 2 * states]], axis=1), "seq").astype(jnp.bfloat16)
        beta_grad = contract(dpre_low, low, 0, 0)
        select_grad = contract(values, dprojected, 0, 0)
        dvalues = contract(dprojected, select_w, 1, 1) + dvalues
        s = jax.nn.sigmoid(conv_sum)
        dconv = dvalues * (s + conv_sum * s * (1.0 - s))
        conv_w_grad = jnp.stack(
            [jnp.sum(dconv * later(conv_wide, taps - 1 - tap), axis=0) for tap in range(taps)], axis=1
        )
        conv_b_grad = jnp.sum(dconv, axis=0)
        dconv_in = 0.0
        for tap in range(taps):
            dconv_in = dconv_in + sooner(dconv, taps - 1 - tap) * conv_w[:, tap]
        dmixed = jnp.concatenate([dconv_in.astype(jnp.bfloat16), dgate], axis=1)
        vector_grads = jnp.concatenate(
            [conv_w_grad, conv_b_grad[:, None], bias_grad.reshape(channels, 1), skip_grad.reshape(channels, 1)], axis=1
        )
        small_grads = jnp.concatenate(
            [
                jnp.pad(select_grad, ((0, 0), (0, wide - select_grad.shape[1]))),
                beta_grad,
                jnp.pad(vector_grads, ((0, 0), (0, LANE - vector_grads.shape[1]))),
            ],
            axis=1,
        ).reshape(dps, block, wide + rank + LANE)
    out_here = lax.dynamic_index_in_dim(out_part, lax.axis_index("dp"), 0, False).astype(jnp.float32)
    out_grad = out_here + jnp.sum(out_came.astype(jnp.float32), axis=0)
    if small_slice:
        input_grad, in_grad, gain_sums, small_grads = end(
            dmixed, normed, in_w, tokens.reshape(rows, width), cot_here, gain.reshape(1, width), in_weight, small_grads,
            parts, block,
        )
        gain_sums = gain_sums[:, 0]
    else:
        in_grad = summed_rows(contract(normed, dmixed, 0, 0), "dp").astype(jnp.bfloat16)
        in_grad = lax.all_to_all(in_grad.reshape(parts, own, 2 * channels), "seq", 0, 0).astype(jnp.float32)
        in_grad = in_grad.reshape(parts, own, 2, dps, block).transpose(1, 2, 3, 0, 4).reshape(own, 2 * parts * channels)
        gain_sums = jnp.sum(in_grad * in_weight.astype(jnp.float32), axis=1)
        v = summed_rows(contract(dmixed, in_w, 1, 1), "seq") * gain
        du = scale * v - flat * (scale * scale * scale) * jnp.mean(flat * v, axis=-1, keepdims=True)
        input_grad = (cot_here.astype(jnp.float32) + du).astype(jnp.bfloat16)
        small_grads = jnp.sum(lax.all_to_all(small_grads, "dp", 0, 0), axis=0)
    rows_grad = small_grads[:, wide + rank :]
    return (
        result.reshape(tokens.shape),
        input_grad.reshape(tokens.shape),
        gain_sums / norm_gain.astype(jnp.float32),
        in_grad,
        rows_grad[:, :taps],
        rows_grad[:, taps],
        small_grads[:, : select_weight.shape[1]],
        small_grads[:, wide : wide + rank],
        rows_grad[:, taps + 1],
        rows_grad[:, taps + 2],
        out_grad,
    )


def solution(mesh):
    split = P(("dp", "seq"))
    rows = P("dp", "seq", None)
    return jax.shard_map(
        local,
        mesh=mesh,
        in_specs=(rows, rows) + (split,) * 9,
        out_specs=(rows, rows) + (split,) * 9,
        check_vma=False,
    )
```

```python
import jax
import jax.numpy as jnp
from jax import lax
from jax.experimental import pallas as pl
from jax.experimental.pallas import tpu as pltpu
from jax.sharding import PartitionSpec as P

LANE = 128
PER_GROUP = 4


def sigmoid(v):
    return 1.0 / (1.0 + jnp.exp(-v))


def by_eights(value):
    return value.reshape(value.shape[0] // 8, 8, value.shape[1])


def as_rows(value):
    return value.reshape(value.shape[0] * 8, value.shape[2])


def spread_columns(kq, row_ref, pick_ref, key_ref, query_ref, states):
    rows = kq.shape[0]
    high = kq.astype(jnp.bfloat16).astype(jnp.float32)
    rest = kq - high
    middle = rest.astype(jnp.bfloat16).astype(jnp.float32)
    row_ref[...] = by_eights(high + pltpu.roll(middle, 2 * states, 1) + pltpu.roll(rest - middle, 4 * states, 1))
    lane = lax.broadcasted_iota(jnp.int32, (states, LANE), 1)
    entry = lax.broadcasted_iota(jnp.int32, (states, LANE), 0)
    pick = lax.rem(lane, states) == entry

    def body(group, carry):
        for offset in range(8):
            at = pl.multiple_of((group * 8 + offset) * states, states)
            row = jnp.broadcast_to(row_ref[group, offset : offset + 1, :], (states, LANE))
            pick_ref[pl.ds(at, states), :] = jnp.where(pick, row, 0.0).astype(jnp.bfloat16)
        return carry

    lax.fori_loop(0, rows // 8, body, 0)
    term = lax.broadcasted_iota(jnp.int32, (LANE, 2 * LANE), 0)
    side = lax.broadcasted_iota(jnp.int32, (LANE, 2 * LANE), 1)
    is_query = lax.rem(term, 2 * states) >= states
    halves = jnp.where(is_query == (side >= LANE), 1.0, 0.0).astype(jnp.bfloat16)
    both = jnp.dot(pick_ref[...], halves, preferred_element_type=jnp.float32)
    key_ref[...] = both[:, :LANE]
    query_ref[...] = both[:, LANE:]


def sum_eights(half_ref, first):
    total = half_ref[pl.ds(first, 8, stride=8), :]
    for n in range(1, 8):
        total = total + half_ref[pl.ds(first + n, 8, stride=8), :]
    return total


def step_sizes(low, kq, weight_ref, bias_ref, states):
    pre = lax.dot_general(
        low, weight_ref[...], (((1,), (1,)), ((), ())), preferred_element_type=jnp.float32
    )
    beta = sigmoid(pre + bias_ref[...])
    lane = lax.broadcasted_iota(jnp.int32, kq.shape, 1)
    keys = jnp.where(lane < states, kq, 0.0)
    square = jnp.sum(keys * keys, axis=1, keepdims=True)
    return beta, 1.0 / (1.0 + beta * square)


def forward_rows(states, rows, channels, history_ref, state_ref, key_ref, query_ref, rate_ref, input_ref, out_ref, half_ref):
    tiles = channels // LANE
    per_group = min(8, tiles)
    for first in range(0, tiles, per_group):
        columns = [slice((first + j) * LANE, (first + j + 1) * LANE) for j in range(per_group)]

        def body(group, carry):
            carry = list(carry)
            for offset in range(8):
                t = group * 8 + offset
                at = pl.multiple_of(t * states, states)
                key = key_ref[pl.ds(at, states), :]
                query = query_ref[pl.ds(at, states), :]
                square = key * key
                for j, cols in enumerate(columns):
                    history_ref[pl.ds(at, states), cols] = carry[j].astype(jnp.bfloat16)
                    rate = rate_ref[group, offset : offset + 1, cols]
                    fed = input_ref[group, offset : offset + 1, cols]
                    carry[j] = (1.0 - rate * square) * carry[j] + key * fed
                    read = query * carry[j]
                    half_ref[j * 64 + offset * 8 : j * 64 + offset * 8 + 8, :] = read[0:8] + read[8:16]
            for j, cols in enumerate(columns):
                out_ref[group, :, cols] = sum_eights(half_ref, j * 64)
            return tuple(carry)

        done = lax.fori_loop(0, rows // 8, body, tuple(state_ref[:, cols] for cols in columns))
        for cols, state in zip(columns, done):
            state_ref[:, cols] = state


def forward_body(
    states, low_ref, kq_ref, values_ref, gate_ref, weight_ref, bias_ref, skip_ref,
    gated_ref, mixed_ref, history_ref, final_ref,
    state_ref, key_ref, query_ref, rate_ref, input_ref, out_ref, row_ref, pick_ref, half_ref,
):
    rows, channels = values_ref.shape

    @pl.when(pl.program_id(0) == 0)
    def _():
        state_ref[...] = jnp.zeros_like(state_ref)

    beta, inverse = step_sizes(low_ref[...], kq_ref[...], weight_ref, bias_ref, states)
    rates = beta * inverse
    rate_ref[...] = by_eights(rates)
    input_ref[...] = by_eights(rates * values_ref[...].astype(jnp.float32))
    spread_columns(kq_ref[...], row_ref, pick_ref, key_ref, query_ref, states)

    forward_rows(states, rows, channels, history_ref, state_ref, key_ref, query_ref, rate_ref, input_ref, out_ref, half_ref)
    mixed = as_rows(out_ref[...]) + skip_ref[...] * values_ref[...].astype(jnp.float32)
    gate = gate_ref[...]
    mixed_ref[...] = mixed
    gated_ref[...] = (mixed * gate * sigmoid(gate)).astype(jnp.bfloat16)

    @pl.when(pl.program_id(0) == pl.num_programs(0) - 1)
    def _():
        final_ref[...] = state_ref[...]


def forward_scan(low, kq, values, gate, weight, bias, skip, states):
    length, channels = values.shape
    rank = low.shape[1]
    rows = min(128, length)
    blocks = length // rows
    by_row = lambda width: pl.BlockSpec((rows, width), lambda i: (i, 0))
    whole = lambda a: pl.BlockSpec(a.shape, lambda i: (0, 0))
    return pl.pallas_call(
        lambda *refs: forward_body(states, *refs),
        grid=(blocks,),
        in_specs=[by_row(rank), by_row(LANE), by_row(channels), by_row(channels), whole(weight), whole(bias), whole(skip)],
        out_specs=[
            by_row(channels),
            by_row(channels),
            pl.BlockSpec((rows * states, channels), lambda i: (i, 0)),
            pl.BlockSpec((states, channels), lambda i: (0, 0)),
        ],
        out_shape=[
            jax.ShapeDtypeStruct((length, channels), jnp.bfloat16),
            jax.ShapeDtypeStruct((length, channels), jnp.float32),
            jax.ShapeDtypeStruct((length * states, channels), jnp.bfloat16),
            jax.ShapeDtypeStruct((states, channels), jnp.float32),
        ],
        scratch_shapes=[
            pltpu.VMEM((states, channels), jnp.float32),
            pltpu.VMEM((rows * states, LANE), jnp.float32),
            pltpu.VMEM((rows * states, LANE), jnp.float32),
            pltpu.VMEM((rows // 8, 8, channels), jnp.float32),
            pltpu.VMEM((rows // 8, 8, channels), jnp.float32),
            pltpu.VMEM((rows // 8, 8, channels), jnp.float32),
            pltpu.VMEM((rows // 8, 8, LANE), jnp.float32), pltpu.VMEM((rows * states, LANE), jnp.bfloat16),
            pltpu.VMEM((channels // LANE * 64, LANE), jnp.float32),
        ],
        compiler_params=pltpu.CompilerParams(vmem_limit_bytes=48 * 1024 * 1024),
        cost_estimate=pl.CostEstimate(flops=14 * length * states * channels, bytes_accessed=2 * length * states * channels, transcendentals=0),
    )(low, kq, values, gate, weight, bias, skip)


def backward_rows(
    states, rows, channels, history_ref, grad_ref, state_ref, key_ref, query_ref, rate_ref, do_ref, values32_ref,
    fed_ref, kept_ref, part_key_ref, part_query_ref, half_ref,
):
    tiles = channels // LANE
    per_group = min(PER_GROUP, tiles)
    for first in range(0, tiles, per_group):
        columns = [slice((first + j) * LANE, (first + j + 1) * LANE) for j in range(per_group)]

        def body(step, carry):
            grads, lates = list(carry[0]), list(carry[1])
            group = rows // 8 - 1 - step
            for offset in reversed(range(8)):
                t = group * 8 + offset
                at = pl.multiple_of(t * states, states)
                key = key_ref[pl.ds(at, states), :]
                query = query_ref[pl.ds(at, states), :]
                sum_key = None
                sum_query = None
                for j, cols in enumerate(columns):
                    rate = rate_ref[group, offset : offset + 1, cols]
                    out_grad = do_ref[group, offset : offset + 1, cols]
                    value = values32_ref[group, offset : offset + 1, cols]
                    before = history_ref[pl.ds(at, states), cols].astype(jnp.float32)
                    grad = grads[j] + query * out_grad
                    scaled = rate * grad
                    by_key = key * scaled
                    kept = scaled * before
                    kept = key * kept
                    twice = key * kept
                    at_fed = j * 64 + offset * 8
                    at_kept = (per_group + j) * 64 + offset * 8
                    half_ref[at_fed : at_fed + 8, :] = by_key[0:8] + by_key[8:16]
                    half_ref[at_kept : at_kept + 8, :] = twice[0:8] + twice[8:16]
                    term_key = value * scaled - 2.0 * kept
                    term_query = lates[j] * out_grad
                    sum_key = term_key if sum_key is None else sum_key + term_key
                    sum_query = term_query if sum_query is None else sum_query + term_query
                    grads[j] = grad - key * by_key
                    lates[j] = before
                if first == 0:
                    part_key_ref[pl.ds(at, states), :] = sum_key
                    part_query_ref[pl.ds(at, states), :] = sum_query
                else:
                    part_key_ref[pl.ds(at, states), :] += sum_key
                    part_query_ref[pl.ds(at, states), :] += sum_query
            for j, cols in enumerate(columns):
                fed_ref[group, :, cols] = sum_eights(half_ref, j * 64)
                kept_ref[group, :, cols] = sum_eights(half_ref, (per_group + j) * 64)
            return (tuple(grads), tuple(lates))

        start = (tuple(grad_ref[:, cols] for cols in columns), tuple(state_ref[:, cols] for cols in columns))
        grads, lates = lax.fori_loop(0, rows // 8, body, start)
        for cols, grad, late in zip(columns, grads, lates):
            grad_ref[:, cols] = grad
            state_ref[:, cols] = late


def lane_sums(part_ref, wide_ref, states):
    part = part_ref[...]
    high = part.astype(jnp.bfloat16)
    wide_ref[:, :LANE] = high
    wide_ref[:, LANE:] = (part - high.astype(jnp.float32)).astype(jnp.bfloat16)
    ones = jnp.ones((2 * LANE, LANE), jnp.bfloat16)
    part_ref[...] = jnp.dot(wide_ref[...], ones, preferred_element_type=jnp.float32)


def gather_columns(part_key_ref, part_query_ref, wide_ref, placed_ref, rows, states):
    lane_sums(part_key_ref, wide_ref, states)
    lane_sums(part_query_ref, wide_ref, states)
    lane = lax.broadcasted_iota(jnp.int32, (8, LANE), 1)

    def body(group, carry):
        total = jnp.zeros((8, LANE), jnp.float32)
        for n in range(states):
            at = group * 8 * states + n
            total = jnp.where(lane == n, part_key_ref[pl.ds(at, 8, stride=states), :], total)
            total = jnp.where(lane == n + states, part_query_ref[pl.ds(at, 8, stride=states), :], total)
        placed_ref[group] = total
        return carry

    lax.fori_loop(0, rows // 8, body, 0)


def backward_body(
    states, links, low_ref, kq_ref, values_ref, gate_ref, mixed_ref, dgated_ref, history_ref, final_ref, weight_ref, bias_ref, skip_ref,
    result_ref, out_ref, dgate_ref, dpre_ref, dvalues_ref, dlow_ref, dkq_ref, bias_grad_ref, skip_grad_ref, result_came, out_came,
    grad_ref, state_ref, key_ref, query_ref, rate_ref, do_ref, values32_ref, fed_ref, kept_ref, part_key_ref, part_query_ref, row_ref, placed_ref,
    pick_ref, wide_ref, half_ref, *sems,
):
    rows, channels = values_ref.shape
    copies = links(result_ref, out_ref, result_came, out_came, *sems)

    @pl.when(pl.program_id(0) == 0)
    def _():
        grad_ref[...] = jnp.zeros_like(grad_ref)
        state_ref[...] = final_ref[...]
        bias_grad_ref[...] = jnp.zeros_like(bias_grad_ref)
        skip_grad_ref[...] = jnp.zeros_like(skip_grad_ref)
        for copy in copies:
            copy.start()

    beta, inverse = step_sizes(low_ref[...], kq_ref[...], weight_ref, bias_ref, states)
    rate_ref[...] = by_eights(beta * inverse)
    values = values_ref[...].astype(jnp.float32)
    values32_ref[...] = by_eights(values)
    gate = gate_ref[...]
    dgated = dgated_ref[...].astype(jnp.float32)
    s = sigmoid(gate)
    do = dgated * (gate * s)
    do_ref[...] = by_eights(do)
    dgate_ref[...] = (dgated * mixed_ref[...] * (s + gate * s * (1.0 - s))).astype(jnp.bfloat16)
    skip_grad_ref[...] += jnp.sum(do * values, axis=0, keepdims=True)
    spread_columns(kq_ref[...], row_ref, pick_ref, key_ref, query_ref, states)

    backward_rows(
        states, rows, channels, history_ref, grad_ref, state_ref, key_ref, query_ref, rate_ref, do_ref, values32_ref,
        fed_ref, kept_ref, part_key_ref, part_query_ref, half_ref,
    )
    fed = as_rows(fed_ref[...])
    dvalues_ref[...] = fed + skip_ref[...] * as_rows(do_ref[...])
    scaled = as_rows(values32_ref[...]) * fed - as_rows(kept_ref[...])
    beta, inverse = step_sizes(low_ref[...], kq_ref[...], weight_ref, bias_ref, states)
    dpre = scaled * (1.0 - beta) * inverse
    bias_grad_ref[...] += jnp.sum(dpre, axis=0, keepdims=True)
    dpre_low = dpre.astype(jnp.bfloat16)
    dpre_ref[...] = dpre_low
    dlow_ref[...] = jnp.dot(dpre_low, weight_ref[...], preferred_element_type=jnp.float32)
    through = -2.0 * jnp.sum(scaled * beta * inverse, axis=1, keepdims=True)

    gather_columns(part_key_ref, part_query_ref, wide_ref, placed_ref, rows, states)
    lanes = lax.broadcasted_iota(jnp.int32, kq_ref.shape, 1)
    dkq_ref[...] = as_rows(placed_ref[...]) + jnp.where(lanes < states, kq_ref[...] * through, 0.0)

    @pl.when(pl.program_id(0) == pl.num_programs(0) - 1)
    def _():
        for copy in copies:
            copy.wait_recv()
        for copy in copies:
            copy.wait_send()


def exchange(parts, dps, result_ref, out_ref, result_came, out_came, result_send, result_recv, out_send, out_recv):
    d, s = lax.axis_index("dp"), lax.axis_index("seq")

    @pl.when(pl.program_id(0) == 0)
    def _():
        barrier = pltpu.get_barrier_semaphore()
        for k in range(1, parts):
            pl.semaphore_signal(barrier, inc=1, device_id=(d, lax.rem(s + k, parts)), device_id_type=MESH)
        for k in range(1, dps):
            pl.semaphore_signal(barrier, inc=1, device_id=(lax.rem(d + k, dps), s), device_id_type=MESH)
        pl.semaphore_wait(barrier, parts + dps - 2)

    copies = []
    for k in range(1, parts):
        to = lax.rem(s + k, parts)
        copies.append(
            pltpu.make_async_remote_copy(
                src_ref=result_ref.at[to], dst_ref=result_came.at[k - 1], send_sem=result_send.at[k - 1],
                recv_sem=result_recv.at[k - 1], device_id=(d, to), device_id_type=MESH,
            )
        )
    for k in range(1, dps):
        to = lax.rem(d + k, dps)
        copies.append(
            pltpu.make_async_remote_copy(
                src_ref=out_ref.at[to], dst_ref=out_came.at[k - 1], send_sem=out_send.at[k - 1],
                recv_sem=out_recv.at[k - 1], device_id=(to, s), device_id_type=MESH,
            )
        )
    return copies


def backward_scan(low, kq, values, gate, mixed, dgated, history, final, weight, bias, skip, result_part, out_part, states):
    length, channels = values.shape
    rank = low.shape[1]
    rows = min(128, length)
    blocks = length // rows
    by_row = lambda width: pl.BlockSpec((rows, width), lambda i: (blocks - 1 - i, 0))
    whole = lambda a: pl.BlockSpec(a.shape, lambda i: (0, 0))
    total = pl.BlockSpec((1, channels), lambda i: (0, 0))
    wide = pltpu.VMEM((rows // 8, 8, channels), jnp.float32)
    spread = pltpu.VMEM((rows * states, LANE), jnp.float32)
    anywhere = pl.BlockSpec(memory_space=pl.ANY)
    dma = pltpu.SemaphoreType.DMA
    parts, dps = result_part.shape[0], out_part.shape[0]
    links = lambda *refs: exchange(parts, dps, *refs)
    return pl.pallas_call(
        lambda *refs: backward_body(states, links, *refs),
        grid=(blocks,),
        in_specs=[
            by_row(rank), by_row(LANE), by_row(channels), by_row(channels), by_row(channels), by_row(channels),
            pl.BlockSpec((rows * states, channels), lambda i: (blocks - 1 - i, 0)),
            whole(final), whole(weight), whole(bias), whole(skip), anywhere, anywhere,
        ],
        out_specs=[by_row(channels), by_row(channels), by_row(channels), by_row(rank), by_row(LANE), total, total, anywhere, anywhere],
        out_shape=[
            jax.ShapeDtypeStruct((length, channels), jnp.bfloat16),
            jax.ShapeDtypeStruct((length, channels), jnp.bfloat16),
            jax.ShapeDtypeStruct((length, channels), jnp.float32),
            jax.ShapeDtypeStruct((length, rank), jnp.float32),
            jax.ShapeDtypeStruct((length, LANE), jnp.float32),
            jax.ShapeDtypeStruct((1, channels), jnp.float32),
            jax.ShapeDtypeStruct((1, channels), jnp.float32),
            jax.ShapeDtypeStruct((parts - 1,) + result_part.shape[1:], jnp.bfloat16),
            jax.ShapeDtypeStruct((dps - 1,) + out_part.shape[1:], jnp.bfloat16),
        ],
        scratch_shapes=[
            pltpu.VMEM((states, channels), jnp.float32),
            pltpu.VMEM((states, channels), jnp.float32),
            spread, spread, wide, wide, wide, wide, wide, spread, spread,
            pltpu.VMEM((rows // 8, 8, LANE), jnp.float32), pltpu.VMEM((rows // 8, 8, LANE), jnp.float32),
            pltpu.VMEM((rows * states, LANE), jnp.bfloat16), pltpu.VMEM((rows * states, 2 * LANE), jnp.bfloat16),
            pltpu.VMEM((2 * channels // LANE * 64, LANE), jnp.float32),
            dma((parts - 1,)), dma((parts - 1,)), dma((dps - 1,)), dma((dps - 1,)),
        ],
        compiler_params=pltpu.CompilerParams(collective_id=3, has_side_effects=True, vmem_limit_bytes=56 * 1024 * 1024),
        cost_estimate=pl.CostEstimate(flops=30 * length * states * channels, bytes_accessed=2 * length * states * channels, transcendentals=0),
    )(low, kq, values, gate, mixed, dgated, history, final, weight, bias, skip, result_part, out_part)


MESH = pl.DeviceIdType.MESH
GAIN_ROWS = 16


def plane_mates(d):
    core, x, y = lax.rem(d, 2), lax.rem(d // 2, 2), d // 4
    return d + 1 - 2 * core, d + 2 - 4 * x, d + 4 - 8 * y


def start_body(
    parts, block,
    tokens_ref, spread_ref, extra_ref, gain_ref,
    normed_out, weight_out, conv_ref, gate_ref, extra_out,
    tokens_all, normed_all, weight_all, extra_all,
    near_send, near_recv, plane_send, plane_recv, gain_send, gain_recv, line_send, line_recv, local_sem,
):
    d, s = lax.axis_index("dp"), lax.axis_index("seq")
    sib, xm, ym = plane_mates(d)
    own = spread_ref.shape[1]
    rows, width = tokens_ref.shape
    small = extra_ref.shape[0]
    channels = conv_ref.shape[1]
    chunk = rows // 4

    barrier = pltpu.get_barrier_semaphore()
    for mate in (sib, xm, ym):
        pl.semaphore_signal(barrier, inc=1, device_id=(mate, s), device_id_type=MESH)
    for k in range(1, parts):
        pl.semaphore_signal(barrier, inc=1, device_id=(d, lax.rem(s + k, parts)), device_id_type=MESH)
    pl.semaphore_wait(barrier, 3 + parts - 1)

    def remote(src, dst, send, recv, to):
        return pltpu.make_async_remote_copy(
            src_ref=src, dst_ref=dst, send_sem=send, recv_sem=recv, device_id=to, device_id_type=MESH
        )

    def weight_rows(owner, source):
        return weight_all.at[pl.ds(pl.multiple_of((owner * parts + source) * own, own), own), :]

    def extra_rows(owner):
        return extra_all.at[owner]

    def gain_rows(source):
        return extra_all.at[d, pl.ds(pl.multiple_of(small + source * GAIN_ROWS, GAIN_ROWS), GAIN_ROWS), pl.ds(0, LANE)]

    near = []
    for k in range(1, parts):
        to = (d, lax.rem(s + k, parts))
        near.append(remote(spread_ref.at[to[1]], weight_rows(d, s), near_send.at[k], near_recv.at[k], to))
        near.append(remote(gain_ref, gain_rows(s), gain_send.at[k], gain_recv.at[k], to))
    for copy in near:
        copy.start()
    mine = [
        pltpu.make_async_copy(spread_ref.at[s], weight_rows(d, s), local_sem.at[0]),
        pltpu.make_async_copy(gain_ref, gain_rows(s), local_sem.at[1]),
        pltpu.make_async_copy(extra_ref, extra_all.at[d, pl.ds(0, small), :], local_sem.at[2]),
        pltpu.make_async_copy(tokens_ref, tokens_all.at[pl.ds(pl.multiple_of(s * rows, rows), rows), :], local_sem.at[3]),
    ]
    for copy in mine:
        copy.start()

    def token_rows(part, c):
        return tokens_all.at[pl.ds(pl.multiple_of(part * rows + c * chunk, chunk), chunk), :]

    def token_copy(way, distance, c):
        part = s - way * (distance - 1)
        src = tokens_ref.at[pl.ds(c * chunk, chunk), :] if distance == 1 else token_rows(part, c)
        side = 0 if way == 1 else 1
        return remote(
            src, token_rows(part, c), line_send.at[side, distance, c], line_recv.at[side, distance, c], (d, s + way)
        )

    def can_send(way, distance):
        reach = s + 1 < parts if way == 1 else s >= 1
        came = s - (distance - 1) >= 0 if way == 1 else s + (distance - 1) < parts
        return jnp.logical_and(reach, came)

    def arrives(way, distance):
        return s >= distance if way == 1 else s + distance < parts

    def send_tokens(distance, c):
        for way in (1, -1):
            @pl.when(can_send(way, distance))
            def _():
                token_copy(way, distance, c).start()

    def sent_tokens(distance, c):
        for way in (1, -1):
            @pl.when(can_send(way, distance))
            def _():
                token_copy(way, distance, c).wait_send()

    def take_tokens(distance, c):
        for way in (1, -1):
            @pl.when(arrives(way, distance))
            def _():
                part = s - way * distance
                side = 0 if way == 1 else 1
                remote(
                    token_rows(part, c), token_rows(part, c), line_send.at[side, distance, c],
                    line_recv.at[side, distance, c], (d, s),
                ).wait_recv()

    units = parts + 1

    def unit(owner, k):
        return extra_rows(owner) if k == parts else weight_rows(owner, lax.rem(s - k + parts, parts))

    kinds = {"own": (d, 0), "x": (xm, 2), "y": (ym, 4)}

    def plane_copy(owner, k, rel, kind, to):
        return remote(unit(owner, k), unit(owner, k), plane_send.at[kind, k], plane_recv.at[rel, k], (to, s))

    diag = xm + ym - d
    sib_of = lambda mate: mate + sib - d

    def route(k):
        steps = [
            (0, d, 1, 0, sib), (0, d, 2, 1, xm), (0, d, 4, 2, ym),
            (2, xm, 3, 3, sib), (4, ym, 5, 5, sib), (6, diag, 7, 7, sib),
        ]
        steps.append((2, xm, 6, 4, ym) if k % 2 == 0 else (4, ym, 6, 6, xm))
        return steps

    def pass_on(stage, k):
        for at, owner, rel, kind, to in route(k):
            if at == stage:
                plane_copy(owner, k, rel, kind, to).start()

    owners = {1: sib, 2: xm, 3: sib_of(xm), 4: ym, 5: sib_of(ym), 6: diag, 7: sib_of(diag)}

    def take(rel, k):
        plane_copy(owners[rel], k, rel, 0, d).wait_recv()

    for c in range(4):
        send_tokens(1, c)
    mine[0].wait()
    pass_on(0, 0)
    for k in range(1, parts):
        near_wait = remote(
            spread_ref.at[s], weight_rows(d, lax.rem(s - k + parts, parts)), near_send.at[k], near_recv.at[k], (d, s)
        )
        near_wait.wait_recv()
        pass_on(0, k)
    mine[1].wait()
    mine[2].wait()
    for k in range(1, parts):
        remote(gain_ref, gain_rows(lax.rem(s - k + parts, parts)), gain_send.at[k], gain_recv.at[k], (d, s)).wait_recv()
    pass_on(0, parts)
    for k in range(units):
        take(2, k)
        pass_on(2, k)
        take(4, k)
        pass_on(4, k)
        if k < 4:
            take_tokens(1, k)
            send_tokens(2, k)
    for k in range(units):
        take(6, k)
        pass_on(6, k)
        if k < 4:
            take_tokens(2, k)
            send_tokens(3, k)
    for rel in (1, 3, 5, 7):
        for k in range(units):
            take(rel, k)
    mine[3].wait()
    weight_copy = pltpu.make_async_copy(weight_all, weight_out, local_sem.at[4])
    weight_copy.start()
    extra_out[...] = extra_all[...]

    lane = lax.broadcasted_iota(jnp.int32, (1, LANE), 1)
    pieces = []
    for owner in range(extra_all.shape[0]):
        for source in range(0, parts, 2):
            row = small + source * GAIN_ROWS
            even = extra_all[owner, row : row + GAIN_ROWS, 0:LANE].astype(jnp.float32)[0:1]
            odd = extra_all[owner, row + GAIN_ROWS : row + 2 * GAIN_ROWS, 0:LANE].astype(jnp.float32)[0:1]
            pieces.append(jnp.where(lane < own, even, odd))
    gain = jnp.concatenate(pieces, axis=1)

    tile = min(512, channels)

    def work(part):
        for c in range(4):
            at = pl.ds(pl.multiple_of(part * rows + c * chunk, chunk), chunk)
            flat = tokens_all[at, :].astype(jnp.float32)
            scale = lax.rsqrt(jnp.mean(flat * flat, axis=-1, keepdims=True) + 1e-05)
            normed_all[at, :] = (flat * scale * gain).astype(jnp.bfloat16)
        at = pl.ds(pl.multiple_of(part * rows, rows), rows)

        def columns(n, carry):
            left = pl.multiple_of(n * tile, tile)
            right = pl.multiple_of(channels + n * tile, tile)
            conv_ref[at, pl.ds(left, tile)] = jnp.dot(
                normed_all[at, :], weight_all[:, pl.ds(left, tile)], preferred_element_type=jnp.float32
            ).astype(jnp.bfloat16)
            gate_ref[at, pl.ds(left, tile)] = jnp.dot(
                normed_all[at, :], weight_all[:, pl.ds(right, tile)], preferred_element_type=jnp.float32
            )
            return carry

        lax.fori_loop(0, channels // tile, columns, 0)

    def work_at(low, high):
        def each(part, carry):
            away = jnp.abs(part - s)

            @pl.when(jnp.logical_and(away >= low, away <= high))
            def _():
                work(part)

            return carry

        lax.fori_loop(0, parts, each, 0)

    work_at(0, 2)
    for c in range(4):
        take_tokens(3, c)
    work_at(3, 3)
    normed_copy = pltpu.make_async_copy(normed_all, normed_out, local_sem.at[5])
    normed_copy.start()

    for copy in near:
        copy.wait_send()
    for k in range(units):
        for at, owner, rel, kind, to in route(k):
            plane_copy(owner, k, rel, kind, to).wait_send()
    for distance in range(1, parts):
        for c in range(4):
            sent_tokens(distance, c)
    weight_copy.wait()
    normed_copy.wait()


def start(tokens, spread, extra, gain, dps):
    parts, own, both = spread.shape
    rows, width = tokens.shape
    small, lanes = extra.shape
    any_space = pl.BlockSpec(memory_space=pl.ANY)
    vmem = pl.BlockSpec(memory_space=pltpu.VMEM)
    tall = small + parts * GAIN_ROWS
    dma = pltpu.SemaphoreType.DMA
    return pl.pallas_call(
        lambda *refs: start_body(parts, own, *refs),
        out_shape=[
            jax.ShapeDtypeStruct((parts * rows, width), jnp.bfloat16),
            jax.ShapeDtypeStruct((dps * parts * own, both), jnp.bfloat16),
            jax.ShapeDtypeStruct((parts * rows, both // 2), jnp.bfloat16),
            jax.ShapeDtypeStruct((parts * rows, both // 2), jnp.float32),
            jax.ShapeDtypeStruct((dps, tall, lanes), jnp.bfloat16),
        ],
        in_specs=[vmem, vmem, vmem, vmem],
        out_specs=[any_space, any_space, vmem, vmem, vmem],
        scratch_shapes=[
            pltpu.VMEM((parts * rows, width), jnp.bfloat16),
            pltpu.VMEM((parts * rows, width), jnp.bfloat16),
            pltpu.VMEM((dps * parts * own, both), jnp.bfloat16),
            pltpu.VMEM((dps, tall, lanes), jnp.bfloat16),
            dma((parts,)), dma((parts,)),
            dma((8, parts + 1)), dma((8, parts + 1)),
            dma((parts,)), dma((parts,)),
            dma((2, parts, 4)), dma((2, parts, 4)),
            dma((6,)),
        ],
        compiler_params=pltpu.CompilerParams(
            collective_id=1, has_side_effects=True, vmem_limit_bytes=56 * 1024 * 1024
        ),
        cost_estimate=pl.CostEstimate(
            flops=2 * parts * rows * width * both, bytes_accessed=40 * 1024 * 1024, transcendentals=0
        ),
    )(tokens, spread, extra, gain)


def line_sums(parts, rows, terms, came, send, recv):
    d, s = lax.axis_index("dp"), lax.axis_index("seq")
    chunk = rows // 4

    def own_rows(part, c):
        return pl.ds(pl.multiple_of(part * rows + c * chunk, chunk), chunk)

    def slot(way, left, part, c):
        at = parts if way == -1 and left == 0 else part
        return came.at[at, pl.ds(c * chunk, chunk), :]

    def copy_of(way, steps, c):
        side = 0 if way == 1 else 1
        part = s + way * steps
        return pltpu.make_async_remote_copy(
            src_ref=terms.at[own_rows(part, c), :], dst_ref=slot(way, steps - 1, part, c),
            send_sem=send.at[side, steps, c], recv_sem=recv.at[side, steps - 1, c],
            device_id=(d, s + way), device_id_type=MESH,
        )

    def valid(way, steps):
        return s + steps < parts if way == 1 else s >= steps

    def upstream(way):
        return s >= 1 if way == 1 else s + 1 < parts

    def taken(way, left, c):
        side = 0 if way == 1 else 1
        place = slot(way, left, s + way * left, c)
        pltpu.make_async_remote_copy(
            src_ref=place, dst_ref=place, send_sem=send.at[side, left, c], recv_sem=recv.at[side, left, c],
            device_id=(d, s), device_id_type=MESH,
        ).wait_recv()

    def pass_on(steps, c):
        for way in (1, -1):
            @pl.when(valid(way, steps))
            def _():
                if steps < parts - 1:
                    @pl.when(upstream(way))
                    def _():
                        taken(way, steps, c)
                        mine = own_rows(s + way * steps, c)
                        more = came[s + way * steps, c * chunk : (c + 1) * chunk, :]
                        terms[mine, :] = (terms[mine, :].astype(jnp.float32) + more.astype(jnp.float32)).astype(jnp.bfloat16)

                copy_of(way, steps, c).start()

    def total(c):
        for way in (1, -1):
            @pl.when(upstream(way))
            def _():
                taken(way, 0, c)

        at = pl.ds(c * chunk, chunk)
        low = jnp.where(upstream(1), came[s, at, :].astype(jnp.float32), 0.0)
        high = jnp.where(upstream(-1), came[parts, at, :].astype(jnp.float32), 0.0)
        return terms[own_rows(s, c), :].astype(jnp.float32) + low + high

    def sent():
        for steps in range(1, parts):
            for c in range(4):
                for way in (1, -1):
                    @pl.when(valid(way, steps))
                    def _():
                        copy_of(way, steps, c).wait_send()

    return pass_on, total, sent


def end_body(
    parts, block,
    dmixed_ref, normed_ref, weight_ref, tokens_ref, cot_ref, gain_ref, shard_ref, small_ref,
    input_grad_ref, in_grad_ref, gain_grad_ref, small_grad_ref,
    dn, dn_recv, sib_send, sib_recv, q_send, q_recv, total, z_send, z_recv,
    small_sib_send, small_sib_recv, small_q_send, small_q_recv,
    line_send, line_recv, pair_send, pair_recv, cross_send, cross_recv, near_send, near_recv,
):
    d, s = lax.axis_index("dp"), lax.axis_index("seq")
    sib, xm, ym = plane_mates(d)
    diag = xm + ym - d
    own, both = shard_ref.shape[0], dmixed_ref.shape[1]
    rows, width = tokens_ref.shape
    chunk = rows // 4
    tall = parts * own
    tile = min(512, both)

    barrier = pltpu.get_barrier_semaphore()
    for mate in (sib, xm, ym, diag):
        pl.semaphore_signal(barrier, inc=1, device_id=(mate, s), device_id_type=MESH)
    for k in range(1, parts):
        pl.semaphore_signal(barrier, inc=1, device_id=(d, lax.rem(s + k, parts)), device_id_type=MESH)
    pl.semaphore_wait(barrier, 4 + parts - 1)

    def remote(src, dst, send, recv, to):
        return pltpu.make_async_remote_copy(
            src_ref=src, dst_ref=dst, send_sem=send, recv_sem=recv, device_id=to, device_id_type=MESH
        )

    pass_line, line_total, line_sent = line_sums(parts, rows, dn, dn_recv, line_send, line_recv)

    def dn_part(part):
        at = pl.ds(pl.multiple_of(part * rows, rows), rows)

        def columns(n, carry):
            cols = pl.ds(pl.multiple_of(n * tile, tile), tile)
            dn[at, cols] = lax.dot_general(
                dmixed_ref[at, :], weight_ref[cols, :], (((1,), (1,)), ((), ())), preferred_element_type=jnp.float32
            ).astype(jnp.bfloat16)
            return carry

        lax.fori_loop(0, width // tile, columns, 0)

    def each_part(part, carry):
        dn_part(part)
        return carry

    lax.fori_loop(0, parts, each_part, 0)
    for c in range(4):
        pass_line(parts - 1, c)

    def grad_block(owner, store):
        left = pl.ds(pl.multiple_of(owner * tall, tall), tall)

        def columns(n, carry):
            cols = pl.ds(pl.multiple_of(n * tile, tile), tile)
            store(
                cols,
                lax.dot_general(
                    normed_ref[:, left], dmixed_ref[:, cols], (((0,), (0,)), ((), ())),
                    preferred_element_type=jnp.float32,
                ),
            )
            return carry

        lax.fori_loop(0, both // tile, columns, 0)

    mates = (diag, xm, ym, d)
    sib_of = lambda mate: mate + sib - d

    def pair_copy(r):
        return remote(sib_send.at[r], sib_recv.at[r], pair_send.at[0, r], pair_recv.at[0, r], (sib, s))

    def pair_copy_small(r):
        return remote(small_sib_send.at[r], small_sib_recv.at[r], pair_send.at[1, r], pair_recv.at[1, r], (sib, s))

    def cross_copy(r):
        return remote(q_send.at[r], q_recv.at[r], cross_send.at[0, r], cross_recv.at[0, r], (mates[r], s))

    def cross_copy_small(r):
        return remote(small_q_send.at[r], small_q_recv.at[r], cross_send.at[1, r], cross_recv.at[1, r], (mates[r], s))

    for r in range(4):
        def store_pair(cols, value):
            sib_send[r, :, cols] = value.astype(jnp.bfloat16)

        grad_block(sib_of(mates[r]), store_pair)
        pair_copy(r).start()
        small_sib_send[r] = small_ref[sib_of(mates[r])].astype(jnp.bfloat16)
        pair_copy_small(r).start()
        if parts > 2:
            pass_line(parts - 2, r)
    for r in range(4):
        pair_copy(r).wait_recv()
        pair_copy_small(r).wait_recv()
        both_small = small_ref[mates[r]] + small_sib_recv[r].astype(jnp.float32)
        if r < 3:
            def store_cross(cols, value):
                q_send[r, :, cols] = (value + sib_recv[r, :, cols].astype(jnp.float32)).astype(jnp.bfloat16)

            grad_block(mates[r], store_cross)
            cross_copy(r).start()
            small_q_send[r] = both_small.astype(jnp.bfloat16)
            cross_copy_small(r).start()
        else:
            def store_total(cols, value):
                total[:, cols] = value + sib_recv[r, :, cols].astype(jnp.float32)

            grad_block(mates[r], store_total)
            small_grad_ref[...] = both_small
        if parts > 3:
            pass_line(parts - 3, r)

    for r in range(3):
        cross_copy(r).wait_recv()
        cross_copy_small(r).wait_recv()
        total[...] += q_recv[r].astype(jnp.float32)
        small_grad_ref[...] += small_q_recv[r].astype(jnp.float32)
    z_send[...] = total[...].astype(jnp.bfloat16)

    def near_copy(k):
        to = lax.rem(s + k, parts)
        return remote(
            z_send.at[pl.ds(pl.multiple_of(to * own, own), own), :], z_recv.at[k], near_send.at[k], near_recv.at[k], (d, to)
        )

    for k in range(1, parts):
        near_copy(k).start()

    for c in range(4):
        at = pl.ds(c * chunk, chunk)
        v = line_total(c) * gain_ref[...]
        flat = tokens_ref[at, :].astype(jnp.float32)
        scale = lax.rsqrt(jnp.mean(flat * flat, axis=-1, keepdims=True) + 1e-05)
        du = scale * v - flat * (scale * scale * scale) * jnp.mean(flat * v, axis=-1, keepdims=True)
        input_grad_ref[at, :] = (cot_ref[at, :].astype(jnp.float32) + du).astype(jnp.bfloat16)

    channel_blocks = both // block
    gain_total = jnp.zeros((own, block), jnp.float32)
    for k in range(parts):
        source = lax.rem(s - k + parts, parts)
        if k > 0:
            near_copy(k).wait_recv()
        for j in range(channel_blocks):
            cols = slice(j * block, (j + 1) * block)
            if k == 0:
                piece = z_send[pl.ds(pl.multiple_of(s * own, own), own), cols]
            else:
                piece = z_recv[k, :, cols]
            piece = piece.astype(jnp.float32)
            to = pl.ds(pl.multiple_of((j * parts + source) * block, block), block)
            in_grad_ref[:, to] = piece
            gain_total = gain_total + piece * shard_ref[:, to].astype(jnp.float32)
    gain_grad_ref[...] = jnp.broadcast_to(jnp.sum(gain_total, axis=1, keepdims=True), gain_grad_ref.shape)

    for r in range(4):
        pair_copy(r).wait_send()
        pair_copy_small(r).wait_send()
    for r in range(3):
        cross_copy(r).wait_send()
        cross_copy_small(r).wait_send()
    for k in range(1, parts):
        near_copy(k).wait_send()
    line_sent()


def end(dmixed, normed, weight, tokens, cotangent, gain, shard, small, parts, block):
    both = dmixed.shape[1]
    rows, width = tokens.shape
    own = shard.shape[0]
    dps, _, lanes = small.shape
    tall = parts * own
    vmem = pl.BlockSpec(memory_space=pltpu.VMEM)
    dma = pltpu.SemaphoreType.DMA
    low = jnp.bfloat16
    return pl.pallas_call(
        lambda *refs: end_body(parts, block, *refs),
        out_shape=[
            jax.ShapeDtypeStruct((rows, width), low),
            jax.ShapeDtypeStruct((own, parts * both), jnp.float32),
            jax.ShapeDtypeStruct((own, LANE), jnp.float32),
            jax.ShapeDtypeStruct((block, lanes), jnp.float32),
        ],
        in_specs=[vmem] * 8,
        out_specs=[vmem] * 4,
        scratch_shapes=[
            pltpu.VMEM((parts * rows, width), low),
            pltpu.VMEM((parts + 1, rows, width), low),
            pltpu.VMEM((4, tall, both), low), pltpu.VMEM((4, tall, both), low),
            pltpu.VMEM((3, tall, both), low), pltpu.VMEM((3, tall, both), low),
            pltpu.VMEM((tall, both), jnp.float32),
            pltpu.VMEM((tall, both), low), pltpu.VMEM((parts, own, both), low),
            pltpu.VMEM((4, block, lanes), low), pltpu.VMEM((4, block, lanes), low),
            pltpu.VMEM((3, block, lanes), low), pltpu.VMEM((3, block, lanes), low),
            dma((2, parts, 4)), dma((2, parts, 4)),
            dma((2, 4)), dma((2, 4)), dma((2, 3)), dma((2, 3)), dma((parts,)), dma((parts,)),
        ],
        compiler_params=pltpu.CompilerParams(
            collective_id=2, has_side_effects=True, vmem_limit_bytes=60 * 1024 * 1024
        ),
        cost_estimate=pl.CostEstimate(
            flops=4 * parts * rows * width * both, bytes_accessed=30 * 1024 * 1024, transcendentals=0
        ),
    )(dmixed, normed, weight, tokens, cotangent, gain, shard, small)


def linked_forward_body(
    states, parts, dps, taps,
    conv_in_ref, gate_ref, select_ref, conv_w_ref, conv_b_ref, weight_ref, bias_ref, skip_ref, out_shard, cot_shard,
    mixed_ref, history_ref, final_ref, values_ref, low_ref, kq_ref, dgated_ref, result_ref, out_part_ref,
    state_ref, key_ref, query_ref, rate_ref, input_ref, out_ref, row_ref, pick_ref, half_ref,
    part_low, part_kq, came_low, came_kq, sum_low, sum_kq,
    rs_send, rs_recv, ag_send, ag_recv, out_send, out_recv, line_send, line_recv, local_sem,
    out_all, cot_all, gated_all, out_total,
):
    d, s = lax.axis_index("dp"), lax.axis_index("seq")
    step = pl.program_id(0)
    length, channels = values_ref.shape
    rows = gate_ref.shape[0]
    span = length // parts
    block = out_shard.shape[0]
    chunk = span // 4
    packed = LANE // (2 * states)
    short = span // packed

    def remote(src, dst, send, recv, to):
        return pltpu.make_async_remote_copy(
            src_ref=src, dst_ref=dst, send_sem=send, recv_sem=recv, device_id=to, device_id_type=MESH
        )

    def out_rows(owner):
        return out_all.at[pl.ds(pl.multiple_of(owner * block, block), block), :]

    out_copies = []
    for k in range(1, dps):
        out_copies.append(
            remote(out_shard, out_rows(d), out_send.at[k - 1], out_recv.at[k - 1], (lax.rem(d + k, dps), s))
        )

    def cot_rows(part, c):
        return cot_all.at[pl.ds(pl.multiple_of(part * span + c * chunk, chunk), chunk), :]

    def cot_copy(way, distance, c):
        part = s - way * (distance - 1)
        src = cot_shard.at[pl.ds(c * chunk, chunk), :] if distance == 1 else cot_rows(part, c)
        side = 0 if way == 1 else 1
        return remote(
            src, cot_rows(part, c), line_send.at[side, distance, c], line_recv.at[side, distance, c], (d, s + way)
        )

    def can_send(way, distance):
        reach = s + 1 < parts if way == 1 else s >= 1
        came = s - (distance - 1) >= 0 if way == 1 else s + (distance - 1) < parts
        return jnp.logical_and(reach, came)

    def send_cot(distance, c):
        for way in (1, -1):
            @pl.when(can_send(way, distance))
            def _():
                cot_copy(way, distance, c).start()

    def sent_cot(distance, c):
        for way in (1, -1):
            @pl.when(can_send(way, distance))
            def _():
                cot_copy(way, distance, c).wait_send()

    def take_cot(distance, c):
        for way in (1, -1):
            @pl.when(s >= distance if way == 1 else s + distance < parts)
            def _():
                part = s - way * distance
                side = 0 if way == 1 else 1
                remote(
                    cot_rows(part, c), cot_rows(part, c), line_send.at[side, distance, c],
                    line_recv.at[side, distance, c], (d, s),
                ).wait_recv()

    def own_copies():
        return (
            pltpu.make_async_copy(out_shard, out_rows(d), local_sem.at[0]),
            pltpu.make_async_copy(
                cot_shard, cot_all.at[pl.ds(pl.multiple_of(s * span, span), span), :], local_sem.at[1]
            ),
        )

    @pl.when(step == 0)
    def _():
        barrier = pltpu.get_barrier_semaphore()
        for k in range(1, parts):
            pl.semaphore_signal(barrier, inc=1, device_id=(d, lax.rem(s + k, parts)), device_id_type=MESH)
        for k in range(1, dps):
            pl.semaphore_signal(barrier, inc=1, device_id=(lax.rem(d + k, dps), s), device_id_type=MESH)
        pl.semaphore_wait(barrier, parts + dps - 2)
        state_ref[...] = jnp.zeros_like(state_ref)
        for copy in out_copies:
            copy.start()
        for copy in own_copies():
            copy.start()
        for c in range(2):
            send_cot(1, c)

    def rs_copies(k):
        at = lax.rem(s + k, parts)
        return (
            remote(part_low.at[at], came_low.at[k - 1], rs_send.at[0, k - 1], rs_recv.at[0, k - 1], (d, at)),
            remote(part_kq.at[at], came_kq.at[k - 1], rs_send.at[1, k - 1], rs_recv.at[1, k - 1], (d, at)),
        )

    def ag_copies(k):
        to = lax.rem(s + k, parts)
        return (
            remote(sum_low.at[s], sum_low.at[s], ag_send.at[0, k - 1], ag_recv.at[0, k - 1], (d, to)),
            remote(sum_kq.at[s], sum_kq.at[s], ag_send.at[1, k - 1], ag_recv.at[1, k - 1], (d, to)),
        )

    def ag_taken(k, part):
        return (
            remote(sum_low.at[part], sum_low.at[part], ag_send.at[0, k - 1], ag_recv.at[0, k - 1], (d, s)),
            remote(sum_kq.at[part], sum_kq.at[part], ag_send.at[1, k - 1], ag_recv.at[1, k - 1], (d, s)),
        )

    def convolve(part):
        start = pl.multiple_of(part * span, span)
        before = pl.multiple_of(jnp.maximum(start - 16, 0), 16)
        wide = min(256, channels)
        for left in range(0, channels, wide):
            cols = slice(left, left + wide)
            head = conv_in_ref[pl.ds(before, 16), cols].astype(jnp.float32)
            head = jnp.where(part == 0, 0.0, head)
            body = jnp.concatenate([head, conv_in_ref[pl.ds(start, span), cols].astype(jnp.float32)], axis=0)
            total = conv_b_ref[:, cols]
            for tap in range(taps):
                by = taps - 1 - tap
                total = total + body[16 - by : 16 - by + span] * conv_w_ref[tap : tap + 1, cols]
            values_ref[pl.ds(start, span), cols] = (total * sigmoid(total)).astype(jnp.bfloat16)
        projected = jnp.dot(values_ref[pl.ds(start, span), :], select_ref[...], preferred_element_type=jnp.float32)
        part_low[part] = projected[:, :LANE].astype(jnp.bfloat16)
        pack = projected[:short, LANE:]
        for g in range(1, packed):
            pack = pack + pltpu.roll(projected[g * short : (g + 1) * short, LANE:], g * 2 * states, 1)
        part_kq[part] = pack

    @pl.when(step < parts - 1)
    def _():
        convolve(lax.rem(s + 1 + step, parts))

    for k in range(1, parts):
        @pl.when(step == k - 1)
        def _():
            for copy in rs_copies(k):
                copy.start()

    @pl.when(step == parts - 1)
    def _():
        convolve(s)
        low = part_low[s].astype(jnp.float32)
        kq = part_kq[s]
        for k in range(1, parts):
            for copy in rs_copies(k):
                copy.wait_recv()
            low = low + came_low[k - 1].astype(jnp.float32)
            kq = kq + came_kq[k - 1]
        sum_low[s] = low.astype(jnp.bfloat16)
        sum_kq[s] = kq
        for k in range(1, parts):
            for copy in ag_copies(k):
                copy.start()
        for c in range(2, 4):
            send_cot(1, c)

    per_part = span // rows
    at_block = step - parts

    def unpack(part):
        start = pl.multiple_of(part * span, span)
        low_ref[pl.ds(start, span), :] = sum_low[part]
        pack = sum_kq[part]
        lane = lax.broadcasted_iota(jnp.int32, pack.shape, 1)
        for g in range(packed):
            turned = pack if g == 0 else pltpu.roll(pack, LANE - g * 2 * states, 1)
            kq_ref[pl.ds(pl.multiple_of(start + g * short, short), short), :] = jnp.where(lane < 2 * states, turned, 0.0)

    for part in range(parts):
        @pl.when(at_block == part * per_part)
        def _():
            for k in range(1, parts):
                @pl.when(lax.rem(s - k + parts, parts) == part)
                def _():
                    for copy in ag_taken(k, part):
                        copy.wait_recv()

            unpack(part)

    plan = {0: ((1, 0), (1, 1)), 1: ((1, 2), (1, 3)), 2: ((2, 0), (2, 1)), 4: ((2, 2), (2, 3))}
    for at, moves in plan.items():
        @pl.when(at_block == at)
        def _():
            for distance, c in moves:
                take_cot(distance, c)
                send_cot(distance + 1, c)

    @pl.when(jnp.logical_and(at_block >= 0, at_block < length // rows))
    def _():
        here = pl.ds(pl.multiple_of(at_block * rows, rows), rows)
        kq = kq_ref[here, :]
        values = values_ref[here, :].astype(jnp.float32)
        beta, inverse = step_sizes(low_ref[here, :], kq, weight_ref, bias_ref, states)
        rates = beta * inverse
        rate_ref[...] = by_eights(rates)
        input_ref[...] = by_eights(rates * values)
        spread_columns(kq, row_ref, pick_ref, key_ref, query_ref, states)
        forward_rows(states, rows, channels, history_ref, state_ref, key_ref, query_ref, rate_ref, input_ref, out_ref, half_ref)
        mixed = as_rows(out_ref[...]) + skip_ref[...] * values
        gate = gate_ref[...]
        mixed_ref[...] = mixed
        gated_all[here, :] = (mixed * gate * sigmoid(gate)).astype(jnp.bfloat16)

    width = cot_all.shape[1]
    tile = min(512, width)

    def products(part):
        here = pl.ds(pl.multiple_of(part * span, span), span)

        def across(n, carry):
            cols = pl.ds(pl.multiple_of(n * tile, tile), tile)
            result_ref[here, cols] = jnp.dot(
                gated_all[here, :], out_all[:, cols], preferred_element_type=jnp.float32
            ).astype(jnp.bfloat16)
            out_total[:, cols] += lax.dot_general(
                gated_all[here, :], cot_all[here, cols], (((0,), (0,)), ((), ())), preferred_element_type=jnp.float32
            )
            return carry

        lax.fori_loop(0, width // tile, across, 0)
        deep = min(512, channels)

        def along(n, carry):
            cols = pl.ds(pl.multiple_of(n * deep, deep), deep)
            dgated_ref[here, cols] = lax.dot_general(
                cot_all[here, :], out_all[cols, :], (((1,), (1,)), ((), ())), preferred_element_type=jnp.float32
            )
            return carry

        lax.fori_loop(0, channels // deep, along, 0)

    def products_at(low, high):
        def each(part, carry):
            away = jnp.abs(part - s)

            @pl.when(jnp.logical_and(away >= low, away <= high))
            def _():
                products(part)

            return carry

        lax.fori_loop(0, parts, each, 0)

    @pl.when(step == pl.num_programs(0) - 1)
    def _():
        final_ref[...] = state_ref[...]
        out_total[...] = jnp.zeros_like(out_total)
        for copy in own_copies():
            copy.wait()
        for copy in out_copies:
            copy.wait_recv()
        products_at(0, parts - 2)
        for c in range(4):
            take_cot(parts - 1, c)
        products_at(parts - 1, parts - 1)
        out_part_ref[...] = out_total[...].astype(jnp.bfloat16)
        for copy in out_copies:
            copy.wait_send()
        for distance in range(1, parts):
            for c in range(4):
                sent_cot(distance, c)
        for k in range(1, parts):
            for copy in rs_copies(k) + ag_copies(k):
                copy.wait_send()


def linked_forward(conv_in, gate, select, conv_w, conv_b, weight, bias, skip, out_shard, cot_shard, parts, dps, states):
    length, channels = conv_in.shape
    taps = conv_w.shape[0]
    block, width = out_shard.shape
    span = length // parts
    rows = min(128, span)
    blocks = length // rows
    short = span // (LANE // (2 * states))
    at = lambda i: jnp.clip(i - parts, 0, blocks - 1)
    by_row = lambda size: pl.BlockSpec((rows, size), lambda i: (at(i), 0))
    whole = lambda a: pl.BlockSpec(a.shape, lambda i: (0, 0))
    kept = lambda *shape: pl.BlockSpec(shape, lambda i: (0, 0))
    anywhere = pl.BlockSpec(memory_space=pl.ANY)
    dma = pltpu.SemaphoreType.DMA
    f32, low = jnp.float32, jnp.bfloat16
    eights = pltpu.VMEM((rows // 8, 8, channels), f32)
    return pl.pallas_call(
        lambda *refs: linked_forward_body(states, parts, dps, taps, *refs),
        grid=(parts + blocks + 1,),
        in_specs=[
            whole(conv_in), by_row(channels), whole(select), whole(conv_w), whole(conv_b), whole(weight), whole(bias),
            whole(skip), anywhere, anywhere,
        ],
        out_specs=[
            by_row(channels), pl.BlockSpec((rows * states, channels), lambda i: (at(i), 0)),
            kept(states, channels), kept(length, channels), kept(length, LANE), kept(length, LANE),
            kept(length, channels), kept(length, width), kept(dps * block, width),
        ],
        out_shape=[
            jax.ShapeDtypeStruct((length, channels), f32),
            jax.ShapeDtypeStruct((length * states, channels), low),
            jax.ShapeDtypeStruct((states, channels), f32),
            jax.ShapeDtypeStruct((length, channels), low),
            jax.ShapeDtypeStruct((length, LANE), low),
            jax.ShapeDtypeStruct((length, LANE), f32),
            jax.ShapeDtypeStruct((length, channels), f32),
            jax.ShapeDtypeStruct((length, width), low),
            jax.ShapeDtypeStruct((dps * block, width), low),
        ],
        scratch_shapes=[
            pltpu.VMEM((states, channels), f32),
            pltpu.VMEM((rows * states, LANE), f32), pltpu.VMEM((rows * states, LANE), f32),
            eights, eights, eights, pltpu.VMEM((rows // 8, 8, LANE), f32),
            pltpu.VMEM((rows * states, LANE), low), pltpu.VMEM((channels // LANE * 64, LANE), f32),
            pltpu.VMEM((parts, span, LANE), low), pltpu.VMEM((parts, short, LANE), f32),
            pltpu.VMEM((parts - 1, span, LANE), low), pltpu.VMEM((parts - 1, short, LANE), f32),
            pltpu.VMEM((parts, span, LANE), low), pltpu.VMEM((parts, short, LANE), f32),
            dma((2, parts - 1)), dma((2, parts - 1)), dma((2, parts - 1)), dma((2, parts - 1)),
            dma((dps - 1,)), dma((dps - 1,)), dma((2, parts, 4)), dma((2, parts, 4)), dma((2,)),
            pltpu.VMEM((dps * block, width), low), pltpu.VMEM((length, width), low), pltpu.VMEM((length, channels), low),
            pltpu.VMEM((dps * block, width), f32),
        ],
        compiler_params=pltpu.CompilerParams(
            collective_id=4, has_side_effects=True, vmem_limit_bytes=60 * 1024 * 1024
        ),
        cost_estimate=pl.CostEstimate(
            flops=14 * length * states * channels, bytes_accessed=2 * length * states * channels, transcendentals=0
        ),
    )(conv_in, gate, select, conv_w, conv_b, weight, bias, skip, out_shard, cot_shard)


def linked_backward_body(
    states, parts, dps, taps,
    low_ref, kq_ref, gate_ref, mixed_ref, dgated_ref, history_ref, final_ref, weight_ref, bias_ref, skip_ref,
    values_ref, conv_in_ref, select_ref, conv_w_ref, conv_b_ref, tokens_ref, part_ref, out_ref,
    dmixed_ref, small_ref, result_ref, out_grad_ref,
    grad_ref, state_ref, key_ref, query_ref, rate_ref, do_ref, values32_ref, fed_ref, kept_ref, part_key_ref,
    part_query_ref, row_ref, placed_ref, pick_ref, wide_ref, half_ref,
    dvalues_ref, dproj_ref, next_ref, vector_ref, part_low, part_kq, came_low, came_kq, sum_low, sum_kq,
    rs_send, rs_recv, ag_send, ag_recv, result_came, line_send, line_recv, out_send, out_recv,
    out_came, out_here, local_sem,
):
    d, s = lax.axis_index("dp"), lax.axis_index("seq")
    step = pl.program_id(0)
    rows, channels = gate_ref.shape
    length = values_ref.shape[0]
    blocks = length // rows
    span = length // parts
    per_part = span // rows
    packed = LANE // (2 * states)
    short = span // packed
    sel = select_ref.shape[1]

    def remote(src, dst, send, recv, to):
        return pltpu.make_async_remote_copy(
            src_ref=src, dst_ref=dst, send_sem=send, recv_sem=recv, device_id=to, device_id_type=MESH
        )

    copies = []
    for k in range(1, dps):
        to = lax.rem(d + k, dps)
        copies.append(remote(out_ref.at[to], out_came.at[k - 1], out_send.at[k - 1], out_recv.at[k - 1], (to, s)))
    out_copy = pltpu.make_async_copy(out_ref.at[d], out_here, local_sem)
    pass_line, line_total, line_sent = line_sums(parts, span, part_ref, result_came, line_send, line_recv)

    @pl.when(step == 0)
    def _():
        barrier = pltpu.get_barrier_semaphore()
        for k in range(1, parts):
            pl.semaphore_signal(barrier, inc=1, device_id=(d, lax.rem(s + k, parts)), device_id_type=MESH)
        for k in range(1, dps):
            pl.semaphore_signal(barrier, inc=1, device_id=(lax.rem(d + k, dps), s), device_id_type=MESH)
        pl.semaphore_wait(barrier, parts + dps - 2)
        grad_ref[...] = jnp.zeros_like(grad_ref)
        state_ref[...] = final_ref[...]
        next_ref[...] = jnp.zeros_like(next_ref)
        vector_ref[...] = jnp.zeros_like(vector_ref)
        small_ref[...] = jnp.zeros_like(small_ref)
        for copy in copies:
            copy.start()
        out_copy.start()

    def rs_copies(k):
        at = lax.rem(s + k, parts)
        return (
            remote(part_low.at[at], came_low.at[k - 1], rs_send.at[0, k - 1], rs_recv.at[0, k - 1], (d, at)),
            remote(part_kq.at[at], came_kq.at[k - 1], rs_send.at[1, k - 1], rs_recv.at[1, k - 1], (d, at)),
        )

    def ag_copies(k):
        to = lax.rem(s + k, parts)
        return (
            remote(sum_low.at[s], sum_low.at[s], ag_send.at[0, k - 1], ag_recv.at[0, k - 1], (d, to)),
            remote(sum_kq.at[s], sum_kq.at[s], ag_send.at[1, k - 1], ag_recv.at[1, k - 1], (d, to)),
        )

    def ag_taken(k, part):
        return (
            remote(sum_low.at[part], sum_low.at[part], ag_send.at[0, k - 1], ag_recv.at[0, k - 1], (d, s)),
            remote(sum_kq.at[part], sum_kq.at[part], ag_send.at[1, k - 1], ag_recv.at[1, k - 1], (d, s)),
        )

    def add_up():
        low = part_low[s].astype(jnp.float32)
        kq = part_kq[s]
        for k in range(1, parts):
            for copy in rs_copies(k):
                copy.wait_recv()
            low = low + came_low[k - 1].astype(jnp.float32)
            kq = kq + came_kq[k - 1]
        sum_low[s] = low.astype(jnp.bfloat16)
        sum_kq[s] = kq.astype(jnp.bfloat16)
        for k in range(1, parts):
            for copy in ag_copies(k):
                copy.start()

    def conv_back(part):
        for k in range(1, parts):
            @pl.when(lax.rem(s - k + parts, parts) == part)
            def _():
                for copy in ag_taken(k, part):
                    copy.wait_recv()

        here = pl.ds(pl.multiple_of(part * span, span), span)
        before = pl.multiple_of(jnp.maximum(part * span - 16, 0), 16)
        dproj_ref[:, :LANE] = sum_low[part]
        pack = sum_kq[part].astype(jnp.float32)
        lane = lax.broadcasted_iota(jnp.int32, pack.shape, 1)
        for g in range(packed):
            turned = pack if g == 0 else pltpu.roll(pack, LANE - g * 2 * states, 1)
            dproj_ref[g * short : (g + 1) * short, LANE:] = jnp.where(lane < 2 * states, turned, 0.0).astype(jnp.bfloat16)
        wide = min(256, channels)
        for left in range(0, channels, wide):
            cols = slice(left, left + wide)
            small_ref[cols, :sel] += lax.dot_general(
                values_ref[here, cols], dproj_ref[...], (((0,), (0,)), ((), ())), preferred_element_type=jnp.float32
            )
            head = conv_in_ref[pl.ds(before, 16), cols].astype(jnp.float32)
            head = jnp.where(part == 0, 0.0, head)
            body = jnp.concatenate([head, conv_in_ref[here, cols].astype(jnp.float32)], axis=0)
            total = conv_b_ref[:, cols]
            for tap in range(taps):
                by = taps - 1 - tap
                total = total + body[16 - by : 16 - by + span] * conv_w_ref[tap : tap + 1, cols]
            sg = sigmoid(total)
            dvalues = dvalues_ref[here, cols] + lax.dot_general(
                dproj_ref[...], select_ref[cols, :], (((1,), (1,)), ((), ())), preferred_element_type=jnp.float32
            )
            dconv = dvalues * (sg + total * sg * (1.0 - sg))
            vector_ref[taps : taps + 1, cols] += jnp.sum(dconv, axis=0, keepdims=True)
            after = jnp.concatenate([dconv, next_ref[:, cols]], axis=0)
            dconv_in = jnp.zeros_like(dconv)
            for tap in range(taps):
                by = taps - 1 - tap
                shifted = body[16 - by : 16 - by + span]
                vector_ref[tap : tap + 1, cols] += jnp.sum(dconv * shifted, axis=0, keepdims=True)
                dconv_in = dconv_in + after[by : by + span] * conv_w_ref[tap : tap + 1, cols]
            next_ref[:, cols] = dconv[0:8]
            dmixed_ref[here, cols] = dconv_in.astype(jnp.bfloat16)

    plan = tuple(((parts - 1 - i // 2, 2 * (i % 2)), (parts - 1 - i // 2, 2 * (i % 2) + 1)) for i in range(2 * (parts - 1)))
    for at_step, moves in enumerate(plan):
        @pl.when(step == at_step)
        def _():
            for steps, c in moves:
                pass_line(steps, c)

    for part in range(parts):
        ends = (parts - part) * per_part - 1
        sums = min(ends + 3, blocks - 1 if part > 0 else blocks)

        @pl.when(jnp.logical_and(step == sums, s == part))
        def _():
            add_up()

        @pl.when(step == blocks + 1 - part)
        def _():
            conv_back(part)

    @pl.when(step < blocks)
    def _():
        block = blocks - 1 - step
        here = pl.ds(pl.multiple_of(block * rows, rows), rows)
        low, kq = low_ref[...], kq_ref[...]
        beta, inverse = step_sizes(low, kq, weight_ref, bias_ref, states)
        rate_ref[...] = by_eights(beta * inverse)
        values = values_ref[here, :].astype(jnp.float32)
        values32_ref[...] = by_eights(values)
        gate = gate_ref[...]
        dgated = dgated_ref[...].astype(jnp.float32)
        sg = sigmoid(gate)
        do = dgated * (gate * sg)
        do_ref[...] = by_eights(do)
        dmixed_ref[here, channels:] = (dgated * mixed_ref[...] * (sg + gate * sg * (1.0 - sg))).astype(jnp.bfloat16)
        vector_ref[taps + 2 : taps + 3, :] += jnp.sum(do * values, axis=0, keepdims=True)
        spread_columns(kq, row_ref, pick_ref, key_ref, query_ref, states)
        backward_rows(
            states, rows, channels, history_ref, grad_ref, state_ref, key_ref, query_ref, rate_ref, do_ref, values32_ref,
            fed_ref, kept_ref, part_key_ref, part_query_ref, half_ref,
        )
        fed = as_rows(fed_ref[...])
        dvalues_ref[here, :] = fed + skip_ref[...] * as_rows(do_ref[...])
        scaled = as_rows(values32_ref[...]) * fed - as_rows(kept_ref[...])
        beta, inverse = step_sizes(low, kq, weight_ref, bias_ref, states)
        dpre = scaled * (1.0 - beta) * inverse
        vector_ref[taps + 1 : taps + 2, :] += jnp.sum(dpre, axis=0, keepdims=True)
        dpre_low = dpre.astype(jnp.bfloat16)
        small_ref[:, sel : sel + LANE] += lax.dot_general(
            dpre_low, low, (((0,), (0,)), ((), ())), preferred_element_type=jnp.float32
        )
        through = -2.0 * jnp.sum(scaled * beta * inverse, axis=1, keepdims=True)
        gather_columns(part_key_ref, part_query_ref, wide_ref, placed_ref, rows, states)
        lanes = lax.broadcasted_iota(jnp.int32, kq.shape, 1)
        dkq = as_rows(placed_ref[...]) + jnp.where(lanes < states, kq * through, 0.0)
        part = block // per_part
        within = lax.rem(block, per_part)
        part_low[part, pl.ds(pl.multiple_of(within * rows, rows), rows), :] = jnp.dot(
            dpre_low, weight_ref[...], preferred_element_type=jnp.float32
        ).astype(jnp.bfloat16)
        for g in range(packed):
            first = g * short - within * rows

            @pl.when(jnp.logical_and(first >= 0, first < rows))
            def _():
                for w in range(per_part):
                    if w * rows <= g * short < (w + 1) * rows:
                        lo = g * short - w * rows
                        piece = dkq[lo : lo + short]
                        piece = piece if g == 0 else pltpu.roll(piece, g * 2 * states, 1)
                        if g == (per_part - 1) * rows // short:
                            part_kq[part] = piece
                        else:
                            part_kq[part] += piece

        @pl.when(within == 0)
        def _():
            for k in range(1, parts):
                @pl.when(lax.rem(s + k, parts) == part)
                def _():
                    for copy in rs_copies(k):
                        copy.start()

    @pl.when(step == pl.num_programs(0) - 1)
    def _():
        small_ref[:, sel + LANE :] = jnp.transpose(vector_ref[...])
        chunk = span // 4
        for c in range(4):
            at = pl.ds(c * chunk, chunk)
            result_ref[at, :] = (tokens_ref[at, :].astype(jnp.float32) + line_total(c)).astype(jnp.bfloat16)
        line_sent()
        out_copy.wait()
        total = out_here[...].astype(jnp.float32)
        for k in range(1, dps):
            copies[k - 1].wait_recv()
            total = total + out_came[k - 1].astype(jnp.float32)
        out_grad_ref[...] = total
        for copy in copies:
            copy.wait_send()
        for k in range(1, parts):
            for copy in rs_copies(k) + ag_copies(k):
                copy.wait_send()


def linked_backward(
    low, kq, gate, mixed, dgated, history, final, weight, bias, skip, values, conv_in, select, conv_w, conv_b, tokens,
    result_part, out_part, parts, states,
):
    length, channels = values.shape
    dps = out_part.shape[0]
    width = tokens.shape[1]
    taps, sel = conv_w.shape[0], select.shape[1]
    span = length // parts
    rows = min(128, span)
    blocks = length // rows
    short = span // (LANE // (2 * states))
    at = lambda i: jnp.maximum(blocks - 1 - i, 0)
    by_row = lambda size: pl.BlockSpec((rows, size), lambda i: (at(i), 0))
    whole = lambda a: pl.BlockSpec(a.shape, lambda i: (0, 0))
    kept = lambda *shape: pl.BlockSpec(shape, lambda i: (0, 0))
    anywhere = pl.BlockSpec(memory_space=pl.ANY)
    dma = pltpu.SemaphoreType.DMA
    f32, bf16 = jnp.float32, jnp.bfloat16
    wide = pltpu.VMEM((rows // 8, 8, channels), f32)
    eights = pltpu.VMEM((rows // 8, 8, LANE), f32)
    spread = pltpu.VMEM((rows * states, LANE), f32)
    return pl.pallas_call(
        lambda *refs: linked_backward_body(states, parts, dps, taps, *refs),
        grid=(blocks + 2,),
        in_specs=[
            by_row(LANE), by_row(LANE), by_row(channels), by_row(channels), by_row(channels),
            pl.BlockSpec((rows * states, channels), lambda i: (at(i), 0)),
            whole(final), whole(weight), whole(bias), whole(skip), whole(values), whole(conv_in), whole(select),
            whole(conv_w), whole(conv_b), whole(tokens), whole(result_part), anywhere,
        ],
        out_specs=[kept(length, 2 * channels), kept(channels, sel + 2 * LANE), kept(span, width), kept(*out_part.shape[1:])],
        out_shape=[
            jax.ShapeDtypeStruct((length, 2 * channels), bf16),
            jax.ShapeDtypeStruct((channels, sel + 2 * LANE), f32),
            jax.ShapeDtypeStruct((span, width), bf16),
            jax.ShapeDtypeStruct(out_part.shape[1:], f32),
        ],
        scratch_shapes=[
            pltpu.VMEM((states, channels), f32), pltpu.VMEM((states, channels), f32),
            spread, spread, wide, wide, wide, wide, wide, spread, spread, eights, eights,
            pltpu.VMEM((rows * states, LANE), bf16), pltpu.VMEM((rows * states, 2 * LANE), bf16),
            pltpu.VMEM((2 * channels // LANE * 64, LANE), f32),
            pltpu.VMEM((length, channels), f32), pltpu.VMEM((span, sel), bf16), pltpu.VMEM((8, channels), f32),
            pltpu.VMEM((LANE, channels), f32),
            pltpu.VMEM((parts, span, LANE), bf16), pltpu.VMEM((parts, short, LANE), f32),
            pltpu.VMEM((parts - 1, span, LANE), bf16), pltpu.VMEM((parts - 1, short, LANE), f32),
            pltpu.VMEM((parts, span, LANE), bf16), pltpu.VMEM((parts, short, LANE), bf16),
            dma((2, parts - 1)), dma((2, parts - 1)), dma((2, parts - 1)), dma((2, parts - 1)),
            pltpu.VMEM((parts + 1, span, width), bf16), dma((2, parts, 4)), dma((2, parts, 4)),
            dma((dps - 1,)), dma((dps - 1,)), pltpu.VMEM((dps - 1,) + out_part.shape[1:], bf16),
            pltpu.VMEM(out_part.shape[1:], bf16), dma,
        ],
        compiler_params=pltpu.CompilerParams(
            collective_id=5, has_side_effects=True, vmem_limit_bytes=60 * 1024 * 1024
        ),
        cost_estimate=pl.CostEstimate(
            flops=30 * length * states * channels, bytes_accessed=2 * length * states * channels, transcendentals=0
        ),
    )(low, kq, gate, mixed, dgated, history, final, weight, bias, skip, values, conv_in, select, conv_w, conv_b, tokens, result_part, out_part)


def contract(left, right, left_dim, right_dim):
    return lax.dot_general(
        left, right, (((left_dim,), (right_dim,)), ((), ())), preferred_element_type=jnp.float32
    )


def gathered(shard, axis):
    return lax.all_gather(shard, axis, axis=0, tiled=True)


def scattered(total, axis):
    return lax.psum_scatter(total, axis, scatter_dimension=0, tiled=True)


def summed_rows(partial, axis):
    size = lax.axis_size(axis)
    parts = partial.astype(jnp.bfloat16).reshape((size, partial.shape[0] // size) + partial.shape[1:])
    parts = lax.all_to_all(parts, axis, 0, 0)
    return jnp.sum(parts.astype(jnp.float32), axis=0)


def later(rows, by):
    if by == 0:
        return rows
    return jnp.pad(rows, ((by, 0), (0, 0)))[: rows.shape[0]]


def sooner(rows, by):
    if by == 0:
        return rows
    return jnp.pad(rows, ((0, by), (0, 0)))[by:]


def local(
    tokens,
    cotangent,
    norm_gain,
    in_weight,
    conv_weight,
    conv_bias,
    select_weight,
    beta_weight,
    beta_bias,
    skip_gain,
    out_weight,
):
    parts, dps = lax.axis_size("seq"), lax.axis_size("dp")
    rows, width = tokens.shape[1:]
    block = conv_weight.shape[0]
    channels = block * dps
    taps = conv_weight.shape[1]
    rank = beta_weight.shape[1]
    states = (select_weight.shape[1] - rank) // 2
    own = in_weight.shape[0]

    flat = tokens.reshape(rows, width).astype(jnp.float32)
    scale = lax.rsqrt(jnp.mean(flat * flat, axis=-1, keepdims=True) + 1e-05)
    spread = in_weight.reshape(own, 2, dps, parts, block).transpose(3, 0, 1, 2, 4).reshape(parts, own, 2 * channels)
    vectors = jnp.concatenate(
        [conv_weight, conv_bias[:, None], beta_bias[:, None], skip_gain[:, None]], axis=1
    )
    wide = -(-select_weight.shape[1] // LANE) * LANE
    small = jnp.concatenate(
        [
            jnp.pad(select_weight, ((0, 0), (0, wide - select_weight.shape[1]))),
            beta_weight,
            jnp.pad(vectors, ((0, 0), (0, LANE - vectors.shape[1]))),
        ],
        axis=1,
    )
    small_slice = (dps, parts, 2 * own, rank) == (8, 4, LANE, LANE)
    if small_slice:
        doubled = jnp.broadcast_to(jnp.tile(norm_gain.reshape(1, own), (1, 2)), (GAIN_ROWS, LANE))
        normed, in_w, conv_in, gate, extra = start(tokens.reshape(rows, width), spread, small, doubled, dps)
        smalls = extra[:, :block].reshape(channels, small.shape[1])
        gain = extra[:, block:, :own].reshape(dps * parts, GAIN_ROWS, own)[:, 0].reshape(width)
    else:
        gain = gathered(norm_gain, ("dp", "seq"))
        normed = gathered((flat * scale * gain.astype(jnp.float32)).astype(jnp.bfloat16), "seq")
        in_w = gathered(lax.all_to_all(spread, "seq", 0, 0).reshape(parts * own, 2 * channels), "dp")
        smalls = gathered(small, "dp")
        conv_in = jnp.dot(normed, in_w[:, :channels], preferred_element_type=jnp.float32).astype(jnp.bfloat16)
        gate = jnp.dot(normed, in_w[:, channels:], preferred_element_type=jnp.float32)
    gain = gain.astype(jnp.float32)
    select_w = smalls[:, : select_weight.shape[1]]
    beta_w = smalls[:, wide : wide + rank]
    vectors = smalls[:, wide + rank :].astype(jnp.float32)
    conv_w, conv_b = vectors[:, :taps], vectors[:, taps]
    beta_b, skip = vectors[:, taps + 1].reshape(1, channels), vectors[:, taps + 2].reshape(1, channels)
    cot_here = cotangent.reshape(rows, width)
    if small_slice:
        mixed, history, final, values, low, kq, dgated, result_part, out_part = linked_forward(
            conv_in, gate, smalls[:, :wide], conv_w.T, conv_b.reshape(1, channels), beta_w, beta_b, skip, out_weight,
            cot_here, parts, dps, states,
        )
    else:
        conv_wide = conv_in.astype(jnp.float32)
        conv_sum = conv_b
        for tap in range(taps):
            conv_sum = conv_sum + later(conv_wide, taps - 1 - tap) * conv_w[:, tap]
        out_w = gathered(out_weight, "dp")
        cot = gathered(cot_here, "seq")
        values = jax.nn.silu(conv_sum).astype(jnp.bfloat16)
        projected = lax.psum(jnp.dot(values, select_w, preferred_element_type=jnp.float32), "seq")
        low = projected[:, :rank].astype(jnp.bfloat16)
        kq = jnp.pad(projected[:, rank:], ((0, 0), (0, LANE - 2 * states)))
        gated, mixed, history, final = forward_scan(low, kq, values, gate, beta_w, beta_b, skip, states)
        result_part = jnp.dot(gated, out_w, preferred_element_type=jnp.float32).astype(jnp.bfloat16)
        out_part = contract(gated, cot, 0, 0).astype(jnp.bfloat16)
        dgated = contract(cot, out_w, 1, 1)
    out_part = out_part.reshape(dps, block, width)
    if small_slice:
        dmixed, small_grads, result, out_grad = linked_backward(
            low, kq, gate, mixed, dgated, history, final, beta_w, beta_b, skip, values, conv_in, smalls[:, :wide], conv_w.T,
            conv_b.reshape(1, channels), tokens.reshape(rows, width), result_part, out_part, parts, states,
        )
        small_grads = small_grads.reshape(dps, block, wide + rank + LANE)
    else:
        result_part = result_part.reshape(parts, rows, width)
        dgate, dpre_low, dvalues, dlow, dkq, bias_grad, skip_grad, result_came, out_came = backward_scan(
            low, kq, values, gate, mixed, dgated, history, final, beta_w, beta_b, skip, result_part, out_part, states
        )
        part_here = lax.dynamic_index_in_dim(result_part, lax.axis_index("seq"), 0, False).astype(jnp.float32)
        result = (flat + (part_here + jnp.sum(result_came.astype(jnp.float32), axis=0))).astype(jnp.bfloat16)
        out_here = lax.dynamic_index_in_dim(out_part, lax.axis_index("dp"), 0, False).astype(jnp.float32)
        out_grad = out_here + jnp.sum(out_came.astype(jnp.float32), axis=0)
        dprojected = lax.psum(jnp.concatenate([dlow, dkq[:, : 2 * states]], axis=1), "seq").astype(jnp.bfloat16)
        beta_grad = contract(dpre_low, low, 0, 0)
        select_grad = contract(values, dprojected, 0, 0)
        dvalues = contract(dprojected, select_w, 1, 1) + dvalues
        s = jax.nn.sigmoid(conv_sum)
        dconv = dvalues * (s + conv_sum * s * (1.0 - s))
        conv_w_grad = jnp.stack(
            [jnp.sum(dconv * later(conv_wide, taps - 1 - tap), axis=0) for tap in range(taps)], axis=1
        )
        conv_b_grad = jnp.sum(dconv, axis=0)
        dconv_in = 0.0
        for tap in range(taps):
            dconv_in = dconv_in + sooner(dconv, taps - 1 - tap) * conv_w[:, tap]
        dmixed = jnp.concatenate([dconv_in.astype(jnp.bfloat16), dgate], axis=1)
        vector_grads = jnp.concatenate(
            [conv_w_grad, conv_b_grad[:, None], bias_grad.reshape(channels, 1), skip_grad.reshape(channels, 1)], axis=1
        )
        small_grads = jnp.concatenate(
            [
                jnp.pad(select_grad, ((0, 0), (0, wide - select_grad.shape[1]))),
                beta_grad,
                jnp.pad(vector_grads, ((0, 0), (0, LANE - vector_grads.shape[1]))),
            ],
            axis=1,
        ).reshape(dps, block, wide + rank + LANE)
    if small_slice:
        input_grad, in_grad, gain_sums, small_grads = end(
            dmixed, normed, in_w, tokens.reshape(rows, width), cot_here, gain.reshape(1, width), in_weight, small_grads,
            parts, block,
        )
        gain_sums = gain_sums[:, 0]
    else:
        in_grad = summed_rows(contract(normed, dmixed, 0, 0), "dp").astype(jnp.bfloat16)
        in_grad = lax.all_to_all(in_grad.reshape(parts, own, 2 * channels), "seq", 0, 0).astype(jnp.float32)
        in_grad = in_grad.reshape(parts, own, 2, dps, block).transpose(1, 2, 3, 0, 4).reshape(own, 2 * parts * channels)
        gain_sums = jnp.sum(in_grad * in_weight.astype(jnp.float32), axis=1)
        v = summed_rows(contract(dmixed, in_w, 1, 1), "seq") * gain
        du = scale * v - flat * (scale * scale * scale) * jnp.mean(flat * v, axis=-1, keepdims=True)
        input_grad = (cot_here.astype(jnp.float32) + du).astype(jnp.bfloat16)
        small_grads = jnp.sum(lax.all_to_all(small_grads, "dp", 0, 0), axis=0)
    rows_grad = small_grads[:, wide + rank :]
    return (
        result.reshape(tokens.shape),
        input_grad.reshape(tokens.shape),
        gain_sums / norm_gain.astype(jnp.float32),
        in_grad,
        rows_grad[:, :taps],
        rows_grad[:, taps],
        small_grads[:, : select_weight.shape[1]],
        small_grads[:, wide : wide + rank],
        rows_grad[:, taps + 1],
        rows_grad[:, taps + 2],
        out_grad,
    )


def solution(mesh):
    split = P(("dp", "seq"))
    rows = P("dp", "seq", None)
    return jax.shard_map(
        local,
        mesh=mesh,
        in_specs=(rows, rows) + (split,) * 9,
        out_specs=(rows, rows) + (split,) * 9,
        check_vma=False,
    )
```

```python
import jax
import jax.numpy as jnp
from jax import lax
from jax.experimental import pallas as pl
from jax.experimental.pallas import tpu as pltpu
from jax.sharding import PartitionSpec as P

LANE = 128
PER_GROUP = 4


def sigmoid(v):
    return 1.0 / (1.0 + jnp.exp(-v))


def by_eights(value):
    return value.reshape(value.shape[0] // 8, 8, value.shape[1])


def as_rows(value):
    return value.reshape(value.shape[0] * 8, value.shape[2])


def spread_columns(kq, row_ref, pick_ref, key_ref, query_ref, states):
    rows = kq.shape[0]
    high = kq.astype(jnp.bfloat16).astype(jnp.float32)
    rest = kq - high
    middle = rest.astype(jnp.bfloat16).astype(jnp.float32)
    row_ref[...] = by_eights(high + pltpu.roll(middle, 2 * states, 1) + pltpu.roll(rest - middle, 4 * states, 1))
    lane = lax.broadcasted_iota(jnp.int32, (states, LANE), 1)
    entry = lax.broadcasted_iota(jnp.int32, (states, LANE), 0)
    pick = lax.rem(lane, states) == entry

    def body(group, carry):
        for offset in range(8):
            at = pl.multiple_of((group * 8 + offset) * states, states)
            row = jnp.broadcast_to(row_ref[group, offset : offset + 1, :], (states, LANE))
            pick_ref[pl.ds(at, states), :] = jnp.where(pick, row, 0.0).astype(jnp.bfloat16)
        return carry

    lax.fori_loop(0, rows // 8, body, 0)
    term = lax.broadcasted_iota(jnp.int32, (LANE, 2 * LANE), 0)
    side = lax.broadcasted_iota(jnp.int32, (LANE, 2 * LANE), 1)
    is_query = lax.rem(term, 2 * states) >= states
    halves = jnp.where(is_query == (side >= LANE), 1.0, 0.0).astype(jnp.bfloat16)
    both = jnp.dot(pick_ref[...], halves, preferred_element_type=jnp.float32)
    key_ref[...] = both[:, :LANE]
    query_ref[...] = both[:, LANE:]


def sum_eights(half_ref, first):
    total = half_ref[pl.ds(first, 8, stride=8), :]
    for n in range(1, 8):
        total = total + half_ref[pl.ds(first + n, 8, stride=8), :]
    return total


def step_sizes(low, kq, weight_ref, bias_ref, states):
    pre = lax.dot_general(
        low, weight_ref[...], (((1,), (1,)), ((), ())), preferred_element_type=jnp.float32
    )
    beta = sigmoid(pre + bias_ref[...])
    lane = lax.broadcasted_iota(jnp.int32, kq.shape, 1)
    keys = jnp.where(lane < states, kq, 0.0)
    square = jnp.sum(keys * keys, axis=1, keepdims=True)
    return beta, 1.0 / (1.0 + beta * square)


def forward_rows(states, rows, channels, history_ref, state_ref, key_ref, query_ref, rate_ref, input_ref, out_ref, half_ref):
    tiles = channels // LANE
    per_group = min(8, tiles)
    for first in range(0, tiles, per_group):
        columns = [slice((first + j) * LANE, (first + j + 1) * LANE) for j in range(per_group)]

        def body(group, carry):
            carry = list(carry)
            for offset in range(8):
                t = group * 8 + offset
                at = pl.multiple_of(t * states, states)
                key = key_ref[pl.ds(at, states), :]
                query = query_ref[pl.ds(at, states), :]
                square = key * key
                for j, cols in enumerate(columns):
                    history_ref[pl.ds(at, states), cols] = carry[j].astype(jnp.bfloat16)
                    rate = rate_ref[group, offset : offset + 1, cols]
                    fed = input_ref[group, offset : offset + 1, cols]
                    carry[j] = (1.0 - rate * square) * carry[j] + key * fed
                    read = query * carry[j]
                    half_ref[j * 64 + offset * 8 : j * 64 + offset * 8 + 8, :] = read[0:8] + read[8:16]
            for j, cols in enumerate(columns):
                out_ref[group, :, cols] = sum_eights(half_ref, j * 64)
            return tuple(carry)

        done = lax.fori_loop(0, rows // 8, body, tuple(state_ref[:, cols] for cols in columns))
        for cols, state in zip(columns, done):
            state_ref[:, cols] = state


def forward_body(
    states, low_ref, kq_ref, values_ref, gate_ref, weight_ref, bias_ref, skip_ref,
    gated_ref, mixed_ref, history_ref, final_ref,
    state_ref, key_ref, query_ref, rate_ref, input_ref, out_ref, row_ref, pick_ref, half_ref,
):
    rows, channels = values_ref.shape

    @pl.when(pl.program_id(0) == 0)
    def _():
        state_ref[...] = jnp.zeros_like(state_ref)

    beta, inverse = step_sizes(low_ref[...], kq_ref[...], weight_ref, bias_ref, states)
    rates = beta * inverse
    rate_ref[...] = by_eights(rates)
    input_ref[...] = by_eights(rates * values_ref[...].astype(jnp.float32))
    spread_columns(kq_ref[...], row_ref, pick_ref, key_ref, query_ref, states)

    forward_rows(states, rows, channels, history_ref, state_ref, key_ref, query_ref, rate_ref, input_ref, out_ref, half_ref)
    mixed = as_rows(out_ref[...]) + skip_ref[...] * values_ref[...].astype(jnp.float32)
    gate = gate_ref[...]
    mixed_ref[...] = mixed
    gated_ref[...] = (mixed * gate * sigmoid(gate)).astype(jnp.bfloat16)

    @pl.when(pl.program_id(0) == pl.num_programs(0) - 1)
    def _():
        final_ref[...] = state_ref[...]


def forward_scan(low, kq, values, gate, weight, bias, skip, states):
    length, channels = values.shape
    rank = low.shape[1]
    rows = min(128, length)
    blocks = length // rows
    by_row = lambda width: pl.BlockSpec((rows, width), lambda i: (i, 0))
    whole = lambda a: pl.BlockSpec(a.shape, lambda i: (0, 0))
    return pl.pallas_call(
        lambda *refs: forward_body(states, *refs),
        grid=(blocks,),
        in_specs=[by_row(rank), by_row(LANE), by_row(channels), by_row(channels), whole(weight), whole(bias), whole(skip)],
        out_specs=[
            by_row(channels),
            by_row(channels),
            pl.BlockSpec((rows * states, channels), lambda i: (i, 0)),
            pl.BlockSpec((states, channels), lambda i: (0, 0)),
        ],
        out_shape=[
            jax.ShapeDtypeStruct((length, channels), jnp.bfloat16),
            jax.ShapeDtypeStruct((length, channels), jnp.float32),
            jax.ShapeDtypeStruct((length * states, channels), jnp.bfloat16),
            jax.ShapeDtypeStruct((states, channels), jnp.float32),
        ],
        scratch_shapes=[
            pltpu.VMEM((states, channels), jnp.float32),
            pltpu.VMEM((rows * states, LANE), jnp.float32),
            pltpu.VMEM((rows * states, LANE), jnp.float32),
            pltpu.VMEM((rows // 8, 8, channels), jnp.float32),
            pltpu.VMEM((rows // 8, 8, channels), jnp.float32),
            pltpu.VMEM((rows // 8, 8, channels), jnp.float32),
            pltpu.VMEM((rows // 8, 8, LANE), jnp.float32), pltpu.VMEM((rows * states, LANE), jnp.bfloat16),
            pltpu.VMEM((channels // LANE * 64, LANE), jnp.float32),
        ],
        compiler_params=pltpu.CompilerParams(vmem_limit_bytes=48 * 1024 * 1024),
        cost_estimate=pl.CostEstimate(flops=14 * length * states * channels, bytes_accessed=2 * length * states * channels, transcendentals=0),
    )(low, kq, values, gate, weight, bias, skip)


def backward_rows(
    states, rows, channels, history_ref, grad_ref, state_ref, key_ref, query_ref, rate_ref, do_ref, values32_ref,
    fed_ref, kept_ref, part_key_ref, part_query_ref, half_ref,
):
    tiles = channels // LANE
    per_group = min(PER_GROUP, tiles)
    for first in range(0, tiles, per_group):
        columns = [slice((first + j) * LANE, (first + j + 1) * LANE) for j in range(per_group)]

        def body(step, carry):
            grads, lates = list(carry[0]), list(carry[1])
            group = rows // 8 - 1 - step
            for offset in reversed(range(8)):
                t = group * 8 + offset
                at = pl.multiple_of(t * states, states)
                key = key_ref[pl.ds(at, states), :]
                query = query_ref[pl.ds(at, states), :]
                sum_key = None
                sum_query = None
                for j, cols in enumerate(columns):
                    rate = rate_ref[group, offset : offset + 1, cols]
                    out_grad = do_ref[group, offset : offset + 1, cols]
                    value = values32_ref[group, offset : offset + 1, cols]
                    before = history_ref[pl.ds(at, states), cols].astype(jnp.float32)
                    grad = grads[j] + query * out_grad
                    scaled = rate * grad
                    by_key = key * scaled
                    kept = scaled * before
                    kept = key * kept
                    twice = key * kept
                    at_fed = j * 64 + offset * 8
                    at_kept = (per_group + j) * 64 + offset * 8
                    half_ref[at_fed : at_fed + 8, :] = by_key[0:8] + by_key[8:16]
                    half_ref[at_kept : at_kept + 8, :] = twice[0:8] + twice[8:16]
                    term_key = value * scaled - 2.0 * kept
                    term_query = lates[j] * out_grad
                    sum_key = term_key if sum_key is None else sum_key + term_key
                    sum_query = term_query if sum_query is None else sum_query + term_query
                    grads[j] = grad - key * by_key
                    lates[j] = before
                if first == 0:
                    part_key_ref[pl.ds(at, states), :] = sum_key
                    part_query_ref[pl.ds(at, states), :] = sum_query
                else:
                    part_key_ref[pl.ds(at, states), :] += sum_key
                    part_query_ref[pl.ds(at, states), :] += sum_query
            for j, cols in enumerate(columns):
                fed_ref[group, :, cols] = sum_eights(half_ref, j * 64)
                kept_ref[group, :, cols] = sum_eights(half_ref, (per_group + j) * 64)
            return (tuple(grads), tuple(lates))

        start = (tuple(grad_ref[:, cols] for cols in columns), tuple(state_ref[:, cols] for cols in columns))
        grads, lates = lax.fori_loop(0, rows // 8, body, start)
        for cols, grad, late in zip(columns, grads, lates):
            grad_ref[:, cols] = grad
            state_ref[:, cols] = late


def lane_sums(part_ref, wide_ref, states):
    part = part_ref[...]
    high = part.astype(jnp.bfloat16)
    wide_ref[:, :LANE] = high
    wide_ref[:, LANE:] = (part - high.astype(jnp.float32)).astype(jnp.bfloat16)
    ones = jnp.ones((2 * LANE, LANE), jnp.bfloat16)
    part_ref[...] = jnp.dot(wide_ref[...], ones, preferred_element_type=jnp.float32)


def gather_columns(part_key_ref, part_query_ref, wide_ref, placed_ref, rows, states):
    lane_sums(part_key_ref, wide_ref, states)
    lane_sums(part_query_ref, wide_ref, states)
    lane = lax.broadcasted_iota(jnp.int32, (8, LANE), 1)

    def body(group, carry):
        total = jnp.zeros((8, LANE), jnp.float32)
        for n in range(states):
            at = group * 8 * states + n
            total = jnp.where(lane == n, part_key_ref[pl.ds(at, 8, stride=states), :], total)
            total = jnp.where(lane == n + states, part_query_ref[pl.ds(at, 8, stride=states), :], total)
        placed_ref[group] = total
        return carry

    lax.fori_loop(0, rows // 8, body, 0)


def backward_body(
    states, links, low_ref, kq_ref, values_ref, gate_ref, mixed_ref, dgated_ref, history_ref, final_ref, weight_ref, bias_ref, skip_ref,
    result_ref, out_ref, dgate_ref, dpre_ref, dvalues_ref, dlow_ref, dkq_ref, bias_grad_ref, skip_grad_ref, result_came, out_came,
    grad_ref, state_ref, key_ref, query_ref, rate_ref, do_ref, values32_ref, fed_ref, kept_ref, part_key_ref, part_query_ref, row_ref, placed_ref,
    pick_ref, wide_ref, half_ref, *sems,
):
    rows, channels = values_ref.shape
    copies = links(result_ref, out_ref, result_came, out_came, *sems)

    @pl.when(pl.program_id(0) == 0)
    def _():
        grad_ref[...] = jnp.zeros_like(grad_ref)
        state_ref[...] = final_ref[...]
        bias_grad_ref[...] = jnp.zeros_like(bias_grad_ref)
        skip_grad_ref[...] = jnp.zeros_like(skip_grad_ref)
        for copy in copies:
            copy.start()

    beta, inverse = step_sizes(low_ref[...], kq_ref[...], weight_ref, bias_ref, states)
    rate_ref[...] = by_eights(beta * inverse)
    values = values_ref[...].astype(jnp.float32)
    values32_ref[...] = by_eights(values)
    gate = gate_ref[...]
    dgated = dgated_ref[...].astype(jnp.float32)
    s = sigmoid(gate)
    do = dgated * (gate * s)
    do_ref[...] = by_eights(do)
    dgate_ref[...] = (dgated * mixed_ref[...] * (s + gate * s * (1.0 - s))).astype(jnp.bfloat16)
    skip_grad_ref[...] += jnp.sum(do * values, axis=0, keepdims=True)
    spread_columns(kq_ref[...], row_ref, pick_ref, key_ref, query_ref, states)

    backward_rows(
        states, rows, channels, history_ref, grad_ref, state_ref, key_ref, query_ref, rate_ref, do_ref, values32_ref,
        fed_ref, kept_ref, part_key_ref, part_query_ref, half_ref,
    )
    fed = as_rows(fed_ref[...])
    dvalues_ref[...] = fed + skip_ref[...] * as_rows(do_ref[...])
    scaled = as_rows(values32_ref[...]) * fed - as_rows(kept_ref[...])
    beta, inverse = step_sizes(low_ref[...], kq_ref[...], weight_ref, bias_ref, states)
    dpre = scaled * (1.0 - beta) * inverse
    bias_grad_ref[...] += jnp.sum(dpre, axis=0, keepdims=True)
    dpre_low = dpre.astype(jnp.bfloat16)
    dpre_ref[...] = dpre_low
    dlow_ref[...] = jnp.dot(dpre_low, weight_ref[...], preferred_element_type=jnp.float32)
    through = -2.0 * jnp.sum(scaled * beta * inverse, axis=1, keepdims=True)

    gather_columns(part_key_ref, part_query_ref, wide_ref, placed_ref, rows, states)
    lanes = lax.broadcasted_iota(jnp.int32, kq_ref.shape, 1)
    dkq_ref[...] = as_rows(placed_ref[...]) + jnp.where(lanes < states, kq_ref[...] * through, 0.0)

    @pl.when(pl.program_id(0) == pl.num_programs(0) - 1)
    def _():
        for copy in copies:
            copy.wait_recv()
        for copy in copies:
            copy.wait_send()


def exchange(parts, dps, result_ref, out_ref, result_came, out_came, result_send, result_recv, out_send, out_recv):
    d, s = lax.axis_index("dp"), lax.axis_index("seq")

    @pl.when(pl.program_id(0) == 0)
    def _():
        barrier = pltpu.get_barrier_semaphore()
        for k in range(1, parts):
            pl.semaphore_signal(barrier, inc=1, device_id=(d, lax.rem(s + k, parts)), device_id_type=MESH)
        for k in range(1, dps):
            pl.semaphore_signal(barrier, inc=1, device_id=(lax.rem(d + k, dps), s), device_id_type=MESH)
        pl.semaphore_wait(barrier, parts + dps - 2)

    copies = []
    for k in range(1, parts):
        to = lax.rem(s + k, parts)
        copies.append(
            pltpu.make_async_remote_copy(
                src_ref=result_ref.at[to], dst_ref=result_came.at[k - 1], send_sem=result_send.at[k - 1],
                recv_sem=result_recv.at[k - 1], device_id=(d, to), device_id_type=MESH,
            )
        )
    for k in range(1, dps):
        to = lax.rem(d + k, dps)
        copies.append(
            pltpu.make_async_remote_copy(
                src_ref=out_ref.at[to], dst_ref=out_came.at[k - 1], send_sem=out_send.at[k - 1],
                recv_sem=out_recv.at[k - 1], device_id=(to, s), device_id_type=MESH,
            )
        )
    return copies


def backward_scan(low, kq, values, gate, mixed, dgated, history, final, weight, bias, skip, result_part, out_part, states):
    length, channels = values.shape
    rank = low.shape[1]
    rows = min(128, length)
    blocks = length // rows
    by_row = lambda width: pl.BlockSpec((rows, width), lambda i: (blocks - 1 - i, 0))
    whole = lambda a: pl.BlockSpec(a.shape, lambda i: (0, 0))
    total = pl.BlockSpec((1, channels), lambda i: (0, 0))
    wide = pltpu.VMEM((rows // 8, 8, channels), jnp.float32)
    spread = pltpu.VMEM((rows * states, LANE), jnp.float32)
    anywhere = pl.BlockSpec(memory_space=pl.ANY)
    dma = pltpu.SemaphoreType.DMA
    parts, dps = result_part.shape[0], out_part.shape[0]
    links = lambda *refs: exchange(parts, dps, *refs)
    return pl.pallas_call(
        lambda *refs: backward_body(states, links, *refs),
        grid=(blocks,),
        in_specs=[
            by_row(rank), by_row(LANE), by_row(channels), by_row(channels), by_row(channels), by_row(channels),
            pl.BlockSpec((rows * states, channels), lambda i: (blocks - 1 - i, 0)),
            whole(final), whole(weight), whole(bias), whole(skip), anywhere, anywhere,
        ],
        out_specs=[by_row(channels), by_row(channels), by_row(channels), by_row(rank), by_row(LANE), total, total, anywhere, anywhere],
        out_shape=[
            jax.ShapeDtypeStruct((length, channels), jnp.bfloat16),
            jax.ShapeDtypeStruct((length, channels), jnp.bfloat16),
            jax.ShapeDtypeStruct((length, channels), jnp.float32),
            jax.ShapeDtypeStruct((length, rank), jnp.float32),
            jax.ShapeDtypeStruct((length, LANE), jnp.float32),
            jax.ShapeDtypeStruct((1, channels), jnp.float32),
            jax.ShapeDtypeStruct((1, channels), jnp.float32),
            jax.ShapeDtypeStruct((parts - 1,) + result_part.shape[1:], jnp.bfloat16),
            jax.ShapeDtypeStruct((dps - 1,) + out_part.shape[1:], jnp.bfloat16),
        ],
        scratch_shapes=[
            pltpu.VMEM((states, channels), jnp.float32),
            pltpu.VMEM((states, channels), jnp.float32),
            spread, spread, wide, wide, wide, wide, wide, spread, spread,
            pltpu.VMEM((rows // 8, 8, LANE), jnp.float32), pltpu.VMEM((rows // 8, 8, LANE), jnp.float32),
            pltpu.VMEM((rows * states, LANE), jnp.bfloat16), pltpu.VMEM((rows * states, 2 * LANE), jnp.bfloat16),
            pltpu.VMEM((2 * channels // LANE * 64, LANE), jnp.float32),
            dma((parts - 1,)), dma((parts - 1,)), dma((dps - 1,)), dma((dps - 1,)),
        ],
        compiler_params=pltpu.CompilerParams(collective_id=3, has_side_effects=True, vmem_limit_bytes=56 * 1024 * 1024),
        cost_estimate=pl.CostEstimate(flops=30 * length * states * channels, bytes_accessed=2 * length * states * channels, transcendentals=0),
    )(low, kq, values, gate, mixed, dgated, history, final, weight, bias, skip, result_part, out_part)


MESH = pl.DeviceIdType.MESH
GAIN_ROWS = 16


def plane_mates(d):
    core, x, y = lax.rem(d, 2), lax.rem(d // 2, 2), d // 4
    return d + 1 - 2 * core, d + 2 - 4 * x, d + 4 - 8 * y


def start_body(
    parts, block,
    tokens_ref, spread_ref, extra_ref, gain_ref,
    normed_out, weight_out, conv_ref, gate_ref, select_out, beta_out, vector_out, gain_out,
    tokens_all, normed_all, weight_all, extra_all,
    near_send, near_recv, plane_send, plane_recv, gain_send, gain_recv, line_send, line_recv, local_sem,
):
    d, s = lax.axis_index("dp"), lax.axis_index("seq")
    sib, xm, ym = plane_mates(d)
    own = spread_ref.shape[1]
    rows, width = tokens_ref.shape
    small = extra_ref.shape[0]
    channels = conv_ref.shape[1]
    chunk = rows // 4

    barrier = pltpu.get_barrier_semaphore()
    for mate in (sib, xm, ym):
        pl.semaphore_signal(barrier, inc=1, device_id=(mate, s), device_id_type=MESH)
    for k in range(1, parts):
        pl.semaphore_signal(barrier, inc=1, device_id=(d, lax.rem(s + k, parts)), device_id_type=MESH)
    pl.semaphore_wait(barrier, 3 + parts - 1)

    def remote(src, dst, send, recv, to):
        return pltpu.make_async_remote_copy(
            src_ref=src, dst_ref=dst, send_sem=send, recv_sem=recv, device_id=to, device_id_type=MESH
        )

    def weight_rows(owner, source):
        return weight_all.at[pl.ds(pl.multiple_of((owner * parts + source) * own, own), own), :]

    def extra_rows(owner):
        return extra_all.at[owner]

    def gain_rows(source):
        return extra_all.at[d, pl.ds(pl.multiple_of(small + source * GAIN_ROWS, GAIN_ROWS), GAIN_ROWS), pl.ds(0, LANE)]

    near = []
    for k in range(1, parts):
        to = (d, lax.rem(s + k, parts))
        near.append(remote(spread_ref.at[to[1]], weight_rows(d, s), near_send.at[k], near_recv.at[k], to))
        near.append(remote(gain_ref, gain_rows(s), gain_send.at[k], gain_recv.at[k], to))
    for copy in near:
        copy.start()
    mine = [
        pltpu.make_async_copy(spread_ref.at[s], weight_rows(d, s), local_sem.at[0]),
        pltpu.make_async_copy(gain_ref, gain_rows(s), local_sem.at[1]),
        pltpu.make_async_copy(extra_ref, extra_all.at[d, pl.ds(0, small), :], local_sem.at[2]),
        pltpu.make_async_copy(tokens_ref, tokens_all.at[pl.ds(pl.multiple_of(s * rows, rows), rows), :], local_sem.at[3]),
    ]
    for copy in mine:
        copy.start()

    def token_rows(part, c):
        return tokens_all.at[pl.ds(pl.multiple_of(part * rows + c * chunk, chunk), chunk), :]

    def token_copy(way, distance, c):
        part = s - way * (distance - 1)
        src = tokens_ref.at[pl.ds(c * chunk, chunk), :] if distance == 1 else token_rows(part, c)
        side = 0 if way == 1 else 1
        return remote(
            src, token_rows(part, c), line_send.at[side, distance, c], line_recv.at[side, distance, c], (d, s + way)
        )

    def can_send(way, distance):
        reach = s + 1 < parts if way == 1 else s >= 1
        came = s - (distance - 1) >= 0 if way == 1 else s + (distance - 1) < parts
        return jnp.logical_and(reach, came)

    def arrives(way, distance):
        return s >= distance if way == 1 else s + distance < parts

    def send_tokens(distance, c):
        for way in (1, -1):
            @pl.when(can_send(way, distance))
            def _():
                token_copy(way, distance, c).start()

    def sent_tokens(distance, c):
        for way in (1, -1):
            @pl.when(can_send(way, distance))
            def _():
                token_copy(way, distance, c).wait_send()

    def take_tokens(distance, c):
        for way in (1, -1):
            @pl.when(arrives(way, distance))
            def _():
                part = s - way * distance
                side = 0 if way == 1 else 1
                remote(
                    token_rows(part, c), token_rows(part, c), line_send.at[side, distance, c],
                    line_recv.at[side, distance, c], (d, s),
                ).wait_recv()

    units = parts + 1

    def unit(owner, k):
        return extra_rows(owner) if k == parts else weight_rows(owner, lax.rem(s - k + parts, parts))

    kinds = {"own": (d, 0), "x": (xm, 2), "y": (ym, 4)}

    def plane_copy(owner, k, rel, kind, to):
        return remote(unit(owner, k), unit(owner, k), plane_send.at[kind, k], plane_recv.at[rel, k], (to, s))

    diag = xm + ym - d
    sib_of = lambda mate: mate + sib - d

    def route(k):
        steps = [
            (0, d, 1, 0, sib), (0, d, 2, 1, xm), (0, d, 4, 2, ym),
            (2, xm, 3, 3, sib), (4, ym, 5, 5, sib), (6, diag, 7, 7, sib),
        ]
        steps.append((2, xm, 6, 4, ym) if k % 2 == 0 else (4, ym, 6, 6, xm))
        return steps

    def pass_on(stage, k):
        for at, owner, rel, kind, to in route(k):
            if at == stage:
                plane_copy(owner, k, rel, kind, to).start()

    owners = {1: sib, 2: xm, 3: sib_of(xm), 4: ym, 5: sib_of(ym), 6: diag, 7: sib_of(diag)}

    def take(rel, k):
        plane_copy(owners[rel], k, rel, 0, d).wait_recv()

    for c in range(4):
        send_tokens(1, c)
    mine[0].wait()
    pass_on(0, 0)
    for k in range(1, parts):
        near_wait = remote(
            spread_ref.at[s], weight_rows(d, lax.rem(s - k + parts, parts)), near_send.at[k], near_recv.at[k], (d, s)
        )
        near_wait.wait_recv()
        pass_on(0, k)
    mine[1].wait()
    mine[2].wait()
    for k in range(1, parts):
        remote(gain_ref, gain_rows(lax.rem(s - k + parts, parts)), gain_send.at[k], gain_recv.at[k], (d, s)).wait_recv()
    pass_on(0, parts)
    for k in range(units):
        take(2, k)
        pass_on(2, k)
        take(4, k)
        pass_on(4, k)
        if k < 4:
            take_tokens(1, k)
            send_tokens(2, k)
    for k in range(units):
        take(6, k)
        pass_on(6, k)
        if k < 4:
            take_tokens(2, k)
            send_tokens(3, k)
    for rel in (1, 3, 5, 7):
        for k in range(units):
            take(rel, k)
    mine[3].wait()
    weight_copy = pltpu.make_async_copy(weight_all, weight_out, local_sem.at[4])
    weight_copy.start()
    sel = select_out.shape[1]
    for owner in range(extra_all.shape[0]):
        here = slice(owner * small, (owner + 1) * small)
        select_out[here, :] = extra_all[owner, 0:small, 0:sel]
        beta_out[here, :] = extra_all[owner, 0:small, sel : sel + LANE]
        vectors = extra_all[owner, 0:small, sel + LANE : sel + 2 * LANE].astype(jnp.float32)
        vector_out[:, here] = jnp.transpose(vectors)[: vector_out.shape[0]]

    lane = lax.broadcasted_iota(jnp.int32, (1, LANE), 1)
    pieces = []
    for owner in range(extra_all.shape[0]):
        for source in range(0, parts, 2):
            row = small + source * GAIN_ROWS
            even = extra_all[owner, row : row + GAIN_ROWS, 0:LANE].astype(jnp.float32)[0:1]
            odd = extra_all[owner, row + GAIN_ROWS : row + 2 * GAIN_ROWS, 0:LANE].astype(jnp.float32)[0:1]
            pieces.append(jnp.where(lane < own, even, odd))
    gain = jnp.concatenate(pieces, axis=1)
    gain_out[...] = gain

    tile = min(512, channels)

    def work(part):
        for c in range(4):
            at = pl.ds(pl.multiple_of(part * rows + c * chunk, chunk), chunk)
            flat = tokens_all[at, :].astype(jnp.float32)
            scale = lax.rsqrt(jnp.mean(flat * flat, axis=-1, keepdims=True) + 1e-05)
            normed_all[at, :] = (flat * scale * gain).astype(jnp.bfloat16)
        at = pl.ds(pl.multiple_of(part * rows, rows), rows)

        def columns(n, carry):
            left = pl.multiple_of(n * tile, tile)
            right = pl.multiple_of(channels + n * tile, tile)
            conv_ref[at, pl.ds(left, tile)] = jnp.dot(
                normed_all[at, :], weight_all[:, pl.ds(left, tile)], preferred_element_type=jnp.float32
            ).astype(jnp.bfloat16)
            gate_ref[at, pl.ds(left, tile)] = jnp.dot(
                normed_all[at, :], weight_all[:, pl.ds(right, tile)], preferred_element_type=jnp.float32
            )
            return carry

        lax.fori_loop(0, channels // tile, columns, 0)

    def work_at(low, high):
        def each(part, carry):
            away = jnp.abs(part - s)

            @pl.when(jnp.logical_and(away >= low, away <= high))
            def _():
                work(part)

            return carry

        lax.fori_loop(0, parts, each, 0)

    work_at(0, 2)
    for c in range(4):
        take_tokens(3, c)
    work_at(3, 3)
    normed_copy = pltpu.make_async_copy(normed_all, normed_out, local_sem.at[5])
    normed_copy.start()

    for copy in near:
        copy.wait_send()
    for k in range(units):
        for at, owner, rel, kind, to in route(k):
            plane_copy(owner, k, rel, kind, to).wait_send()
    for distance in range(1, parts):
        for c in range(4):
            sent_tokens(distance, c)
    weight_copy.wait()
    normed_copy.wait()


def start(tokens, spread, extra, gain, dps):
    parts, own, both = spread.shape
    rows, width = tokens.shape
    small, lanes = extra.shape
    any_space = pl.BlockSpec(memory_space=pl.ANY)
    vmem = pl.BlockSpec(memory_space=pltpu.VMEM)
    tall = small + parts * GAIN_ROWS
    dma = pltpu.SemaphoreType.DMA
    return pl.pallas_call(
        lambda *refs: start_body(parts, own, *refs),
        out_shape=[
            jax.ShapeDtypeStruct((parts * rows, width), jnp.bfloat16),
            jax.ShapeDtypeStruct((dps * parts * own, both), jnp.bfloat16),
            jax.ShapeDtypeStruct((parts * rows, both // 2), jnp.bfloat16),
            jax.ShapeDtypeStruct((parts * rows, both // 2), jnp.float32),
            jax.ShapeDtypeStruct((dps * small, lanes - 2 * LANE), jnp.bfloat16),
            jax.ShapeDtypeStruct((dps * small, LANE), jnp.bfloat16),
            jax.ShapeDtypeStruct((8, dps * small), jnp.float32),
            jax.ShapeDtypeStruct((1, width), jnp.float32),
        ],
        in_specs=[vmem, vmem, vmem, vmem],
        out_specs=[any_space, any_space, vmem, vmem, vmem, vmem, vmem, vmem],
        scratch_shapes=[
            pltpu.VMEM((parts * rows, width), jnp.bfloat16),
            pltpu.VMEM((parts * rows, width), jnp.bfloat16),
            pltpu.VMEM((dps * parts * own, both), jnp.bfloat16),
            pltpu.VMEM((dps, tall, lanes), jnp.bfloat16),
            dma((parts,)), dma((parts,)),
            dma((8, parts + 1)), dma((8, parts + 1)),
            dma((parts,)), dma((parts,)),
            dma((2, parts, 4)), dma((2, parts, 4)),
            dma((6,)),
        ],
        compiler_params=pltpu.CompilerParams(
            collective_id=1, has_side_effects=True, vmem_limit_bytes=56 * 1024 * 1024
        ),
        cost_estimate=pl.CostEstimate(
            flops=2 * parts * rows * width * both, bytes_accessed=40 * 1024 * 1024, transcendentals=0
        ),
    )(tokens, spread, extra, gain)


def line_sums(parts, rows, terms, came, send, recv):
    d, s = lax.axis_index("dp"), lax.axis_index("seq")
    chunk = rows // 4

    def own_rows(part, c):
        return pl.ds(pl.multiple_of(part * rows + c * chunk, chunk), chunk)

    def slot(way, left, part, c):
        at = parts if way == -1 and left == 0 else part
        return came.at[at, pl.ds(c * chunk, chunk), :]

    def copy_of(way, steps, c):
        side = 0 if way == 1 else 1
        part = s + way * steps
        return pltpu.make_async_remote_copy(
            src_ref=terms.at[own_rows(part, c), :], dst_ref=slot(way, steps - 1, part, c),
            send_sem=send.at[side, steps, c], recv_sem=recv.at[side, steps - 1, c],
            device_id=(d, s + way), device_id_type=MESH,
        )

    def valid(way, steps):
        return s + steps < parts if way == 1 else s >= steps

    def upstream(way):
        return s >= 1 if way == 1 else s + 1 < parts

    def taken(way, left, c):
        side = 0 if way == 1 else 1
        place = slot(way, left, s + way * left, c)
        pltpu.make_async_remote_copy(
            src_ref=place, dst_ref=place, send_sem=send.at[side, left, c], recv_sem=recv.at[side, left, c],
            device_id=(d, s), device_id_type=MESH,
        ).wait_recv()

    def pass_on(steps, c):
        for way in (1, -1):
            @pl.when(valid(way, steps))
            def _():
                if steps < parts - 1:
                    @pl.when(upstream(way))
                    def _():
                        taken(way, steps, c)
                        mine = own_rows(s + way * steps, c)
                        more = came[s + way * steps, c * chunk : (c + 1) * chunk, :]
                        terms[mine, :] = (terms[mine, :].astype(jnp.float32) + more.astype(jnp.float32)).astype(jnp.bfloat16)

                copy_of(way, steps, c).start()

    def total(c):
        for way in (1, -1):
            @pl.when(upstream(way))
            def _():
                taken(way, 0, c)

        at = pl.ds(c * chunk, chunk)
        low = jnp.where(upstream(1), came[s, at, :].astype(jnp.float32), 0.0)
        high = jnp.where(upstream(-1), came[parts, at, :].astype(jnp.float32), 0.0)
        return terms[own_rows(s, c), :].astype(jnp.float32) + low + high

    def sent():
        for steps in range(1, parts):
            for c in range(4):
                for way in (1, -1):
                    @pl.when(valid(way, steps))
                    def _():
                        copy_of(way, steps, c).wait_send()

    return pass_on, total, sent


def end_body(
    parts, block,
    dmixed_hbm, normed_hbm, weight_hbm, tokens_hbm, cot_hbm, gain_ref, shard_hbm, small_hbm,
    input_grad_ref, in_grad_ref, gain_grad_ref, small_grad_ref,
    dn, dn_recv, sib_send, sib_recv, q_send, q_recv, total, z_send, z_recv,
    small_sib_send, small_sib_recv, small_q_send, small_q_recv,
    line_send, line_recv, pair_send, pair_recv, cross_send, cross_recv, near_send, near_recv,
    dmixed_ref, normed_ref, weight_ref, tokens_ref, cot_ref, shard_ref, small_ref, load_sem,
):
    d, s = lax.axis_index("dp"), lax.axis_index("seq")
    sib, xm, ym = plane_mates(d)
    diag = xm + ym - d
    own, both = shard_ref.shape[0], dmixed_ref.shape[1]
    rows, width = tokens_ref.shape
    chunk = rows // 4
    tall = parts * own
    tile = min(512, both)

    loads = [
        pltpu.make_async_copy(src, dst, load_sem.at[i])
        for i, (src, dst) in enumerate(
            (
                (dmixed_hbm, dmixed_ref), (weight_hbm, weight_ref), (normed_hbm, normed_ref), (small_hbm, small_ref),
                (tokens_hbm, tokens_ref), (cot_hbm, cot_ref), (shard_hbm, shard_ref),
            )
        )
    ]
    for load in loads[:2]:
        load.start()
    barrier = pltpu.get_barrier_semaphore()
    for mate in (sib, xm, ym, diag):
        pl.semaphore_signal(barrier, inc=1, device_id=(mate, s), device_id_type=MESH)
    for k in range(1, parts):
        pl.semaphore_signal(barrier, inc=1, device_id=(d, lax.rem(s + k, parts)), device_id_type=MESH)
    pl.semaphore_wait(barrier, 4 + parts - 1)

    def remote(src, dst, send, recv, to):
        return pltpu.make_async_remote_copy(
            src_ref=src, dst_ref=dst, send_sem=send, recv_sem=recv, device_id=to, device_id_type=MESH
        )

    pass_line, line_total, line_sent = line_sums(parts, rows, dn, dn_recv, line_send, line_recv)

    def dn_part(part):
        at = pl.ds(pl.multiple_of(part * rows, rows), rows)

        def columns(n, carry):
            cols = pl.ds(pl.multiple_of(n * tile, tile), tile)
            dn[at, cols] = lax.dot_general(
                dmixed_ref[at, :], weight_ref[cols, :], (((1,), (1,)), ((), ())), preferred_element_type=jnp.float32
            ).astype(jnp.bfloat16)
            return carry

        lax.fori_loop(0, width // tile, columns, 0)

    far = (parts - 1) * (1 - s // 2)
    next_far = lax.rem(2 - 2 * s + 10, 5)
    nearer = 1 + lax.rem(s, 2)
    for load in loads[:2]:
        load.wait()
    for load in loads[2:]:
        load.start()
    dn_part(far)
    for c in range(4):
        pass_line(parts - 1, c)
    for load in loads[2:4]:
        load.wait()

    def grad_block(owner, store):
        left = pl.ds(pl.multiple_of(owner * tall, tall), tall)

        def columns(n, carry):
            cols = pl.ds(pl.multiple_of(n * tile, tile), tile)
            store(
                cols,
                lax.dot_general(
                    normed_ref[:, left], dmixed_ref[:, cols], (((0,), (0,)), ((), ())),
                    preferred_element_type=jnp.float32,
                ),
            )
            return carry

        lax.fori_loop(0, both // tile, columns, 0)

    mates = (diag, xm, ym, d)
    sib_of = lambda mate: mate + sib - d

    def pair_copy(r):
        return remote(sib_send.at[r], sib_recv.at[r], pair_send.at[0, r], pair_recv.at[0, r], (sib, s))

    def pair_copy_small(r):
        return remote(small_sib_send.at[r], small_sib_recv.at[r], pair_send.at[1, r], pair_recv.at[1, r], (sib, s))

    def cross_copy(r):
        return remote(q_send.at[r], q_recv.at[r], cross_send.at[0, r], cross_recv.at[0, r], (mates[r], s))

    def cross_copy_small(r):
        return remote(small_q_send.at[r], small_q_recv.at[r], cross_send.at[1, r], cross_recv.at[1, r], (mates[r], s))

    for r in range(4):
        def store_pair(cols, value):
            sib_send[r, :, cols] = value.astype(jnp.bfloat16)

        grad_block(sib_of(mates[r]), store_pair)
        pair_copy(r).start()
        small_sib_send[r] = small_ref[sib_of(mates[r])].astype(jnp.bfloat16)
        pair_copy_small(r).start()
    dn_part(next_far)
    for r in range(4):
        pair_copy(r).wait_recv()
        pair_copy_small(r).wait_recv()
        both_small = small_ref[mates[r]] + small_sib_recv[r].astype(jnp.float32)
        if r < 3:
            def store_cross(cols, value):
                q_send[r, :, cols] = (value + sib_recv[r, :, cols].astype(jnp.float32)).astype(jnp.bfloat16)

            grad_block(mates[r], store_cross)
            cross_copy(r).start()
            small_q_send[r] = both_small.astype(jnp.bfloat16)
            cross_copy_small(r).start()
        else:
            def store_total(cols, value):
                total[:, cols] = value + sib_recv[r, :, cols].astype(jnp.float32)

            grad_block(mates[r], store_total)
            small_grad_ref[...] = both_small
        pass_line(parts - 2, r)
        if r == 2:
            dn_part(nearer)
            dn_part(s)
    for c in range(4):
        pass_line(parts - 3, c)
    for load in loads[4:]:
        load.wait()

    for r in range(3):
        cross_copy(r).wait_recv()
        cross_copy_small(r).wait_recv()
        total[...] += q_recv[r].astype(jnp.float32)
        small_grad_ref[...] += small_q_recv[r].astype(jnp.float32)
    z_send[...] = total[...].astype(jnp.bfloat16)

    def near_copy(k):
        to = lax.rem(s + k, parts)
        return remote(
            z_send.at[pl.ds(pl.multiple_of(to * own, own), own), :], z_recv.at[k], near_send.at[k], near_recv.at[k], (d, to)
        )

    for k in range(1, parts):
        near_copy(k).start()

    for c in range(4):
        at = pl.ds(c * chunk, chunk)
        v = line_total(c) * gain_ref[...]
        flat = tokens_ref[at, :].astype(jnp.float32)
        scale = lax.rsqrt(jnp.mean(flat * flat, axis=-1, keepdims=True) + 1e-05)
        du = scale * v - flat * (scale * scale * scale) * jnp.mean(flat * v, axis=-1, keepdims=True)
        input_grad_ref[at, :] = (cot_ref[at, :].astype(jnp.float32) + du).astype(jnp.bfloat16)

    channel_blocks = both // block
    gain_total = jnp.zeros((own, block), jnp.float32)
    for k in range(parts):
        source = lax.rem(s - k + parts, parts)
        if k > 0:
            near_copy(k).wait_recv()
        for j in range(channel_blocks):
            cols = slice(j * block, (j + 1) * block)
            if k == 0:
                piece = z_send[pl.ds(pl.multiple_of(s * own, own), own), cols]
            else:
                piece = z_recv[k, :, cols]
            to = pl.ds(pl.multiple_of((j * parts + source) * block, block), block)
            in_grad_ref[:, to] = piece
            gain_total = gain_total + piece.astype(jnp.float32) * shard_ref[:, to].astype(jnp.float32)
    gain_grad_ref[...] = jnp.broadcast_to(jnp.sum(gain_total, axis=1, keepdims=True), gain_grad_ref.shape)

    for r in range(4):
        pair_copy(r).wait_send()
        pair_copy_small(r).wait_send()
    for r in range(3):
        cross_copy(r).wait_send()
        cross_copy_small(r).wait_send()
    for k in range(1, parts):
        near_copy(k).wait_send()
    line_sent()


def end(dmixed, normed, weight, tokens, cotangent, gain, shard, small, parts, block):
    both = dmixed.shape[1]
    rows, width = tokens.shape
    own = shard.shape[0]
    dps, _, lanes = small.shape
    tall = parts * own
    vmem = pl.BlockSpec(memory_space=pltpu.VMEM)
    anywhere = pl.BlockSpec(memory_space=pl.ANY)
    dma = pltpu.SemaphoreType.DMA
    low = jnp.bfloat16
    return pl.pallas_call(
        lambda *refs: end_body(parts, block, *refs),
        out_shape=[
            jax.ShapeDtypeStruct((rows, width), low),
            jax.ShapeDtypeStruct((own, parts * both), low),
            jax.ShapeDtypeStruct((own, LANE), jnp.float32),
            jax.ShapeDtypeStruct((block, lanes), jnp.float32),
        ],
        in_specs=[anywhere] * 5 + [vmem] + [anywhere] * 2,
        out_specs=[vmem] * 4,
        scratch_shapes=[
            pltpu.VMEM((parts * rows, width), low),
            pltpu.VMEM((parts + 1, rows, width), low),
            pltpu.VMEM((4, tall, both), low), pltpu.VMEM((4, tall, both), low),
            pltpu.VMEM((3, tall, both), low), pltpu.VMEM((3, tall, both), low),
            pltpu.VMEM((tall, both), jnp.float32),
            pltpu.VMEM((tall, both), low), pltpu.VMEM((parts, own, both), low),
            pltpu.VMEM((4, block, lanes), low), pltpu.VMEM((4, block, lanes), low),
            pltpu.VMEM((3, block, lanes), low), pltpu.VMEM((3, block, lanes), low),
            dma((2, parts, 4)), dma((2, parts, 4)),
            dma((2, 4)), dma((2, 4)), dma((2, 3)), dma((2, 3)), dma((parts,)), dma((parts,)),
            *[pltpu.VMEM(a.shape, a.dtype) for a in (dmixed, normed, weight, tokens, cotangent, shard, small)], dma((7,)),
        ],
        compiler_params=pltpu.CompilerParams(
            collective_id=2, has_side_effects=True, vmem_limit_bytes=60 * 1024 * 1024
        ),
        cost_estimate=pl.CostEstimate(
            flops=4 * parts * rows * width * both, bytes_accessed=30 * 1024 * 1024, transcendentals=0
        ),
    )(dmixed, normed, weight, tokens, cotangent, gain, shard, small)


def linked_forward_body(
    states, parts, dps, taps,
    conv_in_ref, gate_ref, select_ref, vector_ref, weight_ref, out_shard, cot_shard,
    mixed_ref, history_ref, final_ref, values_out, low_ref, kq_ref, dgated_out, result_out, out_part_ref,
    state_ref, key_ref, query_ref, rate_ref, input_ref, out_ref, row_ref, pick_ref, half_ref,
    part_low, part_kq, came_low, came_kq, sum_low, sum_kq,
    rs_send, rs_recv, ag_send, ag_recv, out_send, out_recv, line_send, line_recv, local_sem,
    out_all, cot_all, gated_all, out_total, values_ref, dgated_ref, result_ref, leave_sem,
):
    d, s = lax.axis_index("dp"), lax.axis_index("seq")
    step = pl.program_id(0)
    length, channels = values_ref.shape
    rows = gate_ref.shape[0]
    span = length // parts
    block = out_shard.shape[0]
    chunk = span // 4
    packed = LANE // (2 * states)
    conv_w_ref, conv_b_ref = vector_ref, vector_ref[taps : taps + 1, :]
    bias_ref, skip_ref = vector_ref[taps + 1 : taps + 2, :], vector_ref[taps + 2 : taps + 3, :]
    short = span // packed

    def remote(src, dst, send, recv, to):
        return pltpu.make_async_remote_copy(
            src_ref=src, dst_ref=dst, send_sem=send, recv_sem=recv, device_id=to, device_id_type=MESH
        )

    def out_rows(owner):
        return out_all.at[pl.ds(pl.multiple_of(owner * block, block), block), :]

    out_copies = []
    for k in range(1, dps):
        out_copies.append(
            remote(out_shard, out_rows(d), out_send.at[k - 1], out_recv.at[k - 1], (lax.rem(d + k, dps), s))
        )

    def cot_rows(part, c):
        return cot_all.at[pl.ds(pl.multiple_of(part * span + c * chunk, chunk), chunk), :]

    def cot_copy(way, distance, c):
        part = s - way * (distance - 1)
        src = cot_shard.at[pl.ds(c * chunk, chunk), :] if distance == 1 else cot_rows(part, c)
        side = 0 if way == 1 else 1
        return remote(
            src, cot_rows(part, c), line_send.at[side, distance, c], line_recv.at[side, distance, c], (d, s + way)
        )

    def can_send(way, distance):
        reach = s + 1 < parts if way == 1 else s >= 1
        came = s - (distance - 1) >= 0 if way == 1 else s + (distance - 1) < parts
        return jnp.logical_and(reach, came)

    def send_cot(distance, c):
        for way in (1, -1):
            @pl.when(can_send(way, distance))
            def _():
                cot_copy(way, distance, c).start()

    def sent_cot(distance, c):
        for way in (1, -1):
            @pl.when(can_send(way, distance))
            def _():
                cot_copy(way, distance, c).wait_send()

    def take_cot(distance, c):
        for way in (1, -1):
            @pl.when(s >= distance if way == 1 else s + distance < parts)
            def _():
                part = s - way * distance
                side = 0 if way == 1 else 1
                remote(
                    cot_rows(part, c), cot_rows(part, c), line_send.at[side, distance, c],
                    line_recv.at[side, distance, c], (d, s),
                ).wait_recv()

    def own_copies():
        return (
            pltpu.make_async_copy(out_shard, out_rows(d), local_sem.at[0]),
            pltpu.make_async_copy(
                cot_shard, cot_all.at[pl.ds(pl.multiple_of(s * span, span), span), :], local_sem.at[1]
            ),
        )

    @pl.when(step == 0)
    def _():
        barrier = pltpu.get_barrier_semaphore()
        for k in range(1, parts):
            pl.semaphore_signal(barrier, inc=1, device_id=(d, lax.rem(s + k, parts)), device_id_type=MESH)
        for k in range(1, dps):
            pl.semaphore_signal(barrier, inc=1, device_id=(lax.rem(d + k, dps), s), device_id_type=MESH)
        pl.semaphore_wait(barrier, parts + dps - 2)
        state_ref[...] = jnp.zeros_like(state_ref)
        for copy in out_copies:
            copy.start()
        for copy in own_copies():
            copy.start()
        for c in range(2):
            send_cot(1, c)

    def rs_copies(k):
        at = lax.rem(s + k, parts)
        return (
            remote(part_low.at[at], came_low.at[k - 1], rs_send.at[0, k - 1], rs_recv.at[0, k - 1], (d, at)),
            remote(part_kq.at[at], came_kq.at[k - 1], rs_send.at[1, k - 1], rs_recv.at[1, k - 1], (d, at)),
        )

    def ag_copies(k):
        to = lax.rem(s + k, parts)
        return (
            remote(sum_low.at[s], sum_low.at[s], ag_send.at[0, k - 1], ag_recv.at[0, k - 1], (d, to)),
            remote(sum_kq.at[s], sum_kq.at[s], ag_send.at[1, k - 1], ag_recv.at[1, k - 1], (d, to)),
        )

    def ag_taken(k, part):
        return (
            remote(sum_low.at[part], sum_low.at[part], ag_send.at[0, k - 1], ag_recv.at[0, k - 1], (d, s)),
            remote(sum_kq.at[part], sum_kq.at[part], ag_send.at[1, k - 1], ag_recv.at[1, k - 1], (d, s)),
        )

    def convolve(part):
        start = pl.multiple_of(part * span, span)
        before = pl.multiple_of(jnp.maximum(start - 16, 0), 16)
        wide = min(256, channels)
        for left in range(0, channels, wide):
            cols = slice(left, left + wide)
            head = conv_in_ref[pl.ds(before, 16), cols].astype(jnp.float32)
            head = jnp.where(part == 0, 0.0, head)
            body = jnp.concatenate([head, conv_in_ref[pl.ds(start, span), cols].astype(jnp.float32)], axis=0)
            total = conv_b_ref[:, cols]
            for tap in range(taps):
                by = taps - 1 - tap
                total = total + body[16 - by : 16 - by + span] * conv_w_ref[tap : tap + 1, cols]
            values_ref[pl.ds(start, span), cols] = (total * sigmoid(total)).astype(jnp.bfloat16)
        projected = jnp.dot(values_ref[pl.ds(start, span), :], select_ref[...], preferred_element_type=jnp.float32)
        part_low[part] = projected[:, :LANE].astype(jnp.bfloat16)
        pack = projected[:short, LANE:]
        for g in range(1, packed):
            pack = pack + pltpu.roll(projected[g * short : (g + 1) * short, LANE:], g * 2 * states, 1)
        part_kq[part] = pack

    @pl.when(step < parts - 1)
    def _():
        convolve(lax.rem(s + 1 + step, parts))

    for k in range(1, parts):
        @pl.when(step == k - 1)
        def _():
            for copy in rs_copies(k):
                copy.start()

    @pl.when(step == parts - 1)
    def _():
        convolve(s)
        low = part_low[s].astype(jnp.float32)
        kq = part_kq[s]
        for k in range(1, parts):
            for copy in rs_copies(k):
                copy.wait_recv()
            low = low + came_low[k - 1].astype(jnp.float32)
            kq = kq + came_kq[k - 1]
        sum_low[s] = low.astype(jnp.bfloat16)
        sum_kq[s] = kq
        for k in range(1, parts):
            for copy in ag_copies(k):
                copy.start()
        for c in range(2, 4):
            send_cot(1, c)

    per_part = span // rows
    at_block = step - parts

    def unpack(part):
        start = pl.multiple_of(part * span, span)
        low_ref[pl.ds(start, span), :] = sum_low[part]
        pack = sum_kq[part]
        lane = lax.broadcasted_iota(jnp.int32, pack.shape, 1)
        for g in range(packed):
            turned = pack if g == 0 else pltpu.roll(pack, LANE - g * 2 * states, 1)
            kq_ref[pl.ds(pl.multiple_of(start + g * short, short), short), :] = jnp.where(lane < 2 * states, turned, 0.0)

    for part in range(parts):
        @pl.when(at_block == part * per_part)
        def _():
            for k in range(1, parts):
                @pl.when(lax.rem(s - k + parts, parts) == part)
                def _():
                    for copy in ag_taken(k, part):
                        copy.wait_recv()

            unpack(part)

    plan = {0: ((1, 0), (1, 1)), 1: ((1, 2), (1, 3)), 2: ((2, 0), (2, 1)), 4: ((2, 2), (2, 3))}
    for at, moves in plan.items():
        @pl.when(at_block == at)
        def _():
            for distance, c in moves:
                take_cot(distance, c)
                send_cot(distance + 1, c)

    @pl.when(jnp.logical_and(at_block >= 0, at_block < length // rows))
    def _():
        here = pl.ds(pl.multiple_of(at_block * rows, rows), rows)
        kq = kq_ref[here, :]
        values = values_ref[here, :].astype(jnp.float32)
        beta, inverse = step_sizes(low_ref[here, :], kq, weight_ref, bias_ref, states)
        rates = beta * inverse
        rate_ref[...] = by_eights(rates)
        input_ref[...] = by_eights(rates * values)
        spread_columns(kq, row_ref, pick_ref, key_ref, query_ref, states)
        forward_rows(states, rows, channels, history_ref, state_ref, key_ref, query_ref, rate_ref, input_ref, out_ref, half_ref)
        mixed = as_rows(out_ref[...]) + skip_ref[...] * values
        gate = gate_ref[...]
        mixed_ref[...] = mixed
        gated_all[here, :] = (mixed * gate * sigmoid(gate)).astype(jnp.bfloat16)

    width = cot_all.shape[1]
    tile = min(512, width)

    def leaving(part):
        here = pl.ds(pl.multiple_of(part * span, span), span)
        return (
            pltpu.make_async_copy(dgated_ref.at[here, :], dgated_out.at[here, :], leave_sem.at[part, 0]),
            pltpu.make_async_copy(result_ref.at[here, :], result_out.at[here, :], leave_sem.at[part, 1]),
        )

    values_copy = pltpu.make_async_copy(values_ref, values_out, local_sem.at[2])

    @pl.when(step == parts)
    def _():
        values_copy.start()

    def products(part):
        here = pl.ds(pl.multiple_of(part * span, span), span)

        def across(n, carry):
            cols = pl.ds(pl.multiple_of(n * tile, tile), tile)
            result_ref[here, cols] = jnp.dot(
                gated_all[here, :], out_all[:, cols], preferred_element_type=jnp.float32
            ).astype(jnp.bfloat16)
            out_total[:, cols] += lax.dot_general(
                gated_all[here, :], cot_all[here, cols], (((0,), (0,)), ((), ())), preferred_element_type=jnp.float32
            )
            return carry

        lax.fori_loop(0, width // tile, across, 0)
        deep = min(512, channels)

        def along(n, carry):
            cols = pl.ds(pl.multiple_of(n * deep, deep), deep)
            dgated_ref[here, cols] = lax.dot_general(
                cot_all[here, :], out_all[cols, :], (((1,), (1,)), ((), ())), preferred_element_type=jnp.float32
            )
            return carry

        lax.fori_loop(0, channels // deep, along, 0)
        for copy in leaving(part):
            copy.start()

    def products_at(low, high):
        def each(part, carry):
            away = jnp.abs(part - s)

            @pl.when(jnp.logical_and(away >= low, away <= high))
            def _():
                products(part)

            return carry

        lax.fori_loop(0, parts, each, 0)

    @pl.when(step == pl.num_programs(0) - 1)
    def _():
        final_ref[...] = state_ref[...]
        out_total[...] = jnp.zeros_like(out_total)
        for copy in own_copies():
            copy.wait()
        for copy in out_copies:
            copy.wait_recv()
        products_at(0, parts - 2)
        for c in range(4):
            take_cot(parts - 1, c)
        products_at(parts - 1, parts - 1)
        out_part_ref[...] = out_total[...].astype(jnp.bfloat16)
        values_copy.wait()
        for part in range(parts):
            for copy in leaving(part):
                copy.wait()
        for copy in out_copies:
            copy.wait_send()
        for distance in range(1, parts):
            for c in range(4):
                sent_cot(distance, c)
        for k in range(1, parts):
            for copy in rs_copies(k) + ag_copies(k):
                copy.wait_send()


def linked_forward(conv_in, gate, select, vectors, weight, out_shard, cot_shard, parts, dps, taps, states):
    length, channels = conv_in.shape
    block, width = out_shard.shape
    span = length // parts
    rows = min(128, span)
    blocks = length // rows
    short = span // (LANE // (2 * states))
    at = lambda i: jnp.clip(i - parts, 0, blocks - 1)
    by_row = lambda size: pl.BlockSpec((rows, size), lambda i: (at(i), 0))
    whole = lambda a: pl.BlockSpec(a.shape, lambda i: (0, 0))
    kept = lambda *shape: pl.BlockSpec(shape, lambda i: (0, 0))
    anywhere = pl.BlockSpec(memory_space=pl.ANY)
    dma = pltpu.SemaphoreType.DMA
    f32, low = jnp.float32, jnp.bfloat16
    eights = pltpu.VMEM((rows // 8, 8, channels), f32)
    return pl.pallas_call(
        lambda *refs: linked_forward_body(states, parts, dps, taps, *refs),
        grid=(parts + blocks + 1,),
        in_specs=[
            whole(conv_in), by_row(channels), whole(select), whole(vectors), whole(weight), anywhere, anywhere,
        ],
        out_specs=[
            by_row(channels), pl.BlockSpec((rows * states, channels), lambda i: (at(i), 0)),
            kept(states, channels), anywhere, kept(length, LANE), kept(length, LANE),
            anywhere, anywhere, kept(dps * block, width),
        ],
        out_shape=[
            jax.ShapeDtypeStruct((length, channels), f32),
            jax.ShapeDtypeStruct((length * states, channels), low),
            jax.ShapeDtypeStruct((states, channels), f32),
            jax.ShapeDtypeStruct((length, channels), low),
            jax.ShapeDtypeStruct((length, LANE), low),
            jax.ShapeDtypeStruct((length, LANE), f32),
            jax.ShapeDtypeStruct((length, channels), f32),
            jax.ShapeDtypeStruct((length, width), low),
            jax.ShapeDtypeStruct((dps * block, width), low),
        ],
        scratch_shapes=[
            pltpu.VMEM((states, channels), f32),
            pltpu.VMEM((rows * states, LANE), f32), pltpu.VMEM((rows * states, LANE), f32),
            eights, eights, eights, pltpu.VMEM((rows // 8, 8, LANE), f32),
            pltpu.VMEM((rows * states, LANE), low), pltpu.VMEM((channels // LANE * 64, LANE), f32),
            pltpu.VMEM((parts, span, LANE), low), pltpu.VMEM((parts, short, LANE), f32),
            pltpu.VMEM((parts - 1, span, LANE), low), pltpu.VMEM((parts - 1, short, LANE), f32),
            pltpu.VMEM((parts, span, LANE), low), pltpu.VMEM((parts, short, LANE), f32),
            dma((2, parts - 1)), dma((2, parts - 1)), dma((2, parts - 1)), dma((2, parts - 1)),
            dma((dps - 1,)), dma((dps - 1,)), dma((2, parts, 4)), dma((2, parts, 4)), dma((3,)),
            pltpu.VMEM((dps * block, width), low), pltpu.VMEM((length, width), low), pltpu.VMEM((length, channels), low),
            pltpu.VMEM((dps * block, width), f32), pltpu.VMEM((length, channels), low),
            pltpu.VMEM((length, channels), f32), pltpu.VMEM((length, width), low), dma((parts, 2)),
        ],
        compiler_params=pltpu.CompilerParams(
            collective_id=4, has_side_effects=True, vmem_limit_bytes=60 * 1024 * 1024
        ),
        cost_estimate=pl.CostEstimate(
            flops=14 * length * states * channels, bytes_accessed=2 * length * states * channels, transcendentals=0
        ),
    )(conv_in, gate, select, vectors, weight, out_shard, cot_shard)


def linked_backward_body(
    states, parts, dps, taps,
    low_ref, kq_ref, gate_ref, mixed_ref, dgated_ref, history_ref, final_ref, weight_ref,
    values_ref, conv_in_ref, select_ref, given_ref, tokens_ref, part_hbm, out_ref,
    dmixed_out, small_ref, result_ref, out_grad_ref,
    grad_ref, state_ref, key_ref, query_ref, rate_ref, do_ref, values32_ref, fed_ref, kept_ref, part_key_ref,
    part_query_ref, row_ref, placed_ref, pick_ref, wide_ref, half_ref,
    dvalues_ref, dproj_ref, next_ref, vector_ref, part_low, part_kq, came_low, came_kq, sum_low, sum_kq,
    rs_send, rs_recv, ag_send, ag_recv, result_came, line_send, line_recv, out_send, out_recv,
    out_came, out_here, local_sem, dmixed_ref, part_ref, leave_sem,
):
    d, s = lax.axis_index("dp"), lax.axis_index("seq")
    step = pl.program_id(0)
    rows, channels = gate_ref.shape
    length = values_ref.shape[0]
    blocks = length // rows
    span = length // parts
    per_part = span // rows
    packed = LANE // (2 * states)
    short = span // packed
    sel = select_ref.shape[1]
    conv_w_ref, conv_b_ref = given_ref, given_ref[taps : taps + 1, :]
    bias_ref, skip_ref = given_ref[taps + 1 : taps + 2, :], given_ref[taps + 2 : taps + 3, :]

    def remote(src, dst, send, recv, to):
        return pltpu.make_async_remote_copy(
            src_ref=src, dst_ref=dst, send_sem=send, recv_sem=recv, device_id=to, device_id_type=MESH
        )

    copies = []
    for k in range(1, dps):
        to = lax.rem(d + k, dps)
        copies.append(remote(out_ref.at[to], out_came.at[k - 1], out_send.at[k - 1], out_recv.at[k - 1], (to, s)))
    out_copy = pltpu.make_async_copy(out_ref.at[d], out_here, local_sem.at[0])
    part_copy = pltpu.make_async_copy(part_hbm, part_ref, local_sem.at[1])
    pass_line, line_total, line_sent = line_sums(parts, span, part_ref, result_came, line_send, line_recv)

    @pl.when(step == 0)
    def _():
        part_copy.start()
        barrier = pltpu.get_barrier_semaphore()
        for k in range(1, parts):
            pl.semaphore_signal(barrier, inc=1, device_id=(d, lax.rem(s + k, parts)), device_id_type=MESH)
        for k in range(1, dps):
            pl.semaphore_signal(barrier, inc=1, device_id=(lax.rem(d + k, dps), s), device_id_type=MESH)
        pl.semaphore_wait(barrier, parts + dps - 2)
        grad_ref[...] = jnp.zeros_like(grad_ref)
        state_ref[...] = final_ref[...]
        next_ref[...] = jnp.zeros_like(next_ref)
        vector_ref[...] = jnp.zeros_like(vector_ref)
        small_ref[...] = jnp.zeros_like(small_ref)
        for copy in copies:
            copy.start()
        out_copy.start()
        part_copy.wait()

    def rs_copies(k):
        at = lax.rem(s + k, parts)
        return (
            remote(part_low.at[at], came_low.at[k - 1], rs_send.at[0, k - 1], rs_recv.at[0, k - 1], (d, at)),
            remote(part_kq.at[at], came_kq.at[k - 1], rs_send.at[1, k - 1], rs_recv.at[1, k - 1], (d, at)),
        )

    def ag_copies(k):
        to = lax.rem(s + k, parts)
        return (
            remote(sum_low.at[s], sum_low.at[s], ag_send.at[0, k - 1], ag_recv.at[0, k - 1], (d, to)),
            remote(sum_kq.at[s], sum_kq.at[s], ag_send.at[1, k - 1], ag_recv.at[1, k - 1], (d, to)),
        )

    def ag_taken(k, part):
        return (
            remote(sum_low.at[part], sum_low.at[part], ag_send.at[0, k - 1], ag_recv.at[0, k - 1], (d, s)),
            remote(sum_kq.at[part], sum_kq.at[part], ag_send.at[1, k - 1], ag_recv.at[1, k - 1], (d, s)),
        )

    def add_up():
        low = part_low[s].astype(jnp.float32)
        kq = part_kq[s]
        for k in range(1, parts):
            for copy in rs_copies(k):
                copy.wait_recv()
            low = low + came_low[k - 1].astype(jnp.float32)
            kq = kq + came_kq[k - 1]
        sum_low[s] = low.astype(jnp.bfloat16)
        sum_kq[s] = kq.astype(jnp.bfloat16)
        for k in range(1, parts):
            for copy in ag_copies(k):
                copy.start()

    def leaving(part):
        here = pl.ds(pl.multiple_of(part * span, span), span)
        return pltpu.make_async_copy(dmixed_ref.at[here, :], dmixed_out.at[here, :], leave_sem.at[part])

    def conv_back(part):
        for k in range(1, parts):
            @pl.when(lax.rem(s - k + parts, parts) == part)
            def _():
                for copy in ag_taken(k, part):
                    copy.wait_recv()

        here = pl.ds(pl.multiple_of(part * span, span), span)
        before = pl.multiple_of(jnp.maximum(part * span - 16, 0), 16)
        dproj_ref[:, :LANE] = sum_low[part]
        pack = sum_kq[part].astype(jnp.float32)
        lane = lax.broadcasted_iota(jnp.int32, pack.shape, 1)
        for g in range(packed):
            turned = pack if g == 0 else pltpu.roll(pack, LANE - g * 2 * states, 1)
            dproj_ref[g * short : (g + 1) * short, LANE:] = jnp.where(lane < 2 * states, turned, 0.0).astype(jnp.bfloat16)
        wide = min(256, channels)
        for left in range(0, channels, wide):
            cols = slice(left, left + wide)
            small_ref[cols, :sel] += lax.dot_general(
                values_ref[here, cols], dproj_ref[...], (((0,), (0,)), ((), ())), preferred_element_type=jnp.float32
            )
            head = conv_in_ref[pl.ds(before, 16), cols].astype(jnp.float32)
            head = jnp.where(part == 0, 0.0, head)
            body = jnp.concatenate([head, conv_in_ref[here, cols].astype(jnp.float32)], axis=0)
            total = conv_b_ref[:, cols]
            for tap in range(taps):
                by = taps - 1 - tap
                total = total + body[16 - by : 16 - by + span] * conv_w_ref[tap : tap + 1, cols]
            sg = sigmoid(total)
            dvalues = dvalues_ref[here, cols] + lax.dot_general(
                dproj_ref[...], select_ref[cols, :], (((1,), (1,)), ((), ())), preferred_element_type=jnp.float32
            )
            dconv = dvalues * (sg + total * sg * (1.0 - sg))
            vector_ref[taps : taps + 1, cols] += jnp.sum(dconv, axis=0, keepdims=True)
            after = jnp.concatenate([dconv, next_ref[:, cols]], axis=0)
            dconv_in = jnp.zeros_like(dconv)
            for tap in range(taps):
                by = taps - 1 - tap
                shifted = body[16 - by : 16 - by + span]
                vector_ref[tap : tap + 1, cols] += jnp.sum(dconv * shifted, axis=0, keepdims=True)
                dconv_in = dconv_in + after[by : by + span] * conv_w_ref[tap : tap + 1, cols]
            next_ref[:, cols] = dconv[0:8]
            dmixed_ref[here, cols] = dconv_in.astype(jnp.bfloat16)
        leaving(part).start()

    plan = (
        ((3, 0), (3, 1)), ((3, 2),), ((3, 3), (2, 0)), ((2, 1),), ((2, 2), (2, 3)), ((1, 0),), ((1, 1), (1, 2)), ((1, 3),),
    )
    for at_step, moves in enumerate(plan):
        @pl.when(step == at_step)
        def _():
            for steps, c in moves:
                pass_line(steps, c)

    for part in range(parts):
        ends = (parts - part) * per_part - 1
        sums = min(ends + 3, blocks - 1 if part > 0 else blocks)

        @pl.when(jnp.logical_and(step == sums, s == part))
        def _():
            add_up()

        @pl.when(step == blocks + 1 - part)
        def _():
            conv_back(part)

    @pl.when(step < blocks)
    def _():
        block = blocks - 1 - step
        here = pl.ds(pl.multiple_of(block * rows, rows), rows)
        low, kq = low_ref[...], kq_ref[...]
        beta, inverse = step_sizes(low, kq, weight_ref, bias_ref, states)
        rate_ref[...] = by_eights(beta * inverse)
        values = values_ref[here, :].astype(jnp.float32)
        values32_ref[...] = by_eights(values)
        gate = gate_ref[...]
        dgated = dgated_ref[...].astype(jnp.float32)
        sg = sigmoid(gate)
        do = dgated * (gate * sg)
        do_ref[...] = by_eights(do)
        dmixed_ref[here, channels:] = (dgated * mixed_ref[...] * (sg + gate * sg * (1.0 - sg))).astype(jnp.bfloat16)
        vector_ref[taps + 2 : taps + 3, :] += jnp.sum(do * values, axis=0, keepdims=True)
        spread_columns(kq, row_ref, pick_ref, key_ref, query_ref, states)
        backward_rows(
            states, rows, channels, history_ref, grad_ref, state_ref, key_ref, query_ref, rate_ref, do_ref, values32_ref,
            fed_ref, kept_ref, part_key_ref, part_query_ref, half_ref,
        )
        fed = as_rows(fed_ref[...])
        dvalues_ref[here, :] = fed + skip_ref[...] * as_rows(do_ref[...])
        scaled = as_rows(values32_ref[...]) * fed - as_rows(kept_ref[...])
        beta, inverse = step_sizes(low, kq, weight_ref, bias_ref, states)
        dpre = scaled * (1.0 - beta) * inverse
        vector_ref[taps + 1 : taps + 2, :] += jnp.sum(dpre, axis=0, keepdims=True)
        dpre_low = dpre.astype(jnp.bfloat16)
        small_ref[:, sel : sel + LANE] += lax.dot_general(
            dpre_low, low, (((0,), (0,)), ((), ())), preferred_element_type=jnp.float32
        )
        through = -2.0 * jnp.sum(scaled * beta * inverse, axis=1, keepdims=True)
        gather_columns(part_key_ref, part_query_ref, wide_ref, placed_ref, rows, states)
        lanes = lax.broadcasted_iota(jnp.int32, kq.shape, 1)
        dkq = as_rows(placed_ref[...]) + jnp.where(lanes < states, kq * through, 0.0)
        part = block // per_part
        within = lax.rem(block, per_part)
        part_low[part, pl.ds(pl.multiple_of(within * rows, rows), rows), :] = jnp.dot(
            dpre_low, weight_ref[...], preferred_element_type=jnp.float32
        ).astype(jnp.bfloat16)
        for g in range(packed):
            first = g * short - within * rows

            @pl.when(jnp.logical_and(first >= 0, first < rows))
            def _():
                for w in range(per_part):
                    if w * rows <= g * short < (w + 1) * rows:
                        lo = g * short - w * rows
                        piece = dkq[lo : lo + short]
                        piece = piece if g == 0 else pltpu.roll(piece, g * 2 * states, 1)
                        if g == (per_part - 1) * rows // short:
                            part_kq[part] = piece
                        else:
                            part_kq[part] += piece

        @pl.when(within == 0)
        def _():
            for k in range(1, parts):
                @pl.when(lax.rem(s + k, parts) == part)
                def _():
                    for copy in rs_copies(k):
                        copy.start()

    @pl.when(step == pl.num_programs(0) - 1)
    def _():
        small_ref[:, sel + LANE :] = jnp.transpose(vector_ref[...])
        chunk = span // 4
        for c in range(4):
            at = pl.ds(c * chunk, chunk)
            result_ref[at, :] = (tokens_ref[at, :].astype(jnp.float32) + line_total(c)).astype(jnp.bfloat16)
        line_sent()
        for part in range(parts):
            leaving(part).wait()
        out_copy.wait()
        total = out_here[...].astype(jnp.float32)
        for k in range(1, dps):
            copies[k - 1].wait_recv()
            total = total + out_came[k - 1].astype(jnp.float32)
        out_grad_ref[...] = total
        for copy in copies:
            copy.wait_send()
        for k in range(1, parts):
            for copy in rs_copies(k) + ag_copies(k):
                copy.wait_send()


def linked_backward(
    low, kq, gate, mixed, dgated, history, final, weight, values, conv_in, select, vectors, tokens, result_part, out_part,
    parts, taps, states,
):
    length, channels = values.shape
    dps = out_part.shape[0]
    width = tokens.shape[1]
    sel = select.shape[1]
    span = length // parts
    rows = min(128, span)
    blocks = length // rows
    short = span // (LANE // (2 * states))
    at = lambda i: jnp.maximum(blocks - 1 - i, 0)
    by_row = lambda size: pl.BlockSpec((rows, size), lambda i: (at(i), 0))
    whole = lambda a: pl.BlockSpec(a.shape, lambda i: (0, 0))
    kept = lambda *shape: pl.BlockSpec(shape, lambda i: (0, 0))
    anywhere = pl.BlockSpec(memory_space=pl.ANY)
    dma = pltpu.SemaphoreType.DMA
    f32, bf16 = jnp.float32, jnp.bfloat16
    wide = pltpu.VMEM((rows // 8, 8, channels), f32)
    eights = pltpu.VMEM((rows // 8, 8, LANE), f32)
    spread = pltpu.VMEM((rows * states, LANE), f32)
    return pl.pallas_call(
        lambda *refs: linked_backward_body(states, parts, dps, taps, *refs),
        grid=(blocks + 2,),
        in_specs=[
            by_row(LANE), by_row(LANE), by_row(channels), by_row(channels), by_row(channels),
            pl.BlockSpec((rows * states, channels), lambda i: (at(i), 0)),
            whole(final), whole(weight), whole(values), whole(conv_in), whole(select), whole(vectors), whole(tokens),
            anywhere, anywhere,
        ],
        out_specs=[anywhere, kept(channels, sel + 2 * LANE), kept(span, width), kept(*out_part.shape[1:])],
        out_shape=[
            jax.ShapeDtypeStruct((length, 2 * channels), bf16),
            jax.ShapeDtypeStruct((channels, sel + 2 * LANE), f32),
            jax.ShapeDtypeStruct((span, width), bf16),
            jax.ShapeDtypeStruct(out_part.shape[1:], f32),
        ],
        scratch_shapes=[
            pltpu.VMEM((states, channels), f32), pltpu.VMEM((states, channels), f32),
            spread, spread, wide, wide, wide, wide, wide, spread, spread, eights, eights,
            pltpu.VMEM((rows * states, LANE), bf16), pltpu.VMEM((rows * states, 2 * LANE), bf16),
            pltpu.VMEM((2 * channels // LANE * 64, LANE), f32),
            pltpu.VMEM((length, channels), f32), pltpu.VMEM((span, sel), bf16), pltpu.VMEM((8, channels), f32),
            pltpu.VMEM((LANE, channels), f32),
            pltpu.VMEM((parts, span, LANE), bf16), pltpu.VMEM((parts, short, LANE), f32),
            pltpu.VMEM((parts - 1, span, LANE), bf16), pltpu.VMEM((parts - 1, short, LANE), f32),
            pltpu.VMEM((parts, span, LANE), bf16), pltpu.VMEM((parts, short, LANE), bf16),
            dma((2, parts - 1)), dma((2, parts - 1)), dma((2, parts - 1)), dma((2, parts - 1)),
            pltpu.VMEM((parts + 1, span, width), bf16), dma((2, parts, 4)), dma((2, parts, 4)),
            dma((dps - 1,)), dma((dps - 1,)), pltpu.VMEM((dps - 1,) + out_part.shape[1:], bf16),
            pltpu.VMEM(out_part.shape[1:], bf16), dma((2,)), pltpu.VMEM((length, 2 * channels), bf16),
            pltpu.VMEM((length, width), bf16), dma((parts,)),
        ],
        compiler_params=pltpu.CompilerParams(
            collective_id=5, has_side_effects=True, vmem_limit_bytes=60 * 1024 * 1024
        ),
        cost_estimate=pl.CostEstimate(
            flops=30 * length * states * channels, bytes_accessed=2 * length * states * channels, transcendentals=0
        ),
    )(low, kq, gate, mixed, dgated, history, final, weight, values, conv_in, select, vectors, tokens, result_part, out_part)


def contract(left, right, left_dim, right_dim):
    return lax.dot_general(
        left, right, (((left_dim,), (right_dim,)), ((), ())), preferred_element_type=jnp.float32
    )


def gathered(shard, axis):
    return lax.all_gather(shard, axis, axis=0, tiled=True)


def scattered(total, axis):
    return lax.psum_scatter(total, axis, scatter_dimension=0, tiled=True)


def summed_rows(partial, axis):
    size = lax.axis_size(axis)
    parts = partial.astype(jnp.bfloat16).reshape((size, partial.shape[0] // size) + partial.shape[1:])
    parts = lax.all_to_all(parts, axis, 0, 0)
    return jnp.sum(parts.astype(jnp.float32), axis=0)


def later(rows, by):
    if by == 0:
        return rows
    return jnp.pad(rows, ((by, 0), (0, 0)))[: rows.shape[0]]


def sooner(rows, by):
    if by == 0:
        return rows
    return jnp.pad(rows, ((0, by), (0, 0)))[by:]


def local(
    tokens,
    cotangent,
    norm_gain,
    in_weight,
    conv_weight,
    conv_bias,
    select_weight,
    beta_weight,
    beta_bias,
    skip_gain,
    out_weight,
):
    parts, dps = lax.axis_size("seq"), lax.axis_size("dp")
    rows, width = tokens.shape[1:]
    block = conv_weight.shape[0]
    channels = block * dps
    taps = conv_weight.shape[1]
    rank = beta_weight.shape[1]
    states = (select_weight.shape[1] - rank) // 2
    own = in_weight.shape[0]

    flat = tokens.reshape(rows, width).astype(jnp.float32)
    scale = lax.rsqrt(jnp.mean(flat * flat, axis=-1, keepdims=True) + 1e-05)
    spread = in_weight.reshape(own, 2, dps, parts, block).transpose(3, 0, 1, 2, 4).reshape(parts, own, 2 * channels)
    vectors = jnp.concatenate(
        [conv_weight, conv_bias[:, None], beta_bias[:, None], skip_gain[:, None]], axis=1
    )
    wide = -(-select_weight.shape[1] // LANE) * LANE
    small = jnp.concatenate(
        [
            jnp.pad(select_weight, ((0, 0), (0, wide - select_weight.shape[1]))),
            beta_weight,
            jnp.pad(vectors, ((0, 0), (0, LANE - vectors.shape[1]))),
        ],
        axis=1,
    )
    small_slice = (dps, parts, 2 * own, rank) == (8, 4, LANE, LANE)
    if small_slice:
        doubled = jnp.broadcast_to(jnp.tile(norm_gain.reshape(1, own), (1, 2)), (GAIN_ROWS, LANE))
        normed, in_w, conv_in, gate, select_w, beta_w, vectors, gain = start(
            tokens.reshape(rows, width), spread, small, doubled, dps
        )
    else:
        gain = gathered(norm_gain, ("dp", "seq"))
        normed = gathered((flat * scale * gain.astype(jnp.float32)).astype(jnp.bfloat16), "seq")
        in_w = gathered(lax.all_to_all(spread, "seq", 0, 0).reshape(parts * own, 2 * channels), "dp")
        smalls = gathered(small, "dp")
        conv_in = jnp.dot(normed, in_w[:, :channels], preferred_element_type=jnp.float32).astype(jnp.bfloat16)
        gate = jnp.dot(normed, in_w[:, channels:], preferred_element_type=jnp.float32)
    cot_here = cotangent.reshape(rows, width)
    if small_slice:
        mixed, history, final, values, low, kq, dgated, result_part, out_part = linked_forward(
            conv_in, gate, select_w, vectors, beta_w, out_weight, cot_here, parts, dps, taps, states,
        )
    else:
        gain = gain.astype(jnp.float32)
        select_w = smalls[:, : select_weight.shape[1]]
        beta_w = smalls[:, wide : wide + rank]
        vectors = smalls[:, wide + rank :].astype(jnp.float32)
        conv_w, conv_b = vectors[:, :taps], vectors[:, taps]
        beta_b, skip = vectors[:, taps + 1].reshape(1, channels), vectors[:, taps + 2].reshape(1, channels)
        conv_wide = conv_in.astype(jnp.float32)
        conv_sum = conv_b
        for tap in range(taps):
            conv_sum = conv_sum + later(conv_wide, taps - 1 - tap) * conv_w[:, tap]
        out_w = gathered(out_weight, "dp")
        cot = gathered(cot_here, "seq")
        values = jax.nn.silu(conv_sum).astype(jnp.bfloat16)
        projected = lax.psum(jnp.dot(values, select_w, preferred_element_type=jnp.float32), "seq")
        low = projected[:, :rank].astype(jnp.bfloat16)
        kq = jnp.pad(projected[:, rank:], ((0, 0), (0, LANE - 2 * states)))
        gated, mixed, history, final = forward_scan(low, kq, values, gate, beta_w, beta_b, skip, states)
        result_part = jnp.dot(gated, out_w, preferred_element_type=jnp.float32).astype(jnp.bfloat16)
        out_part = contract(gated, cot, 0, 0).astype(jnp.bfloat16)
        dgated = contract(cot, out_w, 1, 1)
    out_part = out_part.reshape(dps, block, width)
    if small_slice:
        dmixed, small_grads, result, out_grad = linked_backward(
            low, kq, gate, mixed, dgated, history, final, beta_w, values, conv_in, select_w, vectors,
            tokens.reshape(rows, width), result_part, out_part, parts, taps, states,
        )
        small_grads = small_grads.reshape(dps, block, wide + rank + LANE)
    else:
        result_part = result_part.reshape(parts, rows, width)
        dgate, dpre_low, dvalues, dlow, dkq, bias_grad, skip_grad, result_came, out_came = backward_scan(
            low, kq, values, gate, mixed, dgated, history, final, beta_w, beta_b, skip, result_part, out_part, states
        )
        part_here = lax.dynamic_index_in_dim(result_part, lax.axis_index("seq"), 0, False).astype(jnp.float32)
        result = (flat + (part_here + jnp.sum(result_came.astype(jnp.float32), axis=0))).astype(jnp.bfloat16)
        out_here = lax.dynamic_index_in_dim(out_part, lax.axis_index("dp"), 0, False).astype(jnp.float32)
        out_grad = out_here + jnp.sum(out_came.astype(jnp.float32), axis=0)
        dprojected = lax.psum(jnp.concatenate([dlow, dkq[:, : 2 * states]], axis=1), "seq").astype(jnp.bfloat16)
        beta_grad = contract(dpre_low, low, 0, 0)
        select_grad = contract(values, dprojected, 0, 0)
        dvalues = contract(dprojected, select_w, 1, 1) + dvalues
        s = jax.nn.sigmoid(conv_sum)
        dconv = dvalues * (s + conv_sum * s * (1.0 - s))
        conv_w_grad = jnp.stack(
            [jnp.sum(dconv * later(conv_wide, taps - 1 - tap), axis=0) for tap in range(taps)], axis=1
        )
        conv_b_grad = jnp.sum(dconv, axis=0)
        dconv_in = 0.0
        for tap in range(taps):
            dconv_in = dconv_in + sooner(dconv, taps - 1 - tap) * conv_w[:, tap]
        dmixed = jnp.concatenate([dconv_in.astype(jnp.bfloat16), dgate], axis=1)
        vector_grads = jnp.concatenate(
            [conv_w_grad, conv_b_grad[:, None], bias_grad.reshape(channels, 1), skip_grad.reshape(channels, 1)], axis=1
        )
        small_grads = jnp.concatenate(
            [
                jnp.pad(select_grad, ((0, 0), (0, wide - select_grad.shape[1]))),
                beta_grad,
                jnp.pad(vector_grads, ((0, 0), (0, LANE - vector_grads.shape[1]))),
            ],
            axis=1,
        ).reshape(dps, block, wide + rank + LANE)
    if small_slice:
        input_grad, in_grad, gain_sums, small_grads = end(
            dmixed, normed, in_w, tokens.reshape(rows, width), cot_here, gain, in_weight, small_grads,
            parts, block,
        )
        gain_sums = gain_sums[:, 0]
    else:
        in_grad = summed_rows(contract(normed, dmixed, 0, 0), "dp").astype(jnp.bfloat16)
        in_grad = lax.all_to_all(in_grad.reshape(parts, own, 2 * channels), "seq", 0, 0).astype(jnp.float32)
        in_grad = in_grad.reshape(parts, own, 2, dps, block).transpose(1, 2, 3, 0, 4).reshape(own, 2 * parts * channels)
        gain_sums = jnp.sum(in_grad * in_weight.astype(jnp.float32), axis=1)
        v = summed_rows(contract(dmixed, in_w, 1, 1), "seq") * gain
        du = scale * v - flat * (scale * scale * scale) * jnp.mean(flat * v, axis=-1, keepdims=True)
        input_grad = (cot_here.astype(jnp.float32) + du).astype(jnp.bfloat16)
        small_grads = jnp.sum(lax.all_to_all(small_grads, "dp", 0, 0), axis=0)
    rows_grad = small_grads[:, wide + rank :]
    return (
        result.reshape(tokens.shape),
        input_grad.reshape(tokens.shape),
        gain_sums / norm_gain.astype(jnp.float32),
        in_grad.astype(jnp.float32),
        rows_grad[:, :taps],
        rows_grad[:, taps],
        small_grads[:, : select_weight.shape[1]],
        small_grads[:, wide : wide + rank],
        rows_grad[:, taps + 1],
        rows_grad[:, taps + 2],
        out_grad,
    )


def solution(mesh):
    split = P(("dp", "seq"))
    rows = P("dp", "seq", None)
    return jax.shard_map(
        local,
        mesh=mesh,
        in_specs=(rows, rows) + (split,) * 9,
        out_specs=(rows, rows) + (split,) * 9,
        check_vma=False,
    )
```

```python
import jax
import jax.numpy as jnp
from jax import lax
from jax.experimental import pallas as pl
from jax.experimental.pallas import tpu as pltpu
from jax.sharding import PartitionSpec as P

LANE = 128
PER_GROUP = 4


def sigmoid(v):
    return 1.0 / (1.0 + jnp.exp(-v))


def by_eights(value):
    return value.reshape(value.shape[0] // 8, 8, value.shape[1])


def as_rows(value):
    return value.reshape(value.shape[0] * 8, value.shape[2])


def spread_columns(kq, row_ref, pick_ref, key_ref, query_ref, states):
    rows = kq.shape[0]
    high = kq.astype(jnp.bfloat16).astype(jnp.float32)
    rest = kq - high
    middle = rest.astype(jnp.bfloat16).astype(jnp.float32)
    row_ref[...] = by_eights(high + pltpu.roll(middle, 2 * states, 1) + pltpu.roll(rest - middle, 4 * states, 1))
    lane = lax.broadcasted_iota(jnp.int32, (states, LANE), 1)
    entry = lax.broadcasted_iota(jnp.int32, (states, LANE), 0)
    pick = lax.rem(lane, states) == entry

    def body(group, carry):
        for offset in range(8):
            at = pl.multiple_of((group * 8 + offset) * states, states)
            row = jnp.broadcast_to(row_ref[group, offset : offset + 1, :], (states, LANE))
            pick_ref[pl.ds(at, states), :] = jnp.where(pick, row, 0.0).astype(jnp.bfloat16)
        return carry

    lax.fori_loop(0, rows // 8, body, 0)
    term = lax.broadcasted_iota(jnp.int32, (LANE, 2 * LANE), 0)
    side = lax.broadcasted_iota(jnp.int32, (LANE, 2 * LANE), 1)
    is_query = lax.rem(term, 2 * states) >= states
    halves = jnp.where(is_query == (side >= LANE), 1.0, 0.0).astype(jnp.bfloat16)
    both = jnp.dot(pick_ref[...], halves, preferred_element_type=jnp.float32)
    key_ref[...] = both[:, :LANE]
    query_ref[...] = both[:, LANE:]


def sum_eights(half_ref, first):
    total = half_ref[pl.ds(first, 8, stride=8), :]
    for n in range(1, 8):
        total = total + half_ref[pl.ds(first + n, 8, stride=8), :]
    return total


def step_sizes(low, kq, weight_ref, bias_ref, states):
    pre = lax.dot_general(
        low, weight_ref[...], (((1,), (1,)), ((), ())), preferred_element_type=jnp.float32
    )
    beta = sigmoid(pre + bias_ref[...])
    lane = lax.broadcasted_iota(jnp.int32, kq.shape, 1)
    keys = jnp.where(lane < states, kq, 0.0)
    square = jnp.sum(keys * keys, axis=1, keepdims=True)
    return beta, 1.0 / (1.0 + beta * square)


def forward_rows(states, rows, channels, history_ref, state_ref, key_ref, query_ref, rate_ref, input_ref, out_ref, half_ref):
    tiles = channels // LANE
    per_group = min(8, tiles)
    for first in range(0, tiles, per_group):
        columns = [slice((first + j) * LANE, (first + j + 1) * LANE) for j in range(per_group)]

        def body(group, carry):
            carry = list(carry)
            for offset in range(8):
                t = group * 8 + offset
                at = pl.multiple_of(t * states, states)
                key = key_ref[pl.ds(at, states), :]
                query = query_ref[pl.ds(at, states), :]
                square = key * key
                for j, cols in enumerate(columns):
                    history_ref[pl.ds(at, states), cols] = carry[j].astype(jnp.bfloat16)
                    rate = rate_ref[group, offset : offset + 1, cols]
                    fed = input_ref[group, offset : offset + 1, cols]
                    carry[j] = (1.0 - rate * square) * carry[j] + key * fed
                    read = query * carry[j]
                    half_ref[j * 64 + offset * 8 : j * 64 + offset * 8 + 8, :] = read[0:8] + read[8:16]
            for j, cols in enumerate(columns):
                out_ref[group, :, cols] = sum_eights(half_ref, j * 64)
            return tuple(carry)

        done = lax.fori_loop(0, rows // 8, body, tuple(state_ref[:, cols] for cols in columns))
        for cols, state in zip(columns, done):
            state_ref[:, cols] = state


def forward_body(
    states, low_ref, kq_ref, values_ref, gate_ref, weight_ref, bias_ref, skip_ref,
    gated_ref, mixed_ref, history_ref, final_ref,
    state_ref, key_ref, query_ref, rate_ref, input_ref, out_ref, row_ref, pick_ref, half_ref,
):
    rows, channels = values_ref.shape

    @pl.when(pl.program_id(0) == 0)
    def _():
        state_ref[...] = jnp.zeros_like(state_ref)

    beta, inverse = step_sizes(low_ref[...], kq_ref[...], weight_ref, bias_ref, states)
    rates = beta * inverse
    rate_ref[...] = by_eights(rates)
    input_ref[...] = by_eights(rates * values_ref[...].astype(jnp.float32))
    spread_columns(kq_ref[...], row_ref, pick_ref, key_ref, query_ref, states)

    forward_rows(states, rows, channels, history_ref, state_ref, key_ref, query_ref, rate_ref, input_ref, out_ref, half_ref)
    mixed = as_rows(out_ref[...]) + skip_ref[...] * values_ref[...].astype(jnp.float32)
    gate = gate_ref[...]
    mixed_ref[...] = mixed
    gated_ref[...] = (mixed * gate * sigmoid(gate)).astype(jnp.bfloat16)

    @pl.when(pl.program_id(0) == pl.num_programs(0) - 1)
    def _():
        final_ref[...] = state_ref[...]


def forward_scan(low, kq, values, gate, weight, bias, skip, states):
    length, channels = values.shape
    rank = low.shape[1]
    rows = min(128, length)
    blocks = length // rows
    by_row = lambda width: pl.BlockSpec((rows, width), lambda i: (i, 0))
    whole = lambda a: pl.BlockSpec(a.shape, lambda i: (0, 0))
    return pl.pallas_call(
        lambda *refs: forward_body(states, *refs),
        grid=(blocks,),
        in_specs=[by_row(rank), by_row(LANE), by_row(channels), by_row(channels), whole(weight), whole(bias), whole(skip)],
        out_specs=[
            by_row(channels),
            by_row(channels),
            pl.BlockSpec((rows * states, channels), lambda i: (i, 0)),
            pl.BlockSpec((states, channels), lambda i: (0, 0)),
        ],
        out_shape=[
            jax.ShapeDtypeStruct((length, channels), jnp.bfloat16),
            jax.ShapeDtypeStruct((length, channels), jnp.float32),
            jax.ShapeDtypeStruct((length * states, channels), jnp.bfloat16),
            jax.ShapeDtypeStruct((states, channels), jnp.float32),
        ],
        scratch_shapes=[
            pltpu.VMEM((states, channels), jnp.float32),
            pltpu.VMEM((rows * states, LANE), jnp.float32),
            pltpu.VMEM((rows * states, LANE), jnp.float32),
            pltpu.VMEM((rows // 8, 8, channels), jnp.float32),
            pltpu.VMEM((rows // 8, 8, channels), jnp.float32),
            pltpu.VMEM((rows // 8, 8, channels), jnp.float32),
            pltpu.VMEM((rows // 8, 8, LANE), jnp.float32), pltpu.VMEM((rows * states, LANE), jnp.bfloat16),
            pltpu.VMEM((channels // LANE * 64, LANE), jnp.float32),
        ],
        compiler_params=pltpu.CompilerParams(vmem_limit_bytes=48 * 1024 * 1024),
        cost_estimate=pl.CostEstimate(flops=14 * length * states * channels, bytes_accessed=2 * length * states * channels, transcendentals=0),
    )(low, kq, values, gate, weight, bias, skip)


def backward_rows(
    states, rows, channels, history_ref, grad_ref, state_ref, key_ref, query_ref, rate_ref, do_ref, values32_ref,
    fed_ref, kept_ref, part_key_ref, part_query_ref, half_ref,
):
    tiles = channels // LANE
    per_group = min(PER_GROUP, tiles)
    for first in range(0, tiles, per_group):
        columns = [slice((first + j) * LANE, (first + j + 1) * LANE) for j in range(per_group)]

        def body(step, carry):
            grads, lates = list(carry[0]), list(carry[1])
            group = rows // 8 - 1 - step
            for offset in reversed(range(8)):
                t = group * 8 + offset
                at = pl.multiple_of(t * states, states)
                key = key_ref[pl.ds(at, states), :]
                query = query_ref[pl.ds(at, states), :]
                sum_key = None
                sum_query = None
                for j, cols in enumerate(columns):
                    rate = rate_ref[group, offset : offset + 1, cols]
                    out_grad = do_ref[group, offset : offset + 1, cols]
                    value = values32_ref[group, offset : offset + 1, cols]
                    before = history_ref[pl.ds(at, states), cols].astype(jnp.float32)
                    grad = grads[j] + query * out_grad
                    scaled = rate * grad
                    by_key = key * scaled
                    kept = scaled * before
                    kept = key * kept
                    twice = key * kept
                    at_fed = j * 64 + offset * 8
                    at_kept = (per_group + j) * 64 + offset * 8
                    half_ref[at_fed : at_fed + 8, :] = by_key[0:8] + by_key[8:16]
                    half_ref[at_kept : at_kept + 8, :] = twice[0:8] + twice[8:16]
                    term_key = value * scaled - 2.0 * kept
                    term_query = lates[j] * out_grad
                    sum_key = term_key if sum_key is None else sum_key + term_key
                    sum_query = term_query if sum_query is None else sum_query + term_query
                    grads[j] = grad - key * by_key
                    lates[j] = before
                if first == 0:
                    part_key_ref[pl.ds(at, states), :] = sum_key
                    part_query_ref[pl.ds(at, states), :] = sum_query
                else:
                    part_key_ref[pl.ds(at, states), :] += sum_key
                    part_query_ref[pl.ds(at, states), :] += sum_query
            for j, cols in enumerate(columns):
                fed_ref[group, :, cols] = sum_eights(half_ref, j * 64)
                kept_ref[group, :, cols] = sum_eights(half_ref, (per_group + j) * 64)
            return (tuple(grads), tuple(lates))

        start = (tuple(grad_ref[:, cols] for cols in columns), tuple(state_ref[:, cols] for cols in columns))
        grads, lates = lax.fori_loop(0, rows // 8, body, start)
        for cols, grad, late in zip(columns, grads, lates):
            grad_ref[:, cols] = grad
            state_ref[:, cols] = late


def lane_sums(part_ref, wide_ref, states):
    part = part_ref[...]
    high = part.astype(jnp.bfloat16)
    wide_ref[:, :LANE] = high
    wide_ref[:, LANE:] = (part - high.astype(jnp.float32)).astype(jnp.bfloat16)
    ones = jnp.ones((2 * LANE, LANE), jnp.bfloat16)
    part_ref[...] = jnp.dot(wide_ref[...], ones, preferred_element_type=jnp.float32)


def gather_columns(part_key_ref, part_query_ref, wide_ref, placed_ref, rows, states):
    lane_sums(part_key_ref, wide_ref, states)
    lane_sums(part_query_ref, wide_ref, states)
    lane = lax.broadcasted_iota(jnp.int32, (8, LANE), 1)

    def body(group, carry):
        total = jnp.zeros((8, LANE), jnp.float32)
        for n in range(states):
            at = group * 8 * states + n
            total = jnp.where(lane == n, part_key_ref[pl.ds(at, 8, stride=states), :], total)
            total = jnp.where(lane == n + states, part_query_ref[pl.ds(at, 8, stride=states), :], total)
        placed_ref[group] = total
        return carry

    lax.fori_loop(0, rows // 8, body, 0)


def backward_body(
    states, links, low_ref, kq_ref, values_ref, gate_ref, mixed_ref, dgated_ref, history_ref, final_ref, weight_ref, bias_ref, skip_ref,
    result_ref, out_ref, dgate_ref, dpre_ref, dvalues_ref, dlow_ref, dkq_ref, bias_grad_ref, skip_grad_ref, result_came, out_came,
    grad_ref, state_ref, key_ref, query_ref, rate_ref, do_ref, values32_ref, fed_ref, kept_ref, part_key_ref, part_query_ref, row_ref, placed_ref,
    pick_ref, wide_ref, half_ref, *sems,
):
    rows, channels = values_ref.shape
    copies = links(result_ref, out_ref, result_came, out_came, *sems)

    @pl.when(pl.program_id(0) == 0)
    def _():
        grad_ref[...] = jnp.zeros_like(grad_ref)
        state_ref[...] = final_ref[...]
        bias_grad_ref[...] = jnp.zeros_like(bias_grad_ref)
        skip_grad_ref[...] = jnp.zeros_like(skip_grad_ref)
        for copy in copies:
            copy.start()

    beta, inverse = step_sizes(low_ref[...], kq_ref[...], weight_ref, bias_ref, states)
    rate_ref[...] = by_eights(beta * inverse)
    values = values_ref[...].astype(jnp.float32)
    values32_ref[...] = by_eights(values)
    gate = gate_ref[...]
    dgated = dgated_ref[...].astype(jnp.float32)
    s = sigmoid(gate)
    do = dgated * (gate * s)
    do_ref[...] = by_eights(do)
    dgate_ref[...] = (dgated * mixed_ref[...] * (s + gate * s * (1.0 - s))).astype(jnp.bfloat16)
    skip_grad_ref[...] += jnp.sum(do * values, axis=0, keepdims=True)
    spread_columns(kq_ref[...], row_ref, pick_ref, key_ref, query_ref, states)

    backward_rows(
        states, rows, channels, history_ref, grad_ref, state_ref, key_ref, query_ref, rate_ref, do_ref, values32_ref,
        fed_ref, kept_ref, part_key_ref, part_query_ref, half_ref,
    )
    fed = as_rows(fed_ref[...])
    dvalues_ref[...] = fed + skip_ref[...] * as_rows(do_ref[...])
    scaled = as_rows(values32_ref[...]) * fed - as_rows(kept_ref[...])
    beta, inverse = step_sizes(low_ref[...], kq_ref[...], weight_ref, bias_ref, states)
    dpre = scaled * (1.0 - beta) * inverse
    bias_grad_ref[...] += jnp.sum(dpre, axis=0, keepdims=True)
    dpre_low = dpre.astype(jnp.bfloat16)
    dpre_ref[...] = dpre_low
    dlow_ref[...] = jnp.dot(dpre_low, weight_ref[...], preferred_element_type=jnp.float32)
    through = -2.0 * jnp.sum(scaled * beta * inverse, axis=1, keepdims=True)

    gather_columns(part_key_ref, part_query_ref, wide_ref, placed_ref, rows, states)
    lanes = lax.broadcasted_iota(jnp.int32, kq_ref.shape, 1)
    dkq_ref[...] = as_rows(placed_ref[...]) + jnp.where(lanes < states, kq_ref[...] * through, 0.0)

    @pl.when(pl.program_id(0) == pl.num_programs(0) - 1)
    def _():
        for copy in copies:
            copy.wait_recv()
        for copy in copies:
            copy.wait_send()


def exchange(parts, dps, result_ref, out_ref, result_came, out_came, result_send, result_recv, out_send, out_recv):
    d, s = lax.axis_index("dp"), lax.axis_index("seq")

    @pl.when(pl.program_id(0) == 0)
    def _():
        barrier = pltpu.get_barrier_semaphore()
        for k in range(1, parts):
            pl.semaphore_signal(barrier, inc=1, device_id=(d, lax.rem(s + k, parts)), device_id_type=MESH)
        for k in range(1, dps):
            pl.semaphore_signal(barrier, inc=1, device_id=(lax.rem(d + k, dps), s), device_id_type=MESH)
        pl.semaphore_wait(barrier, parts + dps - 2)

    copies = []
    for k in range(1, parts):
        to = lax.rem(s + k, parts)
        copies.append(
            pltpu.make_async_remote_copy(
                src_ref=result_ref.at[to], dst_ref=result_came.at[k - 1], send_sem=result_send.at[k - 1],
                recv_sem=result_recv.at[k - 1], device_id=(d, to), device_id_type=MESH,
            )
        )
    for k in range(1, dps):
        to = lax.rem(d + k, dps)
        copies.append(
            pltpu.make_async_remote_copy(
                src_ref=out_ref.at[to], dst_ref=out_came.at[k - 1], send_sem=out_send.at[k - 1],
                recv_sem=out_recv.at[k - 1], device_id=(to, s), device_id_type=MESH,
            )
        )
    return copies


def backward_scan(low, kq, values, gate, mixed, dgated, history, final, weight, bias, skip, result_part, out_part, states):
    length, channels = values.shape
    rank = low.shape[1]
    rows = min(128, length)
    blocks = length // rows
    by_row = lambda width: pl.BlockSpec((rows, width), lambda i: (blocks - 1 - i, 0))
    whole = lambda a: pl.BlockSpec(a.shape, lambda i: (0, 0))
    total = pl.BlockSpec((1, channels), lambda i: (0, 0))
    wide = pltpu.VMEM((rows // 8, 8, channels), jnp.float32)
    spread = pltpu.VMEM((rows * states, LANE), jnp.float32)
    anywhere = pl.BlockSpec(memory_space=pl.ANY)
    dma = pltpu.SemaphoreType.DMA
    parts, dps = result_part.shape[0], out_part.shape[0]
    links = lambda *refs: exchange(parts, dps, *refs)
    return pl.pallas_call(
        lambda *refs: backward_body(states, links, *refs),
        grid=(blocks,),
        in_specs=[
            by_row(rank), by_row(LANE), by_row(channels), by_row(channels), by_row(channels), by_row(channels),
            pl.BlockSpec((rows * states, channels), lambda i: (blocks - 1 - i, 0)),
            whole(final), whole(weight), whole(bias), whole(skip), anywhere, anywhere,
        ],
        out_specs=[by_row(channels), by_row(channels), by_row(channels), by_row(rank), by_row(LANE), total, total, anywhere, anywhere],
        out_shape=[
            jax.ShapeDtypeStruct((length, channels), jnp.bfloat16),
            jax.ShapeDtypeStruct((length, channels), jnp.bfloat16),
            jax.ShapeDtypeStruct((length, channels), jnp.float32),
            jax.ShapeDtypeStruct((length, rank), jnp.float32),
            jax.ShapeDtypeStruct((length, LANE), jnp.float32),
            jax.ShapeDtypeStruct((1, channels), jnp.float32),
            jax.ShapeDtypeStruct((1, channels), jnp.float32),
            jax.ShapeDtypeStruct((parts - 1,) + result_part.shape[1:], jnp.bfloat16),
            jax.ShapeDtypeStruct((dps - 1,) + out_part.shape[1:], jnp.bfloat16),
        ],
        scratch_shapes=[
            pltpu.VMEM((states, channels), jnp.float32),
            pltpu.VMEM((states, channels), jnp.float32),
            spread, spread, wide, wide, wide, wide, wide, spread, spread,
            pltpu.VMEM((rows // 8, 8, LANE), jnp.float32), pltpu.VMEM((rows // 8, 8, LANE), jnp.float32),
            pltpu.VMEM((rows * states, LANE), jnp.bfloat16), pltpu.VMEM((rows * states, 2 * LANE), jnp.bfloat16),
            pltpu.VMEM((2 * channels // LANE * 64, LANE), jnp.float32),
            dma((parts - 1,)), dma((parts - 1,)), dma((dps - 1,)), dma((dps - 1,)),
        ],
        compiler_params=pltpu.CompilerParams(collective_id=3, has_side_effects=True, vmem_limit_bytes=56 * 1024 * 1024),
        cost_estimate=pl.CostEstimate(flops=30 * length * states * channels, bytes_accessed=2 * length * states * channels, transcendentals=0),
    )(low, kq, values, gate, mixed, dgated, history, final, weight, bias, skip, result_part, out_part)


MESH = pl.DeviceIdType.MESH
GAIN_ROWS = 16


def plane_mates(d):
    core, x, y = lax.rem(d, 2), lax.rem(d // 2, 2), d // 4
    return d + 1 - 2 * core, d + 2 - 4 * x, d + 4 - 8 * y


def start_body(
    parts, block,
    tokens_ref, in_weight_ref, extra_ref, gain_ref, cot_ref,
    normed_out, weight_out, conv_ref, gate_ref, select_out, beta_out, vector_out, gain_out, cot_early,
    tokens_all, normed_all, weight_all, extra_all,
    near_send, near_recv, plane_send, plane_recv, gain_send, gain_recv, line_send, line_recv, local_sem, early_send, early_recv, spread_ref,
):
    d, s = lax.axis_index("dp"), lax.axis_index("seq")
    sib, xm, ym = plane_mates(d)
    own = spread_ref.shape[1]
    rows, width = tokens_ref.shape
    small = extra_ref.shape[0]
    channels = conv_ref.shape[1]
    chunk = rows // 4

    for j in range(spread_ref.shape[2] // block):
        for q in range(parts):
            first = (j * parts + q) * block
            spread_ref[q, :, j * block : (j + 1) * block] = in_weight_ref[:, first : first + block]

    barrier = pltpu.get_barrier_semaphore()
    for mate in (sib, xm, ym):
        pl.semaphore_signal(barrier, inc=1, device_id=(mate, s), device_id_type=MESH)
    for k in range(1, parts):
        pl.semaphore_signal(barrier, inc=1, device_id=(d, lax.rem(s + k, parts)), device_id_type=MESH)
    pl.semaphore_wait(barrier, 3 + parts - 1)

    def remote(src, dst, send, recv, to):
        return pltpu.make_async_remote_copy(
            src_ref=src, dst_ref=dst, send_sem=send, recv_sem=recv, device_id=to, device_id_type=MESH
        )

    def weight_rows(owner, source):
        return weight_all.at[pl.ds(pl.multiple_of((owner * parts + source) * own, own), own), :]

    def extra_rows(owner):
        return extra_all.at[owner]

    def gain_rows(source):
        return extra_all.at[d, pl.ds(pl.multiple_of(small + source * GAIN_ROWS, GAIN_ROWS), GAIN_ROWS), pl.ds(0, LANE)]

    near = []
    for k in range(1, parts):
        to = (d, lax.rem(s + k, parts))
        near.append(remote(spread_ref.at[to[1]], weight_rows(d, s), near_send.at[k], near_recv.at[k], to))
        near.append(remote(gain_ref, gain_rows(s), gain_send.at[k], gain_recv.at[k], to))
    for copy in near:
        copy.start()
    mine = [
        pltpu.make_async_copy(spread_ref.at[s], weight_rows(d, s), local_sem.at[0]),
        pltpu.make_async_copy(gain_ref, gain_rows(s), local_sem.at[1]),
        pltpu.make_async_copy(extra_ref, extra_all.at[d, pl.ds(0, small), :], local_sem.at[2]),
        pltpu.make_async_copy(tokens_ref, tokens_all.at[pl.ds(pl.multiple_of(s * rows, rows), rows), :], local_sem.at[3]),
    ]
    for copy in mine:
        copy.start()

    def token_rows(part, c):
        return tokens_all.at[pl.ds(pl.multiple_of(part * rows + c * chunk, chunk), chunk), :]

    def token_copy(way, distance, c):
        part = s - way * (distance - 1)
        src = tokens_ref.at[pl.ds(c * chunk, chunk), :] if distance == 1 else token_rows(part, c)
        side = 0 if way == 1 else 1
        return remote(
            src, token_rows(part, c), line_send.at[side, distance, c], line_recv.at[side, distance, c], (d, s + way)
        )

    def can_send(way, distance):
        reach = s + 1 < parts if way == 1 else s >= 1
        came = s - (distance - 1) >= 0 if way == 1 else s + (distance - 1) < parts
        return jnp.logical_and(reach, came)

    def arrives(way, distance):
        return s >= distance if way == 1 else s + distance < parts

    def send_tokens(distance, c):
        for way in (1, -1):
            @pl.when(can_send(way, distance))
            def _():
                token_copy(way, distance, c).start()

    def sent_tokens(distance, c):
        for way in (1, -1):
            @pl.when(can_send(way, distance))
            def _():
                token_copy(way, distance, c).wait_send()

    def take_tokens(distance, c):
        for way in (1, -1):
            @pl.when(arrives(way, distance))
            def _():
                part = s - way * distance
                side = 0 if way == 1 else 1
                remote(
                    token_rows(part, c), token_rows(part, c), line_send.at[side, distance, c],
                    line_recv.at[side, distance, c], (d, s),
                ).wait_recv()

    inner = jnp.logical_and(s >= 1, s + 1 < parts)

    def early_copy(way):
        side = 0 if way == 1 else 1
        return remote(cot_ref, cot_early.at[side], early_send.at[side], early_recv.at[side], (d, s + way))

    def sends_early(way):
        return s + 2 < parts if way == 1 else s >= 2

    units = parts + 1

    def unit(owner, k):
        return extra_rows(owner) if k == parts else weight_rows(owner, lax.rem(s - k + parts, parts))

    kinds = {"own": (d, 0), "x": (xm, 2), "y": (ym, 4)}

    def plane_copy(owner, k, rel, kind, to):
        return remote(unit(owner, k), unit(owner, k), plane_send.at[kind, k], plane_recv.at[rel, k], (to, s))

    diag = xm + ym - d
    sib_of = lambda mate: mate + sib - d

    def route(k):
        steps = [
            (0, d, 1, 0, sib), (0, d, 2, 1, xm), (0, d, 4, 2, ym),
            (2, xm, 3, 3, sib), (4, ym, 5, 5, sib), (6, diag, 7, 7, sib),
        ]
        steps.append((2, xm, 6, 4, ym) if k % 2 == 0 else (4, ym, 6, 6, xm))
        return steps

    def pass_on(stage, k):
        for at, owner, rel, kind, to in route(k):
            if at == stage:
                plane_copy(owner, k, rel, kind, to).start()

    owners = {1: sib, 2: xm, 3: sib_of(xm), 4: ym, 5: sib_of(ym), 6: diag, 7: sib_of(diag)}

    def take(rel, k):
        plane_copy(owners[rel], k, rel, 0, d).wait_recv()

    for c in range(4):
        send_tokens(1, c)
    mine[0].wait()
    pass_on(0, 0)
    for k in range(1, parts):
        near_wait = remote(
            spread_ref.at[s], weight_rows(d, lax.rem(s - k + parts, parts)), near_send.at[k], near_recv.at[k], (d, s)
        )
        near_wait.wait_recv()
        pass_on(0, k)
    mine[1].wait()
    mine[2].wait()
    for k in range(1, parts):
        remote(gain_ref, gain_rows(lax.rem(s - k + parts, parts)), gain_send.at[k], gain_recv.at[k], (d, s)).wait_recv()
    pass_on(0, parts)
    for k in range(units):
        take(2, k)
        pass_on(2, k)
        take(4, k)
        pass_on(4, k)
        if k < 4:
            take_tokens(1, k)
            send_tokens(2, k)
    for way in (1, -1):
        @pl.when(sends_early(way))
        def _():
            early_copy(way).start()

    for k in range(units):
        take(6, k)
        pass_on(6, k)
        if k < 4:
            take_tokens(2, k)
            send_tokens(3, k)
    for rel in (1, 3, 5, 7):
        for k in range(units):
            take(rel, k)
    mine[3].wait()
    weight_copy = pltpu.make_async_copy(weight_all, weight_out, local_sem.at[4])
    weight_copy.start()
    sel = select_out.shape[1]
    for owner in range(extra_all.shape[0]):
        here = slice(owner * small, (owner + 1) * small)
        select_out[here, :] = extra_all[owner, 0:small, 0:sel]
        beta_out[here, :] = extra_all[owner, 0:small, sel : sel + LANE]
        vectors = extra_all[owner, 0:small, sel + LANE : sel + 2 * LANE].astype(jnp.float32)
        vector_out[:, here] = jnp.transpose(vectors)[: vector_out.shape[0]]

    lane = lax.broadcasted_iota(jnp.int32, (1, LANE), 1)
    pieces = []
    for owner in range(extra_all.shape[0]):
        for source in range(0, parts, 2):
            row = small + source * GAIN_ROWS
            even = extra_all[owner, row : row + GAIN_ROWS, 0:LANE].astype(jnp.float32)[0:1]
            odd = extra_all[owner, row + GAIN_ROWS : row + 2 * GAIN_ROWS, 0:LANE].astype(jnp.float32)[0:1]
            pieces.append(jnp.where(lane < own, even, odd))
    gain = jnp.concatenate(pieces, axis=1)
    gain_out[...] = gain

    tile = min(512, channels)

    def work(part):
        for c in range(4):
            at = pl.ds(pl.multiple_of(part * rows + c * chunk, chunk), chunk)
            flat = tokens_all[at, :].astype(jnp.float32)
            scale = lax.rsqrt(jnp.mean(flat * flat, axis=-1, keepdims=True) + 1e-05)
            normed_all[at, :] = (flat * scale * gain).astype(jnp.bfloat16)
        at = pl.ds(pl.multiple_of(part * rows, rows), rows)

        def columns(n, carry):
            left = pl.multiple_of(n * tile, tile)
            right = pl.multiple_of(channels + n * tile, tile)
            conv_ref[at, pl.ds(left, tile)] = jnp.dot(
                normed_all[at, :], weight_all[:, pl.ds(left, tile)], preferred_element_type=jnp.float32
            ).astype(jnp.bfloat16)
            gate_ref[at, pl.ds(left, tile)] = jnp.dot(
                normed_all[at, :], weight_all[:, pl.ds(right, tile)], preferred_element_type=jnp.float32
            )
            return carry

        lax.fori_loop(0, channels // tile, columns, 0)

    def work_at(low, high):
        def each(part, carry):
            away = jnp.abs(part - s)

            @pl.when(jnp.logical_and(away >= low, away <= high))
            def _():
                work(part)

            return carry

        lax.fori_loop(0, parts, each, 0)

    work_at(0, 2)
    for c in range(4):
        take_tokens(3, c)
    work_at(3, 3)
    normed_copy = pltpu.make_async_copy(normed_all, normed_out, local_sem.at[5])
    normed_copy.start()

    for way in (1, -1):
        @pl.when(inner)
        def _():
            early_copy(way).wait_recv()

        @pl.when(sends_early(way))
        def _():
            early_copy(way).wait_send()

    for copy in near:
        copy.wait_send()
    for k in range(units):
        for at, owner, rel, kind, to in route(k):
            plane_copy(owner, k, rel, kind, to).wait_send()
    for distance in range(1, parts):
        for c in range(4):
            sent_tokens(distance, c)
    weight_copy.wait()
    normed_copy.wait()


def start(tokens, in_weight, extra, gain, cotangent, parts, dps):
    own, both = in_weight.shape[0], in_weight.shape[1] // parts
    rows, width = tokens.shape
    small, lanes = extra.shape
    any_space = pl.BlockSpec(memory_space=pl.ANY)
    vmem = pl.BlockSpec(memory_space=pltpu.VMEM)
    tall = small + parts * GAIN_ROWS
    dma = pltpu.SemaphoreType.DMA
    return pl.pallas_call(
        lambda *refs: start_body(parts, small, *refs),
        out_shape=[
            jax.ShapeDtypeStruct((parts * rows, width), jnp.bfloat16),
            jax.ShapeDtypeStruct((dps * parts * own, both), jnp.bfloat16),
            jax.ShapeDtypeStruct((parts * rows, both // 2), jnp.bfloat16),
            jax.ShapeDtypeStruct((parts * rows, both // 2), jnp.float32),
            jax.ShapeDtypeStruct((dps * small, lanes - 2 * LANE), jnp.bfloat16),
            jax.ShapeDtypeStruct((dps * small, LANE), jnp.bfloat16),
            jax.ShapeDtypeStruct((8, dps * small), jnp.float32),
            jax.ShapeDtypeStruct((1, width), jnp.float32),
            jax.ShapeDtypeStruct((2, rows, width), jnp.bfloat16),
        ],
        in_specs=[vmem, vmem, vmem, vmem, any_space],
        out_specs=[any_space, any_space, vmem, vmem, vmem, vmem, vmem, vmem, any_space],
        scratch_shapes=[
            pltpu.VMEM((parts * rows, width), jnp.bfloat16),
            pltpu.VMEM((parts * rows, width), jnp.bfloat16),
            pltpu.VMEM((dps * parts * own, both), jnp.bfloat16),
            pltpu.VMEM((dps, tall, lanes), jnp.bfloat16),
            dma((parts,)), dma((parts,)),
            dma((8, parts + 1)), dma((8, parts + 1)),
            dma((parts,)), dma((parts,)),
            dma((2, parts, 4)), dma((2, parts, 4)),
            dma((6,)), dma((2,)), dma((2,)), pltpu.VMEM((parts, own, both), jnp.bfloat16),
        ],
        compiler_params=pltpu.CompilerParams(
            collective_id=1, has_side_effects=True, vmem_limit_bytes=56 * 1024 * 1024
        ),
        cost_estimate=pl.CostEstimate(
            flops=2 * parts * rows * width * both, bytes_accessed=40 * 1024 * 1024, transcendentals=0
        ),
    )(tokens, in_weight, extra, gain, cotangent)


def line_sums(parts, rows, terms, came, send, recv, early=None):
    d, s = lax.axis_index("dp"), lax.axis_index("seq")
    chunk = rows // 4

    def own_rows(part, c):
        return pl.ds(pl.multiple_of(part * rows + c * chunk, chunk), chunk)

    def slot(way, left, part, c):
        at = parts if way == -1 and left == 0 else part
        return came.at[at, pl.ds(c * chunk, chunk), :]

    def copy_of(way, steps, c):
        side = 0 if way == 1 else 1
        part = s + way * steps
        return pltpu.make_async_remote_copy(
            src_ref=terms.at[own_rows(part, c), :], dst_ref=slot(way, steps - 1, part, c),
            send_sem=send.at[side, steps, c], recv_sem=recv.at[side, steps - 1, c],
            device_id=(d, s + way), device_id_type=MESH,
        )

    def valid(way, steps):
        if early is not None and steps == 1:
            return jnp.logical_and(s >= 1, s + 1 < parts)
        return s + steps < parts if way == 1 else s >= steps

    def ends_here(way):
        least = 1 if early is None else 2
        return s >= least if way == 1 else s + least < parts

    def upstream(way):
        return s >= 1 if way == 1 else s + 1 < parts

    def taken(way, left, c):
        side = 0 if way == 1 else 1
        place = slot(way, left, s + way * left, c)
        pltpu.make_async_remote_copy(
            src_ref=place, dst_ref=place, send_sem=send.at[side, left, c], recv_sem=recv.at[side, left, c],
            device_id=(d, s), device_id_type=MESH,
        ).wait_recv()

    def pass_on(steps, c):
        for way in (1, -1):
            @pl.when(valid(way, steps))
            def _():
                if steps < parts - 1:
                    @pl.when(upstream(way))
                    def _():
                        taken(way, steps, c)
                        mine = own_rows(s + way * steps, c)
                        more = came[s + way * steps, c * chunk : (c + 1) * chunk, :]
                        terms[mine, :] = (terms[mine, :].astype(jnp.float32) + more.astype(jnp.float32)).astype(jnp.bfloat16)

                copy_of(way, steps, c).start()

    def total(c):
        for way in (1, -1):
            @pl.when(ends_here(way))
            def _():
                taken(way, 0, c)

        at = pl.ds(c * chunk, chunk)
        low = jnp.where(ends_here(1), came[s, at, :].astype(jnp.float32), 0.0)
        high = jnp.where(ends_here(-1), came[parts, at, :].astype(jnp.float32), 0.0)
        total = terms[own_rows(s, c), :].astype(jnp.float32) + low + high
        if early is not None:
            total = total + jnp.where(jnp.logical_or(s == 1, s == parts - 2), early[at, :].astype(jnp.float32), 0.0)
        return total

    def sent():
        for steps in range(1, parts):
            for c in range(4):
                for way in (1, -1):
                    @pl.when(valid(way, steps))
                    def _():
                        copy_of(way, steps, c).wait_send()

    return pass_on, total, sent


def end_body(
    parts, block,
    dmixed_hbm, normed_hbm, weight_hbm, tokens_hbm, cot_hbm, gain_ref, shard_hbm, small_hbm,
    input_grad_ref, in_grad_ref, gain_grad_ref, small_grad_ref,
    dn, dn_recv, sib_send, sib_recv, q_send, q_recv, total, z_send, z_recv,
    small_sib_send, small_sib_recv, small_q_send, small_q_recv,
    line_send, line_recv, pair_send, pair_recv, cross_send, cross_recv, near_send, near_recv,
    dmixed_ref, normed_ref, weight_ref, tokens_ref, cot_ref, shard_ref, small_ref, load_sem,
):
    d, s = lax.axis_index("dp"), lax.axis_index("seq")
    sib, xm, ym = plane_mates(d)
    diag = xm + ym - d
    own, both = shard_ref.shape[0], dmixed_ref.shape[1]
    rows, width = tokens_ref.shape
    chunk = rows // 4
    tall = parts * own
    tile = min(512, both)

    loads = [
        pltpu.make_async_copy(src, dst, load_sem.at[i])
        for i, (src, dst) in enumerate(
            (
                (dmixed_hbm, dmixed_ref), (weight_hbm, weight_ref), (normed_hbm, normed_ref), (small_hbm, small_ref),
                (tokens_hbm, tokens_ref), (cot_hbm, cot_ref), (shard_hbm, shard_ref),
            )
        )
    ]
    for load in loads[:2]:
        load.start()
    barrier = pltpu.get_barrier_semaphore()
    for mate in (sib, xm, ym, diag):
        pl.semaphore_signal(barrier, inc=1, device_id=(mate, s), device_id_type=MESH)
    for k in range(1, parts):
        pl.semaphore_signal(barrier, inc=1, device_id=(d, lax.rem(s + k, parts)), device_id_type=MESH)
    pl.semaphore_wait(barrier, 4 + parts - 1)

    def remote(src, dst, send, recv, to):
        return pltpu.make_async_remote_copy(
            src_ref=src, dst_ref=dst, send_sem=send, recv_sem=recv, device_id=to, device_id_type=MESH
        )

    pass_line, line_total, line_sent = line_sums(parts, rows, dn, dn_recv, line_send, line_recv)

    def dn_part(part):
        at = pl.ds(pl.multiple_of(part * rows, rows), rows)

        def columns(n, carry):
            cols = pl.ds(pl.multiple_of(n * tile, tile), tile)
            dn[at, cols] = lax.dot_general(
                dmixed_ref[at, :], weight_ref[cols, :], (((1,), (1,)), ((), ())), preferred_element_type=jnp.float32
            ).astype(jnp.bfloat16)
            return carry

        lax.fori_loop(0, width // tile, columns, 0)

    far = (parts - 1) * (1 - s // 2)
    next_far = lax.rem(2 - 2 * s + 10, 5)
    nearer = 1 + lax.rem(s, 2)
    for load in loads[:2]:
        load.wait()
    for load in loads[2:]:
        load.start()
    dn_part(far)
    for c in range(4):
        pass_line(parts - 1, c)
    for load in loads[2:4]:
        load.wait()

    def grad_block(owner, store):
        left = pl.ds(pl.multiple_of(owner * tall, tall), tall)

        def columns(n, carry):
            cols = pl.ds(pl.multiple_of(n * tile, tile), tile)
            store(
                cols,
                lax.dot_general(
                    normed_ref[:, left], dmixed_ref[:, cols], (((0,), (0,)), ((), ())),
                    preferred_element_type=jnp.float32,
                ),
            )
            return carry

        lax.fori_loop(0, both // tile, columns, 0)

    mates = (diag, xm, ym, d)
    sib_of = lambda mate: mate + sib - d

    def pair_copy(r):
        return remote(sib_send.at[r], sib_recv.at[r], pair_send.at[0, r], pair_recv.at[0, r], (sib, s))

    def pair_copy_small(r):
        return remote(small_sib_send.at[r], small_sib_recv.at[r], pair_send.at[1, r], pair_recv.at[1, r], (sib, s))

    def cross_copy(r):
        return remote(q_send.at[r], q_recv.at[r], cross_send.at[0, r], cross_recv.at[0, r], (mates[r], s))

    def cross_copy_small(r):
        return remote(small_q_send.at[r], small_q_recv.at[r], cross_send.at[1, r], cross_recv.at[1, r], (mates[r], s))

    for r in range(4):
        def store_pair(cols, value):
            sib_send[r, :, cols] = value.astype(jnp.bfloat16)

        grad_block(sib_of(mates[r]), store_pair)
        pair_copy(r).start()
        small_sib_send[r] = small_ref[sib_of(mates[r])].astype(jnp.bfloat16)
        pair_copy_small(r).start()
    dn_part(next_far)
    for r in range(4):
        pair_copy(r).wait_recv()
        pair_copy_small(r).wait_recv()
        both_small = small_ref[mates[r]] + small_sib_recv[r].astype(jnp.float32)
        if r < 3:
            def store_cross(cols, value):
                q_send[r, :, cols] = (value + sib_recv[r, :, cols].astype(jnp.float32)).astype(jnp.bfloat16)

            grad_block(mates[r], store_cross)
            cross_copy(r).start()
            small_q_send[r] = both_small.astype(jnp.bfloat16)
            cross_copy_small(r).start()
        else:
            def store_total(cols, value):
                total[:, cols] = value + sib_recv[r, :, cols].astype(jnp.float32)

            grad_block(mates[r], store_total)
            small_grad_ref[...] = both_small
        pass_line(parts - 2, r)
        if r == 2:
            dn_part(nearer)
            dn_part(s)
    for c in range(4):
        pass_line(parts - 3, c)
    for load in loads[4:]:
        load.wait()

    for r in range(3):
        cross_copy(r).wait_recv()
        cross_copy_small(r).wait_recv()
        total[...] += q_recv[r].astype(jnp.float32)
        small_grad_ref[...] += small_q_recv[r].astype(jnp.float32)
    z_send[...] = total[...].astype(jnp.bfloat16)

    def near_copy(k):
        to = lax.rem(s + k, parts)
        return remote(
            z_send.at[pl.ds(pl.multiple_of(to * own, own), own), :], z_recv.at[k], near_send.at[k], near_recv.at[k], (d, to)
        )

    for k in range(1, parts):
        near_copy(k).start()

    for c in range(4):
        at = pl.ds(c * chunk, chunk)
        v = line_total(c) * gain_ref[...]
        flat = tokens_ref[at, :].astype(jnp.float32)
        scale = lax.rsqrt(jnp.mean(flat * flat, axis=-1, keepdims=True) + 1e-05)
        du = scale * v - flat * (scale * scale * scale) * jnp.mean(flat * v, axis=-1, keepdims=True)
        input_grad_ref[at, :] = (cot_ref[at, :].astype(jnp.float32) + du).astype(jnp.bfloat16)

    channel_blocks = both // block
    gain_total = jnp.zeros((own, block), jnp.float32)
    for k in range(parts):
        source = lax.rem(s - k + parts, parts)
        if k > 0:
            near_copy(k).wait_recv()
        for j in range(channel_blocks):
            cols = slice(j * block, (j + 1) * block)
            if k == 0:
                piece = z_send[pl.ds(pl.multiple_of(s * own, own), own), cols]
            else:
                piece = z_recv[k, :, cols]
            to = pl.ds(pl.multiple_of((j * parts + source) * block, block), block)
            in_grad_ref[:, to] = piece
            gain_total = gain_total + piece.astype(jnp.float32) * shard_ref[:, to].astype(jnp.float32)
    gain_grad_ref[...] = jnp.broadcast_to(jnp.sum(gain_total, axis=1, keepdims=True), gain_grad_ref.shape)

    for r in range(4):
        pair_copy(r).wait_send()
        pair_copy_small(r).wait_send()
    for r in range(3):
        cross_copy(r).wait_send()
        cross_copy_small(r).wait_send()
    for k in range(1, parts):
        near_copy(k).wait_send()
    line_sent()


def end(dmixed, normed, weight, tokens, cotangent, gain, shard, small, parts, block):
    both = dmixed.shape[1]
    rows, width = tokens.shape
    own = shard.shape[0]
    dps, _, lanes = small.shape
    tall = parts * own
    vmem = pl.BlockSpec(memory_space=pltpu.VMEM)
    anywhere = pl.BlockSpec(memory_space=pl.ANY)
    dma = pltpu.SemaphoreType.DMA
    low = jnp.bfloat16
    return pl.pallas_call(
        lambda *refs: end_body(parts, block, *refs),
        out_shape=[
            jax.ShapeDtypeStruct((rows, width), low),
            jax.ShapeDtypeStruct((own, parts * both), low),
            jax.ShapeDtypeStruct((own, LANE), jnp.float32),
            jax.ShapeDtypeStruct((block, lanes), jnp.float32),
        ],
        in_specs=[anywhere] * 5 + [vmem] + [anywhere] * 2,
        out_specs=[vmem] * 4,
        scratch_shapes=[
            pltpu.VMEM((parts * rows, width), low),
            pltpu.VMEM((parts + 1, rows, width), low),
            pltpu.VMEM((4, tall, both), low), pltpu.VMEM((4, tall, both), low),
            pltpu.VMEM((3, tall, both), low), pltpu.VMEM((3, tall, both), low),
            pltpu.VMEM((tall, both), jnp.float32),
            pltpu.VMEM((tall, both), low), pltpu.VMEM((parts, own, both), low),
            pltpu.VMEM((4, block, lanes), low), pltpu.VMEM((4, block, lanes), low),
            pltpu.VMEM((3, block, lanes), low), pltpu.VMEM((3, block, lanes), low),
            dma((2, parts, 4)), dma((2, parts, 4)),
            dma((2, 4)), dma((2, 4)), dma((2, 3)), dma((2, 3)), dma((parts,)), dma((parts,)),
            *[pltpu.VMEM(a.shape, a.dtype) for a in (dmixed, normed, weight, tokens, cotangent, shard, small)], dma((7,)),
        ],
        compiler_params=pltpu.CompilerParams(
            collective_id=2, has_side_effects=True, vmem_limit_bytes=60 * 1024 * 1024
        ),
        cost_estimate=pl.CostEstimate(
            flops=4 * parts * rows * width * both, bytes_accessed=30 * 1024 * 1024, transcendentals=0
        ),
    )(dmixed, normed, weight, tokens, cotangent, gain, shard, small)


def linked_forward_body(
    states, parts, dps, taps,
    conv_in_ref, gate_ref, select_ref, vector_ref, weight_ref, out_shard, cot_shard, cot_early,
    mixed_ref, history_ref, final_ref, values_out, low_ref, kq_ref, dgated_out, result_out, out_part_ref, early_out,
    state_ref, key_ref, query_ref, rate_ref, input_ref, out_ref, row_ref, pick_ref, half_ref,
    part_low, part_kq, came_low, came_kq, sum_low, sum_kq,
    rs_send, rs_recv, ag_send, ag_recv, out_send, out_recv, line_send, line_recv, local_sem,
    out_all, cot_all, gated_all, out_total, values_ref, dgated_ref, result_ref, leave_sem, early_send, early_recv,
):
    d, s = lax.axis_index("dp"), lax.axis_index("seq")
    step = pl.program_id(0)
    length, channels = values_ref.shape
    rows = gate_ref.shape[0]
    span = length // parts
    block = out_shard.shape[0]
    chunk = span // 4
    packed = LANE // (2 * states)
    conv_w_ref, conv_b_ref = vector_ref, vector_ref[taps : taps + 1, :]
    bias_ref, skip_ref = vector_ref[taps + 1 : taps + 2, :], vector_ref[taps + 2 : taps + 3, :]
    short = span // packed

    def remote(src, dst, send, recv, to):
        return pltpu.make_async_remote_copy(
            src_ref=src, dst_ref=dst, send_sem=send, recv_sem=recv, device_id=to, device_id_type=MESH
        )

    def out_rows(owner):
        return out_all.at[pl.ds(pl.multiple_of(owner * block, block), block), :]

    out_copies = []
    for k in range(1, dps):
        out_copies.append(
            remote(out_shard, out_rows(d), out_send.at[k - 1], out_recv.at[k - 1], (lax.rem(d + k, dps), s))
        )

    inner = jnp.logical_and(s >= 1, s + 1 < parts)

    def cot_rows(part, c):
        return cot_all.at[pl.ds(pl.multiple_of(part * span + c * chunk, chunk), chunk), :]

    def cot_copy(way, distance, c):
        part = s - way * (distance - 1)
        side = 0 if way == 1 else 1
        piece = pl.ds(c * chunk, chunk)
        src = {1: cot_shard.at[piece, :], 2: cot_early.at[side, piece, :]}.get(distance)
        src = cot_rows(part, c) if src is None else src
        return remote(
            src, cot_rows(part, c), line_send.at[side, distance, c], line_recv.at[side, distance, c], (d, s + way)
        )

    def can_send(way, distance):
        if distance == 1:
            return s == parts - 2 if way == 1 else s == 1
        came = s >= distance - 1 if way == 1 else s + distance - 1 < parts
        return jnp.logical_and(inner, came)

    def arrives(way, distance):
        if distance == 1:
            return s == parts - 1 if way == 1 else s == 0
        return s >= distance if way == 1 else s + distance < parts

    def into_end(way):
        return s == parts - 2 if way == 1 else s == 1

    def send_cot(distance, c, which=None):
        for way in (1, -1):
            go = can_send(way, distance)
            if which is not None:
                go = jnp.logical_and(go, into_end(way) if which else jnp.logical_not(into_end(way)))

            @pl.when(go)
            def _():
                cot_copy(way, distance, c).start()

    def sent_cot(distance, c):
        for way in (1, -1):
            @pl.when(can_send(way, distance))
            def _():
                cot_copy(way, distance, c).wait_send()

    def take_cot(distance, c):
        for way in (1, -1):
            @pl.when(arrives(way, distance))
            def _():
                part = s - way * distance
                side = 0 if way == 1 else 1
                remote(
                    cot_rows(part, c), cot_rows(part, c), line_send.at[side, distance, c],
                    line_recv.at[side, distance, c], (d, s),
                ).wait_recv()

    def early_rows(way):
        side = 0 if way == 1 else 1
        return pltpu.make_async_copy(
            cot_early.at[side], cot_all.at[pl.ds(pl.multiple_of((s - way) * span, span), span), :], local_sem.at[3 + side]
        )

    def early_result(way):
        part = 1 if way == 1 else parts - 2
        side = 0 if way == 1 else 1
        return remote(
            result_ref.at[pl.ds(part * span, span), :], early_out, early_send.at[side], early_recv.at[side], (d, s + way)
        )

    def sends_result(way):
        return s == 0 if way == 1 else s == parts - 1

    def takes_result(way):
        return s == 1 if way == 1 else s == parts - 2

    def own_copies():
        return (
            pltpu.make_async_copy(out_shard, out_rows(d), local_sem.at[0]),
            pltpu.make_async_copy(
                cot_shard, cot_all.at[pl.ds(pl.multiple_of(s * span, span), span), :], local_sem.at[1]
            ),
        )

    @pl.when(step == 0)
    def _():
        barrier = pltpu.get_barrier_semaphore()
        for k in range(1, parts):
            pl.semaphore_signal(barrier, inc=1, device_id=(d, lax.rem(s + k, parts)), device_id_type=MESH)
        for k in range(1, dps):
            pl.semaphore_signal(barrier, inc=1, device_id=(lax.rem(d + k, dps), s), device_id_type=MESH)
        pl.semaphore_wait(barrier, parts + dps - 2)
        state_ref[...] = jnp.zeros_like(state_ref)
        for copy in out_copies:
            copy.start()
        for copy in own_copies():
            copy.start()
        for way in (1, -1):
            @pl.when(inner)
            def _():
                early_rows(way).start()

        send_cot(1, 0)
        send_cot(2, 0, False)

    def rs_copies(k):
        at = lax.rem(s + k, parts)
        return (
            remote(part_low.at[at], came_low.at[k - 1], rs_send.at[0, k - 1], rs_recv.at[0, k - 1], (d, at)),
            remote(part_kq.at[at], came_kq.at[k - 1], rs_send.at[1, k - 1], rs_recv.at[1, k - 1], (d, at)),
        )

    def ag_copies(k):
        to = lax.rem(s + k, parts)
        return (
            remote(sum_low.at[s], sum_low.at[s], ag_send.at[0, k - 1], ag_recv.at[0, k - 1], (d, to)),
            remote(sum_kq.at[s], sum_kq.at[s], ag_send.at[1, k - 1], ag_recv.at[1, k - 1], (d, to)),
        )

    def ag_taken(k, part):
        return (
            remote(sum_low.at[part], sum_low.at[part], ag_send.at[0, k - 1], ag_recv.at[0, k - 1], (d, s)),
            remote(sum_kq.at[part], sum_kq.at[part], ag_send.at[1, k - 1], ag_recv.at[1, k - 1], (d, s)),
        )

    def convolve(part):
        start = pl.multiple_of(part * span, span)
        before = pl.multiple_of(jnp.maximum(start - 16, 0), 16)
        wide = min(256, channels)
        for left in range(0, channels, wide):
            cols = slice(left, left + wide)
            head = conv_in_ref[pl.ds(before, 16), cols].astype(jnp.float32)
            head = jnp.where(part == 0, 0.0, head)
            body = jnp.concatenate([head, conv_in_ref[pl.ds(start, span), cols].astype(jnp.float32)], axis=0)
            total = conv_b_ref[:, cols]
            for tap in range(taps):
                by = taps - 1 - tap
                total = total + body[16 - by : 16 - by + span] * conv_w_ref[tap : tap + 1, cols]
            values_ref[pl.ds(start, span), cols] = (total * sigmoid(total)).astype(jnp.bfloat16)
        projected = jnp.dot(values_ref[pl.ds(start, span), :], select_ref[...], preferred_element_type=jnp.float32)
        part_low[part] = projected[:, :LANE].astype(jnp.bfloat16)
        pack = projected[:short, LANE:]
        for g in range(1, packed):
            pack = pack + pltpu.roll(projected[g * short : (g + 1) * short, LANE:], g * 2 * states, 1)
        part_kq[part] = pack

    @pl.when(step < parts - 1)
    def _():
        convolve(lax.rem(s + 1 + step, parts))

    for k in range(1, parts):
        @pl.when(step == k - 1)
        def _():
            for copy in rs_copies(k):
                copy.start()

    @pl.when(step == parts - 1)
    def _():
        convolve(s)
        low = part_low[s].astype(jnp.float32)
        kq = part_kq[s]
        for k in range(1, parts):
            for copy in rs_copies(k):
                copy.wait_recv()
            low = low + came_low[k - 1].astype(jnp.float32)
            kq = kq + came_kq[k - 1]
        sum_low[s] = low.astype(jnp.bfloat16)
        sum_kq[s] = kq
        for k in range(1, parts):
            for copy in ag_copies(k):
                copy.start()
        send_cot(1, 1)
        send_cot(2, 1, False)

    per_part = span // rows
    at_block = step - parts

    def unpack(part):
        start = pl.multiple_of(part * span, span)
        low_ref[pl.ds(start, span), :] = sum_low[part]
        pack = sum_kq[part]
        lane = lax.broadcasted_iota(jnp.int32, pack.shape, 1)
        for g in range(packed):
            turned = pack if g == 0 else pltpu.roll(pack, LANE - g * 2 * states, 1)
            kq_ref[pl.ds(pl.multiple_of(start + g * short, short), short), :] = jnp.where(lane < 2 * states, turned, 0.0)

    for part in range(parts):
        @pl.when(at_block == part * per_part)
        def _():
            for k in range(1, parts):
                @pl.when(lax.rem(s - k + parts, parts) == part)
                def _():
                    for copy in ag_taken(k, part):
                        copy.wait_recv()

            unpack(part)

    plan = (
        (("own", 2), ("inner", 2), ("own", 3)), (("inner", 3), ("outer", 0)), (("outer", 1), ("outer", 2)),
        (("outer", 3), ("last", 0)), (("last", 1),), (("last", 2),), (("last", 3),),
    )
    for at, moves in enumerate(plan):
        @pl.when(at_block == at)
        def _():
            for kind, c in moves:
                if kind == "own":
                    send_cot(1, c)
                elif kind == "last":
                    take_cot(2, c)
                    send_cot(3, c)
                else:
                    send_cot(2, c, kind == "outer")

    @pl.when(jnp.logical_and(at_block >= 0, at_block < length // rows))
    def _():
        here = pl.ds(pl.multiple_of(at_block * rows, rows), rows)
        kq = kq_ref[here, :]
        values = values_ref[here, :].astype(jnp.float32)
        beta, inverse = step_sizes(low_ref[here, :], kq, weight_ref, bias_ref, states)
        rates = beta * inverse
        rate_ref[...] = by_eights(rates)
        input_ref[...] = by_eights(rates * values)
        spread_columns(kq, row_ref, pick_ref, key_ref, query_ref, states)
        forward_rows(states, rows, channels, history_ref, state_ref, key_ref, query_ref, rate_ref, input_ref, out_ref, half_ref)
        mixed = as_rows(out_ref[...]) + skip_ref[...] * values
        gate = gate_ref[...]
        mixed_ref[...] = mixed
        gated_all[here, :] = (mixed * gate * sigmoid(gate)).astype(jnp.bfloat16)

    width = cot_all.shape[1]
    tile = min(512, width)

    def leaving(part, which):
        here = pl.ds(pl.multiple_of(part * span, span), span)
        ref, out = ((dgated_ref, dgated_out), (result_ref, result_out))[which]
        return pltpu.make_async_copy(ref.at[here, :], out.at[here, :], leave_sem.at[part, which])

    values_copy = pltpu.make_async_copy(values_ref, values_out, local_sem.at[2])

    @pl.when(step == parts)
    def _():
        values_copy.start()

    def products(part):
        here = pl.ds(pl.multiple_of(part * span, span), span)

        def across(n, carry):
            cols = pl.ds(pl.multiple_of(n * tile, tile), tile)
            out_total[:, cols] += lax.dot_general(
                gated_all[here, :], cot_all[here, cols], (((0,), (0,)), ((), ())), preferred_element_type=jnp.float32
            )
            return carry

        lax.fori_loop(0, width // tile, across, 0)
        deep = min(512, channels)

        def along(n, carry):
            cols = pl.ds(pl.multiple_of(n * deep, deep), deep)
            dgated_ref[here, cols] = lax.dot_general(
                cot_all[here, :], out_all[cols, :], (((1,), (1,)), ((), ())), preferred_element_type=jnp.float32
            )
            return carry

        lax.fori_loop(0, channels // deep, along, 0)
        leaving(part, 0).start()

    def result_terms(part):
        here = pl.ds(part * span, span)

        def across(n, carry):
            cols = pl.ds(pl.multiple_of(n * tile, tile), tile)
            result_ref[here, cols] = jnp.dot(
                gated_all[here, :], out_all[:, cols], preferred_element_type=jnp.float32
            ).astype(jnp.bfloat16)
            return carry

        lax.fori_loop(0, width // tile, across, 0)
        leaving(part, 1).start()

    @pl.when(at_block == length // rows - per_part)
    def _():
        own_copies()[0].wait()
        for copy in out_copies:
            copy.wait_recv()
        for part in range(parts - 1):
            result_terms(part)
        for way in (1, -1):
            @pl.when(sends_result(way))
            def _():
                early_result(way).start()

    def products_at(low, high):
        def each(part, carry):
            away = jnp.abs(part - s)

            @pl.when(jnp.logical_and(away >= low, away <= high))
            def _():
                products(part)

            return carry

        lax.fori_loop(0, parts, each, 0)

    @pl.when(step == pl.num_programs(0) - 1)
    def _():
        final_ref[...] = state_ref[...]
        out_total[...] = jnp.zeros_like(out_total)
        own_copies()[1].wait()
        for way in (1, -1):
            @pl.when(inner)
            def _():
                early_rows(way).wait()

        result_terms(parts - 1)
        products_at(0, 0)
        for c in range(4):
            take_cot(1, c)
        products_at(1, 1)
        products_at(2, parts - 2)
        for c in range(4):
            take_cot(parts - 1, c)
        products_at(parts - 1, parts - 1)
        out_part_ref[...] = out_total[...].astype(jnp.bfloat16)
        values_copy.wait()
        for way in (1, -1):
            @pl.when(takes_result(way))
            def _():
                early_result(way).wait_recv()

            @pl.when(sends_result(way))
            def _():
                early_result(way).wait_send()

        for part in range(parts):
            leaving(part, 0).wait()
            leaving(part, 1).wait()
        for copy in out_copies:
            copy.wait_send()
        for distance in range(1, parts):
            for c in range(4):
                sent_cot(distance, c)
        for k in range(1, parts):
            for copy in rs_copies(k) + ag_copies(k):
                copy.wait_send()


def linked_forward(
    conv_in, gate, select, vectors, weight, out_shard, cot_shard, cot_early, parts, dps, taps, states
):
    length, channels = conv_in.shape
    block, width = out_shard.shape
    span = length // parts
    rows = min(128, span)
    blocks = length // rows
    short = span // (LANE // (2 * states))
    at = lambda i: jnp.clip(i - parts, 0, blocks - 1)
    by_row = lambda size: pl.BlockSpec((rows, size), lambda i: (at(i), 0))
    whole = lambda a: pl.BlockSpec(a.shape, lambda i: (0, 0))
    kept = lambda *shape: pl.BlockSpec(shape, lambda i: (0, 0))
    anywhere = pl.BlockSpec(memory_space=pl.ANY)
    dma = pltpu.SemaphoreType.DMA
    f32, low = jnp.float32, jnp.bfloat16
    eights = pltpu.VMEM((rows // 8, 8, channels), f32)
    return pl.pallas_call(
        lambda *refs: linked_forward_body(states, parts, dps, taps, *refs),
        grid=(parts + blocks + 1,),
        in_specs=[
            whole(conv_in), by_row(channels), whole(select), whole(vectors), whole(weight), anywhere, anywhere,
            anywhere,
        ],
        out_specs=[
            by_row(channels), pl.BlockSpec((rows * states, channels), lambda i: (at(i), 0)),
            kept(states, channels), anywhere, kept(length, LANE), kept(length, LANE),
            anywhere, anywhere, kept(dps * block, width), anywhere,
        ],
        out_shape=[
            jax.ShapeDtypeStruct((length, channels), f32),
            jax.ShapeDtypeStruct((length * states, channels), low),
            jax.ShapeDtypeStruct((states, channels), f32),
            jax.ShapeDtypeStruct((length, channels), low),
            jax.ShapeDtypeStruct((length, LANE), low),
            jax.ShapeDtypeStruct((length, LANE), f32),
            jax.ShapeDtypeStruct((length, channels), f32),
            jax.ShapeDtypeStruct((length, width), low),
            jax.ShapeDtypeStruct((dps * block, width), low),
            jax.ShapeDtypeStruct((span, width), low),
        ],
        scratch_shapes=[
            pltpu.VMEM((states, channels), f32),
            pltpu.VMEM((rows * states, LANE), f32), pltpu.VMEM((rows * states, LANE), f32),
            eights, eights, eights, pltpu.VMEM((rows // 8, 8, LANE), f32),
            pltpu.VMEM((rows * states, LANE), low), pltpu.VMEM((channels // LANE * 64, LANE), f32),
            pltpu.VMEM((parts, span, LANE), low), pltpu.VMEM((parts, short, LANE), f32),
            pltpu.VMEM((parts - 1, span, LANE), low), pltpu.VMEM((parts - 1, short, LANE), f32),
            pltpu.VMEM((parts, span, LANE), low), pltpu.VMEM((parts, short, LANE), f32),
            dma((2, parts - 1)), dma((2, parts - 1)), dma((2, parts - 1)), dma((2, parts - 1)),
            dma((dps - 1,)), dma((dps - 1,)), dma((2, parts, 4)), dma((2, parts, 4)), dma((5,)),
            pltpu.VMEM((dps * block, width), low), pltpu.VMEM((length, width), low), pltpu.VMEM((length, channels), low),
            pltpu.VMEM((dps * block, width), f32), pltpu.VMEM((length, channels), low),
            pltpu.VMEM((length, channels), f32), pltpu.VMEM((length, width), low), dma((parts, 2)), dma((2,)), dma((2,)),
        ],
        compiler_params=pltpu.CompilerParams(
            collective_id=4, has_side_effects=True, vmem_limit_bytes=60 * 1024 * 1024
        ),
        cost_estimate=pl.CostEstimate(
            flops=14 * length * states * channels, bytes_accessed=2 * length * states * channels, transcendentals=0
        ),
    )(conv_in, gate, select, vectors, weight, out_shard, cot_shard, cot_early)


def linked_backward_body(
    states, parts, dps, taps,
    low_ref, kq_ref, gate_ref, mixed_ref, dgated_ref, history_ref, final_ref, weight_ref,
    values_ref, conv_in_ref, select_ref, given_ref, tokens_ref, early_ref, part_hbm, out_ref,
    dmixed_out, small_ref, result_ref, out_grad_ref,
    grad_ref, state_ref, key_ref, query_ref, rate_ref, do_ref, values32_ref, fed_ref, kept_ref, part_key_ref,
    part_query_ref, row_ref, placed_ref, pick_ref, wide_ref, half_ref,
    dvalues_ref, dproj_ref, next_ref, vector_ref, part_low, part_kq, came_low, came_kq, sum_low, sum_kq,
    rs_send, rs_recv, ag_send, ag_recv, result_came, line_send, line_recv, out_send, out_recv,
    out_came, out_here, local_sem, dmixed_ref, part_ref, leave_sem,
):
    d, s = lax.axis_index("dp"), lax.axis_index("seq")
    step = pl.program_id(0)
    rows, channels = gate_ref.shape
    length = values_ref.shape[0]
    blocks = length // rows
    span = length // parts
    per_part = span // rows
    packed = LANE // (2 * states)
    short = span // packed
    sel = select_ref.shape[1]
    conv_w_ref, conv_b_ref = given_ref, given_ref[taps : taps + 1, :]
    bias_ref, skip_ref = given_ref[taps + 1 : taps + 2, :], given_ref[taps + 2 : taps + 3, :]

    def remote(src, dst, send, recv, to):
        return pltpu.make_async_remote_copy(
            src_ref=src, dst_ref=dst, send_sem=send, recv_sem=recv, device_id=to, device_id_type=MESH
        )

    copies = []
    for k in range(1, dps):
        to = lax.rem(d + k, dps)
        copies.append(remote(out_ref.at[to], out_came.at[k - 1], out_send.at[k - 1], out_recv.at[k - 1], (to, s)))
    out_copy = pltpu.make_async_copy(out_ref.at[d], out_here, local_sem.at[0])
    part_copy = pltpu.make_async_copy(part_hbm, part_ref, local_sem.at[1])
    pass_line, line_total, line_sent = line_sums(parts, span, part_ref, result_came, line_send, line_recv, early_ref)

    @pl.when(step == 0)
    def _():
        part_copy.start()
        barrier = pltpu.get_barrier_semaphore()
        for k in range(1, parts):
            pl.semaphore_signal(barrier, inc=1, device_id=(d, lax.rem(s + k, parts)), device_id_type=MESH)
        for k in range(1, dps):
            pl.semaphore_signal(barrier, inc=1, device_id=(lax.rem(d + k, dps), s), device_id_type=MESH)
        pl.semaphore_wait(barrier, parts + dps - 2)
        grad_ref[...] = jnp.zeros_like(grad_ref)
        state_ref[...] = final_ref[...]
        next_ref[...] = jnp.zeros_like(next_ref)
        vector_ref[...] = jnp.zeros_like(vector_ref)
        small_ref[...] = jnp.zeros_like(small_ref)
        for copy in copies:
            copy.start()
        out_copy.start()
        part_copy.wait()

    def rs_copies(k):
        at = lax.rem(s + k, parts)
        return (
            remote(part_low.at[at], came_low.at[k - 1], rs_send.at[0, k - 1], rs_recv.at[0, k - 1], (d, at)),
            remote(part_kq.at[at], came_kq.at[k - 1], rs_send.at[1, k - 1], rs_recv.at[1, k - 1], (d, at)),
        )

    def ag_copies(k):
        to = lax.rem(s + k, parts)
        return (
            remote(sum_low.at[s], sum_low.at[s], ag_send.at[0, k - 1], ag_recv.at[0, k - 1], (d, to)),
            remote(sum_kq.at[s], sum_kq.at[s], ag_send.at[1, k - 1], ag_recv.at[1, k - 1], (d, to)),
        )

    def ag_taken(k, part):
        return (
            remote(sum_low.at[part], sum_low.at[part], ag_send.at[0, k - 1], ag_recv.at[0, k - 1], (d, s)),
            remote(sum_kq.at[part], sum_kq.at[part], ag_send.at[1, k - 1], ag_recv.at[1, k - 1], (d, s)),
        )

    def add_up():
        low = part_low[s].astype(jnp.float32)
        kq = part_kq[s]
        for k in range(1, parts):
            for copy in rs_copies(k):
                copy.wait_recv()
            low = low + came_low[k - 1].astype(jnp.float32)
            kq = kq + came_kq[k - 1]
        sum_low[s] = low.astype(jnp.bfloat16)
        sum_kq[s] = kq.astype(jnp.bfloat16)
        for k in range(1, parts):
            for copy in ag_copies(k):
                copy.start()

    def leaving(part):
        here = pl.ds(pl.multiple_of(part * span, span), span)
        return pltpu.make_async_copy(dmixed_ref.at[here, :], dmixed_out.at[here, :], leave_sem.at[part])

    def conv_back(part):
        for k in range(1, parts):
            @pl.when(lax.rem(s - k + parts, parts) == part)
            def _():
                for copy in ag_taken(k, part):
                    copy.wait_recv()

        here = pl.ds(pl.multiple_of(part * span, span), span)
        before = pl.multiple_of(jnp.maximum(part * span - 16, 0), 16)
        dproj_ref[:, :LANE] = sum_low[part]
        pack = sum_kq[part].astype(jnp.float32)
        lane = lax.broadcasted_iota(jnp.int32, pack.shape, 1)
        for g in range(packed):
            turned = pack if g == 0 else pltpu.roll(pack, LANE - g * 2 * states, 1)
            dproj_ref[g * short : (g + 1) * short, LANE:] = jnp.where(lane < 2 * states, turned, 0.0).astype(jnp.bfloat16)
        wide = min(256, channels)
        for left in range(0, channels, wide):
            cols = slice(left, left + wide)
            small_ref[cols, :sel] += lax.dot_general(
                values_ref[here, cols], dproj_ref[...], (((0,), (0,)), ((), ())), preferred_element_type=jnp.float32
            )
            head = conv_in_ref[pl.ds(before, 16), cols].astype(jnp.float32)
            head = jnp.where(part == 0, 0.0, head)
            body = jnp.concatenate([head, conv_in_ref[here, cols].astype(jnp.float32)], axis=0)
            total = conv_b_ref[:, cols]
            for tap in range(taps):
                by = taps - 1 - tap
                total = total + body[16 - by : 16 - by + span] * conv_w_ref[tap : tap + 1, cols]
            sg = sigmoid(total)
            dvalues = dvalues_ref[here, cols] + lax.dot_general(
                dproj_ref[...], select_ref[cols, :], (((1,), (1,)), ((), ())), preferred_element_type=jnp.float32
            )
            dconv = dvalues * (sg + total * sg * (1.0 - sg))
            vector_ref[taps : taps + 1, cols] += jnp.sum(dconv, axis=0, keepdims=True)
            after = jnp.concatenate([dconv, next_ref[:, cols]], axis=0)
            dconv_in = jnp.zeros_like(dconv)
            for tap in range(taps):
                by = taps - 1 - tap
                shifted = body[16 - by : 16 - by + span]
                vector_ref[tap : tap + 1, cols] += jnp.sum(dconv * shifted, axis=0, keepdims=True)
                dconv_in = dconv_in + after[by : by + span] * conv_w_ref[tap : tap + 1, cols]
            next_ref[:, cols] = dconv[0:8]
            dmixed_ref[here, cols] = dconv_in.astype(jnp.bfloat16)
        leaving(part).start()

    plan = (((3, 0), (3, 1)), ((3, 2), (3, 3)), ((2, 0), (2, 1)), ((2, 2), (2, 3)), ((1, 0), (1, 1)), ((1, 2), (1, 3)))
    for at_step, moves in enumerate(plan):
        @pl.when(step == at_step)
        def _():
            for steps, c in moves:
                pass_line(steps, c)

    for part in range(parts):
        ends = (parts - part) * per_part - 1
        sums = min(ends + 3, blocks - 1 if part > 0 else blocks)

        @pl.when(jnp.logical_and(step == sums, s == part))
        def _():
            add_up()

        @pl.when(step == blocks + 1 - part)
        def _():
            conv_back(part)

    @pl.when(step < blocks)
    def _():
        block = blocks - 1 - step
        here = pl.ds(pl.multiple_of(block * rows, rows), rows)
        low, kq = low_ref[...], kq_ref[...]
        beta, inverse = step_sizes(low, kq, weight_ref, bias_ref, states)
        rate_ref[...] = by_eights(beta * inverse)
        values = values_ref[here, :].astype(jnp.float32)
        values32_ref[...] = by_eights(values)
        gate = gate_ref[...]
        dgated = dgated_ref[...].astype(jnp.float32)
        sg = sigmoid(gate)
        do = dgated * (gate * sg)
        do_ref[...] = by_eights(do)
        dmixed_ref[here, channels:] = (dgated * mixed_ref[...] * (sg + gate * sg * (1.0 - sg))).astype(jnp.bfloat16)
        vector_ref[taps + 2 : taps + 3, :] += jnp.sum(do * values, axis=0, keepdims=True)
        spread_columns(kq, row_ref, pick_ref, key_ref, query_ref, states)
        backward_rows(
            states, rows, channels, history_ref, grad_ref, state_ref, key_ref, query_ref, rate_ref, do_ref, values32_ref,
            fed_ref, kept_ref, part_key_ref, part_query_ref, half_ref,
        )
        fed = as_rows(fed_ref[...])
        dvalues_ref[here, :] = fed + skip_ref[...] * as_rows(do_ref[...])
        scaled = as_rows(values32_ref[...]) * fed - as_rows(kept_ref[...])
        beta, inverse = step_sizes(low, kq, weight_ref, bias_ref, states)
        dpre = scaled * (1.0 - beta) * inverse
        vector_ref[taps + 1 : taps + 2, :] += jnp.sum(dpre, axis=0, keepdims=True)
        dpre_low = dpre.astype(jnp.bfloat16)
        small_ref[:, sel : sel + LANE] += lax.dot_general(
            dpre_low, low, (((0,), (0,)), ((), ())), preferred_element_type=jnp.float32
        )
        through = -2.0 * jnp.sum(scaled * beta * inverse, axis=1, keepdims=True)
        gather_columns(part_key_ref, part_query_ref, wide_ref, placed_ref, rows, states)
        lanes = lax.broadcasted_iota(jnp.int32, kq.shape, 1)
        dkq = as_rows(placed_ref[...]) + jnp.where(lanes < states, kq * through, 0.0)
        part = block // per_part
        within = lax.rem(block, per_part)
        part_low[part, pl.ds(pl.multiple_of(within * rows, rows), rows), :] = jnp.dot(
            dpre_low, weight_ref[...], preferred_element_type=jnp.float32
        ).astype(jnp.bfloat16)
        for g in range(packed):
            first = g * short - within * rows

            @pl.when(jnp.logical_and(first >= 0, first < rows))
            def _():
                for w in range(per_part):
                    if w * rows <= g * short < (w + 1) * rows:
                        lo = g * short - w * rows
                        piece = dkq[lo : lo + short]
                        piece = piece if g == 0 else pltpu.roll(piece, g * 2 * states, 1)
                        if g == (per_part - 1) * rows // short:
                            part_kq[part] = piece
                        else:
                            part_kq[part] += piece

        @pl.when(within == 0)
        def _():
            for k in range(1, parts):
                @pl.when(lax.rem(s + k, parts) == part)
                def _():
                    for copy in rs_copies(k):
                        copy.start()

    @pl.when(step == pl.num_programs(0) - 1)
    def _():
        small_ref[:, sel + LANE :] = jnp.transpose(vector_ref[...])
        chunk = span // 4
        for c in range(4):
            at = pl.ds(c * chunk, chunk)
            result_ref[at, :] = (tokens_ref[at, :].astype(jnp.float32) + line_total(c)).astype(jnp.bfloat16)
        line_sent()
        for part in range(parts):
            leaving(part).wait()
        out_copy.wait()
        total = out_here[...].astype(jnp.float32)
        for k in range(1, dps):
            copies[k - 1].wait_recv()
            total = total + out_came[k - 1].astype(jnp.float32)
        out_grad_ref[...] = total
        for copy in copies:
            copy.wait_send()
        for k in range(1, parts):
            for copy in rs_copies(k) + ag_copies(k):
                copy.wait_send()


def linked_backward(
    low, kq, gate, mixed, dgated, history, final, weight, values, conv_in, select, vectors, tokens, early,
    result_part, out_part, parts, taps, states,
):
    length, channels = values.shape
    dps = out_part.shape[0]
    width = tokens.shape[1]
    sel = select.shape[1]
    span = length // parts
    rows = min(128, span)
    blocks = length // rows
    short = span // (LANE // (2 * states))
    at = lambda i: jnp.maximum(blocks - 1 - i, 0)
    by_row = lambda size: pl.BlockSpec((rows, size), lambda i: (at(i), 0))
    whole = lambda a: pl.BlockSpec(a.shape, lambda i: (0, 0))
    kept = lambda *shape: pl.BlockSpec(shape, lambda i: (0, 0))
    anywhere = pl.BlockSpec(memory_space=pl.ANY)
    dma = pltpu.SemaphoreType.DMA
    f32, bf16 = jnp.float32, jnp.bfloat16
    wide = pltpu.VMEM((rows // 8, 8, channels), f32)
    eights = pltpu.VMEM((rows // 8, 8, LANE), f32)
    spread = pltpu.VMEM((rows * states, LANE), f32)
    return pl.pallas_call(
        lambda *refs: linked_backward_body(states, parts, dps, taps, *refs),
        grid=(blocks + 2,),
        in_specs=[
            by_row(LANE), by_row(LANE), by_row(channels), by_row(channels), by_row(channels),
            pl.BlockSpec((rows * states, channels), lambda i: (at(i), 0)),
            whole(final), whole(weight), whole(values), whole(conv_in), whole(select), whole(vectors), whole(tokens),
            whole(early), anywhere, anywhere,
        ],
        out_specs=[anywhere, kept(channels, sel + 2 * LANE), kept(span, width), kept(*out_part.shape[1:])],
        out_shape=[
            jax.ShapeDtypeStruct((length, 2 * channels), bf16),
            jax.ShapeDtypeStruct((channels, sel + 2 * LANE), f32),
            jax.ShapeDtypeStruct((span, width), bf16),
            jax.ShapeDtypeStruct(out_part.shape[1:], f32),
        ],
        scratch_shapes=[
            pltpu.VMEM((states, channels), f32), pltpu.VMEM((states, channels), f32),
            spread, spread, wide, wide, wide, wide, wide, spread, spread, eights, eights,
            pltpu.VMEM((rows * states, LANE), bf16), pltpu.VMEM((rows * states, 2 * LANE), bf16),
            pltpu.VMEM((2 * channels // LANE * 64, LANE), f32),
            pltpu.VMEM((length, channels), f32), pltpu.VMEM((span, sel), bf16), pltpu.VMEM((8, channels), f32),
            pltpu.VMEM((LANE, channels), f32),
            pltpu.VMEM((parts, span, LANE), bf16), pltpu.VMEM((parts, short, LANE), f32),
            pltpu.VMEM((parts - 1, span, LANE), bf16), pltpu.VMEM((parts - 1, short, LANE), f32),
            pltpu.VMEM((parts, span, LANE), bf16), pltpu.VMEM((parts, short, LANE), bf16),
            dma((2, parts - 1)), dma((2, parts - 1)), dma((2, parts - 1)), dma((2, parts - 1)),
            pltpu.VMEM((parts + 1, span, width), bf16), dma((2, parts, 4)), dma((2, parts, 4)),
            dma((dps - 1,)), dma((dps - 1,)), pltpu.VMEM((dps - 1,) + out_part.shape[1:], bf16),
            pltpu.VMEM(out_part.shape[1:], bf16), dma((2,)), pltpu.VMEM((length, 2 * channels), bf16),
            pltpu.VMEM((length, width), bf16), dma((parts,)),
        ],
        compiler_params=pltpu.CompilerParams(
            collective_id=5, has_side_effects=True, vmem_limit_bytes=60 * 1024 * 1024
        ),
        cost_estimate=pl.CostEstimate(
            flops=30 * length * states * channels, bytes_accessed=2 * length * states * channels, transcendentals=0
        ),
    )(low, kq, gate, mixed, dgated, history, final, weight, values, conv_in, select, vectors, tokens, early, result_part, out_part)


def contract(left, right, left_dim, right_dim):
    return lax.dot_general(
        left, right, (((left_dim,), (right_dim,)), ((), ())), preferred_element_type=jnp.float32
    )


def gathered(shard, axis):
    return lax.all_gather(shard, axis, axis=0, tiled=True)


def scattered(total, axis):
    return lax.psum_scatter(total, axis, scatter_dimension=0, tiled=True)


def summed_rows(partial, axis):
    size = lax.axis_size(axis)
    parts = partial.astype(jnp.bfloat16).reshape((size, partial.shape[0] // size) + partial.shape[1:])
    parts = lax.all_to_all(parts, axis, 0, 0)
    return jnp.sum(parts.astype(jnp.float32), axis=0)


def later(rows, by):
    if by == 0:
        return rows
    return jnp.pad(rows, ((by, 0), (0, 0)))[: rows.shape[0]]


def sooner(rows, by):
    if by == 0:
        return rows
    return jnp.pad(rows, ((0, by), (0, 0)))[by:]


def local(
    tokens,
    cotangent,
    norm_gain,
    in_weight,
    conv_weight,
    conv_bias,
    select_weight,
    beta_weight,
    beta_bias,
    skip_gain,
    out_weight,
):
    parts, dps = lax.axis_size("seq"), lax.axis_size("dp")
    rows, width = tokens.shape[1:]
    block = conv_weight.shape[0]
    channels = block * dps
    taps = conv_weight.shape[1]
    rank = beta_weight.shape[1]
    states = (select_weight.shape[1] - rank) // 2
    own = in_weight.shape[0]

    flat = tokens.reshape(rows, width).astype(jnp.float32)
    scale = lax.rsqrt(jnp.mean(flat * flat, axis=-1, keepdims=True) + 1e-05)
    vectors = jnp.concatenate(
        [conv_weight, conv_bias[:, None], beta_bias[:, None], skip_gain[:, None]], axis=1
    )
    wide = -(-select_weight.shape[1] // LANE) * LANE
    small = jnp.concatenate(
        [
            jnp.pad(select_weight, ((0, 0), (0, wide - select_weight.shape[1]))),
            beta_weight,
            jnp.pad(vectors, ((0, 0), (0, LANE - vectors.shape[1]))),
        ],
        axis=1,
    )
    small_slice = (dps, parts, 2 * own, rank) == (8, 4, LANE, LANE)
    if small_slice:
        doubled = jnp.broadcast_to(jnp.tile(norm_gain.reshape(1, own), (1, 2)), (GAIN_ROWS, LANE))
        normed, in_w, conv_in, gate, select_w, beta_w, vectors, gain, cot_early = start(
            tokens.reshape(rows, width), in_weight, small, doubled, cotangent.reshape(rows, width), parts, dps
        )
    else:
        gain = gathered(norm_gain, ("dp", "seq"))
        normed = gathered((flat * scale * gain.astype(jnp.float32)).astype(jnp.bfloat16), "seq")
        spread = in_weight.reshape(own, 2, dps, parts, block).transpose(3, 0, 1, 2, 4).reshape(parts, own, 2 * channels)
        in_w = gathered(lax.all_to_all(spread, "seq", 0, 0).reshape(parts * own, 2 * channels), "dp")
        smalls = gathered(small, "dp")
        conv_in = jnp.dot(normed, in_w[:, :channels], preferred_element_type=jnp.float32).astype(jnp.bfloat16)
        gate = jnp.dot(normed, in_w[:, channels:], preferred_element_type=jnp.float32)
    cot_here = cotangent.reshape(rows, width)
    if small_slice:
        mixed, history, final, values, low, kq, dgated, result_part, out_part, early = linked_forward(
            conv_in, gate, select_w, vectors, beta_w, out_weight, cot_here, cot_early, parts, dps, taps, states,
        )
    else:
        gain = gain.astype(jnp.float32)
        select_w = smalls[:, : select_weight.shape[1]]
        beta_w = smalls[:, wide : wide + rank]
        vectors = smalls[:, wide + rank :].astype(jnp.float32)
        conv_w, conv_b = vectors[:, :taps], vectors[:, taps]
        beta_b, skip = vectors[:, taps + 1].reshape(1, channels), vectors[:, taps + 2].reshape(1, channels)
        conv_wide = conv_in.astype(jnp.float32)
        conv_sum = conv_b
        for tap in range(taps):
            conv_sum = conv_sum + later(conv_wide, taps - 1 - tap) * conv_w[:, tap]
        out_w = gathered(out_weight, "dp")
        cot = gathered(cot_here, "seq")
        values = jax.nn.silu(conv_sum).astype(jnp.bfloat16)
        projected = lax.psum(jnp.dot(values, select_w, preferred_element_type=jnp.float32), "seq")
        low = projected[:, :rank].astype(jnp.bfloat16)
        kq = jnp.pad(projected[:, rank:], ((0, 0), (0, LANE - 2 * states)))
        gated, mixed, history, final = forward_scan(low, kq, values, gate, beta_w, beta_b, skip, states)
        result_part = jnp.dot(gated, out_w, preferred_element_type=jnp.float32).astype(jnp.bfloat16)
        out_part = contract(gated, cot, 0, 0).astype(jnp.bfloat16)
        dgated = contract(cot, out_w, 1, 1)
    out_part = out_part.reshape(dps, block, width)
    if small_slice:
        dmixed, small_grads, result, out_grad = linked_backward(
            low, kq, gate, mixed, dgated, history, final, beta_w, values, conv_in, select_w, vectors,
            tokens.reshape(rows, width), early, result_part, out_part, parts, taps, states,
        )
        small_grads = small_grads.reshape(dps, block, wide + rank + LANE)
    else:
        result_part = result_part.reshape(parts, rows, width)
        dgate, dpre_low, dvalues, dlow, dkq, bias_grad, skip_grad, result_came, out_came = backward_scan(
            low, kq, values, gate, mixed, dgated, history, final, beta_w, beta_b, skip, result_part, out_part, states
        )
        part_here = lax.dynamic_index_in_dim(result_part, lax.axis_index("seq"), 0, False).astype(jnp.float32)
        result = (flat + (part_here + jnp.sum(result_came.astype(jnp.float32), axis=0))).astype(jnp.bfloat16)
        out_here = lax.dynamic_index_in_dim(out_part, lax.axis_index("dp"), 0, False).astype(jnp.float32)
        out_grad = out_here + jnp.sum(out_came.astype(jnp.float32), axis=0)
        dprojected = lax.psum(jnp.concatenate([dlow, dkq[:, : 2 * states]], axis=1), "seq").astype(jnp.bfloat16)
        beta_grad = contract(dpre_low, low, 0, 0)
        select_grad = contract(values, dprojected, 0, 0)
        dvalues = contract(dprojected, select_w, 1, 1) + dvalues
        s = jax.nn.sigmoid(conv_sum)
        dconv = dvalues * (s + conv_sum * s * (1.0 - s))
        conv_w_grad = jnp.stack(
            [jnp.sum(dconv * later(conv_wide, taps - 1 - tap), axis=0) for tap in range(taps)], axis=1
        )
        conv_b_grad = jnp.sum(dconv, axis=0)
        dconv_in = 0.0
        for tap in range(taps):
            dconv_in = dconv_in + sooner(dconv, taps - 1 - tap) * conv_w[:, tap]
        dmixed = jnp.concatenate([dconv_in.astype(jnp.bfloat16), dgate], axis=1)
        vector_grads = jnp.concatenate(
            [conv_w_grad, conv_b_grad[:, None], bias_grad.reshape(channels, 1), skip_grad.reshape(channels, 1)], axis=1
        )
        small_grads = jnp.concatenate(
            [
                jnp.pad(select_grad, ((0, 0), (0, wide - select_grad.shape[1]))),
                beta_grad,
                jnp.pad(vector_grads, ((0, 0), (0, LANE - vector_grads.shape[1]))),
            ],
            axis=1,
        ).reshape(dps, block, wide + rank + LANE)
    if small_slice:
        input_grad, in_grad, gain_sums, small_grads = end(
            dmixed, normed, in_w, tokens.reshape(rows, width), cot_here, gain, in_weight, small_grads,
            parts, block,
        )
        gain_sums = gain_sums[:, 0]
    else:
        in_grad = summed_rows(contract(normed, dmixed, 0, 0), "dp").astype(jnp.bfloat16)
        in_grad = lax.all_to_all(in_grad.reshape(parts, own, 2 * channels), "seq", 0, 0).astype(jnp.float32)
        in_grad = in_grad.reshape(parts, own, 2, dps, block).transpose(1, 2, 3, 0, 4).reshape(own, 2 * parts * channels)
        gain_sums = jnp.sum(in_grad * in_weight.astype(jnp.float32), axis=1)
        v = summed_rows(contract(dmixed, in_w, 1, 1), "seq") * gain
        du = scale * v - flat * (scale * scale * scale) * jnp.mean(flat * v, axis=-1, keepdims=True)
        input_grad = (cot_here.astype(jnp.float32) + du).astype(jnp.bfloat16)
        small_grads = jnp.sum(lax.all_to_all(small_grads, "dp", 0, 0), axis=0)
    rows_grad = small_grads[:, wide + rank :]
    return (
        result.reshape(tokens.shape),
        input_grad.reshape(tokens.shape),
        gain_sums / norm_gain.astype(jnp.float32),
        in_grad.astype(jnp.float32),
        rows_grad[:, :taps],
        rows_grad[:, taps],
        small_grads[:, : select_weight.shape[1]],
        small_grads[:, wide : wide + rank],
        rows_grad[:, taps + 1],
        rows_grad[:, taps + 2],
        out_grad,
    )


def solution(mesh):
    split = P(("dp", "seq"))
    rows = P("dp", "seq", None)
    return jax.shard_map(
        local,
        mesh=mesh,
        in_specs=(rows, rows) + (split,) * 9,
        out_specs=(rows, rows) + (split,) * 9,
        check_vma=False,
    )
```

```python
import jax
import jax.numpy as jnp
from jax import lax
from jax.experimental import pallas as pl
from jax.experimental.pallas import tpu as pltpu
from jax.sharding import PartitionSpec as P

LANE = 128
PER_GROUP = 4


def sigmoid(v):
    return 1.0 / (1.0 + jnp.exp(-v))


def by_eights(value):
    return value.reshape(value.shape[0] // 8, 8, value.shape[1])


def as_rows(value):
    return value.reshape(value.shape[0] * 8, value.shape[2])


def spread_columns(kq, row_ref, pick_ref, key_ref, query_ref, states):
    rows = kq.shape[0]
    high = kq.astype(jnp.bfloat16).astype(jnp.float32)
    rest = kq - high
    middle = rest.astype(jnp.bfloat16).astype(jnp.float32)
    row_ref[...] = by_eights(high + pltpu.roll(middle, 2 * states, 1) + pltpu.roll(rest - middle, 4 * states, 1))
    lane = lax.broadcasted_iota(jnp.int32, (states, LANE), 1)
    entry = lax.broadcasted_iota(jnp.int32, (states, LANE), 0)
    pick = lax.rem(lane, states) == entry

    def body(group, carry):
        for offset in range(8):
            at = pl.multiple_of((group * 8 + offset) * states, states)
            row = jnp.broadcast_to(row_ref[group, offset : offset + 1, :], (states, LANE))
            pick_ref[pl.ds(at, states), :] = jnp.where(pick, row, 0.0).astype(jnp.bfloat16)
        return carry

    lax.fori_loop(0, rows // 8, body, 0)
    term = lax.broadcasted_iota(jnp.int32, (LANE, 2 * LANE), 0)
    side = lax.broadcasted_iota(jnp.int32, (LANE, 2 * LANE), 1)
    is_query = lax.rem(term, 2 * states) >= states
    halves = jnp.where(is_query == (side >= LANE), 1.0, 0.0).astype(jnp.bfloat16)
    both = jnp.dot(pick_ref[...], halves, preferred_element_type=jnp.float32)
    key_ref[...] = both[:, :LANE]
    query_ref[...] = both[:, LANE:]


def sum_eights(half_ref, first):
    total = half_ref[pl.ds(first, 8, stride=8), :]
    for n in range(1, 8):
        total = total + half_ref[pl.ds(first + n, 8, stride=8), :]
    return total


def step_sizes(low, kq, weight_ref, bias_ref, states):
    pre = lax.dot_general(
        low, weight_ref[...], (((1,), (1,)), ((), ())), preferred_element_type=jnp.float32
    )
    beta = sigmoid(pre + bias_ref[...])
    lane = lax.broadcasted_iota(jnp.int32, kq.shape, 1)
    keys = jnp.where(lane < states, kq, 0.0)
    square = jnp.sum(keys * keys, axis=1, keepdims=True)
    return beta, 1.0 / (1.0 + beta * square)


def forward_rows(states, rows, channels, history_ref, state_ref, key_ref, query_ref, rate_ref, input_ref, out_ref, half_ref):
    tiles = channels // LANE
    per_group = min(8, tiles)
    for first in range(0, tiles, per_group):
        columns = [slice((first + j) * LANE, (first + j + 1) * LANE) for j in range(per_group)]

        def body(group, carry):
            carry = list(carry)
            for offset in range(8):
                t = group * 8 + offset
                at = pl.multiple_of(t * states, states)
                key = key_ref[pl.ds(at, states), :]
                query = query_ref[pl.ds(at, states), :]
                square = key * key
                for j, cols in enumerate(columns):
                    history_ref[pl.ds(at, states), cols] = carry[j].astype(jnp.bfloat16)
                    rate = rate_ref[group, offset : offset + 1, cols]
                    fed = input_ref[group, offset : offset + 1, cols]
                    carry[j] = (1.0 - rate * square) * carry[j] + key * fed
                    read = query * carry[j]
                    half_ref[j * 64 + offset * 8 : j * 64 + offset * 8 + 8, :] = read[0:8] + read[8:16]
            for j, cols in enumerate(columns):
                out_ref[group, :, cols] = sum_eights(half_ref, j * 64)
            return tuple(carry)

        done = lax.fori_loop(0, rows // 8, body, tuple(state_ref[:, cols] for cols in columns))
        for cols, state in zip(columns, done):
            state_ref[:, cols] = state


def forward_body(
    states, low_ref, kq_ref, values_ref, gate_ref, weight_ref, bias_ref, skip_ref,
    gated_ref, mixed_ref, history_ref, final_ref,
    state_ref, key_ref, query_ref, rate_ref, input_ref, out_ref, row_ref, pick_ref, half_ref,
):
    rows, channels = values_ref.shape

    @pl.when(pl.program_id(0) == 0)
    def _():
        state_ref[...] = jnp.zeros_like(state_ref)

    beta, inverse = step_sizes(low_ref[...], kq_ref[...], weight_ref, bias_ref, states)
    rates = beta * inverse
    rate_ref[...] = by_eights(rates)
    input_ref[...] = by_eights(rates * values_ref[...].astype(jnp.float32))
    spread_columns(kq_ref[...], row_ref, pick_ref, key_ref, query_ref, states)

    forward_rows(states, rows, channels, history_ref, state_ref, key_ref, query_ref, rate_ref, input_ref, out_ref, half_ref)
    mixed = as_rows(out_ref[...]) + skip_ref[...] * values_ref[...].astype(jnp.float32)
    gate = gate_ref[...]
    mixed_ref[...] = mixed
    gated_ref[...] = (mixed * gate * sigmoid(gate)).astype(jnp.bfloat16)

    @pl.when(pl.program_id(0) == pl.num_programs(0) - 1)
    def _():
        final_ref[...] = state_ref[...]


def forward_scan(low, kq, values, gate, weight, bias, skip, states):
    length, channels = values.shape
    rank = low.shape[1]
    rows = min(128, length)
    blocks = length // rows
    by_row = lambda width: pl.BlockSpec((rows, width), lambda i: (i, 0))
    whole = lambda a: pl.BlockSpec(a.shape, lambda i: (0, 0))
    return pl.pallas_call(
        lambda *refs: forward_body(states, *refs),
        grid=(blocks,),
        in_specs=[by_row(rank), by_row(LANE), by_row(channels), by_row(channels), whole(weight), whole(bias), whole(skip)],
        out_specs=[
            by_row(channels),
            by_row(channels),
            pl.BlockSpec((rows * states, channels), lambda i: (i, 0)),
            pl.BlockSpec((states, channels), lambda i: (0, 0)),
        ],
        out_shape=[
            jax.ShapeDtypeStruct((length, channels), jnp.bfloat16),
            jax.ShapeDtypeStruct((length, channels), jnp.float32),
            jax.ShapeDtypeStruct((length * states, channels), jnp.bfloat16),
            jax.ShapeDtypeStruct((states, channels), jnp.float32),
        ],
        scratch_shapes=[
            pltpu.VMEM((states, channels), jnp.float32),
            pltpu.VMEM((rows * states, LANE), jnp.float32),
            pltpu.VMEM((rows * states, LANE), jnp.float32),
            pltpu.VMEM((rows // 8, 8, channels), jnp.float32),
            pltpu.VMEM((rows // 8, 8, channels), jnp.float32),
            pltpu.VMEM((rows // 8, 8, channels), jnp.float32),
            pltpu.VMEM((rows // 8, 8, LANE), jnp.float32), pltpu.VMEM((rows * states, LANE), jnp.bfloat16),
            pltpu.VMEM((channels // LANE * 64, LANE), jnp.float32),
        ],
        compiler_params=pltpu.CompilerParams(vmem_limit_bytes=48 * 1024 * 1024),
        cost_estimate=pl.CostEstimate(flops=14 * length * states * channels, bytes_accessed=2 * length * states * channels, transcendentals=0),
    )(low, kq, values, gate, weight, bias, skip)


def backward_rows(
    states, rows, channels, history_ref, grad_ref, state_ref, key_ref, query_ref, rate_ref, do_ref, values32_ref,
    fed_ref, kept_ref, part_key_ref, part_query_ref, half_ref,
):
    tiles = channels // LANE
    per_group = min(PER_GROUP, tiles)
    for first in range(0, tiles, per_group):
        columns = [slice((first + j) * LANE, (first + j + 1) * LANE) for j in range(per_group)]

        def body(step, carry):
            grads, lates = list(carry[0]), list(carry[1])
            group = rows // 8 - 1 - step
            for offset in reversed(range(8)):
                t = group * 8 + offset
                at = pl.multiple_of(t * states, states)
                key = key_ref[pl.ds(at, states), :]
                query = query_ref[pl.ds(at, states), :]
                sum_key = None
                sum_query = None
                for j, cols in enumerate(columns):
                    rate = rate_ref[group, offset : offset + 1, cols]
                    out_grad = do_ref[group, offset : offset + 1, cols]
                    value = values32_ref[group, offset : offset + 1, cols]
                    before = history_ref[pl.ds(at, states), cols].astype(jnp.float32)
                    grad = grads[j] + query * out_grad
                    scaled = rate * grad
                    by_key = key * scaled
                    kept = scaled * before
                    kept = key * kept
                    twice = key * kept
                    at_fed = j * 64 + offset * 8
                    at_kept = (per_group + j) * 64 + offset * 8
                    half_ref[at_fed : at_fed + 8, :] = by_key[0:8] + by_key[8:16]
                    half_ref[at_kept : at_kept + 8, :] = twice[0:8] + twice[8:16]
                    term_key = value * scaled - 2.0 * kept
                    term_query = lates[j] * out_grad
                    sum_key = term_key if sum_key is None else sum_key + term_key
                    sum_query = term_query if sum_query is None else sum_query + term_query
                    grads[j] = grad - key * by_key
                    lates[j] = before
                if first == 0:
                    part_key_ref[pl.ds(at, states), :] = sum_key
                    part_query_ref[pl.ds(at, states), :] = sum_query
                else:
                    part_key_ref[pl.ds(at, states), :] += sum_key
                    part_query_ref[pl.ds(at, states), :] += sum_query
            for j, cols in enumerate(columns):
                fed_ref[group, :, cols] = sum_eights(half_ref, j * 64)
                kept_ref[group, :, cols] = sum_eights(half_ref, (per_group + j) * 64)
            return (tuple(grads), tuple(lates))

        start = (tuple(grad_ref[:, cols] for cols in columns), tuple(state_ref[:, cols] for cols in columns))
        grads, lates = lax.fori_loop(0, rows // 8, body, start)
        for cols, grad, late in zip(columns, grads, lates):
            grad_ref[:, cols] = grad
            state_ref[:, cols] = late


def lane_sums(part_ref):
    ones = jnp.ones((LANE, LANE), jnp.bfloat16)
    part_ref[...] = jnp.dot(part_ref[...].astype(jnp.bfloat16), ones, preferred_element_type=jnp.float32)


def gather_columns(part_key_ref, part_query_ref, placed_ref, rows, states):
    lane_sums(part_key_ref)
    lane_sums(part_query_ref)
    lane = lax.broadcasted_iota(jnp.int32, (8, LANE), 1)

    def body(group, carry):
        total = jnp.zeros((8, LANE), jnp.float32)
        for n in range(states):
            at = group * 8 * states + n
            total = jnp.where(lane == n, part_key_ref[pl.ds(at, 8, stride=states), :], total)
            total = jnp.where(lane == n + states, part_query_ref[pl.ds(at, 8, stride=states), :], total)
        placed_ref[group] = total
        return carry

    lax.fori_loop(0, rows // 8, body, 0)


def backward_body(
    states, links, low_ref, kq_ref, values_ref, gate_ref, mixed_ref, dgated_ref, history_ref, final_ref, weight_ref, bias_ref, skip_ref,
    result_ref, out_ref, dgate_ref, dpre_ref, dvalues_ref, dlow_ref, dkq_ref, bias_grad_ref, skip_grad_ref, result_came, out_came,
    grad_ref, state_ref, key_ref, query_ref, rate_ref, do_ref, values32_ref, fed_ref, kept_ref, part_key_ref, part_query_ref, row_ref, placed_ref,
    pick_ref, half_ref, *sems,
):
    rows, channels = values_ref.shape
    copies = links(result_ref, out_ref, result_came, out_came, *sems)

    @pl.when(pl.program_id(0) == 0)
    def _():
        grad_ref[...] = jnp.zeros_like(grad_ref)
        state_ref[...] = final_ref[...]
        bias_grad_ref[...] = jnp.zeros_like(bias_grad_ref)
        skip_grad_ref[...] = jnp.zeros_like(skip_grad_ref)
        for copy in copies:
            copy.start()

    beta, inverse = step_sizes(low_ref[...], kq_ref[...], weight_ref, bias_ref, states)
    rate_ref[...] = by_eights(beta * inverse)
    values = values_ref[...].astype(jnp.float32)
    values32_ref[...] = by_eights(values)
    gate = gate_ref[...]
    dgated = dgated_ref[...].astype(jnp.float32)
    s = sigmoid(gate)
    do = dgated * (gate * s)
    do_ref[...] = by_eights(do)
    dgate_ref[...] = (dgated * mixed_ref[...] * (s + gate * s * (1.0 - s))).astype(jnp.bfloat16)
    skip_grad_ref[...] += jnp.sum(do * values, axis=0, keepdims=True)
    spread_columns(kq_ref[...], row_ref, pick_ref, key_ref, query_ref, states)

    backward_rows(
        states, rows, channels, history_ref, grad_ref, state_ref, key_ref, query_ref, rate_ref, do_ref, values32_ref,
        fed_ref, kept_ref, part_key_ref, part_query_ref, half_ref,
    )
    fed = as_rows(fed_ref[...])
    dvalues_ref[...] = fed + skip_ref[...] * as_rows(do_ref[...])
    scaled = as_rows(values32_ref[...]) * fed - as_rows(kept_ref[...])
    beta, inverse = step_sizes(low_ref[...], kq_ref[...], weight_ref, bias_ref, states)
    dpre = scaled * (1.0 - beta) * inverse
    bias_grad_ref[...] += jnp.sum(dpre, axis=0, keepdims=True)
    dpre_low = dpre.astype(jnp.bfloat16)
    dpre_ref[...] = dpre_low
    dlow_ref[...] = jnp.dot(dpre_low, weight_ref[...], preferred_element_type=jnp.float32)
    through = -2.0 * jnp.sum(scaled * beta * inverse, axis=1, keepdims=True)

    gather_columns(part_key_ref, part_query_ref, placed_ref, rows, states)
    lanes = lax.broadcasted_iota(jnp.int32, kq_ref.shape, 1)
    dkq_ref[...] = as_rows(placed_ref[...]) + jnp.where(lanes < states, kq_ref[...] * through, 0.0)

    @pl.when(pl.program_id(0) == pl.num_programs(0) - 1)
    def _():
        for copy in copies:
            copy.wait_recv()
        for copy in copies:
            copy.wait_send()


def exchange(parts, dps, result_ref, out_ref, result_came, out_came, result_send, result_recv, out_send, out_recv):
    d, s = lax.axis_index("dp"), lax.axis_index("seq")

    @pl.when(pl.program_id(0) == 0)
    def _():
        barrier = pltpu.get_barrier_semaphore()
        for k in range(1, parts):
            pl.semaphore_signal(barrier, inc=1, device_id=(d, lax.rem(s + k, parts)), device_id_type=MESH)
        for k in range(1, dps):
            pl.semaphore_signal(barrier, inc=1, device_id=(lax.rem(d + k, dps), s), device_id_type=MESH)
        pl.semaphore_wait(barrier, parts + dps - 2)

    copies = []
    for k in range(1, parts):
        to = lax.rem(s + k, parts)
        copies.append(
            pltpu.make_async_remote_copy(
                src_ref=result_ref.at[to], dst_ref=result_came.at[k - 1], send_sem=result_send.at[k - 1],
                recv_sem=result_recv.at[k - 1], device_id=(d, to), device_id_type=MESH,
            )
        )
    for k in range(1, dps):
        to = lax.rem(d + k, dps)
        copies.append(
            pltpu.make_async_remote_copy(
                src_ref=out_ref.at[to], dst_ref=out_came.at[k - 1], send_sem=out_send.at[k - 1],
                recv_sem=out_recv.at[k - 1], device_id=(to, s), device_id_type=MESH,
            )
        )
    return copies


def backward_scan(low, kq, values, gate, mixed, dgated, history, final, weight, bias, skip, result_part, out_part, states):
    length, channels = values.shape
    rank = low.shape[1]
    rows = min(128, length)
    blocks = length // rows
    by_row = lambda width: pl.BlockSpec((rows, width), lambda i: (blocks - 1 - i, 0))
    whole = lambda a: pl.BlockSpec(a.shape, lambda i: (0, 0))
    total = pl.BlockSpec((1, channels), lambda i: (0, 0))
    wide = pltpu.VMEM((rows // 8, 8, channels), jnp.float32)
    spread = pltpu.VMEM((rows * states, LANE), jnp.float32)
    anywhere = pl.BlockSpec(memory_space=pl.ANY)
    dma = pltpu.SemaphoreType.DMA
    parts, dps = result_part.shape[0], out_part.shape[0]
    links = lambda *refs: exchange(parts, dps, *refs)
    return pl.pallas_call(
        lambda *refs: backward_body(states, links, *refs),
        grid=(blocks,),
        in_specs=[
            by_row(rank), by_row(LANE), by_row(channels), by_row(channels), by_row(channels), by_row(channels),
            pl.BlockSpec((rows * states, channels), lambda i: (blocks - 1 - i, 0)),
            whole(final), whole(weight), whole(bias), whole(skip), anywhere, anywhere,
        ],
        out_specs=[by_row(channels), by_row(channels), by_row(channels), by_row(rank), by_row(LANE), total, total, anywhere, anywhere],
        out_shape=[
            jax.ShapeDtypeStruct((length, channels), jnp.bfloat16),
            jax.ShapeDtypeStruct((length, channels), jnp.bfloat16),
            jax.ShapeDtypeStruct((length, channels), jnp.float32),
            jax.ShapeDtypeStruct((length, rank), jnp.float32),
            jax.ShapeDtypeStruct((length, LANE), jnp.float32),
            jax.ShapeDtypeStruct((1, channels), jnp.float32),
            jax.ShapeDtypeStruct((1, channels), jnp.float32),
            jax.ShapeDtypeStruct((parts - 1,) + result_part.shape[1:], jnp.bfloat16),
            jax.ShapeDtypeStruct((dps - 1,) + out_part.shape[1:], jnp.bfloat16),
        ],
        scratch_shapes=[
            pltpu.VMEM((states, channels), jnp.float32),
            pltpu.VMEM((states, channels), jnp.float32),
            spread, spread, wide, wide, wide, wide, wide, spread, spread,
            pltpu.VMEM((rows // 8, 8, LANE), jnp.float32), pltpu.VMEM((rows // 8, 8, LANE), jnp.float32),
            pltpu.VMEM((rows * states, LANE), jnp.bfloat16),
            pltpu.VMEM((2 * channels // LANE * 64, LANE), jnp.float32),
            dma((parts - 1,)), dma((parts - 1,)), dma((dps - 1,)), dma((dps - 1,)),
        ],
        compiler_params=pltpu.CompilerParams(collective_id=3, has_side_effects=True, vmem_limit_bytes=56 * 1024 * 1024),
        cost_estimate=pl.CostEstimate(flops=30 * length * states * channels, bytes_accessed=2 * length * states * channels, transcendentals=0),
    )(low, kq, values, gate, mixed, dgated, history, final, weight, bias, skip, result_part, out_part)


MESH = pl.DeviceIdType.MESH
GAIN_ROWS = 16


def plane_mates(d):
    core, x, y = lax.rem(d, 2), lax.rem(d // 2, 2), d // 4
    return d + 1 - 2 * core, d + 2 - 4 * x, d + 4 - 8 * y


def start_body(
    parts, block,
    tokens_ref, in_weight_ref, extra_ref, gain_ref, cot_ref,
    normed_out, weight_out, conv_ref, gate_ref, select_out, beta_out, vector_out, gain_out, cot_early,
    tokens_all, normed_all, weight_all, extra_all,
    near_send, near_recv, plane_send, plane_recv, gain_send, gain_recv, line_send, line_recv, local_sem, early_send, early_recv, spread_ref,
):
    d, s = lax.axis_index("dp"), lax.axis_index("seq")
    sib, xm, ym = plane_mates(d)
    own = spread_ref.shape[1]
    rows, width = tokens_ref.shape
    small = extra_ref.shape[0]
    channels = conv_ref.shape[1]
    chunk = rows // 4

    for j in range(spread_ref.shape[2] // block):
        for q in range(parts):
            first = (j * parts + q) * block
            spread_ref[q, :, j * block : (j + 1) * block] = in_weight_ref[:, first : first + block]

    barrier = pltpu.get_barrier_semaphore()
    for mate in (sib, xm, ym):
        pl.semaphore_signal(barrier, inc=1, device_id=(mate, s), device_id_type=MESH)
    for k in range(1, parts):
        pl.semaphore_signal(barrier, inc=1, device_id=(d, lax.rem(s + k, parts)), device_id_type=MESH)
    pl.semaphore_wait(barrier, 3 + parts - 1)

    def remote(src, dst, send, recv, to):
        return pltpu.make_async_remote_copy(
            src_ref=src, dst_ref=dst, send_sem=send, recv_sem=recv, device_id=to, device_id_type=MESH
        )

    def weight_rows(owner, source):
        return weight_all.at[pl.ds(pl.multiple_of((owner * parts + source) * own, own), own), :]

    def extra_rows(owner):
        return extra_all.at[owner]

    def gain_rows(source):
        return extra_all.at[d, pl.ds(pl.multiple_of(small + source * GAIN_ROWS, GAIN_ROWS), GAIN_ROWS), pl.ds(0, LANE)]

    near = []
    for k in range(1, parts):
        to = (d, lax.rem(s + k, parts))
        near.append(remote(spread_ref.at[to[1]], weight_rows(d, s), near_send.at[k], near_recv.at[k], to))
        near.append(remote(gain_ref, gain_rows(s), gain_send.at[k], gain_recv.at[k], to))
    for copy in near:
        copy.start()
    mine = [
        pltpu.make_async_copy(spread_ref.at[s], weight_rows(d, s), local_sem.at[0]),
        pltpu.make_async_copy(gain_ref, gain_rows(s), local_sem.at[1]),
        pltpu.make_async_copy(extra_ref, extra_all.at[d, pl.ds(0, small), :], local_sem.at[2]),
        pltpu.make_async_copy(tokens_ref, tokens_all.at[pl.ds(pl.multiple_of(s * rows, rows), rows), :], local_sem.at[3]),
    ]
    for copy in mine:
        copy.start()

    def token_rows(part, c):
        return tokens_all.at[pl.ds(pl.multiple_of(part * rows + c * chunk, chunk), chunk), :]

    def token_copy(way, distance, c):
        part = s - way * (distance - 1)
        src = tokens_ref.at[pl.ds(c * chunk, chunk), :] if distance == 1 else token_rows(part, c)
        side = 0 if way == 1 else 1
        return remote(
            src, token_rows(part, c), line_send.at[side, distance, c], line_recv.at[side, distance, c], (d, s + way)
        )

    def can_send(way, distance):
        reach = s + 1 < parts if way == 1 else s >= 1
        came = s - (distance - 1) >= 0 if way == 1 else s + (distance - 1) < parts
        return jnp.logical_and(reach, came)

    def arrives(way, distance):
        return s >= distance if way == 1 else s + distance < parts

    def send_tokens(distance, c):
        for way in (1, -1):
            @pl.when(can_send(way, distance))
            def _():
                token_copy(way, distance, c).start()

    def sent_tokens(distance, c):
        for way in (1, -1):
            @pl.when(can_send(way, distance))
            def _():
                token_copy(way, distance, c).wait_send()

    def take_tokens(distance, c):
        for way in (1, -1):
            @pl.when(arrives(way, distance))
            def _():
                part = s - way * distance
                side = 0 if way == 1 else 1
                remote(
                    token_rows(part, c), token_rows(part, c), line_send.at[side, distance, c],
                    line_recv.at[side, distance, c], (d, s),
                ).wait_recv()

    inner = jnp.logical_and(s >= 1, s + 1 < parts)

    def early_copy(way):
        side = 0 if way == 1 else 1
        return remote(cot_ref, cot_early.at[side], early_send.at[side], early_recv.at[side], (d, s + way))

    def last_copy(way):
        side = 0 if way == 1 else 1
        piece = pl.ds(0, chunk)
        return remote(
            cot_ref.at[piece, :], cot_early.at[side, piece, :], early_send.at[2 + side], early_recv.at[2 + side], (d, s + way)
        )

    def sends_last(way):
        return s == parts - 2 if way == 1 else s == 1

    def takes_last(way):
        return s == parts - 1 if way == 1 else s == 0

    def sends_early(way):
        return s + 2 < parts if way == 1 else s >= 2

    units = parts + 1

    def unit(owner, k):
        return extra_rows(owner) if k == parts else weight_rows(owner, lax.rem(s - k + parts, parts))

    kinds = {"own": (d, 0), "x": (xm, 2), "y": (ym, 4)}

    def plane_copy(owner, k, rel, kind, to):
        return remote(unit(owner, k), unit(owner, k), plane_send.at[kind, k], plane_recv.at[rel, k], (to, s))

    diag = xm + ym - d
    sib_of = lambda mate: mate + sib - d

    def route(k):
        steps = [
            (0, d, 1, 0, sib), (0, d, 2, 1, xm), (0, d, 4, 2, ym),
            (2, xm, 3, 3, sib), (4, ym, 5, 5, sib), (6, diag, 7, 7, sib),
        ]
        steps.append((2, xm, 6, 4, ym) if k % 2 == 0 else (4, ym, 6, 6, xm))
        return steps

    def pass_on(stage, k):
        for at, owner, rel, kind, to in route(k):
            if at == stage:
                plane_copy(owner, k, rel, kind, to).start()

    owners = {1: sib, 2: xm, 3: sib_of(xm), 4: ym, 5: sib_of(ym), 6: diag, 7: sib_of(diag)}

    def take(rel, k):
        plane_copy(owners[rel], k, rel, 0, d).wait_recv()

    for c in range(4):
        send_tokens(1, c)
    mine[0].wait()
    pass_on(0, 0)
    for k in range(1, parts):
        near_wait = remote(
            spread_ref.at[s], weight_rows(d, lax.rem(s - k + parts, parts)), near_send.at[k], near_recv.at[k], (d, s)
        )
        near_wait.wait_recv()
        pass_on(0, k)
    mine[1].wait()
    mine[2].wait()
    for k in range(1, parts):
        remote(gain_ref, gain_rows(lax.rem(s - k + parts, parts)), gain_send.at[k], gain_recv.at[k], (d, s)).wait_recv()
    pass_on(0, parts)
    for k in range(units):
        take(2, k)
        pass_on(2, k)
        take(4, k)
        pass_on(4, k)
        if k < 4:
            take_tokens(1, k)
            send_tokens(2, k)
    for way in (1, -1):
        @pl.when(sends_early(way))
        def _():
            early_copy(way).start()

    for k in range(units):
        take(6, k)
        pass_on(6, k)
        if k < 4:
            take_tokens(2, k)
            send_tokens(3, k)
    for way in (1, -1):
        @pl.when(sends_last(way))
        def _():
            last_copy(way).start()

    for rel in (1, 3, 5, 7):
        for k in range(units):
            take(rel, k)
    mine[3].wait()
    weight_copy = pltpu.make_async_copy(weight_all, weight_out, local_sem.at[4])
    weight_copy.start()
    sel = select_out.shape[1]
    for owner in range(extra_all.shape[0]):
        here = slice(owner * small, (owner + 1) * small)
        select_out[here, :] = extra_all[owner, 0:small, 0:sel]
        beta_out[here, :] = extra_all[owner, 0:small, sel : sel + LANE]
        vectors = extra_all[owner, 0:small, sel + LANE : sel + 2 * LANE].astype(jnp.float32)
        vector_out[:, here] = jnp.transpose(vectors)[: vector_out.shape[0]]

    lane = lax.broadcasted_iota(jnp.int32, (1, LANE), 1)
    pieces = []
    for owner in range(extra_all.shape[0]):
        for source in range(0, parts, 2):
            row = small + source * GAIN_ROWS
            even = extra_all[owner, row : row + GAIN_ROWS, 0:LANE].astype(jnp.float32)[0:1]
            odd = extra_all[owner, row + GAIN_ROWS : row + 2 * GAIN_ROWS, 0:LANE].astype(jnp.float32)[0:1]
            pieces.append(jnp.where(lane < own, even, odd))
    gain = jnp.concatenate(pieces, axis=1)
    gain_out[...] = gain

    tile = min(512, channels)

    def work(part):
        for c in range(4):
            at = pl.ds(pl.multiple_of(part * rows + c * chunk, chunk), chunk)
            flat = tokens_all[at, :].astype(jnp.float32)
            scale = lax.rsqrt(jnp.mean(flat * flat, axis=-1, keepdims=True) + 1e-05)
            normed_all[at, :] = (flat * scale * gain).astype(jnp.bfloat16)
        at = pl.ds(pl.multiple_of(part * rows, rows), rows)

        def columns(n, carry):
            left = pl.multiple_of(n * tile, tile)
            right = pl.multiple_of(channels + n * tile, tile)
            conv_ref[at, pl.ds(left, tile)] = jnp.dot(
                normed_all[at, :], weight_all[:, pl.ds(left, tile)], preferred_element_type=jnp.float32
            ).astype(jnp.bfloat16)
            gate_ref[at, pl.ds(left, tile)] = jnp.dot(
                normed_all[at, :], weight_all[:, pl.ds(right, tile)], preferred_element_type=jnp.float32
            )
            return carry

        lax.fori_loop(0, channels // tile, columns, 0)

    def work_at(low, high):
        def each(part, carry):
            away = jnp.abs(part - s)

            @pl.when(jnp.logical_and(away >= low, away <= high))
            def _():
                work(part)

            return carry

        lax.fori_loop(0, parts, each, 0)

    work_at(0, 2)
    for c in range(4):
        take_tokens(3, c)
    work_at(3, 3)
    normed_copy = pltpu.make_async_copy(normed_all, normed_out, local_sem.at[5])
    normed_copy.start()

    for way in (1, -1):
        @pl.when(inner)
        def _():
            early_copy(way).wait_recv()

        @pl.when(sends_early(way))
        def _():
            early_copy(way).wait_send()

        @pl.when(takes_last(way))
        def _():
            last_copy(way).wait_recv()

        @pl.when(sends_last(way))
        def _():
            last_copy(way).wait_send()

    for copy in near:
        copy.wait_send()
    for k in range(units):
        for at, owner, rel, kind, to in route(k):
            plane_copy(owner, k, rel, kind, to).wait_send()
    for distance in range(1, parts):
        for c in range(4):
            sent_tokens(distance, c)
    weight_copy.wait()
    normed_copy.wait()


def start(tokens, in_weight, extra, gain, cotangent, parts, dps):
    own, both = in_weight.shape[0], in_weight.shape[1] // parts
    rows, width = tokens.shape
    small, lanes = extra.shape
    any_space = pl.BlockSpec(memory_space=pl.ANY)
    vmem = pl.BlockSpec(memory_space=pltpu.VMEM)
    tall = small + parts * GAIN_ROWS
    dma = pltpu.SemaphoreType.DMA
    return pl.pallas_call(
        lambda *refs: start_body(parts, small, *refs),
        out_shape=[
            jax.ShapeDtypeStruct((parts * rows, width), jnp.bfloat16),
            jax.ShapeDtypeStruct((dps * parts * own, both), jnp.bfloat16),
            jax.ShapeDtypeStruct((parts * rows, both // 2), jnp.bfloat16),
            jax.ShapeDtypeStruct((parts * rows, both // 2), jnp.float32),
            jax.ShapeDtypeStruct((dps * small, lanes - 2 * LANE), jnp.bfloat16),
            jax.ShapeDtypeStruct((dps * small, LANE), jnp.bfloat16),
            jax.ShapeDtypeStruct((8, dps * small), jnp.float32),
            jax.ShapeDtypeStruct((1, width), jnp.float32),
            jax.ShapeDtypeStruct((2, rows, width), jnp.bfloat16),
        ],
        in_specs=[vmem, vmem, vmem, vmem, any_space],
        out_specs=[any_space, any_space, vmem, vmem, vmem, vmem, vmem, vmem, any_space],
        scratch_shapes=[
            pltpu.VMEM((parts * rows, width), jnp.bfloat16),
            pltpu.VMEM((parts * rows, width), jnp.bfloat16),
            pltpu.VMEM((dps * parts * own, both), jnp.bfloat16),
            pltpu.VMEM((dps, tall, lanes), jnp.bfloat16),
            dma((parts,)), dma((parts,)),
            dma((8, parts + 1)), dma((8, parts + 1)),
            dma((parts,)), dma((parts,)),
            dma((2, parts, 4)), dma((2, parts, 4)),
            dma((6,)), dma((4,)), dma((4,)), pltpu.VMEM((parts, own, both), jnp.bfloat16),
        ],
        compiler_params=pltpu.CompilerParams(
            collective_id=1, has_side_effects=True, vmem_limit_bytes=56 * 1024 * 1024
        ),
        cost_estimate=pl.CostEstimate(
            flops=2 * parts * rows * width * both, bytes_accessed=40 * 1024 * 1024, transcendentals=0
        ),
    )(tokens, in_weight, extra, gain, cotangent)


def line_sums(parts, rows, terms, came, send, recv, early=None):
    d, s = lax.axis_index("dp"), lax.axis_index("seq")
    chunk = rows // 4

    def own_rows(part, c):
        return pl.ds(pl.multiple_of(part * rows + c * chunk, chunk), chunk)

    def slot(way, left, part, c):
        at = parts if way == -1 and left == 0 else part
        return came.at[at, pl.ds(c * chunk, chunk), :]

    def copy_of(way, steps, c):
        side = 0 if way == 1 else 1
        part = s + way * steps
        return pltpu.make_async_remote_copy(
            src_ref=terms.at[own_rows(part, c), :], dst_ref=slot(way, steps - 1, part, c),
            send_sem=send.at[side, steps, c], recv_sem=recv.at[side, steps - 1, c],
            device_id=(d, s + way), device_id_type=MESH,
        )

    def valid(way, steps):
        if early is not None and steps == 1:
            return jnp.logical_and(s >= 1, s + 1 < parts)
        return s + steps < parts if way == 1 else s >= steps

    def ends_here(way):
        least = 1 if early is None else 2
        return s >= least if way == 1 else s + least < parts

    def upstream(way):
        return s >= 1 if way == 1 else s + 1 < parts

    def taken(way, left, c):
        side = 0 if way == 1 else 1
        place = slot(way, left, s + way * left, c)
        pltpu.make_async_remote_copy(
            src_ref=place, dst_ref=place, send_sem=send.at[side, left, c], recv_sem=recv.at[side, left, c],
            device_id=(d, s), device_id_type=MESH,
        ).wait_recv()

    def pass_on(steps, c):
        for way in (1, -1):
            @pl.when(valid(way, steps))
            def _():
                if steps < parts - 1:
                    @pl.when(upstream(way))
                    def _():
                        taken(way, steps, c)
                        mine = own_rows(s + way * steps, c)
                        more = came[s + way * steps, c * chunk : (c + 1) * chunk, :]
                        terms[mine, :] = (terms[mine, :].astype(jnp.float32) + more.astype(jnp.float32)).astype(jnp.bfloat16)

                copy_of(way, steps, c).start()

    def total(c):
        for way in (1, -1):
            @pl.when(ends_here(way))
            def _():
                taken(way, 0, c)

        at = pl.ds(c * chunk, chunk)
        low = jnp.where(ends_here(1), came[s, at, :].astype(jnp.float32), 0.0)
        high = jnp.where(ends_here(-1), came[parts, at, :].astype(jnp.float32), 0.0)
        total = terms[own_rows(s, c), :].astype(jnp.float32) + low + high
        if early is not None:
            total = total + jnp.where(jnp.logical_or(s == 1, s == parts - 2), early[at, :].astype(jnp.float32), 0.0)
        return total

    def sent():
        for steps in range(1, parts):
            for c in range(4):
                for way in (1, -1):
                    @pl.when(valid(way, steps))
                    def _():
                        copy_of(way, steps, c).wait_send()

    return pass_on, total, sent


def end_body(
    parts, block,
    dmixed_hbm, normed_hbm, weight_hbm, tokens_hbm, cot_hbm, gain_ref, shard_hbm, small_hbm,
    input_grad_ref, in_grad_ref, gain_grad_ref, small_grad_ref,
    dn, dn_recv, sib_send, sib_recv, q_send, q_recv, total, z_send, z_recv,
    small_sib_send, small_sib_recv, small_q_send, small_q_recv,
    line_send, line_recv, pair_send, pair_recv, cross_send, cross_recv, near_send, near_recv,
    dmixed_ref, normed_ref, weight_ref, tokens_ref, cot_ref, shard_ref, small_ref, load_sem,
):
    d, s = lax.axis_index("dp"), lax.axis_index("seq")
    sib, xm, ym = plane_mates(d)
    diag = xm + ym - d
    own, both = shard_ref.shape[0], dmixed_ref.shape[1]
    rows, width = tokens_ref.shape
    chunk = rows // 4
    tall = parts * own
    tile = min(512, both)

    loads = [
        pltpu.make_async_copy(src, dst, load_sem.at[i])
        for i, (src, dst) in enumerate(
            (
                (dmixed_hbm, dmixed_ref), (weight_hbm, weight_ref), (normed_hbm, normed_ref), (small_hbm, small_ref),
                (tokens_hbm, tokens_ref), (cot_hbm, cot_ref), (shard_hbm, shard_ref),
            )
        )
    ]
    for load in loads[:2]:
        load.start()
    barrier = pltpu.get_barrier_semaphore()
    for mate in (sib, xm, ym, diag):
        pl.semaphore_signal(barrier, inc=1, device_id=(mate, s), device_id_type=MESH)
    for k in range(1, parts):
        pl.semaphore_signal(barrier, inc=1, device_id=(d, lax.rem(s + k, parts)), device_id_type=MESH)
    pl.semaphore_wait(barrier, 4 + parts - 1)

    def remote(src, dst, send, recv, to):
        return pltpu.make_async_remote_copy(
            src_ref=src, dst_ref=dst, send_sem=send, recv_sem=recv, device_id=to, device_id_type=MESH
        )

    pass_line, line_total, line_sent = line_sums(parts, rows, dn, dn_recv, line_send, line_recv)

    def dn_part(part):
        at = pl.ds(pl.multiple_of(part * rows, rows), rows)

        def columns(n, carry):
            cols = pl.ds(pl.multiple_of(n * tile, tile), tile)
            dn[at, cols] = lax.dot_general(
                dmixed_ref[at, :], weight_ref[cols, :], (((1,), (1,)), ((), ())), preferred_element_type=jnp.float32
            ).astype(jnp.bfloat16)
            return carry

        lax.fori_loop(0, width // tile, columns, 0)

    far = (parts - 1) * (1 - s // 2)
    next_far = lax.rem(2 - 2 * s + 10, 5)
    nearer = 1 + lax.rem(s, 2)
    for load in loads[:2]:
        load.wait()
    for load in loads[2:]:
        load.start()
    dn_part(far)
    for c in range(4):
        pass_line(parts - 1, c)
    for load in loads[2:4]:
        load.wait()

    def grad_block(owner, store):
        left = pl.ds(pl.multiple_of(owner * tall, tall), tall)

        def columns(n, carry):
            cols = pl.ds(pl.multiple_of(n * tile, tile), tile)
            store(
                cols,
                lax.dot_general(
                    normed_ref[:, left], dmixed_ref[:, cols], (((0,), (0,)), ((), ())),
                    preferred_element_type=jnp.float32,
                ),
            )
            return carry

        lax.fori_loop(0, both // tile, columns, 0)

    mates = (diag, xm, ym, d)
    sib_of = lambda mate: mate + sib - d

    def pair_copy(r):
        return remote(sib_send.at[r], sib_recv.at[r], pair_send.at[0, r], pair_recv.at[0, r], (sib, s))

    def pair_copy_small(r):
        return remote(small_sib_send.at[r], small_sib_recv.at[r], pair_send.at[1, r], pair_recv.at[1, r], (sib, s))

    def cross_copy(r):
        return remote(q_send.at[r], q_recv.at[r], cross_send.at[0, r], cross_recv.at[0, r], (mates[r], s))

    def cross_copy_small(r):
        return remote(small_q_send.at[r], small_q_recv.at[r], cross_send.at[1, r], cross_recv.at[1, r], (mates[r], s))

    for r in range(4):
        def store_pair(cols, value):
            sib_send[r, :, cols] = value.astype(jnp.bfloat16)

        grad_block(sib_of(mates[r]), store_pair)
        pair_copy(r).start()
        small_sib_send[r] = small_ref[sib_of(mates[r])].astype(jnp.bfloat16)
        pair_copy_small(r).start()
    dn_part(next_far)
    for r in range(4):
        pair_copy(r).wait_recv()
        pair_copy_small(r).wait_recv()
        both_small = small_ref[mates[r]] + small_sib_recv[r].astype(jnp.float32)
        if r < 3:
            def store_cross(cols, value):
                q_send[r, :, cols] = (value + sib_recv[r, :, cols].astype(jnp.float32)).astype(jnp.bfloat16)

            grad_block(mates[r], store_cross)
            cross_copy(r).start()
            small_q_send[r] = both_small.astype(jnp.bfloat16)
            cross_copy_small(r).start()
        else:
            def store_total(cols, value):
                total[:, cols] = value + sib_recv[r, :, cols].astype(jnp.float32)

            grad_block(mates[r], store_total)
            small_grad_ref[...] = both_small
        pass_line(parts - 2, r)
        if r == 2:
            dn_part(nearer)
            dn_part(s)
    for c in range(4):
        pass_line(parts - 3, c)
    for load in loads[4:]:
        load.wait()

    for r in range(3):
        cross_copy(r).wait_recv()
        cross_copy_small(r).wait_recv()
        total[...] += q_recv[r].astype(jnp.float32)
        small_grad_ref[...] += small_q_recv[r].astype(jnp.float32)
    z_send[...] = total[...].astype(jnp.bfloat16)

    def near_copy(k):
        to = lax.rem(s + k, parts)
        return remote(
            z_send.at[pl.ds(pl.multiple_of(to * own, own), own), :], z_recv.at[k], near_send.at[k], near_recv.at[k], (d, to)
        )

    for k in range(1, parts):
        near_copy(k).start()

    for c in range(4):
        at = pl.ds(c * chunk, chunk)
        v = line_total(c) * gain_ref[...]
        flat = tokens_ref[at, :].astype(jnp.float32)
        scale = lax.rsqrt(jnp.mean(flat * flat, axis=-1, keepdims=True) + 1e-05)
        du = scale * v - flat * (scale * scale * scale) * jnp.mean(flat * v, axis=-1, keepdims=True)
        input_grad_ref[at, :] = (cot_ref[at, :].astype(jnp.float32) + du).astype(jnp.bfloat16)

    channel_blocks = both // block
    gain_total = jnp.zeros((own, block), jnp.float32)
    for k in range(parts):
        source = lax.rem(s - k + parts, parts)
        if k > 0:
            near_copy(k).wait_recv()
        for j in range(channel_blocks):
            cols = slice(j * block, (j + 1) * block)
            if k == 0:
                piece = z_send[pl.ds(pl.multiple_of(s * own, own), own), cols]
            else:
                piece = z_recv[k, :, cols]
            to = pl.ds(pl.multiple_of((j * parts + source) * block, block), block)
            in_grad_ref[:, to] = piece
            gain_total = gain_total + piece.astype(jnp.float32) * shard_ref[:, to].astype(jnp.float32)
    gain_grad_ref[...] = jnp.broadcast_to(jnp.sum(gain_total, axis=1, keepdims=True), gain_grad_ref.shape)

    for r in range(4):
        pair_copy(r).wait_send()
        pair_copy_small(r).wait_send()
    for r in range(3):
        cross_copy(r).wait_send()
        cross_copy_small(r).wait_send()
    for k in range(1, parts):
        near_copy(k).wait_send()
    line_sent()


def end(dmixed, normed, weight, tokens, cotangent, gain, shard, small, parts, block):
    both = dmixed.shape[1]
    rows, width = tokens.shape
    own = shard.shape[0]
    dps, _, lanes = small.shape
    tall = parts * own
    vmem = pl.BlockSpec(memory_space=pltpu.VMEM)
    anywhere = pl.BlockSpec(memory_space=pl.ANY)
    dma = pltpu.SemaphoreType.DMA
    low = jnp.bfloat16
    return pl.pallas_call(
        lambda *refs: end_body(parts, block, *refs),
        out_shape=[
            jax.ShapeDtypeStruct((rows, width), low),
            jax.ShapeDtypeStruct((own, parts * both), low),
            jax.ShapeDtypeStruct((own, LANE), jnp.float32),
            jax.ShapeDtypeStruct((block, lanes), jnp.float32),
        ],
        in_specs=[anywhere] * 5 + [vmem] + [anywhere] * 2,
        out_specs=[vmem] * 4,
        scratch_shapes=[
            pltpu.VMEM((parts * rows, width), low),
            pltpu.VMEM((parts + 1, rows, width), low),
            pltpu.VMEM((4, tall, both), low), pltpu.VMEM((4, tall, both), low),
            pltpu.VMEM((3, tall, both), low), pltpu.VMEM((3, tall, both), low),
            pltpu.VMEM((tall, both), jnp.float32),
            pltpu.VMEM((tall, both), low), pltpu.VMEM((parts, own, both), low),
            pltpu.VMEM((4, block, lanes), low), pltpu.VMEM((4, block, lanes), low),
            pltpu.VMEM((3, block, lanes), low), pltpu.VMEM((3, block, lanes), low),
            dma((2, parts, 4)), dma((2, parts, 4)),
            dma((2, 4)), dma((2, 4)), dma((2, 3)), dma((2, 3)), dma((parts,)), dma((parts,)),
            *[pltpu.VMEM(a.shape, a.dtype) for a in (dmixed, normed, weight, tokens, cotangent, shard, small)], dma((7,)),
        ],
        compiler_params=pltpu.CompilerParams(
            collective_id=2, has_side_effects=True, vmem_limit_bytes=60 * 1024 * 1024
        ),
        cost_estimate=pl.CostEstimate(
            flops=4 * parts * rows * width * both, bytes_accessed=30 * 1024 * 1024, transcendentals=0
        ),
    )(dmixed, normed, weight, tokens, cotangent, gain, shard, small)


def linked_forward_body(
    states, parts, dps, taps,
    conv_in_ref, gate_ref, select_ref, vector_ref, weight_ref, out_shard, cot_shard, cot_early,
    mixed_ref, history_ref, final_ref, values_out, low_ref, kq_ref, dgated_out, result_out, out_part_ref, early_out, key_ref, query_ref,
    state_ref, rate_ref, input_ref, out_ref, row_ref, pick_ref, half_ref,
    part_low, part_kq, came_low, came_kq, sum_low, sum_kq,
    rs_send, rs_recv, ag_send, ag_recv, out_send, out_recv, line_send, line_recv, local_sem,
    out_all, cot_all, gated_all, out_total, values_ref, dgated_ref, result_ref, leave_sem, early_send, early_recv,
):
    d, s = lax.axis_index("dp"), lax.axis_index("seq")
    step = pl.program_id(0)
    length, channels = values_ref.shape
    rows = gate_ref.shape[0]
    span = length // parts
    block = out_shard.shape[0]
    chunk = span // 4
    packed = LANE // (2 * states)
    conv_w_ref, conv_b_ref = vector_ref, vector_ref[taps : taps + 1, :]
    bias_ref, skip_ref = vector_ref[taps + 1 : taps + 2, :], vector_ref[taps + 2 : taps + 3, :]
    short = span // packed

    def remote(src, dst, send, recv, to):
        return pltpu.make_async_remote_copy(
            src_ref=src, dst_ref=dst, send_sem=send, recv_sem=recv, device_id=to, device_id_type=MESH
        )

    def out_rows(owner):
        return out_all.at[pl.ds(pl.multiple_of(owner * block, block), block), :]

    out_copies = []
    for k in range(1, dps):
        out_copies.append(
            remote(out_shard, out_rows(d), out_send.at[k - 1], out_recv.at[k - 1], (lax.rem(d + k, dps), s))
        )

    inner = jnp.logical_and(s >= 1, s + 1 < parts)

    def cot_rows(part, c):
        return cot_all.at[pl.ds(pl.multiple_of(part * span + c * chunk, chunk), chunk), :]

    def cot_copy(way, distance, c):
        part = s - way * (distance - 1)
        side = 0 if way == 1 else 1
        piece = pl.ds(c * chunk, chunk)
        src = {1: cot_shard.at[piece, :], 2: cot_early.at[side, piece, :]}.get(distance)
        src = cot_rows(part, c) if src is None else src
        return remote(
            src, cot_rows(part, c), line_send.at[side, distance, c], line_recv.at[side, distance, c], (d, s + way)
        )

    def can_send(way, distance):
        if distance == 1:
            return s == parts - 2 if way == 1 else s == 1
        came = s >= distance - 1 if way == 1 else s + distance - 1 < parts
        return jnp.logical_and(inner, came)

    def arrives(way, distance):
        if distance == 1:
            return s == parts - 1 if way == 1 else s == 0
        return s >= distance if way == 1 else s + distance < parts

    def into_end(way):
        return s == parts - 2 if way == 1 else s == 1

    def send_cot(distance, c, which=None):
        for way in (1, -1):
            go = can_send(way, distance)
            if which is not None:
                go = jnp.logical_and(go, into_end(way) if which else jnp.logical_not(into_end(way)))

            @pl.when(go)
            def _():
                cot_copy(way, distance, c).start()

    def sent_cot(distance, c):
        for way in (1, -1):
            @pl.when(can_send(way, distance))
            def _():
                cot_copy(way, distance, c).wait_send()

    def take_cot(distance, c):
        for way in (1, -1):
            @pl.when(arrives(way, distance))
            def _():
                part = s - way * distance
                side = 0 if way == 1 else 1
                remote(
                    cot_rows(part, c), cot_rows(part, c), line_send.at[side, distance, c],
                    line_recv.at[side, distance, c], (d, s),
                ).wait_recv()

    def end_rows(way):
        side = 0 if way == 1 else 1
        return pltpu.make_async_copy(
            cot_early.at[side, pl.ds(0, chunk), :], cot_rows(s - way, 0), local_sem.at[3 + side]
        )

    def early_rows(way):
        side = 0 if way == 1 else 1
        return pltpu.make_async_copy(
            cot_early.at[side], cot_all.at[pl.ds(pl.multiple_of((s - way) * span, span), span), :], local_sem.at[3 + side]
        )

    def early_result(way):
        part = 1 if way == 1 else parts - 2
        side = 0 if way == 1 else 1
        return remote(
            result_ref.at[pl.ds(part * span, span), :], early_out, early_send.at[side], early_recv.at[side], (d, s + way)
        )

    def sends_result(way):
        return s == 0 if way == 1 else s == parts - 1

    def takes_result(way):
        return s == 1 if way == 1 else s == parts - 2

    def own_copy(which):
        if which == 0:
            return pltpu.make_async_copy(out_shard, out_rows(d), local_sem.at[0])
        here = pl.ds(pl.multiple_of(s * span, span), span)
        return pltpu.make_async_copy(cot_shard, cot_all.at[here, :], local_sem.at[1])

    @pl.when(step == 0)
    def _():
        barrier = pltpu.get_barrier_semaphore()
        for k in range(1, parts):
            pl.semaphore_signal(barrier, inc=1, device_id=(d, lax.rem(s + k, parts)), device_id_type=MESH)
        for k in range(1, dps):
            pl.semaphore_signal(barrier, inc=1, device_id=(lax.rem(d + k, dps), s), device_id_type=MESH)
        pl.semaphore_wait(barrier, parts + dps - 2)
        state_ref[...] = jnp.zeros_like(state_ref)
        for copy in out_copies:
            copy.start()
        own_copy(0).start()
        own_copy(1).start()
        for way in (1, -1):
            @pl.when(inner)
            def _():
                early_rows(way).start()

            @pl.when(arrives(way, 1))
            def _():
                end_rows(way).start()

        send_cot(1, 1)
        send_cot(2, 0, False)

    def rs_copies(k):
        at = lax.rem(s + k, parts)
        return (
            remote(part_low.at[at], came_low.at[k - 1], rs_send.at[0, k - 1], rs_recv.at[0, k - 1], (d, at)),
            remote(part_kq.at[at], came_kq.at[k - 1], rs_send.at[1, k - 1], rs_recv.at[1, k - 1], (d, at)),
        )

    def ag_copies(k):
        to = lax.rem(s + k, parts)
        return (
            remote(sum_low.at[s], sum_low.at[s], ag_send.at[0, k - 1], ag_recv.at[0, k - 1], (d, to)),
            remote(sum_kq.at[s], sum_kq.at[s], ag_send.at[1, k - 1], ag_recv.at[1, k - 1], (d, to)),
        )

    def ag_taken(k, part):
        return (
            remote(sum_low.at[part], sum_low.at[part], ag_send.at[0, k - 1], ag_recv.at[0, k - 1], (d, s)),
            remote(sum_kq.at[part], sum_kq.at[part], ag_send.at[1, k - 1], ag_recv.at[1, k - 1], (d, s)),
        )

    def convolve(part):
        start = pl.multiple_of(part * span, span)
        before = pl.multiple_of(jnp.maximum(start - 16, 0), 16)
        wide = min(256, channels)
        for left in range(0, channels, wide):
            cols = slice(left, left + wide)
            head = conv_in_ref[pl.ds(before, 16), cols].astype(jnp.float32)
            head = jnp.where(part == 0, 0.0, head)
            body = jnp.concatenate([head, conv_in_ref[pl.ds(start, span), cols].astype(jnp.float32)], axis=0)
            total = conv_b_ref[:, cols]
            for tap in range(taps):
                by = taps - 1 - tap
                total = total + body[16 - by : 16 - by + span] * conv_w_ref[tap : tap + 1, cols]
            values_ref[pl.ds(start, span), cols] = (total * sigmoid(total)).astype(jnp.bfloat16)
        projected = jnp.dot(values_ref[pl.ds(start, span), :], select_ref[...], preferred_element_type=jnp.float32)
        part_low[part] = projected[:, :LANE].astype(jnp.bfloat16)
        pack = projected[:short, LANE:]
        for g in range(1, packed):
            pack = pack + pltpu.roll(projected[g * short : (g + 1) * short, LANE:], g * 2 * states, 1)
        part_kq[part] = pack

    @pl.when(step < parts - 1)
    def _():
        convolve(lax.rem(s + 1 + step, parts))

    for k in range(1, parts):
        @pl.when(step == k - 1)
        def _():
            for copy in rs_copies(k):
                copy.start()

    @pl.when(step == parts - 2)
    def _():
        send_cot(1, 2)

    @pl.when(step == parts - 1)
    def _():
        convolve(s)
        low = part_low[s].astype(jnp.float32)
        kq = part_kq[s]
        for k in range(1, parts):
            for copy in rs_copies(k):
                copy.wait_recv()
            low = low + came_low[k - 1].astype(jnp.float32)
            kq = kq + came_kq[k - 1]
        sum_low[s] = low.astype(jnp.bfloat16)
        sum_kq[s] = kq
        for k in range(1, parts):
            for copy in ag_copies(k):
                copy.start()
        send_cot(1, 3)
        send_cot(2, 1, False)

    per_part = span // rows
    at_block = step - parts

    def unpack(part):
        start = pl.multiple_of(part * span, span)
        low_ref[pl.ds(start, span), :] = sum_low[part]
        pack = sum_kq[part]
        lane = lax.broadcasted_iota(jnp.int32, pack.shape, 1)
        for g in range(packed):
            turned = pack if g == 0 else pltpu.roll(pack, LANE - g * 2 * states, 1)
            kq_ref[pl.ds(pl.multiple_of(start + g * short, short), short), :] = jnp.where(lane < 2 * states, turned, 0.0)

    for part in range(parts):
        @pl.when(at_block == part * per_part)
        def _():
            for k in range(1, parts):
                @pl.when(lax.rem(s - k + parts, parts) == part)
                def _():
                    for copy in ag_taken(k, part):
                        copy.wait_recv()

            unpack(part)

    plan = (
        (("outer", 0), ("inner", 2)), (("outer", 1), ("inner", 3)), (("outer", 2), ("outer", 3)), (("last", 0),),
        (("last", 1), ("last", 2)), (("last", 3),),
    )
    for at, moves in enumerate(plan):
        @pl.when(at_block == at)
        def _():
            for kind, c in moves:
                if kind == "last":
                    take_cot(2, c)
                    send_cot(3, c)
                else:
                    send_cot(2, c, kind == "outer")

    @pl.when(jnp.logical_and(at_block >= 0, at_block < length // rows))
    def _():
        here = pl.ds(pl.multiple_of(at_block * rows, rows), rows)
        kq = kq_ref[here, :]
        values = values_ref[here, :].astype(jnp.float32)
        beta, inverse = step_sizes(low_ref[here, :], kq, weight_ref, bias_ref, states)
        rates = beta * inverse
        rate_ref[...] = by_eights(rates)
        input_ref[...] = by_eights(rates * values)
        spread_columns(kq, row_ref, pick_ref, key_ref, query_ref, states)
        forward_rows(states, rows, channels, history_ref, state_ref, key_ref, query_ref, rate_ref, input_ref, out_ref, half_ref)
        mixed = as_rows(out_ref[...]) + skip_ref[...] * values
        gate = gate_ref[...]
        mixed_ref[...] = mixed
        gated_all[here, :] = (mixed * gate * sigmoid(gate)).astype(jnp.bfloat16)

    width = cot_all.shape[1]
    tile = min(512, width)

    def leaving(part, which):
        here = pl.ds(pl.multiple_of(part * span, span), span)
        ref, out = ((dgated_ref, dgated_out), (result_ref, result_out))[which]
        return pltpu.make_async_copy(ref.at[here, :], out.at[here, :], leave_sem.at[part, which])

    values_copy = pltpu.make_async_copy(values_ref, values_out, local_sem.at[2])

    @pl.when(step == parts)
    def _():
        values_copy.start()

    def products(part):
        here = pl.ds(pl.multiple_of(part * span, span), span)

        def across(n, carry):
            cols = pl.ds(pl.multiple_of(n * tile, tile), tile)
            out_total[:, cols] += lax.dot_general(
                gated_all[here, :], cot_all[here, cols], (((0,), (0,)), ((), ())), preferred_element_type=jnp.float32
            )
            return carry

        lax.fori_loop(0, width // tile, across, 0)
        deep = min(512, channels)

        def along(n, carry):
            cols = pl.ds(pl.multiple_of(n * deep, deep), deep)
            dgated_ref[here, cols] = lax.dot_general(
                cot_all[here, :], out_all[cols, :], (((1,), (1,)), ((), ())), preferred_element_type=jnp.float32
            )
            return carry

        lax.fori_loop(0, channels // deep, along, 0)
        leaving(part, 0).start()

    def result_terms(part):
        here = pl.ds(part * span, span)

        def across(n, carry):
            cols = pl.ds(pl.multiple_of(n * tile, tile), tile)
            result_ref[here, cols] = jnp.dot(
                gated_all[here, :], out_all[:, cols], preferred_element_type=jnp.float32
            ).astype(jnp.bfloat16)
            return carry

        lax.fori_loop(0, width // tile, across, 0)
        leaving(part, 1).start()

    @pl.when(at_block == length // rows - per_part)
    def _():
        own_copy(0).wait()
        for copy in out_copies:
            copy.wait_recv()
        for part in range(parts - 1):
            result_terms(part)
        for way in (1, -1):
            @pl.when(sends_result(way))
            def _():
                early_result(way).start()

    def products_at(low, high):
        def each(part, carry):
            away = jnp.abs(part - s)

            @pl.when(jnp.logical_and(away >= low, away <= high))
            def _():
                products(part)

            return carry

        lax.fori_loop(0, parts, each, 0)

    @pl.when(step == pl.num_programs(0) - 1)
    def _():
        final_ref[...] = state_ref[...]
        out_total[...] = jnp.zeros_like(out_total)
        own_copy(1).wait()
        for way in (1, -1):
            @pl.when(inner)
            def _():
                early_rows(way).wait()

            @pl.when(arrives(way, 1))
            def _():
                end_rows(way).wait()

        result_terms(parts - 1)
        products_at(0, 0)
        for c in range(1, 4):
            take_cot(1, c)
        products_at(1, 1)
        products_at(2, parts - 2)
        for c in range(4):
            take_cot(parts - 1, c)
        products_at(parts - 1, parts - 1)
        out_part_ref[...] = out_total[...].astype(jnp.bfloat16)
        values_copy.wait()
        for way in (1, -1):
            @pl.when(takes_result(way))
            def _():
                early_result(way).wait_recv()

            @pl.when(sends_result(way))
            def _():
                early_result(way).wait_send()

        for part in range(parts):
            leaving(part, 0).wait()
            leaving(part, 1).wait()
        for copy in out_copies:
            copy.wait_send()
        for distance in range(1, parts):
            for c in range(1 if distance == 1 else 0, 4):
                sent_cot(distance, c)
        for k in range(1, parts):
            for copy in rs_copies(k) + ag_copies(k):
                copy.wait_send()


def linked_forward(
    conv_in, gate, select, vectors, weight, out_shard, cot_shard, cot_early, parts, dps, taps, states
):
    length, channels = conv_in.shape
    block, width = out_shard.shape
    span = length // parts
    rows = min(128, span)
    blocks = length // rows
    short = span // (LANE // (2 * states))
    at = lambda i: jnp.clip(i - parts, 0, blocks - 1)
    by_row = lambda size: pl.BlockSpec((rows, size), lambda i: (at(i), 0))
    whole = lambda a: pl.BlockSpec(a.shape, lambda i: (0, 0))
    kept = lambda *shape: pl.BlockSpec(shape, lambda i: (0, 0))
    anywhere = pl.BlockSpec(memory_space=pl.ANY)
    dma = pltpu.SemaphoreType.DMA
    f32, low = jnp.float32, jnp.bfloat16
    eights = pltpu.VMEM((rows // 8, 8, channels), f32)
    return pl.pallas_call(
        lambda *refs: linked_forward_body(states, parts, dps, taps, *refs),
        grid=(parts + blocks + 1,),
        in_specs=[
            whole(conv_in), by_row(channels), whole(select), whole(vectors), whole(weight), anywhere, anywhere,
            anywhere,
        ],
        out_specs=[
            by_row(channels), pl.BlockSpec((rows * states, channels), lambda i: (at(i), 0)),
            kept(states, channels), anywhere, kept(length, LANE), kept(length, LANE),
            anywhere, anywhere, kept(dps * block, width), anywhere,
            pl.BlockSpec((rows * states, LANE), lambda i: (at(i), 0)), pl.BlockSpec((rows * states, LANE), lambda i: (at(i), 0)),
        ],
        out_shape=[
            jax.ShapeDtypeStruct((length, channels), f32),
            jax.ShapeDtypeStruct((length * states, channels), low),
            jax.ShapeDtypeStruct((states, channels), f32),
            jax.ShapeDtypeStruct((length, channels), low),
            jax.ShapeDtypeStruct((length, LANE), low),
            jax.ShapeDtypeStruct((length, LANE), f32),
            jax.ShapeDtypeStruct((length, channels), f32),
            jax.ShapeDtypeStruct((length, width), low),
            jax.ShapeDtypeStruct((dps * block, width), low),
            jax.ShapeDtypeStruct((span, width), low),
            jax.ShapeDtypeStruct((length * states, LANE), f32),
            jax.ShapeDtypeStruct((length * states, LANE), f32),
        ],
        scratch_shapes=[
            pltpu.VMEM((states, channels), f32),
            eights, eights, eights, pltpu.VMEM((rows // 8, 8, LANE), f32),
            pltpu.VMEM((rows * states, LANE), low), pltpu.VMEM((channels // LANE * 64, LANE), f32),
            pltpu.VMEM((parts, span, LANE), low), pltpu.VMEM((parts, short, LANE), f32),
            pltpu.VMEM((parts - 1, span, LANE), low), pltpu.VMEM((parts - 1, short, LANE), f32),
            pltpu.VMEM((parts, span, LANE), low), pltpu.VMEM((parts, short, LANE), f32),
            dma((2, parts - 1)), dma((2, parts - 1)), dma((2, parts - 1)), dma((2, parts - 1)),
            dma((dps - 1,)), dma((dps - 1,)), dma((2, parts, 4)), dma((2, parts, 4)), dma((5,)),
            pltpu.VMEM((dps * block, width), low), pltpu.VMEM((length, width), low), pltpu.VMEM((length, channels), low),
            pltpu.VMEM((dps * block, width), f32), pltpu.VMEM((length, channels), low),
            pltpu.VMEM((length, channels), f32), pltpu.VMEM((length, width), low), dma((parts, 2)), dma((2,)), dma((2,)),
        ],
        compiler_params=pltpu.CompilerParams(
            collective_id=4, has_side_effects=True, vmem_limit_bytes=60 * 1024 * 1024
        ),
        cost_estimate=pl.CostEstimate(
            flops=14 * length * states * channels, bytes_accessed=2 * length * states * channels, transcendentals=0
        ),
    )(conv_in, gate, select, vectors, weight, out_shard, cot_shard, cot_early)


def linked_backward_body(
    states, parts, dps, taps,
    low_ref, kq_ref, gate_ref, mixed_ref, dgated_ref, history_ref, final_ref, weight_ref,
    values_ref, conv_in_ref, select_ref, given_ref, tokens_ref, early_ref, key_ref, query_ref, part_hbm, out_ref,
    dmixed_out, small_ref, result_ref, out_grad_ref,
    grad_ref, state_ref, rate_ref, inverse_ref, do_ref, values32_ref, fed_ref, kept_ref, part_key_ref,
    part_query_ref, placed_ref, half_ref,
    dvalues_ref, dproj_ref, next_ref, vector_ref, part_low, part_kq, came_low, came_kq, sum_low, sum_kq,
    rs_send, rs_recv, ag_send, ag_recv, result_came, line_send, line_recv, out_send, out_recv,
    out_came, out_here, local_sem, dmixed_ref, part_ref, leave_sem,
):
    d, s = lax.axis_index("dp"), lax.axis_index("seq")
    step = pl.program_id(0)
    rows, channels = gate_ref.shape
    length = values_ref.shape[0]
    blocks = length // rows
    span = length // parts
    per_part = span // rows
    packed = LANE // (2 * states)
    short = span // packed
    sel = select_ref.shape[1]
    conv_w_ref, conv_b_ref = given_ref, given_ref[taps : taps + 1, :]
    bias_ref, skip_ref = given_ref[taps + 1 : taps + 2, :], given_ref[taps + 2 : taps + 3, :]

    def remote(src, dst, send, recv, to):
        return pltpu.make_async_remote_copy(
            src_ref=src, dst_ref=dst, send_sem=send, recv_sem=recv, device_id=to, device_id_type=MESH
        )

    copies = []
    for k in range(1, dps):
        to = lax.rem(d + k, dps)
        copies.append(remote(out_ref.at[to], out_came.at[k - 1], out_send.at[k - 1], out_recv.at[k - 1], (to, s)))
    out_copy = pltpu.make_async_copy(out_ref.at[d], out_here, local_sem.at[0])
    part_copy = pltpu.make_async_copy(part_hbm, part_ref, local_sem.at[1])
    pass_line, line_total, line_sent = line_sums(parts, span, part_ref, result_came, line_send, line_recv, early_ref)

    @pl.when(step == 0)
    def _():
        part_copy.start()
        barrier = pltpu.get_barrier_semaphore()
        for k in range(1, parts):
            pl.semaphore_signal(barrier, inc=1, device_id=(d, lax.rem(s + k, parts)), device_id_type=MESH)
        for k in range(1, dps):
            pl.semaphore_signal(barrier, inc=1, device_id=(lax.rem(d + k, dps), s), device_id_type=MESH)
        pl.semaphore_wait(barrier, parts + dps - 2)
        grad_ref[...] = jnp.zeros_like(grad_ref)
        state_ref[...] = final_ref[...]
        next_ref[...] = jnp.zeros_like(next_ref)
        vector_ref[...] = jnp.zeros_like(vector_ref)
        small_ref[...] = jnp.zeros_like(small_ref)
        for copy in copies:
            copy.start()
        out_copy.start()
        part_copy.wait()

    def rs_copies(k):
        at = lax.rem(s + k, parts)
        return (
            remote(part_low.at[at], came_low.at[k - 1], rs_send.at[0, k - 1], rs_recv.at[0, k - 1], (d, at)),
            remote(part_kq.at[at], came_kq.at[k - 1], rs_send.at[1, k - 1], rs_recv.at[1, k - 1], (d, at)),
        )

    def ag_copies(k):
        to = lax.rem(s + k, parts)
        return (
            remote(sum_low.at[s], sum_low.at[s], ag_send.at[0, k - 1], ag_recv.at[0, k - 1], (d, to)),
            remote(sum_kq.at[s], sum_kq.at[s], ag_send.at[1, k - 1], ag_recv.at[1, k - 1], (d, to)),
        )

    def ag_taken(k, part):
        return (
            remote(sum_low.at[part], sum_low.at[part], ag_send.at[0, k - 1], ag_recv.at[0, k - 1], (d, s)),
            remote(sum_kq.at[part], sum_kq.at[part], ag_send.at[1, k - 1], ag_recv.at[1, k - 1], (d, s)),
        )

    def add_up():
        low = part_low[s].astype(jnp.float32)
        kq = part_kq[s]
        for k in range(1, parts):
            for copy in rs_copies(k):
                copy.wait_recv()
            low = low + came_low[k - 1].astype(jnp.float32)
            kq = kq + came_kq[k - 1]
        sum_low[s] = low.astype(jnp.bfloat16)
        sum_kq[s] = kq.astype(jnp.bfloat16)
        for k in range(1, parts):
            for copy in ag_copies(k):
                copy.start()

    def leaving(part):
        here = pl.ds(pl.multiple_of(part * span, span), span)
        return pltpu.make_async_copy(dmixed_ref.at[here, :], dmixed_out.at[here, :], leave_sem.at[part])

    def conv_back(part):
        for k in range(1, parts):
            @pl.when(lax.rem(s - k + parts, parts) == part)
            def _():
                for copy in ag_taken(k, part):
                    copy.wait_recv()

        here = pl.ds(pl.multiple_of(part * span, span), span)
        before = pl.multiple_of(jnp.maximum(part * span - 16, 0), 16)
        dproj_ref[:, :LANE] = sum_low[part]
        pack = sum_kq[part].astype(jnp.float32)
        lane = lax.broadcasted_iota(jnp.int32, pack.shape, 1)
        for g in range(packed):
            turned = pack if g == 0 else pltpu.roll(pack, LANE - g * 2 * states, 1)
            dproj_ref[g * short : (g + 1) * short, LANE:] = jnp.where(lane < 2 * states, turned, 0.0).astype(jnp.bfloat16)
        wide = min(256, channels)
        for left in range(0, channels, wide):
            cols = slice(left, left + wide)
            small_ref[cols, :sel] += lax.dot_general(
                values_ref[here, cols], dproj_ref[...], (((0,), (0,)), ((), ())), preferred_element_type=jnp.float32
            )
            head = conv_in_ref[pl.ds(before, 16), cols].astype(jnp.float32)
            head = jnp.where(part == 0, 0.0, head)
            body = jnp.concatenate([head, conv_in_ref[here, cols].astype(jnp.float32)], axis=0)
            total = conv_b_ref[:, cols]
            for tap in range(taps):
                by = taps - 1 - tap
                total = total + body[16 - by : 16 - by + span] * conv_w_ref[tap : tap + 1, cols]
            sg = sigmoid(total)
            dvalues = dvalues_ref[here, cols] + lax.dot_general(
                dproj_ref[...], select_ref[cols, :], (((1,), (1,)), ((), ())), preferred_element_type=jnp.float32
            )
            dconv = dvalues * (sg + total * sg * (1.0 - sg))
            vector_ref[taps : taps + 1, cols] += jnp.sum(dconv, axis=0, keepdims=True)
            after = jnp.concatenate([dconv, next_ref[:, cols]], axis=0)
            dconv_in = jnp.zeros_like(dconv)
            for tap in range(taps):
                by = taps - 1 - tap
                shifted = body[16 - by : 16 - by + span]
                vector_ref[tap : tap + 1, cols] += jnp.sum(dconv * shifted, axis=0, keepdims=True)
                dconv_in = dconv_in + after[by : by + span] * conv_w_ref[tap : tap + 1, cols]
            next_ref[:, cols] = dconv[0:8]
            dmixed_ref[here, cols] = dconv_in.astype(jnp.bfloat16)
        leaving(part).start()

    plan = (((3, 0), (3, 1)), ((3, 2), (3, 3)), ((2, 0), (2, 1)), ((2, 2), (2, 3)), ((1, 0), (1, 1)), ((1, 2), (1, 3)))
    for at_step, moves in enumerate(plan):
        @pl.when(step == at_step)
        def _():
            for steps, c in moves:
                pass_line(steps, c)

    for part in range(parts):
        ends = (parts - part) * per_part - 1
        sums = min(ends + 3, blocks - 1 if part > 0 else blocks)

        @pl.when(jnp.logical_and(step == sums, s == part))
        def _():
            add_up()

        @pl.when(step == blocks + 1 - part)
        def _():
            conv_back(part)

    @pl.when(step < blocks)
    def _():
        block = blocks - 1 - step
        here = pl.ds(pl.multiple_of(block * rows, rows), rows)
        low, kq = low_ref[...], kq_ref[...]
        beta, inverse = step_sizes(low, kq, weight_ref, bias_ref, states)
        rate_ref[...] = by_eights(beta * inverse)
        inverse_ref[...] = inverse
        values = values_ref[here, :].astype(jnp.float32)
        values32_ref[...] = by_eights(values)
        gate = gate_ref[...]
        dgated = dgated_ref[...].astype(jnp.float32)
        sg = sigmoid(gate)
        do = dgated * (gate * sg)
        do_ref[...] = by_eights(do)
        dmixed_ref[here, channels:] = (dgated * mixed_ref[...] * (sg + gate * sg * (1.0 - sg))).astype(jnp.bfloat16)
        vector_ref[taps + 2 : taps + 3, :] += jnp.sum(do * values, axis=0, keepdims=True)
        backward_rows(
            states, rows, channels, history_ref, grad_ref, state_ref, key_ref, query_ref, rate_ref, do_ref, values32_ref,
            fed_ref, kept_ref, part_key_ref, part_query_ref, half_ref,
        )
        fed = as_rows(fed_ref[...])
        dvalues_ref[here, :] = fed + skip_ref[...] * as_rows(do_ref[...])
        scaled = as_rows(values32_ref[...]) * fed - as_rows(kept_ref[...])
        rates = as_rows(rate_ref[...])
        dpre = scaled * (inverse_ref[...] - rates)
        vector_ref[taps + 1 : taps + 2, :] += jnp.sum(dpre, axis=0, keepdims=True)
        dpre_low = dpre.astype(jnp.bfloat16)
        small_ref[:, sel : sel + LANE] += lax.dot_general(
            dpre_low, low, (((0,), (0,)), ((), ())), preferred_element_type=jnp.float32
        )
        through = -2.0 * jnp.sum(scaled * rates, axis=1, keepdims=True)
        gather_columns(part_key_ref, part_query_ref, placed_ref, rows, states)
        lanes = lax.broadcasted_iota(jnp.int32, kq.shape, 1)
        dkq = as_rows(placed_ref[...]) + jnp.where(lanes < states, kq * through, 0.0)
        part = block // per_part
        within = lax.rem(block, per_part)
        part_low[part, pl.ds(pl.multiple_of(within * rows, rows), rows), :] = jnp.dot(
            dpre_low, weight_ref[...], preferred_element_type=jnp.float32
        ).astype(jnp.bfloat16)
        for g in range(packed):
            first = g * short - within * rows

            @pl.when(jnp.logical_and(first >= 0, first < rows))
            def _():
                for w in range(per_part):
                    if w * rows <= g * short < (w + 1) * rows:
                        lo = g * short - w * rows
                        piece = dkq[lo : lo + short]
                        piece = piece if g == 0 else pltpu.roll(piece, g * 2 * states, 1)
                        if g == (per_part - 1) * rows // short:
                            part_kq[part] = piece
                        else:
                            part_kq[part] += piece

        @pl.when(within == 0)
        def _():
            for k in range(1, parts):
                @pl.when(lax.rem(s + k, parts) == part)
                def _():
                    for copy in rs_copies(k):
                        copy.start()

    @pl.when(step == pl.num_programs(0) - 1)
    def _():
        small_ref[:, sel + LANE :] = jnp.transpose(vector_ref[...])
        chunk = span // 4
        for c in range(4):
            at = pl.ds(c * chunk, chunk)
            result_ref[at, :] = (tokens_ref[at, :].astype(jnp.float32) + line_total(c)).astype(jnp.bfloat16)
        line_sent()
        for part in range(parts):
            leaving(part).wait()
        out_copy.wait()
        total = out_here[...].astype(jnp.float32)
        for k in range(1, dps):
            copies[k - 1].wait_recv()
            total = total + out_came[k - 1].astype(jnp.float32)
        out_grad_ref[...] = total
        for copy in copies:
            copy.wait_send()
        for k in range(1, parts):
            for copy in rs_copies(k) + ag_copies(k):
                copy.wait_send()


def linked_backward(
    low, kq, gate, mixed, dgated, history, final, weight, values, conv_in, select, vectors, tokens, early,
    key, query, result_part, out_part, parts, taps, states,
):
    length, channels = values.shape
    dps = out_part.shape[0]
    width = tokens.shape[1]
    sel = select.shape[1]
    span = length // parts
    rows = min(128, span)
    blocks = length // rows
    short = span // (LANE // (2 * states))
    at = lambda i: jnp.maximum(blocks - 1 - i, 0)
    by_row = lambda size: pl.BlockSpec((rows, size), lambda i: (at(i), 0))
    whole = lambda a: pl.BlockSpec(a.shape, lambda i: (0, 0))
    kept = lambda *shape: pl.BlockSpec(shape, lambda i: (0, 0))
    anywhere = pl.BlockSpec(memory_space=pl.ANY)
    dma = pltpu.SemaphoreType.DMA
    f32, bf16 = jnp.float32, jnp.bfloat16
    wide = pltpu.VMEM((rows // 8, 8, channels), f32)
    eights = pltpu.VMEM((rows // 8, 8, LANE), f32)
    spread = pltpu.VMEM((rows * states, LANE), f32)
    return pl.pallas_call(
        lambda *refs: linked_backward_body(states, parts, dps, taps, *refs),
        grid=(blocks + 2,),
        in_specs=[
            by_row(LANE), by_row(LANE), by_row(channels), by_row(channels), by_row(channels),
            pl.BlockSpec((rows * states, channels), lambda i: (at(i), 0)),
            whole(final), whole(weight), whole(values), whole(conv_in), whole(select), whole(vectors), whole(tokens),
            whole(early), pl.BlockSpec((rows * states, LANE), lambda i: (at(i), 0)),
            pl.BlockSpec((rows * states, LANE), lambda i: (at(i), 0)), anywhere, anywhere,
        ],
        out_specs=[anywhere, kept(channels, sel + 2 * LANE), kept(span, width), kept(*out_part.shape[1:])],
        out_shape=[
            jax.ShapeDtypeStruct((length, 2 * channels), bf16),
            jax.ShapeDtypeStruct((channels, sel + 2 * LANE), f32),
            jax.ShapeDtypeStruct((span, width), bf16),
            jax.ShapeDtypeStruct(out_part.shape[1:], f32),
        ],
        scratch_shapes=[
            pltpu.VMEM((states, channels), f32), pltpu.VMEM((states, channels), f32),
            wide, pltpu.VMEM((rows, channels), f32), wide, wide, wide, wide, spread, spread, eights,
            pltpu.VMEM((2 * channels // LANE * 64, LANE), f32),
            pltpu.VMEM((length, channels), f32), pltpu.VMEM((span, sel), bf16), pltpu.VMEM((8, channels), f32),
            pltpu.VMEM((LANE, channels), f32),
            pltpu.VMEM((parts, span, LANE), bf16), pltpu.VMEM((parts, short, LANE), f32),
            pltpu.VMEM((parts - 1, span, LANE), bf16), pltpu.VMEM((parts - 1, short, LANE), f32),
            pltpu.VMEM((parts, span, LANE), bf16), pltpu.VMEM((parts, short, LANE), bf16),
            dma((2, parts - 1)), dma((2, parts - 1)), dma((2, parts - 1)), dma((2, parts - 1)),
            pltpu.VMEM((parts + 1, span, width), bf16), dma((2, parts, 4)), dma((2, parts, 4)),
            dma((dps - 1,)), dma((dps - 1,)), pltpu.VMEM((dps - 1,) + out_part.shape[1:], bf16),
            pltpu.VMEM(out_part.shape[1:], bf16), dma((2,)), pltpu.VMEM((length, 2 * channels), bf16),
            pltpu.VMEM((length, width), bf16), dma((parts,)),
        ],
        compiler_params=pltpu.CompilerParams(
            collective_id=5, has_side_effects=True, vmem_limit_bytes=60 * 1024 * 1024
        ),
        cost_estimate=pl.CostEstimate(
            flops=30 * length * states * channels, bytes_accessed=2 * length * states * channels, transcendentals=0
        ),
    )(low, kq, gate, mixed, dgated, history, final, weight, values, conv_in, select, vectors, tokens, early, key, query, result_part, out_part)


def contract(left, right, left_dim, right_dim):
    return lax.dot_general(
        left, right, (((left_dim,), (right_dim,)), ((), ())), preferred_element_type=jnp.float32
    )


def gathered(shard, axis):
    return lax.all_gather(shard, axis, axis=0, tiled=True)


def scattered(total, axis):
    return lax.psum_scatter(total, axis, scatter_dimension=0, tiled=True)


def summed_rows(partial, axis):
    size = lax.axis_size(axis)
    parts = partial.astype(jnp.bfloat16).reshape((size, partial.shape[0] // size) + partial.shape[1:])
    parts = lax.all_to_all(parts, axis, 0, 0)
    return jnp.sum(parts.astype(jnp.float32), axis=0)


def later(rows, by):
    if by == 0:
        return rows
    return jnp.pad(rows, ((by, 0), (0, 0)))[: rows.shape[0]]


def sooner(rows, by):
    if by == 0:
        return rows
    return jnp.pad(rows, ((0, by), (0, 0)))[by:]


def local(
    tokens,
    cotangent,
    norm_gain,
    in_weight,
    conv_weight,
    conv_bias,
    select_weight,
    beta_weight,
    beta_bias,
    skip_gain,
    out_weight,
):
    parts, dps = lax.axis_size("seq"), lax.axis_size("dp")
    rows, width = tokens.shape[1:]
    block = conv_weight.shape[0]
    channels = block * dps
    taps = conv_weight.shape[1]
    rank = beta_weight.shape[1]
    states = (select_weight.shape[1] - rank) // 2
    own = in_weight.shape[0]

    flat = tokens.reshape(rows, width).astype(jnp.float32)
    scale = lax.rsqrt(jnp.mean(flat * flat, axis=-1, keepdims=True) + 1e-05)
    vectors = jnp.concatenate(
        [conv_weight, conv_bias[:, None], beta_bias[:, None], skip_gain[:, None]], axis=1
    )
    wide = -(-select_weight.shape[1] // LANE) * LANE
    small = jnp.concatenate(
        [
            jnp.pad(select_weight, ((0, 0), (0, wide - select_weight.shape[1]))),
            beta_weight,
            jnp.pad(vectors, ((0, 0), (0, LANE - vectors.shape[1]))),
        ],
        axis=1,
    )
    small_slice = (dps, parts, 2 * own, rank) == (8, 4, LANE, LANE)
    if small_slice:
        doubled = jnp.broadcast_to(jnp.tile(norm_gain.reshape(1, own), (1, 2)), (GAIN_ROWS, LANE))
        normed, in_w, conv_in, gate, select_w, beta_w, vectors, gain, cot_early = start(
            tokens.reshape(rows, width), in_weight, small, doubled, cotangent.reshape(rows, width), parts, dps
        )
    else:
        gain = gathered(norm_gain, ("dp", "seq"))
        normed = gathered((flat * scale * gain.astype(jnp.float32)).astype(jnp.bfloat16), "seq")
        spread = in_weight.reshape(own, 2, dps, parts, block).transpose(3, 0, 1, 2, 4).reshape(parts, own, 2 * channels)
        in_w = gathered(lax.all_to_all(spread, "seq", 0, 0).reshape(parts * own, 2 * channels), "dp")
        smalls = gathered(small, "dp")
        conv_in = jnp.dot(normed, in_w[:, :channels], preferred_element_type=jnp.float32).astype(jnp.bfloat16)
        gate = jnp.dot(normed, in_w[:, channels:], preferred_element_type=jnp.float32)
    cot_here = cotangent.reshape(rows, width)
    if small_slice:
        mixed, history, final, values, low, kq, dgated, result_part, out_part, early, key, query = linked_forward(
            conv_in, gate, select_w, vectors, beta_w, out_weight, cot_here, cot_early, parts, dps, taps, states,
        )
    else:
        gain = gain.astype(jnp.float32)
        select_w = smalls[:, : select_weight.shape[1]]
        beta_w = smalls[:, wide : wide + rank]
        vectors = smalls[:, wide + rank :].astype(jnp.float32)
        conv_w, conv_b = vectors[:, :taps], vectors[:, taps]
        beta_b, skip = vectors[:, taps + 1].reshape(1, channels), vectors[:, taps + 2].reshape(1, channels)
        conv_wide = conv_in.astype(jnp.float32)
        conv_sum = conv_b
        for tap in range(taps):
            conv_sum = conv_sum + later(conv_wide, taps - 1 - tap) * conv_w[:, tap]
        out_w = gathered(out_weight, "dp")
        cot = gathered(cot_here, "seq")
        values = jax.nn.silu(conv_sum).astype(jnp.bfloat16)
        projected = lax.psum(jnp.dot(values, select_w, preferred_element_type=jnp.float32), "seq")
        low = projected[:, :rank].astype(jnp.bfloat16)
        kq = jnp.pad(projected[:, rank:], ((0, 0), (0, LANE - 2 * states)))
        gated, mixed, history, final = forward_scan(low, kq, values, gate, beta_w, beta_b, skip, states)
        result_part = jnp.dot(gated, out_w, preferred_element_type=jnp.float32).astype(jnp.bfloat16)
        out_part = contract(gated, cot, 0, 0).astype(jnp.bfloat16)
        dgated = contract(cot, out_w, 1, 1)
    out_part = out_part.reshape(dps, block, width)
    if small_slice:
        dmixed, small_grads, result, out_grad = linked_backward(
            low, kq, gate, mixed, dgated, history, final, beta_w, values, conv_in, select_w, vectors,
            tokens.reshape(rows, width), early, key, query, result_part, out_part, parts, taps, states,
        )
        small_grads = small_grads.reshape(dps, block, wide + rank + LANE)
    else:
        result_part = result_part.reshape(parts, rows, width)
        dgate, dpre_low, dvalues, dlow, dkq, bias_grad, skip_grad, result_came, out_came = backward_scan(
            low, kq, values, gate, mixed, dgated, history, final, beta_w, beta_b, skip, result_part, out_part, states
        )
        part_here = lax.dynamic_index_in_dim(result_part, lax.axis_index("seq"), 0, False).astype(jnp.float32)
        result = (flat + (part_here + jnp.sum(result_came.astype(jnp.float32), axis=0))).astype(jnp.bfloat16)
        out_here = lax.dynamic_index_in_dim(out_part, lax.axis_index("dp"), 0, False).astype(jnp.float32)
        out_grad = out_here + jnp.sum(out_came.astype(jnp.float32), axis=0)
        dprojected = lax.psum(jnp.concatenate([dlow, dkq[:, : 2 * states]], axis=1), "seq").astype(jnp.bfloat16)
        beta_grad = contract(dpre_low, low, 0, 0)
        select_grad = contract(values, dprojected, 0, 0)
        dvalues = contract(dprojected, select_w, 1, 1) + dvalues
        s = jax.nn.sigmoid(conv_sum)
        dconv = dvalues * (s + conv_sum * s * (1.0 - s))
        conv_w_grad = jnp.stack(
            [jnp.sum(dconv * later(conv_wide, taps - 1 - tap), axis=0) for tap in range(taps)], axis=1
        )
        conv_b_grad = jnp.sum(dconv, axis=0)
        dconv_in = 0.0
        for tap in range(taps):
            dconv_in = dconv_in + sooner(dconv, taps - 1 - tap) * conv_w[:, tap]
        dmixed = jnp.concatenate([dconv_in.astype(jnp.bfloat16), dgate], axis=1)
        vector_grads = jnp.concatenate(
            [conv_w_grad, conv_b_grad[:, None], bias_grad.reshape(channels, 1), skip_grad.reshape(channels, 1)], axis=1
        )
        small_grads = jnp.concatenate(
            [
                jnp.pad(select_grad, ((0, 0), (0, wide - select_grad.shape[1]))),
                beta_grad,
                jnp.pad(vector_grads, ((0, 0), (0, LANE - vector_grads.shape[1]))),
            ],
            axis=1,
        ).reshape(dps, block, wide + rank + LANE)
    if small_slice:
        input_grad, in_grad, gain_sums, small_grads = end(
            dmixed, normed, in_w, tokens.reshape(rows, width), cot_here, gain, in_weight, small_grads,
            parts, block,
        )
        gain_sums = gain_sums[:, 0]
    else:
        in_grad = summed_rows(contract(normed, dmixed, 0, 0), "dp").astype(jnp.bfloat16)
        in_grad = lax.all_to_all(in_grad.reshape(parts, own, 2 * channels), "seq", 0, 0).astype(jnp.float32)
        in_grad = in_grad.reshape(parts, own, 2, dps, block).transpose(1, 2, 3, 0, 4).reshape(own, 2 * parts * channels)
        gain_sums = jnp.sum(in_grad * in_weight.astype(jnp.float32), axis=1)
        v = summed_rows(contract(dmixed, in_w, 1, 1), "seq") * gain
        du = scale * v - flat * (scale * scale * scale) * jnp.mean(flat * v, axis=-1, keepdims=True)
        input_grad = (cot_here.astype(jnp.float32) + du).astype(jnp.bfloat16)
        small_grads = jnp.sum(lax.all_to_all(small_grads, "dp", 0, 0), axis=0)
    rows_grad = small_grads[:, wide + rank :]
    return (
        result.reshape(tokens.shape),
        input_grad.reshape(tokens.shape),
        gain_sums / norm_gain.astype(jnp.float32),
        in_grad.astype(jnp.float32),
        rows_grad[:, :taps],
        rows_grad[:, taps],
        small_grads[:, : select_weight.shape[1]],
        small_grads[:, wide : wide + rank],
        rows_grad[:, taps + 1],
        rows_grad[:, taps + 2],
        out_grad,
    )


def solution(mesh):
    split = P(("dp", "seq"))
    rows = P("dp", "seq", None)
    return jax.shard_map(
        local,
        mesh=mesh,
        in_specs=(rows, rows) + (split,) * 9,
        out_specs=(rows, rows) + (split,) * 9,
        check_vma=False,
    )
```

```python
import jax
import jax.numpy as jnp
from jax import lax
from jax.experimental import pallas as pl
from jax.experimental.pallas import tpu as pltpu
from jax.sharding import PartitionSpec as P

LANE = 128
PER_GROUP = 4


def sigmoid(v):
    return 1.0 / (1.0 + jnp.exp(-v))


def by_eights(value):
    return value.reshape(value.shape[0] // 8, 8, value.shape[1])


def as_rows(value):
    return value.reshape(value.shape[0] * 8, value.shape[2])


def spread_columns(kq, row_ref, pick_ref, key_ref, query_ref, states):
    rows = kq.shape[0]
    high = kq.astype(jnp.bfloat16).astype(jnp.float32)
    rest = kq - high
    middle = rest.astype(jnp.bfloat16).astype(jnp.float32)
    row_ref[...] = by_eights(high + pltpu.roll(middle, 2 * states, 1) + pltpu.roll(rest - middle, 4 * states, 1))
    lane = lax.broadcasted_iota(jnp.int32, (states, LANE), 1)
    entry = lax.broadcasted_iota(jnp.int32, (states, LANE), 0)
    pick = lax.rem(lane, states) == entry

    def body(group, carry):
        for offset in range(8):
            at = pl.multiple_of((group * 8 + offset) * states, states)
            row = jnp.broadcast_to(row_ref[group, offset : offset + 1, :], (states, LANE))
            pick_ref[pl.ds(at, states), :] = jnp.where(pick, row, 0.0).astype(jnp.bfloat16)
        return carry

    lax.fori_loop(0, rows // 8, body, 0)
    term = lax.broadcasted_iota(jnp.int32, (LANE, 2 * LANE), 0)
    side = lax.broadcasted_iota(jnp.int32, (LANE, 2 * LANE), 1)
    is_query = lax.rem(term, 2 * states) >= states
    halves = jnp.where(is_query == (side >= LANE), 1.0, 0.0).astype(jnp.bfloat16)
    both = jnp.dot(pick_ref[...], halves, preferred_element_type=jnp.float32)
    key_ref[...] = both[:, :LANE]
    query_ref[...] = both[:, LANE:]


def sum_eights(half_ref, first):
    total = half_ref[pl.ds(first, 8, stride=8), :]
    for n in range(1, 8):
        total = total + half_ref[pl.ds(first + n, 8, stride=8), :]
    return total


def step_sizes(low, kq, weight_ref, bias_ref, states):
    pre = lax.dot_general(
        low, weight_ref[...], (((1,), (1,)), ((), ())), preferred_element_type=jnp.float32
    )
    beta = sigmoid(pre + bias_ref[...])
    lane = lax.broadcasted_iota(jnp.int32, kq.shape, 1)
    keys = jnp.where(lane < states, kq, 0.0)
    square = jnp.sum(keys * keys, axis=1, keepdims=True)
    return beta, 1.0 / (1.0 + beta * square)


def forward_rows(states, rows, channels, history_ref, state_ref, key_ref, query_ref, rate_ref, input_ref, out_ref, half_ref):
    tiles = channels // LANE
    per_group = min(8, tiles)
    for first in range(0, tiles, per_group):
        columns = [slice((first + j) * LANE, (first + j + 1) * LANE) for j in range(per_group)]

        def body(group, carry):
            carry = list(carry)
            for offset in range(8):
                t = group * 8 + offset
                at = pl.multiple_of(t * states, states)
                key = key_ref[pl.ds(at, states), :]
                query = query_ref[pl.ds(at, states), :]
                square = key * key
                for j, cols in enumerate(columns):
                    history_ref[pl.ds(at, states), cols] = carry[j].astype(jnp.bfloat16)
                    rate = rate_ref[group, offset : offset + 1, cols]
                    fed = input_ref[group, offset : offset + 1, cols]
                    carry[j] = (1.0 - rate * square) * carry[j] + key * fed
                    read = query * carry[j]
                    half_ref[j * 64 + offset * 8 : j * 64 + offset * 8 + 8, :] = read[0:8] + read[8:16]
            for j, cols in enumerate(columns):
                out_ref[group, :, cols] = sum_eights(half_ref, j * 64)
            return tuple(carry)

        done = lax.fori_loop(0, rows // 8, body, tuple(state_ref[:, cols] for cols in columns))
        for cols, state in zip(columns, done):
            state_ref[:, cols] = state


def forward_body(
    states, low_ref, kq_ref, values_ref, gate_ref, weight_ref, bias_ref, skip_ref,
    gated_ref, mixed_ref, history_ref, final_ref,
    state_ref, key_ref, query_ref, rate_ref, input_ref, out_ref, row_ref, pick_ref, half_ref,
):
    rows, channels = values_ref.shape

    @pl.when(pl.program_id(0) == 0)
    def _():
        state_ref[...] = jnp.zeros_like(state_ref)

    beta, inverse = step_sizes(low_ref[...], kq_ref[...], weight_ref, bias_ref, states)
    rates = beta * inverse
    rate_ref[...] = by_eights(rates)
    input_ref[...] = by_eights(rates * values_ref[...].astype(jnp.float32))
    spread_columns(kq_ref[...], row_ref, pick_ref, key_ref, query_ref, states)

    forward_rows(states, rows, channels, history_ref, state_ref, key_ref, query_ref, rate_ref, input_ref, out_ref, half_ref)
    mixed = as_rows(out_ref[...]) + skip_ref[...] * values_ref[...].astype(jnp.float32)
    gate = gate_ref[...]
    mixed_ref[...] = mixed
    gated_ref[...] = (mixed * gate * sigmoid(gate)).astype(jnp.bfloat16)

    @pl.when(pl.program_id(0) == pl.num_programs(0) - 1)
    def _():
        final_ref[...] = state_ref[...]


def forward_scan(low, kq, values, gate, weight, bias, skip, states):
    length, channels = values.shape
    rank = low.shape[1]
    rows = min(128, length)
    blocks = length // rows
    by_row = lambda width: pl.BlockSpec((rows, width), lambda i: (i, 0))
    whole = lambda a: pl.BlockSpec(a.shape, lambda i: (0, 0))
    return pl.pallas_call(
        lambda *refs: forward_body(states, *refs),
        grid=(blocks,),
        in_specs=[by_row(rank), by_row(LANE), by_row(channels), by_row(channels), whole(weight), whole(bias), whole(skip)],
        out_specs=[
            by_row(channels),
            by_row(channels),
            pl.BlockSpec((rows * states, channels), lambda i: (i, 0)),
            pl.BlockSpec((states, channels), lambda i: (0, 0)),
        ],
        out_shape=[
            jax.ShapeDtypeStruct((length, channels), jnp.bfloat16),
            jax.ShapeDtypeStruct((length, channels), jnp.float32),
            jax.ShapeDtypeStruct((length * states, channels), jnp.bfloat16),
            jax.ShapeDtypeStruct((states, channels), jnp.float32),
        ],
        scratch_shapes=[
            pltpu.VMEM((states, channels), jnp.float32),
            pltpu.VMEM((rows * states, LANE), jnp.float32),
            pltpu.VMEM((rows * states, LANE), jnp.float32),
            pltpu.VMEM((rows // 8, 8, channels), jnp.float32),
            pltpu.VMEM((rows // 8, 8, channels), jnp.float32),
            pltpu.VMEM((rows // 8, 8, channels), jnp.float32),
            pltpu.VMEM((rows // 8, 8, LANE), jnp.float32), pltpu.VMEM((rows * states, LANE), jnp.bfloat16),
            pltpu.VMEM((channels // LANE * 64 + 64, LANE), jnp.float32),
        ],
        compiler_params=pltpu.CompilerParams(vmem_limit_bytes=48 * 1024 * 1024),
        cost_estimate=pl.CostEstimate(flops=14 * length * states * channels, bytes_accessed=2 * length * states * channels, transcendentals=0),
    )(low, kq, values, gate, weight, bias, skip)


def backward_rows(
    states, rows, channels, history_ref, grad_ref, state_ref, key_ref, query_ref, rate_ref, do_ref, values32_ref,
    fed_ref, kept_ref, part_key_ref, part_query_ref, half_ref,
):
    tiles = channels // LANE
    per_group = min(PER_GROUP, tiles)
    for first in range(0, tiles, per_group):
        columns = [slice((first + j) * LANE, (first + j + 1) * LANE) for j in range(per_group)]

        def body(step, carry):
            grads, lates = list(carry[0]), list(carry[1])
            group = rows // 8 - 1 - step
            for offset in reversed(range(8)):
                t = group * 8 + offset
                at = pl.multiple_of(t * states, states)
                key = key_ref[pl.ds(at, states), :]
                query = query_ref[pl.ds(at, states), :]
                sum_key = None
                sum_query = None
                for j, cols in enumerate(columns):
                    rate = rate_ref[group, offset : offset + 1, cols]
                    out_grad = do_ref[group, offset : offset + 1, cols]
                    value = values32_ref[group, offset : offset + 1, cols]
                    before = history_ref[pl.ds(at, states), cols].astype(jnp.float32)
                    grad = grads[j] + query * out_grad
                    scaled = rate * grad
                    by_key = key * scaled
                    kept = scaled * before
                    kept = key * kept
                    twice = key * kept
                    at_fed = j * 64 + offset * 8
                    at_kept = (per_group + j) * 64 + offset * 8
                    half_ref[at_fed : at_fed + 8, :] = by_key[0:8] + by_key[8:16]
                    half_ref[at_kept : at_kept + 8, :] = twice[0:8] + twice[8:16]
                    term_key = value * scaled - 2.0 * kept
                    term_query = lates[j] * out_grad
                    sum_key = term_key if sum_key is None else sum_key + term_key
                    sum_query = term_query if sum_query is None else sum_query + term_query
                    grads[j] = grad - key * by_key
                    lates[j] = before
                if first == 0:
                    part_key_ref[pl.ds(at, states), :] = sum_key
                    part_query_ref[pl.ds(at, states), :] = sum_query
                else:
                    part_key_ref[pl.ds(at, states), :] += sum_key
                    part_query_ref[pl.ds(at, states), :] += sum_query
            for j, cols in enumerate(columns):
                fed_ref[group, :, cols] = sum_eights(half_ref, j * 64)
                kept_ref[group, :, cols] = sum_eights(half_ref, (per_group + j) * 64)
            return (tuple(grads), tuple(lates))

        start = (tuple(grad_ref[:, cols] for cols in columns), tuple(state_ref[:, cols] for cols in columns))
        grads, lates = lax.fori_loop(0, rows // 8, body, start)
        for cols, grad, late in zip(columns, grads, lates):
            grad_ref[:, cols] = grad
            state_ref[:, cols] = late


def lane_sums(part_ref, count):
    ones = jnp.ones((LANE, LANE), jnp.bfloat16)
    part_ref[:count, :] = jnp.dot(part_ref[:count, :].astype(jnp.bfloat16), ones, preferred_element_type=jnp.float32)


def gather_columns(part_key_ref, part_query_ref, placed_ref, rows, states):
    lane_sums(part_key_ref, rows * states)
    lane_sums(part_query_ref, rows * states)
    lane = lax.broadcasted_iota(jnp.int32, (8, LANE), 1)

    def body(group, carry):
        total = jnp.zeros((8, LANE), jnp.float32)
        for n in range(states):
            at = group * 8 * states + n
            total = jnp.where(lane == n, part_key_ref[pl.ds(at, 8, stride=states), :], total)
            total = jnp.where(lane == n + states, part_query_ref[pl.ds(at, 8, stride=states), :], total)
        placed_ref[group] = total
        return carry

    lax.fori_loop(0, rows // 8, body, 0)


def backward_body(
    states, links, low_ref, kq_ref, values_ref, gate_ref, mixed_ref, dgated_ref, history_ref, final_ref, weight_ref, bias_ref, skip_ref,
    result_ref, out_ref, dgate_ref, dpre_ref, dvalues_ref, dlow_ref, dkq_ref, bias_grad_ref, skip_grad_ref, result_came, out_came,
    grad_ref, state_ref, key_ref, query_ref, rate_ref, do_ref, values32_ref, fed_ref, kept_ref, part_key_ref, part_query_ref, row_ref, placed_ref,
    pick_ref, half_ref, *sems,
):
    rows, channels = values_ref.shape
    copies = links(result_ref, out_ref, result_came, out_came, *sems)

    @pl.when(pl.program_id(0) == 0)
    def _():
        grad_ref[...] = jnp.zeros_like(grad_ref)
        state_ref[...] = final_ref[...]
        bias_grad_ref[...] = jnp.zeros_like(bias_grad_ref)
        skip_grad_ref[...] = jnp.zeros_like(skip_grad_ref)
        for copy in copies:
            copy.start()

    beta, inverse = step_sizes(low_ref[...], kq_ref[...], weight_ref, bias_ref, states)
    rate_ref[...] = by_eights(beta * inverse)
    values = values_ref[...].astype(jnp.float32)
    values32_ref[...] = by_eights(values)
    gate = gate_ref[...]
    dgated = dgated_ref[...].astype(jnp.float32)
    s = sigmoid(gate)
    do = dgated * (gate * s)
    do_ref[...] = by_eights(do)
    dgate_ref[...] = (dgated * mixed_ref[...] * (s + gate * s * (1.0 - s))).astype(jnp.bfloat16)
    skip_grad_ref[...] += jnp.sum(do * values, axis=0, keepdims=True)
    spread_columns(kq_ref[...], row_ref, pick_ref, key_ref, query_ref, states)

    backward_rows(
        states, rows, channels, history_ref, grad_ref, state_ref, key_ref, query_ref, rate_ref, do_ref, values32_ref,
        fed_ref, kept_ref, part_key_ref, part_query_ref, half_ref,
    )
    fed = as_rows(fed_ref[...])
    dvalues_ref[...] = fed + skip_ref[...] * as_rows(do_ref[...])
    scaled = as_rows(values32_ref[...]) * fed - as_rows(kept_ref[...])
    beta, inverse = step_sizes(low_ref[...], kq_ref[...], weight_ref, bias_ref, states)
    dpre = scaled * (1.0 - beta) * inverse
    bias_grad_ref[...] += jnp.sum(dpre, axis=0, keepdims=True)
    dpre_low = dpre.astype(jnp.bfloat16)
    dpre_ref[...] = dpre_low
    dlow_ref[...] = jnp.dot(dpre_low, weight_ref[...], preferred_element_type=jnp.float32)
    through = -2.0 * jnp.sum(scaled * beta * inverse, axis=1, keepdims=True)

    gather_columns(part_key_ref, part_query_ref, placed_ref, rows, states)
    lanes = lax.broadcasted_iota(jnp.int32, kq_ref.shape, 1)
    dkq_ref[...] = as_rows(placed_ref[...]) + jnp.where(lanes < states, kq_ref[...] * through, 0.0)

    @pl.when(pl.program_id(0) == pl.num_programs(0) - 1)
    def _():
        for copy in copies:
            copy.wait_recv()
        for copy in copies:
            copy.wait_send()


def exchange(parts, dps, result_ref, out_ref, result_came, out_came, result_send, result_recv, out_send, out_recv):
    d, s = lax.axis_index("dp"), lax.axis_index("seq")

    @pl.when(pl.program_id(0) == 0)
    def _():
        barrier = pltpu.get_barrier_semaphore()
        for k in range(1, parts):
            pl.semaphore_signal(barrier, inc=1, device_id=(d, lax.rem(s + k, parts)), device_id_type=MESH)
        for k in range(1, dps):
            pl.semaphore_signal(barrier, inc=1, device_id=(lax.rem(d + k, dps), s), device_id_type=MESH)
        pl.semaphore_wait(barrier, parts + dps - 2)

    copies = []
    for k in range(1, parts):
        to = lax.rem(s + k, parts)
        copies.append(
            pltpu.make_async_remote_copy(
                src_ref=result_ref.at[to], dst_ref=result_came.at[k - 1], send_sem=result_send.at[k - 1],
                recv_sem=result_recv.at[k - 1], device_id=(d, to), device_id_type=MESH,
            )
        )
    for k in range(1, dps):
        to = lax.rem(d + k, dps)
        copies.append(
            pltpu.make_async_remote_copy(
                src_ref=out_ref.at[to], dst_ref=out_came.at[k - 1], send_sem=out_send.at[k - 1],
                recv_sem=out_recv.at[k - 1], device_id=(to, s), device_id_type=MESH,
            )
        )
    return copies


def backward_scan(low, kq, values, gate, mixed, dgated, history, final, weight, bias, skip, result_part, out_part, states):
    length, channels = values.shape
    rank = low.shape[1]
    rows = min(128, length)
    blocks = length // rows
    by_row = lambda width: pl.BlockSpec((rows, width), lambda i: (blocks - 1 - i, 0))
    whole = lambda a: pl.BlockSpec(a.shape, lambda i: (0, 0))
    total = pl.BlockSpec((1, channels), lambda i: (0, 0))
    wide = pltpu.VMEM((rows // 8, 8, channels), jnp.float32)
    spread = pltpu.VMEM((rows * states, LANE), jnp.float32)
    longer = pltpu.VMEM((rows * states + 8 * states, LANE), jnp.float32)
    anywhere = pl.BlockSpec(memory_space=pl.ANY)
    dma = pltpu.SemaphoreType.DMA
    parts, dps = result_part.shape[0], out_part.shape[0]
    links = lambda *refs: exchange(parts, dps, *refs)
    return pl.pallas_call(
        lambda *refs: backward_body(states, links, *refs),
        grid=(blocks,),
        in_specs=[
            by_row(rank), by_row(LANE), by_row(channels), by_row(channels), by_row(channels), by_row(channels),
            pl.BlockSpec((rows * states, channels), lambda i: (blocks - 1 - i, 0)),
            whole(final), whole(weight), whole(bias), whole(skip), anywhere, anywhere,
        ],
        out_specs=[by_row(channels), by_row(channels), by_row(channels), by_row(rank), by_row(LANE), total, total, anywhere, anywhere],
        out_shape=[
            jax.ShapeDtypeStruct((length, channels), jnp.bfloat16),
            jax.ShapeDtypeStruct((length, channels), jnp.bfloat16),
            jax.ShapeDtypeStruct((length, channels), jnp.float32),
            jax.ShapeDtypeStruct((length, rank), jnp.float32),
            jax.ShapeDtypeStruct((length, LANE), jnp.float32),
            jax.ShapeDtypeStruct((1, channels), jnp.float32),
            jax.ShapeDtypeStruct((1, channels), jnp.float32),
            jax.ShapeDtypeStruct((parts - 1,) + result_part.shape[1:], jnp.bfloat16),
            jax.ShapeDtypeStruct((dps - 1,) + out_part.shape[1:], jnp.bfloat16),
        ],
        scratch_shapes=[
            pltpu.VMEM((states, channels), jnp.float32),
            pltpu.VMEM((states, channels), jnp.float32),
            spread, spread, wide, wide, wide, wide, wide, longer, longer,
            pltpu.VMEM((rows // 8, 8, LANE), jnp.float32), pltpu.VMEM((rows // 8, 8, LANE), jnp.float32),
            pltpu.VMEM((rows * states, LANE), jnp.bfloat16),
            pltpu.VMEM((2 * channels // LANE * 64 + 64, LANE), jnp.float32),
            dma((parts - 1,)), dma((parts - 1,)), dma((dps - 1,)), dma((dps - 1,)),
        ],
        compiler_params=pltpu.CompilerParams(collective_id=3, has_side_effects=True, vmem_limit_bytes=56 * 1024 * 1024),
        cost_estimate=pl.CostEstimate(flops=30 * length * states * channels, bytes_accessed=2 * length * states * channels, transcendentals=0),
    )(low, kq, values, gate, mixed, dgated, history, final, weight, bias, skip, result_part, out_part)


MESH = pl.DeviceIdType.MESH
GAIN_ROWS = 16


def plane_mates(d):
    core, x, y = lax.rem(d, 2), lax.rem(d // 2, 2), d // 4
    return d + 1 - 2 * core, d + 2 - 4 * x, d + 4 - 8 * y


def start_body(
    parts, block,
    tokens_ref, in_weight_ref, extra_ref, gain_ref, cot_ref,
    normed_out, weight_out, conv_ref, gate_ref, select_out, beta_out, vector_out, gain_out, cot_early,
    tokens_all, normed_all, weight_all, extra_all,
    near_send, near_recv, plane_send, plane_recv, gain_send, gain_recv, line_send, line_recv, local_sem, early_send, early_recv, spread_ref,
):
    d, s = lax.axis_index("dp"), lax.axis_index("seq")
    sib, xm, ym = plane_mates(d)
    own = spread_ref.shape[1]
    rows, width = tokens_ref.shape
    small = extra_ref.shape[0]
    channels = conv_ref.shape[1]
    chunk = rows // 4

    for j in range(spread_ref.shape[2] // block):
        for q in range(parts):
            first = (j * parts + q) * block
            spread_ref[q, :, j * block : (j + 1) * block] = in_weight_ref[:, first : first + block]

    barrier = pltpu.get_barrier_semaphore()
    for mate in (sib, xm, ym):
        pl.semaphore_signal(barrier, inc=1, device_id=(mate, s), device_id_type=MESH)
    for k in range(1, parts):
        pl.semaphore_signal(barrier, inc=1, device_id=(d, lax.rem(s + k, parts)), device_id_type=MESH)
    pl.semaphore_wait(barrier, 3 + parts - 1)

    def remote(src, dst, send, recv, to):
        return pltpu.make_async_remote_copy(
            src_ref=src, dst_ref=dst, send_sem=send, recv_sem=recv, device_id=to, device_id_type=MESH
        )

    def weight_rows(owner, source):
        return weight_all.at[pl.ds(pl.multiple_of((owner * parts + source) * own, own), own), :]

    def extra_rows(owner):
        return extra_all.at[owner]

    def gain_rows(source):
        return extra_all.at[d, pl.ds(pl.multiple_of(small + source * GAIN_ROWS, GAIN_ROWS), GAIN_ROWS), pl.ds(0, LANE)]

    near = []
    for k in range(1, parts):
        to = (d, lax.rem(s + k, parts))
        near.append(remote(spread_ref.at[to[1]], weight_rows(d, s), near_send.at[k], near_recv.at[k], to))
        near.append(remote(gain_ref, gain_rows(s), gain_send.at[k], gain_recv.at[k], to))
    for copy in near:
        copy.start()
    mine = [
        pltpu.make_async_copy(spread_ref.at[s], weight_rows(d, s), local_sem.at[0]),
        pltpu.make_async_copy(gain_ref, gain_rows(s), local_sem.at[1]),
        pltpu.make_async_copy(extra_ref, extra_all.at[d, pl.ds(0, small), :], local_sem.at[2]),
        pltpu.make_async_copy(tokens_ref, tokens_all.at[pl.ds(pl.multiple_of(s * rows, rows), rows), :], local_sem.at[3]),
    ]
    for copy in mine:
        copy.start()

    def token_rows(part, c):
        return tokens_all.at[pl.ds(pl.multiple_of(part * rows + c * chunk, chunk), chunk), :]

    def token_copy(way, distance, c):
        part = s - way * (distance - 1)
        src = tokens_ref.at[pl.ds(c * chunk, chunk), :] if distance == 1 else token_rows(part, c)
        side = 0 if way == 1 else 1
        return remote(
            src, token_rows(part, c), line_send.at[side, distance, c], line_recv.at[side, distance, c], (d, s + way)
        )

    def can_send(way, distance):
        reach = s + 1 < parts if way == 1 else s >= 1
        came = s - (distance - 1) >= 0 if way == 1 else s + (distance - 1) < parts
        return jnp.logical_and(reach, came)

    def arrives(way, distance):
        return s >= distance if way == 1 else s + distance < parts

    def send_tokens(distance, c):
        for way in (1, -1):
            @pl.when(can_send(way, distance))
            def _():
                token_copy(way, distance, c).start()

    def sent_tokens(distance, c):
        for way in (1, -1):
            @pl.when(can_send(way, distance))
            def _():
                token_copy(way, distance, c).wait_send()

    def take_tokens(distance, c):
        for way in (1, -1):
            @pl.when(arrives(way, distance))
            def _():
                part = s - way * distance
                side = 0 if way == 1 else 1
                remote(
                    token_rows(part, c), token_rows(part, c), line_send.at[side, distance, c],
                    line_recv.at[side, distance, c], (d, s),
                ).wait_recv()

    inner = jnp.logical_and(s >= 1, s + 1 < parts)

    def early_copy(way):
        side = 0 if way == 1 else 1
        return remote(cot_ref, cot_early.at[side], early_send.at[side], early_recv.at[side], (d, s + way))

    def last_copy(way):
        side = 0 if way == 1 else 1
        piece = pl.ds(0, chunk)
        return remote(
            cot_ref.at[piece, :], cot_early.at[side, piece, :], early_send.at[2 + side], early_recv.at[2 + side], (d, s + way)
        )

    def sends_last(way):
        return s == parts - 2 if way == 1 else s == 1

    def takes_last(way):
        return s == parts - 1 if way == 1 else s == 0

    def sends_early(way):
        return s + 2 < parts if way == 1 else s >= 2

    units = parts + 1

    def unit(owner, k):
        return extra_rows(owner) if k == parts else weight_rows(owner, lax.rem(s - k + parts, parts))

    kinds = {"own": (d, 0), "x": (xm, 2), "y": (ym, 4)}

    def plane_copy(owner, k, rel, kind, to):
        return remote(unit(owner, k), unit(owner, k), plane_send.at[kind, k], plane_recv.at[rel, k], (to, s))

    diag = xm + ym - d
    sib_of = lambda mate: mate + sib - d

    def route(k):
        steps = [
            (0, d, 1, 0, sib), (0, d, 2, 1, xm), (0, d, 4, 2, ym),
            (2, xm, 3, 3, sib), (4, ym, 5, 5, sib), (6, diag, 7, 7, sib),
        ]
        steps.append((2, xm, 6, 4, ym) if k % 2 == 0 else (4, ym, 6, 6, xm))
        return steps

    def pass_on(stage, k):
        for at, owner, rel, kind, to in route(k):
            if at == stage:
                plane_copy(owner, k, rel, kind, to).start()

    owners = {1: sib, 2: xm, 3: sib_of(xm), 4: ym, 5: sib_of(ym), 6: diag, 7: sib_of(diag)}

    def take(rel, k):
        plane_copy(owners[rel], k, rel, 0, d).wait_recv()

    for c in range(4):
        send_tokens(1, c)
    mine[0].wait()
    pass_on(0, 0)
    for k in range(1, parts):
        near_wait = remote(
            spread_ref.at[s], weight_rows(d, lax.rem(s - k + parts, parts)), near_send.at[k], near_recv.at[k], (d, s)
        )
        near_wait.wait_recv()
        pass_on(0, k)
    mine[1].wait()
    mine[2].wait()
    for k in range(1, parts):
        remote(gain_ref, gain_rows(lax.rem(s - k + parts, parts)), gain_send.at[k], gain_recv.at[k], (d, s)).wait_recv()
    pass_on(0, parts)
    for k in range(units):
        take(2, k)
        pass_on(2, k)
        take(4, k)
        pass_on(4, k)
        if k < 4:
            take_tokens(1, k)
            send_tokens(2, k)
    for way in (1, -1):
        @pl.when(sends_early(way))
        def _():
            early_copy(way).start()

    for k in range(units):
        take(6, k)
        pass_on(6, k)
        if k < 4:
            take_tokens(2, k)
            send_tokens(3, k)
    for way in (1, -1):
        @pl.when(sends_last(way))
        def _():
            last_copy(way).start()

    for rel in (1, 3, 5, 7):
        for k in range(units):
            take(rel, k)
    mine[3].wait()
    weight_copy = pltpu.make_async_copy(weight_all, weight_out, local_sem.at[4])
    weight_copy.start()
    sel = select_out.shape[1]
    for owner in range(extra_all.shape[0]):
        here = slice(owner * small, (owner + 1) * small)
        select_out[here, :] = extra_all[owner, 0:small, 0:sel]
        beta_out[here, :] = extra_all[owner, 0:small, sel : sel + LANE]
        vectors = extra_all[owner, 0:small, sel + LANE : sel + 2 * LANE].astype(jnp.float32)
        vector_out[:, here] = jnp.transpose(vectors)[: vector_out.shape[0]]

    lane = lax.broadcasted_iota(jnp.int32, (1, LANE), 1)
    pieces = []
    for owner in range(extra_all.shape[0]):
        for source in range(0, parts, 2):
            row = small + source * GAIN_ROWS
            even = extra_all[owner, row : row + GAIN_ROWS, 0:LANE].astype(jnp.float32)[0:1]
            odd = extra_all[owner, row + GAIN_ROWS : row + 2 * GAIN_ROWS, 0:LANE].astype(jnp.float32)[0:1]
            pieces.append(jnp.where(lane < own, even, odd))
    gain = jnp.concatenate(pieces, axis=1)
    gain_out[...] = gain

    tile = min(512, channels)

    def work(part):
        for c in range(4):
            at = pl.ds(pl.multiple_of(part * rows + c * chunk, chunk), chunk)
            flat = tokens_all[at, :].astype(jnp.float32)
            scale = lax.rsqrt(jnp.mean(flat * flat, axis=-1, keepdims=True) + 1e-05)
            normed_all[at, :] = (flat * scale * gain).astype(jnp.bfloat16)
        at = pl.ds(pl.multiple_of(part * rows, rows), rows)

        def columns(n, carry):
            left = pl.multiple_of(n * tile, tile)
            right = pl.multiple_of(channels + n * tile, tile)
            conv_ref[at, pl.ds(left, tile)] = jnp.dot(
                normed_all[at, :], weight_all[:, pl.ds(left, tile)], preferred_element_type=jnp.float32
            ).astype(jnp.bfloat16)
            gate_ref[at, pl.ds(left, tile)] = jnp.dot(
                normed_all[at, :], weight_all[:, pl.ds(right, tile)], preferred_element_type=jnp.float32
            )
            return carry

        lax.fori_loop(0, channels // tile, columns, 0)

    def work_at(low, high):
        def each(part, carry):
            away = jnp.abs(part - s)

            @pl.when(jnp.logical_and(away >= low, away <= high))
            def _():
                work(part)

            return carry

        lax.fori_loop(0, parts, each, 0)

    work_at(0, 2)
    for c in range(4):
        take_tokens(3, c)
    work_at(3, 3)
    normed_copy = pltpu.make_async_copy(normed_all, normed_out, local_sem.at[5])
    normed_copy.start()

    for way in (1, -1):
        @pl.when(inner)
        def _():
            early_copy(way).wait_recv()

        @pl.when(sends_early(way))
        def _():
            early_copy(way).wait_send()

        @pl.when(takes_last(way))
        def _():
            last_copy(way).wait_recv()

        @pl.when(sends_last(way))
        def _():
            last_copy(way).wait_send()

    for copy in near:
        copy.wait_send()
    for k in range(units):
        for at, owner, rel, kind, to in route(k):
            plane_copy(owner, k, rel, kind, to).wait_send()
    for distance in range(1, parts):
        for c in range(4):
            sent_tokens(distance, c)
    weight_copy.wait()
    normed_copy.wait()


def start(tokens, in_weight, extra, gain, cotangent, parts, dps):
    own, both = in_weight.shape[0], in_weight.shape[1] // parts
    rows, width = tokens.shape
    small, lanes = extra.shape
    any_space = pl.BlockSpec(memory_space=pl.ANY)
    vmem = pl.BlockSpec(memory_space=pltpu.VMEM)
    tall = small + parts * GAIN_ROWS
    dma = pltpu.SemaphoreType.DMA
    return pl.pallas_call(
        lambda *refs: start_body(parts, small, *refs),
        out_shape=[
            jax.ShapeDtypeStruct((parts * rows, width), jnp.bfloat16),
            jax.ShapeDtypeStruct((dps * parts * own, both), jnp.bfloat16),
            jax.ShapeDtypeStruct((parts * rows, both // 2), jnp.bfloat16),
            jax.ShapeDtypeStruct((parts * rows, both // 2), jnp.float32),
            jax.ShapeDtypeStruct((dps * small, lanes - 2 * LANE), jnp.bfloat16),
            jax.ShapeDtypeStruct((dps * small, LANE), jnp.bfloat16),
            jax.ShapeDtypeStruct((8, dps * small), jnp.float32),
            jax.ShapeDtypeStruct((1, width), jnp.float32),
            jax.ShapeDtypeStruct((2, rows, width), jnp.bfloat16),
        ],
        in_specs=[vmem, vmem, vmem, vmem, any_space],
        out_specs=[any_space, any_space, vmem, vmem, vmem, vmem, vmem, vmem, any_space],
        scratch_shapes=[
            pltpu.VMEM((parts * rows, width), jnp.bfloat16),
            pltpu.VMEM((parts * rows, width), jnp.bfloat16),
            pltpu.VMEM((dps * parts * own, both), jnp.bfloat16),
            pltpu.VMEM((dps, tall, lanes), jnp.bfloat16),
            dma((parts,)), dma((parts,)),
            dma((8, parts + 1)), dma((8, parts + 1)),
            dma((parts,)), dma((parts,)),
            dma((2, parts, 4)), dma((2, parts, 4)),
            dma((6,)), dma((4,)), dma((4,)), pltpu.VMEM((parts, own, both), jnp.bfloat16),
        ],
        compiler_params=pltpu.CompilerParams(
            collective_id=1, has_side_effects=True, vmem_limit_bytes=56 * 1024 * 1024
        ),
        cost_estimate=pl.CostEstimate(
            flops=2 * parts * rows * width * both, bytes_accessed=40 * 1024 * 1024, transcendentals=0
        ),
    )(tokens, in_weight, extra, gain, cotangent)


def line_sums(parts, rows, terms, came, send, recv, early=None):
    d, s = lax.axis_index("dp"), lax.axis_index("seq")
    chunk = rows // 4

    def own_rows(part, c):
        return pl.ds(pl.multiple_of(part * rows + c * chunk, chunk), chunk)

    def slot(way, left, part, c):
        at = parts if way == -1 and left == 0 else part
        return came.at[at, pl.ds(c * chunk, chunk), :]

    def copy_of(way, steps, c):
        side = 0 if way == 1 else 1
        part = s + way * steps
        return pltpu.make_async_remote_copy(
            src_ref=terms.at[own_rows(part, c), :], dst_ref=slot(way, steps - 1, part, c),
            send_sem=send.at[side, steps, c], recv_sem=recv.at[side, steps - 1, c],
            device_id=(d, s + way), device_id_type=MESH,
        )

    def valid(way, steps):
        if early is not None and steps == 1:
            return jnp.logical_and(s >= 1, s + 1 < parts)
        return s + steps < parts if way == 1 else s >= steps

    def ends_here(way):
        least = 1 if early is None else 2
        return s >= least if way == 1 else s + least < parts

    def upstream(way):
        return s >= 1 if way == 1 else s + 1 < parts

    def taken(way, left, c):
        side = 0 if way == 1 else 1
        place = slot(way, left, s + way * left, c)
        pltpu.make_async_remote_copy(
            src_ref=place, dst_ref=place, send_sem=send.at[side, left, c], recv_sem=recv.at[side, left, c],
            device_id=(d, s), device_id_type=MESH,
        ).wait_recv()

    def pass_on(steps, c):
        for way in (1, -1):
            @pl.when(valid(way, steps))
            def _():
                if steps < parts - 1:
                    @pl.when(upstream(way))
                    def _():
                        taken(way, steps, c)
                        mine = own_rows(s + way * steps, c)
                        more = came[s + way * steps, c * chunk : (c + 1) * chunk, :]
                        terms[mine, :] = (terms[mine, :].astype(jnp.float32) + more.astype(jnp.float32)).astype(jnp.bfloat16)

                copy_of(way, steps, c).start()

    def total(c):
        for way in (1, -1):
            @pl.when(ends_here(way))
            def _():
                taken(way, 0, c)

        at = pl.ds(c * chunk, chunk)
        low = jnp.where(ends_here(1), came[s, at, :].astype(jnp.float32), 0.0)
        high = jnp.where(ends_here(-1), came[parts, at, :].astype(jnp.float32), 0.0)
        total = terms[own_rows(s, c), :].astype(jnp.float32) + low + high
        if early is not None:
            total = total + jnp.where(jnp.logical_or(s == 1, s == parts - 2), early[at, :].astype(jnp.float32), 0.0)
        return total

    def sent():
        for steps in range(1, parts):
            for c in range(4):
                for way in (1, -1):
                    @pl.when(valid(way, steps))
                    def _():
                        copy_of(way, steps, c).wait_send()

    return pass_on, total, sent


def end_body(
    parts, block,
    dmixed_hbm, normed_hbm, weight_hbm, tokens_hbm, cot_hbm, gain_ref, shard_hbm, small_hbm,
    input_grad_ref, in_grad_ref, gain_grad_ref, small_grad_ref,
    dn, dn_recv, sib_send, sib_recv, q_send, q_recv, total, z_send, z_recv,
    small_sib_send, small_sib_recv, small_q_send, small_q_recv,
    line_send, line_recv, pair_send, pair_recv, cross_send, cross_recv, near_send, near_recv,
    dmixed_ref, normed_ref, weight_ref, tokens_ref, cot_ref, shard_ref, small_ref, load_sem,
):
    d, s = lax.axis_index("dp"), lax.axis_index("seq")
    sib, xm, ym = plane_mates(d)
    diag = xm + ym - d
    own, both = shard_ref.shape[0], dmixed_ref.shape[1]
    rows, width = tokens_ref.shape
    chunk = rows // 4
    tall = parts * own
    tile = min(512, both)

    loads = [
        pltpu.make_async_copy(src, dst, load_sem.at[i])
        for i, (src, dst) in enumerate(
            (
                (dmixed_hbm, dmixed_ref), (weight_hbm, weight_ref), (normed_hbm, normed_ref), (small_hbm, small_ref),
                (tokens_hbm, tokens_ref), (cot_hbm, cot_ref), (shard_hbm, shard_ref),
            )
        )
    ]
    for load in loads[:2]:
        load.start()
    barrier = pltpu.get_barrier_semaphore()
    for mate in (sib, xm, ym, diag):
        pl.semaphore_signal(barrier, inc=1, device_id=(mate, s), device_id_type=MESH)
    for k in range(1, parts):
        pl.semaphore_signal(barrier, inc=1, device_id=(d, lax.rem(s + k, parts)), device_id_type=MESH)
    pl.semaphore_wait(barrier, 4 + parts - 1)

    def remote(src, dst, send, recv, to):
        return pltpu.make_async_remote_copy(
            src_ref=src, dst_ref=dst, send_sem=send, recv_sem=recv, device_id=to, device_id_type=MESH
        )

    pass_line, line_total, line_sent = line_sums(parts, rows, dn, dn_recv, line_send, line_recv)

    def dn_part(part):
        at = pl.ds(pl.multiple_of(part * rows, rows), rows)

        def columns(n, carry):
            cols = pl.ds(pl.multiple_of(n * tile, tile), tile)
            dn[at, cols] = lax.dot_general(
                dmixed_ref[at, :], weight_ref[cols, :], (((1,), (1,)), ((), ())), preferred_element_type=jnp.float32
            ).astype(jnp.bfloat16)
            return carry

        lax.fori_loop(0, width // tile, columns, 0)

    far = (parts - 1) * (1 - s // 2)
    next_far = lax.rem(2 - 2 * s + 10, 5)
    nearer = 1 + lax.rem(s, 2)
    for load in loads[:2]:
        load.wait()
    for load in loads[2:]:
        load.start()
    dn_part(far)
    for c in range(4):
        pass_line(parts - 1, c)
    for load in loads[2:4]:
        load.wait()

    def grad_block(owner, store):
        left = pl.ds(pl.multiple_of(owner * tall, tall), tall)

        def columns(n, carry):
            cols = pl.ds(pl.multiple_of(n * tile, tile), tile)
            store(
                cols,
                lax.dot_general(
                    normed_ref[:, left], dmixed_ref[:, cols], (((0,), (0,)), ((), ())),
                    preferred_element_type=jnp.float32,
                ),
            )
            return carry

        lax.fori_loop(0, both // tile, columns, 0)

    mates = (diag, xm, ym, d)
    sib_of = lambda mate: mate + sib - d

    def pair_copy(r):
        return remote(sib_send.at[r], sib_recv.at[r], pair_send.at[0, r], pair_recv.at[0, r], (sib, s))

    def pair_copy_small(r):
        return remote(small_sib_send.at[r], small_sib_recv.at[r], pair_send.at[1, r], pair_recv.at[1, r], (sib, s))

    def cross_copy(r):
        return remote(q_send.at[r], q_recv.at[r], cross_send.at[0, r], cross_recv.at[0, r], (mates[r], s))

    def cross_copy_small(r):
        return remote(small_q_send.at[r], small_q_recv.at[r], cross_send.at[1, r], cross_recv.at[1, r], (mates[r], s))

    for r in range(4):
        def store_pair(cols, value):
            sib_send[r, :, cols] = value.astype(jnp.bfloat16)

        grad_block(sib_of(mates[r]), store_pair)
        pair_copy(r).start()
        small_sib_send[r] = small_ref[sib_of(mates[r])].astype(jnp.bfloat16)
        pair_copy_small(r).start()
    dn_part(next_far)
    for r in range(4):
        pair_copy(r).wait_recv()
        pair_copy_small(r).wait_recv()
        both_small = small_ref[mates[r]] + small_sib_recv[r].astype(jnp.float32)
        if r < 3:
            def store_cross(cols, value):
                q_send[r, :, cols] = (value + sib_recv[r, :, cols].astype(jnp.float32)).astype(jnp.bfloat16)

            grad_block(mates[r], store_cross)
            cross_copy(r).start()
            small_q_send[r] = both_small.astype(jnp.bfloat16)
            cross_copy_small(r).start()
        else:
            def store_total(cols, value):
                total[:, cols] = value + sib_recv[r, :, cols].astype(jnp.float32)

            grad_block(mates[r], store_total)
            small_grad_ref[...] = both_small
        pass_line(parts - 2, r)
        if r == 2:
            dn_part(nearer)
            dn_part(s)
    for c in range(4):
        pass_line(parts - 3, c)
    for load in loads[4:]:
        load.wait()

    for r in range(3):
        cross_copy(r).wait_recv()
        cross_copy_small(r).wait_recv()
        total[...] += q_recv[r].astype(jnp.float32)
        small_grad_ref[...] += small_q_recv[r].astype(jnp.float32)
    z_send[...] = total[...].astype(jnp.bfloat16)

    def near_copy(k):
        to = lax.rem(s + k, parts)
        return remote(
            z_send.at[pl.ds(pl.multiple_of(to * own, own), own), :], z_recv.at[k], near_send.at[k], near_recv.at[k], (d, to)
        )

    for k in range(1, parts):
        near_copy(k).start()

    for c in range(4):
        at = pl.ds(c * chunk, chunk)
        v = line_total(c) * gain_ref[...]
        flat = tokens_ref[at, :].astype(jnp.float32)
        scale = lax.rsqrt(jnp.mean(flat * flat, axis=-1, keepdims=True) + 1e-05)
        du = scale * v - flat * (scale * scale * scale) * jnp.mean(flat * v, axis=-1, keepdims=True)
        input_grad_ref[at, :] = (cot_ref[at, :].astype(jnp.float32) + du).astype(jnp.bfloat16)

    channel_blocks = both // block
    gain_total = jnp.zeros((own, block), jnp.float32)
    for k in range(parts):
        source = lax.rem(s - k + parts, parts)
        if k > 0:
            near_copy(k).wait_recv()
        for j in range(channel_blocks):
            cols = slice(j * block, (j + 1) * block)
            if k == 0:
                piece = z_send[pl.ds(pl.multiple_of(s * own, own), own), cols]
            else:
                piece = z_recv[k, :, cols]
            to = pl.ds(pl.multiple_of((j * parts + source) * block, block), block)
            in_grad_ref[:, to] = piece
            gain_total = gain_total + piece.astype(jnp.float32) * shard_ref[:, to].astype(jnp.float32)
    gain_grad_ref[...] = jnp.broadcast_to(jnp.sum(gain_total, axis=1, keepdims=True), gain_grad_ref.shape)

    for r in range(4):
        pair_copy(r).wait_send()
        pair_copy_small(r).wait_send()
    for r in range(3):
        cross_copy(r).wait_send()
        cross_copy_small(r).wait_send()
    for k in range(1, parts):
        near_copy(k).wait_send()
    line_sent()


def end(dmixed, normed, weight, tokens, cotangent, gain, shard, small, parts, block):
    both = dmixed.shape[1]
    rows, width = tokens.shape
    own = shard.shape[0]
    dps, _, lanes = small.shape
    tall = parts * own
    vmem = pl.BlockSpec(memory_space=pltpu.VMEM)
    anywhere = pl.BlockSpec(memory_space=pl.ANY)
    dma = pltpu.SemaphoreType.DMA
    low = jnp.bfloat16
    return pl.pallas_call(
        lambda *refs: end_body(parts, block, *refs),
        out_shape=[
            jax.ShapeDtypeStruct((rows, width), low),
            jax.ShapeDtypeStruct((own, parts * both), low),
            jax.ShapeDtypeStruct((own, LANE), jnp.float32),
            jax.ShapeDtypeStruct((block, lanes), jnp.float32),
        ],
        in_specs=[anywhere] * 5 + [vmem] + [anywhere] * 2,
        out_specs=[vmem] * 4,
        scratch_shapes=[
            pltpu.VMEM((parts * rows, width), low),
            pltpu.VMEM((parts + 1, rows, width), low),
            pltpu.VMEM((4, tall, both), low), pltpu.VMEM((4, tall, both), low),
            pltpu.VMEM((3, tall, both), low), pltpu.VMEM((3, tall, both), low),
            pltpu.VMEM((tall, both), jnp.float32),
            pltpu.VMEM((tall, both), low), pltpu.VMEM((parts, own, both), low),
            pltpu.VMEM((4, block, lanes), low), pltpu.VMEM((4, block, lanes), low),
            pltpu.VMEM((3, block, lanes), low), pltpu.VMEM((3, block, lanes), low),
            dma((2, parts, 4)), dma((2, parts, 4)),
            dma((2, 4)), dma((2, 4)), dma((2, 3)), dma((2, 3)), dma((parts,)), dma((parts,)),
            *[pltpu.VMEM(a.shape, a.dtype) for a in (dmixed, normed, weight, tokens, cotangent, shard, small)], dma((7,)),
        ],
        compiler_params=pltpu.CompilerParams(
            collective_id=2, has_side_effects=True, vmem_limit_bytes=60 * 1024 * 1024
        ),
        cost_estimate=pl.CostEstimate(
            flops=4 * parts * rows * width * both, bytes_accessed=30 * 1024 * 1024, transcendentals=0
        ),
    )(dmixed, normed, weight, tokens, cotangent, gain, shard, small)


def linked_forward_body(
    states, parts, dps, taps,
    conv_in_ref, gate_ref, select_ref, vector_ref, weight_ref, out_shard, cot_shard, cot_early,
    mixed_ref, history_ref, final_ref, values_out, low_ref, kq_ref, dgated_out, result_out, out_part_ref, early_out, key_ref, query_ref,
    state_ref, rate_ref, input_ref, out_ref, row_ref, pick_ref, half_ref,
    part_low, part_kq, came_low, came_kq, sum_low, sum_kq,
    rs_send, rs_recv, ag_send, ag_recv, out_send, out_recv, line_send, line_recv, local_sem,
    out_all, cot_all, gated_all, out_total, values_ref, dgated_ref, result_ref, leave_sem, early_send, early_recv,
):
    d, s = lax.axis_index("dp"), lax.axis_index("seq")
    step = pl.program_id(0)
    length, channels = values_ref.shape
    rows = gate_ref.shape[0]
    span = length // parts
    block = out_shard.shape[0]
    chunk = span // 4
    packed = LANE // (2 * states)
    conv_w_ref, conv_b_ref = vector_ref, vector_ref[taps : taps + 1, :]
    bias_ref, skip_ref = vector_ref[taps + 1 : taps + 2, :], vector_ref[taps + 2 : taps + 3, :]
    short = span // packed

    def remote(src, dst, send, recv, to):
        return pltpu.make_async_remote_copy(
            src_ref=src, dst_ref=dst, send_sem=send, recv_sem=recv, device_id=to, device_id_type=MESH
        )

    def out_rows(owner):
        return out_all.at[pl.ds(pl.multiple_of(owner * block, block), block), :]

    out_copies = []
    for k in range(1, dps):
        out_copies.append(
            remote(out_shard, out_rows(d), out_send.at[k - 1], out_recv.at[k - 1], (lax.rem(d + k, dps), s))
        )

    inner = jnp.logical_and(s >= 1, s + 1 < parts)

    def cot_rows(part, c):
        return cot_all.at[pl.ds(pl.multiple_of(part * span + c * chunk, chunk), chunk), :]

    def cot_copy(way, distance, c):
        part = s - way * (distance - 1)
        side = 0 if way == 1 else 1
        piece = pl.ds(c * chunk, chunk)
        src = {1: cot_shard.at[piece, :], 2: cot_early.at[side, piece, :]}.get(distance)
        src = cot_rows(part, c) if src is None else src
        return remote(
            src, cot_rows(part, c), line_send.at[side, distance, c], line_recv.at[side, distance, c], (d, s + way)
        )

    def can_send(way, distance):
        if distance == 1:
            return s == parts - 2 if way == 1 else s == 1
        came = s >= distance - 1 if way == 1 else s + distance - 1 < parts
        return jnp.logical_and(inner, came)

    def arrives(way, distance):
        if distance == 1:
            return s == parts - 1 if way == 1 else s == 0
        return s >= distance if way == 1 else s + distance < parts

    def into_end(way):
        return s == parts - 2 if way == 1 else s == 1

    def send_cot(distance, c, which=None):
        for way in (1, -1):
            go = can_send(way, distance)
            if which is not None:
                go = jnp.logical_and(go, into_end(way) if which else jnp.logical_not(into_end(way)))

            @pl.when(go)
            def _():
                cot_copy(way, distance, c).start()

    def sent_cot(distance, c):
        for way in (1, -1):
            @pl.when(can_send(way, distance))
            def _():
                cot_copy(way, distance, c).wait_send()

    def take_cot(distance, c):
        for way in (1, -1):
            @pl.when(arrives(way, distance))
            def _():
                part = s - way * distance
                side = 0 if way == 1 else 1
                remote(
                    cot_rows(part, c), cot_rows(part, c), line_send.at[side, distance, c],
                    line_recv.at[side, distance, c], (d, s),
                ).wait_recv()

    def end_rows(way):
        side = 0 if way == 1 else 1
        return pltpu.make_async_copy(
            cot_early.at[side, pl.ds(0, chunk), :], cot_rows(s - way, 0), local_sem.at[3 + side]
        )

    def early_rows(way):
        side = 0 if way == 1 else 1
        return pltpu.make_async_copy(
            cot_early.at[side], cot_all.at[pl.ds(pl.multiple_of((s - way) * span, span), span), :], local_sem.at[3 + side]
        )

    def early_result(way):
        part = 1 if way == 1 else parts - 2
        side = 0 if way == 1 else 1
        return remote(
            result_ref.at[pl.ds(part * span, span), :], early_out, early_send.at[side], early_recv.at[side], (d, s + way)
        )

    def sends_result(way):
        return s == 0 if way == 1 else s == parts - 1

    def takes_result(way):
        return s == 1 if way == 1 else s == parts - 2

    def own_copy(which):
        if which == 0:
            return pltpu.make_async_copy(out_shard, out_rows(d), local_sem.at[0])
        here = pl.ds(pl.multiple_of(s * span, span), span)
        return pltpu.make_async_copy(cot_shard, cot_all.at[here, :], local_sem.at[1])

    @pl.when(step == 0)
    def _():
        barrier = pltpu.get_barrier_semaphore()
        for k in range(1, parts):
            pl.semaphore_signal(barrier, inc=1, device_id=(d, lax.rem(s + k, parts)), device_id_type=MESH)
        for k in range(1, dps):
            pl.semaphore_signal(barrier, inc=1, device_id=(lax.rem(d + k, dps), s), device_id_type=MESH)
        pl.semaphore_wait(barrier, parts + dps - 2)
        state_ref[...] = jnp.zeros_like(state_ref)
        for copy in out_copies:
            copy.start()
        own_copy(0).start()
        own_copy(1).start()
        for way in (1, -1):
            @pl.when(inner)
            def _():
                early_rows(way).start()

            @pl.when(arrives(way, 1))
            def _():
                end_rows(way).start()

        send_cot(1, 1)
        send_cot(2, 0, False)

    def rs_copies(k):
        at = lax.rem(s + k, parts)
        return (
            remote(part_low.at[at], came_low.at[k - 1], rs_send.at[0, k - 1], rs_recv.at[0, k - 1], (d, at)),
            remote(part_kq.at[at], came_kq.at[k - 1], rs_send.at[1, k - 1], rs_recv.at[1, k - 1], (d, at)),
        )

    def ag_copies(k):
        to = lax.rem(s + k, parts)
        return (
            remote(sum_low.at[s], sum_low.at[s], ag_send.at[0, k - 1], ag_recv.at[0, k - 1], (d, to)),
            remote(sum_kq.at[s], sum_kq.at[s], ag_send.at[1, k - 1], ag_recv.at[1, k - 1], (d, to)),
        )

    def ag_taken(k, part):
        return (
            remote(sum_low.at[part], sum_low.at[part], ag_send.at[0, k - 1], ag_recv.at[0, k - 1], (d, s)),
            remote(sum_kq.at[part], sum_kq.at[part], ag_send.at[1, k - 1], ag_recv.at[1, k - 1], (d, s)),
        )

    def convolve(part):
        start = pl.multiple_of(part * span, span)
        before = pl.multiple_of(jnp.maximum(start - 16, 0), 16)
        wide = min(256, channels)
        for left in range(0, channels, wide):
            cols = slice(left, left + wide)
            head = conv_in_ref[pl.ds(before, 16), cols].astype(jnp.float32)
            head = jnp.where(part == 0, 0.0, head)
            body = jnp.concatenate([head, conv_in_ref[pl.ds(start, span), cols].astype(jnp.float32)], axis=0)
            total = conv_b_ref[:, cols]
            for tap in range(taps):
                by = taps - 1 - tap
                total = total + body[16 - by : 16 - by + span] * conv_w_ref[tap : tap + 1, cols]
            values_ref[pl.ds(start, span), cols] = (total * sigmoid(total)).astype(jnp.bfloat16)
        projected = jnp.dot(values_ref[pl.ds(start, span), :], select_ref[...], preferred_element_type=jnp.float32)
        part_low[part] = projected[:, :LANE].astype(jnp.bfloat16)
        pack = projected[:short, LANE:]
        for g in range(1, packed):
            pack = pack + pltpu.roll(projected[g * short : (g + 1) * short, LANE:], g * 2 * states, 1)
        part_kq[part] = pack

    @pl.when(step < parts - 1)
    def _():
        convolve(lax.rem(s + 1 + step, parts))

    for k in range(1, parts):
        @pl.when(step == k - 1)
        def _():
            for copy in rs_copies(k):
                copy.start()

    @pl.when(step == parts - 2)
    def _():
        send_cot(1, 2)

    @pl.when(step == parts - 1)
    def _():
        convolve(s)
        low = part_low[s].astype(jnp.float32)
        kq = part_kq[s]
        for k in range(1, parts):
            for copy in rs_copies(k):
                copy.wait_recv()
            low = low + came_low[k - 1].astype(jnp.float32)
            kq = kq + came_kq[k - 1]
        sum_low[s] = low.astype(jnp.bfloat16)
        sum_kq[s] = kq
        for k in range(1, parts):
            for copy in ag_copies(k):
                copy.start()
        send_cot(1, 3)
        send_cot(2, 1, False)

    per_part = span // rows
    at_block = step - parts

    def unpack(part):
        start = pl.multiple_of(part * span, span)
        low_ref[pl.ds(start, span), :] = sum_low[part]
        pack = sum_kq[part]
        lane = lax.broadcasted_iota(jnp.int32, pack.shape, 1)
        for g in range(packed):
            turned = pack if g == 0 else pltpu.roll(pack, LANE - g * 2 * states, 1)
            kq_ref[pl.ds(pl.multiple_of(start + g * short, short), short), :] = jnp.where(lane < 2 * states, turned, 0.0)

    for part in range(parts):
        @pl.when(at_block == part * per_part)
        def _():
            for k in range(1, parts):
                @pl.when(lax.rem(s - k + parts, parts) == part)
                def _():
                    for copy in ag_taken(k, part):
                        copy.wait_recv()

            unpack(part)

    plan = (
        (("outer", 0), ("inner", 2)), (("outer", 1), ("inner", 3)), (("outer", 2), ("outer", 3)), (("last", 0),),
        (("last", 1), ("last", 2)), (("last", 3),),
    )
    for at, moves in enumerate(plan):
        @pl.when(at_block == at)
        def _():
            for kind, c in moves:
                if kind == "last":
                    take_cot(2, c)
                    send_cot(3, c)
                else:
                    send_cot(2, c, kind == "outer")

    @pl.when(jnp.logical_and(at_block >= 0, at_block < length // rows))
    def _():
        here = pl.ds(pl.multiple_of(at_block * rows, rows), rows)
        kq = kq_ref[here, :]
        values = values_ref[here, :].astype(jnp.float32)
        beta, inverse = step_sizes(low_ref[here, :], kq, weight_ref, bias_ref, states)
        rates = beta * inverse
        rate_ref[...] = by_eights(rates)
        input_ref[...] = by_eights(rates * values)
        spread_columns(kq, row_ref, pick_ref, key_ref, query_ref, states)
        forward_rows(states, rows, channels, history_ref, state_ref, key_ref, query_ref, rate_ref, input_ref, out_ref, half_ref)
        mixed = as_rows(out_ref[...]) + skip_ref[...] * values
        gate = gate_ref[...]
        mixed_ref[...] = mixed
        gated_all[here, :] = (mixed * gate * sigmoid(gate)).astype(jnp.bfloat16)

    width = cot_all.shape[1]
    tile = min(512, width)

    def leaving(part, which):
        here = pl.ds(pl.multiple_of(part * span, span), span)
        ref, out = ((dgated_ref, dgated_out), (result_ref, result_out))[which]
        return pltpu.make_async_copy(ref.at[here, :], out.at[here, :], leave_sem.at[part, which])

    values_copy = pltpu.make_async_copy(values_ref, values_out, local_sem.at[2])

    @pl.when(step == parts)
    def _():
        values_copy.start()

    def products(part):
        here = pl.ds(pl.multiple_of(part * span, span), span)

        def across(n, carry):
            cols = pl.ds(pl.multiple_of(n * tile, tile), tile)
            out_total[:, cols] += lax.dot_general(
                gated_all[here, :], cot_all[here, cols], (((0,), (0,)), ((), ())), preferred_element_type=jnp.float32
            )
            return carry

        lax.fori_loop(0, width // tile, across, 0)
        deep = min(512, channels)

        def along(n, carry):
            cols = pl.ds(pl.multiple_of(n * deep, deep), deep)
            dgated_ref[here, cols] = lax.dot_general(
                cot_all[here, :], out_all[cols, :], (((1,), (1,)), ((), ())), preferred_element_type=jnp.float32
            )
            return carry

        lax.fori_loop(0, channels // deep, along, 0)
        leaving(part, 0).start()

    def result_terms(part):
        here = pl.ds(part * span, span)

        def across(n, carry):
            cols = pl.ds(pl.multiple_of(n * tile, tile), tile)
            result_ref[here, cols] = jnp.dot(
                gated_all[here, :], out_all[:, cols], preferred_element_type=jnp.float32
            ).astype(jnp.bfloat16)
            return carry

        lax.fori_loop(0, width // tile, across, 0)
        leaving(part, 1).start()

    @pl.when(at_block == length // rows - per_part)
    def _():
        own_copy(0).wait()
        for copy in out_copies:
            copy.wait_recv()
        for part in range(parts - 1):
            result_terms(part)
        for way in (1, -1):
            @pl.when(sends_result(way))
            def _():
                early_result(way).start()

    def products_at(low, high):
        def each(part, carry):
            away = jnp.abs(part - s)

            @pl.when(jnp.logical_and(away >= low, away <= high))
            def _():
                products(part)

            return carry

        lax.fori_loop(0, parts, each, 0)

    @pl.when(step == pl.num_programs(0) - 1)
    def _():
        final_ref[...] = state_ref[...]
        out_total[...] = jnp.zeros_like(out_total)
        own_copy(1).wait()
        for way in (1, -1):
            @pl.when(inner)
            def _():
                early_rows(way).wait()

            @pl.when(arrives(way, 1))
            def _():
                end_rows(way).wait()

        result_terms(parts - 1)
        products_at(0, 0)
        for c in range(1, 4):
            take_cot(1, c)
        products_at(1, 1)
        products_at(2, parts - 2)
        for c in range(4):
            take_cot(parts - 1, c)
        products_at(parts - 1, parts - 1)
        out_part_ref[...] = out_total[...].astype(jnp.bfloat16)
        values_copy.wait()
        for way in (1, -1):
            @pl.when(takes_result(way))
            def _():
                early_result(way).wait_recv()

            @pl.when(sends_result(way))
            def _():
                early_result(way).wait_send()

        for part in range(parts):
            leaving(part, 0).wait()
            leaving(part, 1).wait()
        for copy in out_copies:
            copy.wait_send()
        for distance in range(1, parts):
            for c in range(1 if distance == 1 else 0, 4):
                sent_cot(distance, c)
        for k in range(1, parts):
            for copy in rs_copies(k) + ag_copies(k):
                copy.wait_send()


def linked_forward(
    conv_in, gate, select, vectors, weight, out_shard, cot_shard, cot_early, parts, dps, taps, states
):
    length, channels = conv_in.shape
    block, width = out_shard.shape
    span = length // parts
    rows = min(128, span)
    blocks = length // rows
    short = span // (LANE // (2 * states))
    at = lambda i: jnp.clip(i - parts, 0, blocks - 1)
    by_row = lambda size: pl.BlockSpec((rows, size), lambda i: (at(i), 0))
    whole = lambda a: pl.BlockSpec(a.shape, lambda i: (0, 0))
    kept = lambda *shape: pl.BlockSpec(shape, lambda i: (0, 0))
    anywhere = pl.BlockSpec(memory_space=pl.ANY)
    dma = pltpu.SemaphoreType.DMA
    f32, low = jnp.float32, jnp.bfloat16
    eights = pltpu.VMEM((rows // 8, 8, channels), f32)
    return pl.pallas_call(
        lambda *refs: linked_forward_body(states, parts, dps, taps, *refs),
        grid=(parts + blocks + 1,),
        in_specs=[
            whole(conv_in), by_row(channels), whole(select), whole(vectors), whole(weight), anywhere, anywhere,
            anywhere,
        ],
        out_specs=[
            by_row(channels), pl.BlockSpec((rows * states, channels), lambda i: (at(i), 0)),
            kept(states, channels), anywhere, kept(length, LANE), kept(length, LANE),
            anywhere, anywhere, kept(dps * block, width), anywhere,
            pl.BlockSpec((rows * states, LANE), lambda i: (at(i), 0)), pl.BlockSpec((rows * states, LANE), lambda i: (at(i), 0)),
        ],
        out_shape=[
            jax.ShapeDtypeStruct((length, channels), f32),
            jax.ShapeDtypeStruct((length * states, channels), low),
            jax.ShapeDtypeStruct((states, channels), f32),
            jax.ShapeDtypeStruct((length, channels), low),
            jax.ShapeDtypeStruct((length, LANE), low),
            jax.ShapeDtypeStruct((length, LANE), f32),
            jax.ShapeDtypeStruct((length, channels), f32),
            jax.ShapeDtypeStruct((length, width), low),
            jax.ShapeDtypeStruct((dps * block, width), low),
            jax.ShapeDtypeStruct((span, width), low),
            jax.ShapeDtypeStruct((length * states, LANE), f32),
            jax.ShapeDtypeStruct((length * states, LANE), f32),
        ],
        scratch_shapes=[
            pltpu.VMEM((states, channels), f32),
            eights, eights, eights, pltpu.VMEM((rows // 8, 8, LANE), f32),
            pltpu.VMEM((rows * states, LANE), low), pltpu.VMEM((channels // LANE * 64 + 64, LANE), f32),
            pltpu.VMEM((parts, span, LANE), low), pltpu.VMEM((parts, short, LANE), f32),
            pltpu.VMEM((parts - 1, span, LANE), low), pltpu.VMEM((parts - 1, short, LANE), f32),
            pltpu.VMEM((parts, span, LANE), low), pltpu.VMEM((parts, short, LANE), f32),
            dma((2, parts - 1)), dma((2, parts - 1)), dma((2, parts - 1)), dma((2, parts - 1)),
            dma((dps - 1,)), dma((dps - 1,)), dma((2, parts, 4)), dma((2, parts, 4)), dma((5,)),
            pltpu.VMEM((dps * block, width), low), pltpu.VMEM((length, width), low), pltpu.VMEM((length, channels), low),
            pltpu.VMEM((dps * block, width), f32), pltpu.VMEM((length, channels), low),
            pltpu.VMEM((length, channels), f32), pltpu.VMEM((length, width), low), dma((parts, 2)), dma((2,)), dma((2,)),
        ],
        compiler_params=pltpu.CompilerParams(
            collective_id=4, has_side_effects=True, vmem_limit_bytes=60 * 1024 * 1024
        ),
        cost_estimate=pl.CostEstimate(
            flops=14 * length * states * channels, bytes_accessed=2 * length * states * channels, transcendentals=0
        ),
    )(conv_in, gate, select, vectors, weight, out_shard, cot_shard, cot_early)


def linked_backward_body(
    states, parts, dps, taps,
    low_ref, kq_ref, gate_ref, mixed_ref, dgated_ref, history_ref, final_ref, weight_ref,
    values_ref, conv_in_ref, select_ref, given_ref, tokens_ref, early_ref, key_ref, query_ref, part_hbm, out_ref,
    dmixed_out, small_ref, result_ref, out_grad_ref,
    grad_ref, state_ref, rate_ref, inverse_ref, do_ref, values32_ref, fed_ref, kept_ref, part_key_ref,
    part_query_ref, placed_ref, half_ref,
    dvalues_ref, dproj_ref, next_ref, vector_ref, part_low, part_kq, came_low, came_kq, sum_low, sum_kq,
    rs_send, rs_recv, ag_send, ag_recv, result_came, line_send, line_recv, out_send, out_recv,
    out_came, out_here, local_sem, dmixed_ref, part_ref, leave_sem,
):
    d, s = lax.axis_index("dp"), lax.axis_index("seq")
    step = pl.program_id(0)
    rows, channels = gate_ref.shape
    length = values_ref.shape[0]
    blocks = length // rows
    span = length // parts
    per_part = span // rows
    packed = LANE // (2 * states)
    short = span // packed
    sel = select_ref.shape[1]
    conv_w_ref, conv_b_ref = given_ref, given_ref[taps : taps + 1, :]
    bias_ref, skip_ref = given_ref[taps + 1 : taps + 2, :], given_ref[taps + 2 : taps + 3, :]

    def remote(src, dst, send, recv, to):
        return pltpu.make_async_remote_copy(
            src_ref=src, dst_ref=dst, send_sem=send, recv_sem=recv, device_id=to, device_id_type=MESH
        )

    copies = []
    for k in range(1, dps):
        to = lax.rem(d + k, dps)
        copies.append(remote(out_ref.at[to], out_came.at[k - 1], out_send.at[k - 1], out_recv.at[k - 1], (to, s)))
    out_copy = pltpu.make_async_copy(out_ref.at[d], out_here, local_sem.at[0])
    part_copy = pltpu.make_async_copy(part_hbm, part_ref, local_sem.at[1])
    pass_line, line_total, line_sent = line_sums(parts, span, part_ref, result_came, line_send, line_recv, early_ref)

    @pl.when(step == 0)
    def _():
        part_copy.start()
        barrier = pltpu.get_barrier_semaphore()
        for k in range(1, parts):
            pl.semaphore_signal(barrier, inc=1, device_id=(d, lax.rem(s + k, parts)), device_id_type=MESH)
        for k in range(1, dps):
            pl.semaphore_signal(barrier, inc=1, device_id=(lax.rem(d + k, dps), s), device_id_type=MESH)
        pl.semaphore_wait(barrier, parts + dps - 2)
        grad_ref[...] = jnp.zeros_like(grad_ref)
        state_ref[...] = final_ref[...]
        next_ref[...] = jnp.zeros_like(next_ref)
        vector_ref[...] = jnp.zeros_like(vector_ref)
        small_ref[...] = jnp.zeros_like(small_ref)
        for copy in copies:
            copy.start()
        out_copy.start()
        part_copy.wait()

    def rs_copies(k):
        at = lax.rem(s + k, parts)
        return (
            remote(part_low.at[at], came_low.at[k - 1], rs_send.at[0, k - 1], rs_recv.at[0, k - 1], (d, at)),
            remote(part_kq.at[at], came_kq.at[k - 1], rs_send.at[1, k - 1], rs_recv.at[1, k - 1], (d, at)),
        )

    def ag_copies(k):
        to = lax.rem(s + k, parts)
        return (
            remote(sum_low.at[s], sum_low.at[s], ag_send.at[0, k - 1], ag_recv.at[0, k - 1], (d, to)),
            remote(sum_kq.at[s], sum_kq.at[s], ag_send.at[1, k - 1], ag_recv.at[1, k - 1], (d, to)),
        )

    def ag_taken(k, part):
        return (
            remote(sum_low.at[part], sum_low.at[part], ag_send.at[0, k - 1], ag_recv.at[0, k - 1], (d, s)),
            remote(sum_kq.at[part], sum_kq.at[part], ag_send.at[1, k - 1], ag_recv.at[1, k - 1], (d, s)),
        )

    def add_up():
        low = part_low[s].astype(jnp.float32)
        kq = part_kq[s]
        for k in range(1, parts):
            for copy in rs_copies(k):
                copy.wait_recv()
            low = low + came_low[k - 1].astype(jnp.float32)
            kq = kq + came_kq[k - 1]
        sum_low[s] = low.astype(jnp.bfloat16)
        sum_kq[s] = kq.astype(jnp.bfloat16)
        for k in range(1, parts):
            for copy in ag_copies(k):
                copy.start()

    def leaving(part):
        here = pl.ds(pl.multiple_of(part * span, span), span)
        return pltpu.make_async_copy(dmixed_ref.at[here, :], dmixed_out.at[here, :], leave_sem.at[part])

    def conv_back(part):
        for k in range(1, parts):
            @pl.when(lax.rem(s - k + parts, parts) == part)
            def _():
                for copy in ag_taken(k, part):
                    copy.wait_recv()

        here = pl.ds(pl.multiple_of(part * span, span), span)
        before = pl.multiple_of(jnp.maximum(part * span - 16, 0), 16)
        dproj_ref[:, :LANE] = sum_low[part]
        pack = sum_kq[part].astype(jnp.float32)
        lane = lax.broadcasted_iota(jnp.int32, pack.shape, 1)
        for g in range(packed):
            turned = pack if g == 0 else pltpu.roll(pack, LANE - g * 2 * states, 1)
            dproj_ref[g * short : (g + 1) * short, LANE:] = jnp.where(lane < 2 * states, turned, 0.0).astype(jnp.bfloat16)
        wide = min(256, channels)
        for left in range(0, channels, wide):
            cols = slice(left, left + wide)
            small_ref[cols, :sel] += lax.dot_general(
                values_ref[here, cols], dproj_ref[...], (((0,), (0,)), ((), ())), preferred_element_type=jnp.float32
            )
            head = conv_in_ref[pl.ds(before, 16), cols].astype(jnp.float32)
            head = jnp.where(part == 0, 0.0, head)
            body = jnp.concatenate([head, conv_in_ref[here, cols].astype(jnp.float32)], axis=0)
            total = conv_b_ref[:, cols]
            for tap in range(taps):
                by = taps - 1 - tap
                total = total + body[16 - by : 16 - by + span] * conv_w_ref[tap : tap + 1, cols]
            sg = sigmoid(total)
            dvalues = dvalues_ref[here, cols] + lax.dot_general(
                dproj_ref[...], select_ref[cols, :], (((1,), (1,)), ((), ())), preferred_element_type=jnp.float32
            )
            dconv = dvalues * (sg + total * sg * (1.0 - sg))
            vector_ref[taps : taps + 1, cols] += jnp.sum(dconv, axis=0, keepdims=True)
            after = jnp.concatenate([dconv, next_ref[:, cols]], axis=0)
            dconv_in = jnp.zeros_like(dconv)
            for tap in range(taps):
                by = taps - 1 - tap
                shifted = body[16 - by : 16 - by + span]
                vector_ref[tap : tap + 1, cols] += jnp.sum(dconv * shifted, axis=0, keepdims=True)
                dconv_in = dconv_in + after[by : by + span] * conv_w_ref[tap : tap + 1, cols]
            next_ref[:, cols] = dconv[0:8]
            dmixed_ref[here, cols] = dconv_in.astype(jnp.bfloat16)
        leaving(part).start()

    plan = (((3, 0), (3, 1)), ((3, 2), (3, 3)), ((2, 0), (2, 1)), ((2, 2), (2, 3)), ((1, 0), (1, 1)), ((1, 2), (1, 3)))
    for at_step, moves in enumerate(plan):
        @pl.when(step == at_step)
        def _():
            for steps, c in moves:
                pass_line(steps, c)

    for part in range(parts):
        ends = (parts - part) * per_part - 1
        sums = min(ends + 3, blocks - 1 if part > 0 else blocks)

        @pl.when(jnp.logical_and(step == sums, s == part))
        def _():
            add_up()

        @pl.when(step == blocks + 1 - part)
        def _():
            conv_back(part)

    @pl.when(step < blocks)
    def _():
        block = blocks - 1 - step
        here = pl.ds(pl.multiple_of(block * rows, rows), rows)
        low, kq = low_ref[...], kq_ref[...]
        beta, inverse = step_sizes(low, kq, weight_ref, bias_ref, states)
        rate_ref[...] = by_eights(beta * inverse)
        inverse_ref[...] = inverse
        values = values_ref[here, :].astype(jnp.float32)
        values32_ref[...] = by_eights(values)
        gate = gate_ref[...]
        dgated = dgated_ref[...].astype(jnp.float32)
        sg = sigmoid(gate)
        do = dgated * (gate * sg)
        do_ref[...] = by_eights(do)
        dmixed_ref[here, channels:] = (dgated * mixed_ref[...] * (sg + gate * sg * (1.0 - sg))).astype(jnp.bfloat16)
        vector_ref[taps + 2 : taps + 3, :] += jnp.sum(do * values, axis=0, keepdims=True)
        backward_rows(
            states, rows, channels, history_ref, grad_ref, state_ref, key_ref, query_ref, rate_ref, do_ref, values32_ref,
            fed_ref, kept_ref, part_key_ref, part_query_ref, half_ref,
        )
        fed = as_rows(fed_ref[...])
        dvalues_ref[here, :] = fed + skip_ref[...] * as_rows(do_ref[...])
        scaled = as_rows(values32_ref[...]) * fed - as_rows(kept_ref[...])
        rates = as_rows(rate_ref[...])
        dpre = scaled * (inverse_ref[...] - rates)
        vector_ref[taps + 1 : taps + 2, :] += jnp.sum(dpre, axis=0, keepdims=True)
        dpre_low = dpre.astype(jnp.bfloat16)
        small_ref[:, sel : sel + LANE] += lax.dot_general(
            dpre_low, low, (((0,), (0,)), ((), ())), preferred_element_type=jnp.float32
        )
        through = -2.0 * jnp.sum(scaled * rates, axis=1, keepdims=True)
        gather_columns(part_key_ref, part_query_ref, placed_ref, rows, states)
        lanes = lax.broadcasted_iota(jnp.int32, kq.shape, 1)
        dkq = as_rows(placed_ref[...]) + jnp.where(lanes < states, kq * through, 0.0)
        part = block // per_part
        within = lax.rem(block, per_part)
        part_low[part, pl.ds(pl.multiple_of(within * rows, rows), rows), :] = jnp.dot(
            dpre_low, weight_ref[...], preferred_element_type=jnp.float32
        ).astype(jnp.bfloat16)
        for g in range(packed):
            first = g * short - within * rows

            @pl.when(jnp.logical_and(first >= 0, first < rows))
            def _():
                for w in range(per_part):
                    if w * rows <= g * short < (w + 1) * rows:
                        lo = g * short - w * rows
                        piece = dkq[lo : lo + short]
                        piece = piece if g == 0 else pltpu.roll(piece, g * 2 * states, 1)
                        if g == (per_part - 1) * rows // short:
                            part_kq[part] = piece
                        else:
                            part_kq[part] += piece

        @pl.when(within == 0)
        def _():
            for k in range(1, parts):
                @pl.when(lax.rem(s + k, parts) == part)
                def _():
                    for copy in rs_copies(k):
                        copy.start()

    @pl.when(step == pl.num_programs(0) - 1)
    def _():
        small_ref[:, sel + LANE :] = jnp.transpose(vector_ref[...])
        chunk = span // 4
        for c in range(4):
            at = pl.ds(c * chunk, chunk)
            result_ref[at, :] = (tokens_ref[at, :].astype(jnp.float32) + line_total(c)).astype(jnp.bfloat16)
        line_sent()
        for part in range(parts):
            leaving(part).wait()
        out_copy.wait()
        total = out_here[...].astype(jnp.float32)
        for k in range(1, dps):
            copies[k - 1].wait_recv()
            total = total + out_came[k - 1].astype(jnp.float32)
        out_grad_ref[...] = total
        for copy in copies:
            copy.wait_send()
        for k in range(1, parts):
            for copy in rs_copies(k) + ag_copies(k):
                copy.wait_send()


def linked_backward(
    low, kq, gate, mixed, dgated, history, final, weight, values, conv_in, select, vectors, tokens, early,
    key, query, result_part, out_part, parts, taps, states,
):
    length, channels = values.shape
    dps = out_part.shape[0]
    width = tokens.shape[1]
    sel = select.shape[1]
    span = length // parts
    rows = min(128, span)
    blocks = length // rows
    short = span // (LANE // (2 * states))
    at = lambda i: jnp.maximum(blocks - 1 - i, 0)
    by_row = lambda size: pl.BlockSpec((rows, size), lambda i: (at(i), 0))
    whole = lambda a: pl.BlockSpec(a.shape, lambda i: (0, 0))
    kept = lambda *shape: pl.BlockSpec(shape, lambda i: (0, 0))
    anywhere = pl.BlockSpec(memory_space=pl.ANY)
    dma = pltpu.SemaphoreType.DMA
    f32, bf16 = jnp.float32, jnp.bfloat16
    wide = pltpu.VMEM((rows // 8, 8, channels), f32)
    eights = pltpu.VMEM((rows // 8, 8, LANE), f32)
    spread = pltpu.VMEM((rows * states + 8 * states, LANE), f32)
    return pl.pallas_call(
        lambda *refs: linked_backward_body(states, parts, dps, taps, *refs),
        grid=(blocks + 2,),
        in_specs=[
            by_row(LANE), by_row(LANE), by_row(channels), by_row(channels), by_row(channels),
            pl.BlockSpec((rows * states, channels), lambda i: (at(i), 0)),
            whole(final), whole(weight), whole(values), whole(conv_in), whole(select), whole(vectors), whole(tokens),
            whole(early), pl.BlockSpec((rows * states, LANE), lambda i: (at(i), 0)),
            pl.BlockSpec((rows * states, LANE), lambda i: (at(i), 0)), anywhere, anywhere,
        ],
        out_specs=[anywhere, kept(channels, sel + 2 * LANE), kept(span, width), kept(*out_part.shape[1:])],
        out_shape=[
            jax.ShapeDtypeStruct((length, 2 * channels), bf16),
            jax.ShapeDtypeStruct((channels, sel + 2 * LANE), f32),
            jax.ShapeDtypeStruct((span, width), bf16),
            jax.ShapeDtypeStruct(out_part.shape[1:], f32),
        ],
        scratch_shapes=[
            pltpu.VMEM((states, channels), f32), pltpu.VMEM((states, channels), f32),
            wide, pltpu.VMEM((rows, channels), f32), wide, wide, wide, wide, spread, spread, eights,
            pltpu.VMEM((2 * channels // LANE * 64 + 64, LANE), f32),
            pltpu.VMEM((length, channels), f32), pltpu.VMEM((span, sel), bf16), pltpu.VMEM((8, channels), f32),
            pltpu.VMEM((LANE, channels), f32),
            pltpu.VMEM((parts, span, LANE), bf16), pltpu.VMEM((parts, short, LANE), f32),
            pltpu.VMEM((parts - 1, span, LANE), bf16), pltpu.VMEM((parts - 1, short, LANE), f32),
            pltpu.VMEM((parts, span, LANE), bf16), pltpu.VMEM((parts, short, LANE), bf16),
            dma((2, parts - 1)), dma((2, parts - 1)), dma((2, parts - 1)), dma((2, parts - 1)),
            pltpu.VMEM((parts + 1, span, width), bf16), dma((2, parts, 4)), dma((2, parts, 4)),
            dma((dps - 1,)), dma((dps - 1,)), pltpu.VMEM((dps - 1,) + out_part.shape[1:], bf16),
            pltpu.VMEM(out_part.shape[1:], bf16), dma((2,)), pltpu.VMEM((length, 2 * channels), bf16),
            pltpu.VMEM((length, width), bf16), dma((parts,)),
        ],
        compiler_params=pltpu.CompilerParams(
            collective_id=5, has_side_effects=True, vmem_limit_bytes=60 * 1024 * 1024
        ),
        cost_estimate=pl.CostEstimate(
            flops=30 * length * states * channels, bytes_accessed=2 * length * states * channels, transcendentals=0
        ),
    )(low, kq, gate, mixed, dgated, history, final, weight, values, conv_in, select, vectors, tokens, early, key, query, result_part, out_part)


def contract(left, right, left_dim, right_dim):
    return lax.dot_general(
        left, right, (((left_dim,), (right_dim,)), ((), ())), preferred_element_type=jnp.float32
    )


def gathered(shard, axis):
    return lax.all_gather(shard, axis, axis=0, tiled=True)


def scattered(total, axis):
    return lax.psum_scatter(total, axis, scatter_dimension=0, tiled=True)


def summed_rows(partial, axis):
    size = lax.axis_size(axis)
    parts = partial.astype(jnp.bfloat16).reshape((size, partial.shape[0] // size) + partial.shape[1:])
    parts = lax.all_to_all(parts, axis, 0, 0)
    return jnp.sum(parts.astype(jnp.float32), axis=0)


def later(rows, by):
    if by == 0:
        return rows
    return jnp.pad(rows, ((by, 0), (0, 0)))[: rows.shape[0]]


def sooner(rows, by):
    if by == 0:
        return rows
    return jnp.pad(rows, ((0, by), (0, 0)))[by:]


def local(
    tokens,
    cotangent,
    norm_gain,
    in_weight,
    conv_weight,
    conv_bias,
    select_weight,
    beta_weight,
    beta_bias,
    skip_gain,
    out_weight,
):
    parts, dps = lax.axis_size("seq"), lax.axis_size("dp")
    rows, width = tokens.shape[1:]
    block = conv_weight.shape[0]
    channels = block * dps
    taps = conv_weight.shape[1]
    rank = beta_weight.shape[1]
    states = (select_weight.shape[1] - rank) // 2
    own = in_weight.shape[0]

    flat = tokens.reshape(rows, width).astype(jnp.float32)
    scale = lax.rsqrt(jnp.mean(flat * flat, axis=-1, keepdims=True) + 1e-05)
    vectors = jnp.concatenate(
        [conv_weight, conv_bias[:, None], beta_bias[:, None], skip_gain[:, None]], axis=1
    )
    wide = -(-select_weight.shape[1] // LANE) * LANE
    small = jnp.concatenate(
        [
            jnp.pad(select_weight, ((0, 0), (0, wide - select_weight.shape[1]))),
            beta_weight,
            jnp.pad(vectors, ((0, 0), (0, LANE - vectors.shape[1]))),
        ],
        axis=1,
    )
    small_slice = (dps, parts, 2 * own, rank) == (8, 4, LANE, LANE)
    if small_slice:
        doubled = jnp.broadcast_to(jnp.tile(norm_gain.reshape(1, own), (1, 2)), (GAIN_ROWS, LANE))
        normed, in_w, conv_in, gate, select_w, beta_w, vectors, gain, cot_early = start(
            tokens.reshape(rows, width), in_weight, small, doubled, cotangent.reshape(rows, width), parts, dps
        )
    else:
        gain = gathered(norm_gain, ("dp", "seq"))
        normed = gathered((flat * scale * gain.astype(jnp.float32)).astype(jnp.bfloat16), "seq")
        spread = in_weight.reshape(own, 2, dps, parts, block).transpose(3, 0, 1, 2, 4).reshape(parts, own, 2 * channels)
        in_w = gathered(lax.all_to_all(spread, "seq", 0, 0).reshape(parts * own, 2 * channels), "dp")
        smalls = gathered(small, "dp")
        conv_in = jnp.dot(normed, in_w[:, :channels], preferred_element_type=jnp.float32).astype(jnp.bfloat16)
        gate = jnp.dot(normed, in_w[:, channels:], preferred_element_type=jnp.float32)
    cot_here = cotangent.reshape(rows, width)
    if small_slice:
        mixed, history, final, values, low, kq, dgated, result_part, out_part, early, key, query = linked_forward(
            conv_in, gate, select_w, vectors, beta_w, out_weight, cot_here, cot_early, parts, dps, taps, states,
        )
    else:
        gain = gain.astype(jnp.float32)
        select_w = smalls[:, : select_weight.shape[1]]
        beta_w = smalls[:, wide : wide + rank]
        vectors = smalls[:, wide + rank :].astype(jnp.float32)
        conv_w, conv_b = vectors[:, :taps], vectors[:, taps]
        beta_b, skip = vectors[:, taps + 1].reshape(1, channels), vectors[:, taps + 2].reshape(1, channels)
        conv_wide = conv_in.astype(jnp.float32)
        conv_sum = conv_b
        for tap in range(taps):
            conv_sum = conv_sum + later(conv_wide, taps - 1 - tap) * conv_w[:, tap]
        out_w = gathered(out_weight, "dp")
        cot = gathered(cot_here, "seq")
        values = jax.nn.silu(conv_sum).astype(jnp.bfloat16)
        projected = lax.psum(jnp.dot(values, select_w, preferred_element_type=jnp.float32), "seq")
        low = projected[:, :rank].astype(jnp.bfloat16)
        kq = jnp.pad(projected[:, rank:], ((0, 0), (0, LANE - 2 * states)))
        gated, mixed, history, final = forward_scan(low, kq, values, gate, beta_w, beta_b, skip, states)
        result_part = jnp.dot(gated, out_w, preferred_element_type=jnp.float32).astype(jnp.bfloat16)
        out_part = contract(gated, cot, 0, 0).astype(jnp.bfloat16)
        dgated = contract(cot, out_w, 1, 1)
    out_part = out_part.reshape(dps, block, width)
    if small_slice:
        dmixed, small_grads, result, out_grad = linked_backward(
            low, kq, gate, mixed, dgated, history, final, beta_w, values, conv_in, select_w, vectors,
            tokens.reshape(rows, width), early, key, query, result_part, out_part, parts, taps, states,
        )
        small_grads = small_grads.reshape(dps, block, wide + rank + LANE)
    else:
        result_part = result_part.reshape(parts, rows, width)
        dgate, dpre_low, dvalues, dlow, dkq, bias_grad, skip_grad, result_came, out_came = backward_scan(
            low, kq, values, gate, mixed, dgated, history, final, beta_w, beta_b, skip, result_part, out_part, states
        )
        part_here = lax.dynamic_index_in_dim(result_part, lax.axis_index("seq"), 0, False).astype(jnp.float32)
        result = (flat + (part_here + jnp.sum(result_came.astype(jnp.float32), axis=0))).astype(jnp.bfloat16)
        out_here = lax.dynamic_index_in_dim(out_part, lax.axis_index("dp"), 0, False).astype(jnp.float32)
        out_grad = out_here + jnp.sum(out_came.astype(jnp.float32), axis=0)
        dprojected = lax.psum(jnp.concatenate([dlow, dkq[:, : 2 * states]], axis=1), "seq").astype(jnp.bfloat16)
        beta_grad = contract(dpre_low, low, 0, 0)
        select_grad = contract(values, dprojected, 0, 0)
        dvalues = contract(dprojected, select_w, 1, 1) + dvalues
        s = jax.nn.sigmoid(conv_sum)
        dconv = dvalues * (s + conv_sum * s * (1.0 - s))
        conv_w_grad = jnp.stack(
            [jnp.sum(dconv * later(conv_wide, taps - 1 - tap), axis=0) for tap in range(taps)], axis=1
        )
        conv_b_grad = jnp.sum(dconv, axis=0)
        dconv_in = 0.0
        for tap in range(taps):
            dconv_in = dconv_in + sooner(dconv, taps - 1 - tap) * conv_w[:, tap]
        dmixed = jnp.concatenate([dconv_in.astype(jnp.bfloat16), dgate], axis=1)
        vector_grads = jnp.concatenate(
            [conv_w_grad, conv_b_grad[:, None], bias_grad.reshape(channels, 1), skip_grad.reshape(channels, 1)], axis=1
        )
        small_grads = jnp.concatenate(
            [
                jnp.pad(select_grad, ((0, 0), (0, wide - select_grad.shape[1]))),
                beta_grad,
                jnp.pad(vector_grads, ((0, 0), (0, LANE - vector_grads.shape[1]))),
            ],
            axis=1,
        ).reshape(dps, block, wide + rank + LANE)
    if small_slice:
        input_grad, in_grad, gain_sums, small_grads = end(
            dmixed, normed, in_w, tokens.reshape(rows, width), cot_here, gain, in_weight, small_grads,
            parts, block,
        )
        gain_sums = gain_sums[:, 0]
    else:
        in_grad = summed_rows(contract(normed, dmixed, 0, 0), "dp").astype(jnp.bfloat16)
        in_grad = lax.all_to_all(in_grad.reshape(parts, own, 2 * channels), "seq", 0, 0).astype(jnp.float32)
        in_grad = in_grad.reshape(parts, own, 2, dps, block).transpose(1, 2, 3, 0, 4).reshape(own, 2 * parts * channels)
        gain_sums = jnp.sum(in_grad * in_weight.astype(jnp.float32), axis=1)
        v = summed_rows(contract(dmixed, in_w, 1, 1), "seq") * gain
        du = scale * v - flat * (scale * scale * scale) * jnp.mean(flat * v, axis=-1, keepdims=True)
        input_grad = (cot_here.astype(jnp.float32) + du).astype(jnp.bfloat16)
        small_grads = jnp.sum(lax.all_to_all(small_grads, "dp", 0, 0), axis=0)
    rows_grad = small_grads[:, wide + rank :]
    return (
        result.reshape(tokens.shape),
        input_grad.reshape(tokens.shape),
        gain_sums / norm_gain.astype(jnp.float32),
        in_grad.astype(jnp.float32),
        rows_grad[:, :taps],
        rows_grad[:, taps],
        small_grads[:, : select_weight.shape[1]],
        small_grads[:, wide : wide + rank],
        rows_grad[:, taps + 1],
        rows_grad[:, taps + 2],
        out_grad,
    )


def solution(mesh):
    split = P(("dp", "seq"))
    rows = P("dp", "seq", None)
    return jax.shard_map(
        local,
        mesh=mesh,
        in_specs=(rows, rows) + (split,) * 9,
        out_specs=(rows, rows) + (split,) * 9,
        check_vma=False,
    )
```

```python
import jax
import jax.numpy as jnp
from jax import lax
from jax.experimental import pallas as pl
from jax.experimental.pallas import tpu as pltpu
from jax.sharding import PartitionSpec as P

LANE = 128
PER_GROUP = 4


def sigmoid(v):
    return 1.0 / (1.0 + jnp.exp(-v))


def by_eights(value):
    return value.reshape(value.shape[0] // 8, 8, value.shape[1])


def as_rows(value):
    return value.reshape(value.shape[0] * 8, value.shape[2])


def spread_columns(kq, row_ref, pick_ref, key_ref, query_ref, states):
    rows = kq.shape[0]
    high = kq.astype(jnp.bfloat16).astype(jnp.float32)
    rest = kq - high
    middle = rest.astype(jnp.bfloat16).astype(jnp.float32)
    row_ref[...] = by_eights(high + pltpu.roll(middle, 2 * states, 1) + pltpu.roll(rest - middle, 4 * states, 1))
    lane = lax.broadcasted_iota(jnp.int32, (states, LANE), 1)
    entry = lax.broadcasted_iota(jnp.int32, (states, LANE), 0)
    pick = lax.rem(lane, states) == entry

    def body(group, carry):
        for offset in range(8):
            at = pl.multiple_of((group * 8 + offset) * states, states)
            row = jnp.broadcast_to(row_ref[group, offset : offset + 1, :], (states, LANE))
            pick_ref[pl.ds(at, states), :] = jnp.where(pick, row, 0.0).astype(jnp.bfloat16)
        return carry

    lax.fori_loop(0, rows // 8, body, 0)
    term = lax.broadcasted_iota(jnp.int32, (LANE, 2 * LANE), 0)
    side = lax.broadcasted_iota(jnp.int32, (LANE, 2 * LANE), 1)
    is_query = lax.rem(term, 2 * states) >= states
    halves = jnp.where(is_query == (side >= LANE), 1.0, 0.0).astype(jnp.bfloat16)
    both = jnp.dot(pick_ref[...], halves, preferred_element_type=jnp.float32)
    key_ref[...] = both[:, :LANE]
    query_ref[...] = both[:, LANE:]


def sum_eights(half_ref, first):
    total = half_ref[pl.ds(first, 8, stride=8), :]
    for n in range(1, 8):
        total = total + half_ref[pl.ds(first + n, 8, stride=8), :]
    return total


def step_sizes(low, kq, weight_ref, bias_ref, states):
    pre = lax.dot_general(
        low, weight_ref[...], (((1,), (1,)), ((), ())), preferred_element_type=jnp.float32
    )
    beta = sigmoid(pre + bias_ref[...])
    lane = lax.broadcasted_iota(jnp.int32, kq.shape, 1)
    keys = jnp.where(lane < states, kq, 0.0)
    square = jnp.sum(keys * keys, axis=1, keepdims=True)
    return beta, 1.0 / (1.0 + beta * square)


def forward_rows(states, rows, channels, history_ref, state_ref, key_ref, query_ref, rate_ref, input_ref, out_ref, half_ref):
    tiles = channels // LANE
    per_group = min(8, tiles)
    for first in range(0, tiles, per_group):
        columns = [slice((first + j) * LANE, (first + j + 1) * LANE) for j in range(per_group)]

        def body(group, carry):
            carry = list(carry)
            for offset in range(8):
                t = group * 8 + offset
                at = pl.multiple_of(t * states, states)
                key = key_ref[pl.ds(at, states), :]
                query = query_ref[pl.ds(at, states), :]
                square = key * key
                for j, cols in enumerate(columns):
                    history_ref[pl.ds(at, states), cols] = carry[j].astype(jnp.bfloat16)
                    rate = rate_ref[group, offset : offset + 1, cols]
                    fed = input_ref[group, offset : offset + 1, cols]
                    carry[j] = (1.0 - rate * square) * carry[j] + key * fed
                    read = query * carry[j]
                    half_ref[j * 64 + offset * 8 : j * 64 + offset * 8 + 8, :] = read[0:8] + read[8:16]
            for j, cols in enumerate(columns):
                out_ref[group, :, cols] = sum_eights(half_ref, j * 64)
            return tuple(carry)

        done = lax.fori_loop(0, rows // 8, body, tuple(state_ref[:, cols] for cols in columns))
        for cols, state in zip(columns, done):
            state_ref[:, cols] = state


def forward_body(
    states, low_ref, kq_ref, values_ref, gate_ref, weight_ref, bias_ref, skip_ref,
    gated_ref, mixed_ref, history_ref, final_ref,
    state_ref, key_ref, query_ref, rate_ref, input_ref, out_ref, row_ref, pick_ref, half_ref,
):
    rows, channels = values_ref.shape

    @pl.when(pl.program_id(0) == 0)
    def _():
        state_ref[...] = jnp.zeros_like(state_ref)

    beta, inverse = step_sizes(low_ref[...], kq_ref[...], weight_ref, bias_ref, states)
    rates = beta * inverse
    rate_ref[...] = by_eights(rates)
    input_ref[...] = by_eights(rates * values_ref[...].astype(jnp.float32))
    spread_columns(kq_ref[...], row_ref, pick_ref, key_ref, query_ref, states)

    forward_rows(states, rows, channels, history_ref, state_ref, key_ref, query_ref, rate_ref, input_ref, out_ref, half_ref)
    mixed = as_rows(out_ref[...]) + skip_ref[...] * values_ref[...].astype(jnp.float32)
    gate = gate_ref[...]
    mixed_ref[...] = mixed
    gated_ref[...] = (mixed * gate * sigmoid(gate)).astype(jnp.bfloat16)

    @pl.when(pl.program_id(0) == pl.num_programs(0) - 1)
    def _():
        final_ref[...] = state_ref[...]


def forward_scan(low, kq, values, gate, weight, bias, skip, states):
    length, channels = values.shape
    rank = low.shape[1]
    rows = min(128, length)
    blocks = length // rows
    by_row = lambda width: pl.BlockSpec((rows, width), lambda i: (i, 0))
    whole = lambda a: pl.BlockSpec(a.shape, lambda i: (0, 0))
    return pl.pallas_call(
        lambda *refs: forward_body(states, *refs),
        grid=(blocks,),
        in_specs=[by_row(rank), by_row(LANE), by_row(channels), by_row(channels), whole(weight), whole(bias), whole(skip)],
        out_specs=[
            by_row(channels),
            by_row(channels),
            pl.BlockSpec((rows * states, channels), lambda i: (i, 0)),
            pl.BlockSpec((states, channels), lambda i: (0, 0)),
        ],
        out_shape=[
            jax.ShapeDtypeStruct((length, channels), jnp.bfloat16),
            jax.ShapeDtypeStruct((length, channels), jnp.float32),
            jax.ShapeDtypeStruct((length * states, channels), jnp.bfloat16),
            jax.ShapeDtypeStruct((states, channels), jnp.float32),
        ],
        scratch_shapes=[
            pltpu.VMEM((states, channels), jnp.float32),
            pltpu.VMEM((rows * states, LANE), jnp.float32),
            pltpu.VMEM((rows * states, LANE), jnp.float32),
            pltpu.VMEM((rows // 8, 8, channels), jnp.float32),
            pltpu.VMEM((rows // 8, 8, channels), jnp.float32),
            pltpu.VMEM((rows // 8, 8, channels), jnp.float32),
            pltpu.VMEM((rows // 8, 8, LANE), jnp.float32), pltpu.VMEM((rows * states, LANE), jnp.bfloat16),
            pltpu.VMEM((channels // LANE * 64 + 64, LANE), jnp.float32),
        ],
        compiler_params=pltpu.CompilerParams(vmem_limit_bytes=48 * 1024 * 1024),
        cost_estimate=pl.CostEstimate(flops=14 * length * states * channels, bytes_accessed=2 * length * states * channels, transcendentals=0),
    )(low, kq, values, gate, weight, bias, skip)


def backward_rows(
    states, rows, channels, history_ref, grad_ref, state_ref, key_ref, query_ref, rate_ref, do_ref, values32_ref,
    fed_ref, kept_ref, part_key_ref, part_query_ref, half_ref,
):
    tiles = channels // LANE
    per_group = min(PER_GROUP, tiles)
    for first in range(0, tiles, per_group):
        columns = [slice((first + j) * LANE, (first + j + 1) * LANE) for j in range(per_group)]

        def body(step, carry):
            grads, lates = list(carry[0]), list(carry[1])
            group = rows // 8 - 1 - step
            for offset in reversed(range(8)):
                t = group * 8 + offset
                at = pl.multiple_of(t * states, states)
                key = key_ref[pl.ds(at, states), :]
                query = query_ref[pl.ds(at, states), :]
                sum_key = None
                sum_query = None
                for j, cols in enumerate(columns):
                    rate = rate_ref[group, offset : offset + 1, cols]
                    out_grad = do_ref[group, offset : offset + 1, cols]
                    value = values32_ref[group, offset : offset + 1, cols]
                    before = history_ref[pl.ds(at, states), cols].astype(jnp.float32)
                    grad = grads[j] + query * out_grad
                    scaled = rate * grad
                    by_key = key * scaled
                    kept = scaled * before
                    kept = key * kept
                    twice = key * kept
                    at_fed = j * 64 + offset * 8
                    at_kept = (per_group + j) * 64 + offset * 8
                    half_ref[at_fed : at_fed + 8, :] = by_key[0:8] + by_key[8:16]
                    half_ref[at_kept : at_kept + 8, :] = twice[0:8] + twice[8:16]
                    term_key = value * scaled - 2.0 * kept
                    term_query = lates[j] * out_grad
                    sum_key = term_key if sum_key is None else sum_key + term_key
                    sum_query = term_query if sum_query is None else sum_query + term_query
                    grads[j] = grad - key * by_key
                    lates[j] = before
                if first == 0:
                    part_key_ref[pl.ds(at, states), :] = sum_key
                    part_query_ref[pl.ds(at, states), :] = sum_query
                else:
                    part_key_ref[pl.ds(at, states), :] += sum_key
                    part_query_ref[pl.ds(at, states), :] += sum_query
            for j, cols in enumerate(columns):
                fed_ref[group, :, cols] = sum_eights(half_ref, j * 64)
                kept_ref[group, :, cols] = sum_eights(half_ref, (per_group + j) * 64)
            return (tuple(grads), tuple(lates))

        start = (tuple(grad_ref[:, cols] for cols in columns), tuple(state_ref[:, cols] for cols in columns))
        grads, lates = lax.fori_loop(0, rows // 8, body, start)
        for cols, grad, late in zip(columns, grads, lates):
            grad_ref[:, cols] = grad
            state_ref[:, cols] = late


def lane_sums(part_ref, count):
    ones = jnp.ones((LANE, LANE), jnp.bfloat16)
    part_ref[:count, :] = jnp.dot(part_ref[:count, :].astype(jnp.bfloat16), ones, preferred_element_type=jnp.float32)


def gather_columns(part_key_ref, part_query_ref, placed_ref, rows, states):
    lane_sums(part_key_ref, rows * states)
    lane_sums(part_query_ref, rows * states)
    lane = lax.broadcasted_iota(jnp.int32, (8, LANE), 1)

    def body(group, carry):
        total = jnp.zeros((8, LANE), jnp.float32)
        for n in range(states):
            at = group * 8 * states + n
            total = jnp.where(lane == n, part_key_ref[pl.ds(at, 8, stride=states), :], total)
            total = jnp.where(lane == n + states, part_query_ref[pl.ds(at, 8, stride=states), :], total)
        placed_ref[group] = total
        return carry

    lax.fori_loop(0, rows // 8, body, 0)


def backward_body(
    states, links, low_ref, kq_ref, values_ref, gate_ref, mixed_ref, dgated_ref, history_ref, final_ref, weight_ref, bias_ref, skip_ref,
    result_ref, out_ref, dgate_ref, dpre_ref, dvalues_ref, dlow_ref, dkq_ref, bias_grad_ref, skip_grad_ref, result_came, out_came,
    grad_ref, state_ref, key_ref, query_ref, rate_ref, do_ref, values32_ref, fed_ref, kept_ref, part_key_ref, part_query_ref, row_ref, placed_ref,
    pick_ref, half_ref, *sems,
):
    rows, channels = values_ref.shape
    copies = links(result_ref, out_ref, result_came, out_came, *sems)

    @pl.when(pl.program_id(0) == 0)
    def _():
        grad_ref[...] = jnp.zeros_like(grad_ref)
        state_ref[...] = final_ref[...]
        bias_grad_ref[...] = jnp.zeros_like(bias_grad_ref)
        skip_grad_ref[...] = jnp.zeros_like(skip_grad_ref)
        for copy in copies:
            copy.start()

    beta, inverse = step_sizes(low_ref[...], kq_ref[...], weight_ref, bias_ref, states)
    rate_ref[...] = by_eights(beta * inverse)
    values = values_ref[...].astype(jnp.float32)
    values32_ref[...] = by_eights(values)
    gate = gate_ref[...]
    dgated = dgated_ref[...].astype(jnp.float32)
    s = sigmoid(gate)
    do = dgated * (gate * s)
    do_ref[...] = by_eights(do)
    dgate_ref[...] = (dgated * mixed_ref[...] * (s + gate * s * (1.0 - s))).astype(jnp.bfloat16)
    skip_grad_ref[...] += jnp.sum(do * values, axis=0, keepdims=True)
    spread_columns(kq_ref[...], row_ref, pick_ref, key_ref, query_ref, states)

    backward_rows(
        states, rows, channels, history_ref, grad_ref, state_ref, key_ref, query_ref, rate_ref, do_ref, values32_ref,
        fed_ref, kept_ref, part_key_ref, part_query_ref, half_ref,
    )
    fed = as_rows(fed_ref[...])
    dvalues_ref[...] = fed + skip_ref[...] * as_rows(do_ref[...])
    scaled = as_rows(values32_ref[...]) * fed - as_rows(kept_ref[...])
    beta, inverse = step_sizes(low_ref[...], kq_ref[...], weight_ref, bias_ref, states)
    dpre = scaled * (1.0 - beta) * inverse
    bias_grad_ref[...] += jnp.sum(dpre, axis=0, keepdims=True)
    dpre_low = dpre.astype(jnp.bfloat16)
    dpre_ref[...] = dpre_low
    dlow_ref[...] = jnp.dot(dpre_low, weight_ref[...], preferred_element_type=jnp.float32)
    through = -2.0 * jnp.sum(scaled * beta * inverse, axis=1, keepdims=True)

    gather_columns(part_key_ref, part_query_ref, placed_ref, rows, states)
    lanes = lax.broadcasted_iota(jnp.int32, kq_ref.shape, 1)
    dkq_ref[...] = as_rows(placed_ref[...]) + jnp.where(lanes < states, kq_ref[...] * through, 0.0)

    @pl.when(pl.program_id(0) == pl.num_programs(0) - 1)
    def _():
        for copy in copies:
            copy.wait_recv()
        for copy in copies:
            copy.wait_send()


def exchange(parts, dps, result_ref, out_ref, result_came, out_came, result_send, result_recv, out_send, out_recv):
    d, s = lax.axis_index("dp"), lax.axis_index("seq")

    @pl.when(pl.program_id(0) == 0)
    def _():
        barrier = pltpu.get_barrier_semaphore()
        for k in range(1, parts):
            pl.semaphore_signal(barrier, inc=1, device_id=(d, lax.rem(s + k, parts)), device_id_type=MESH)
        for k in range(1, dps):
            pl.semaphore_signal(barrier, inc=1, device_id=(lax.rem(d + k, dps), s), device_id_type=MESH)
        pl.semaphore_wait(barrier, parts + dps - 2)

    copies = []
    for k in range(1, parts):
        to = lax.rem(s + k, parts)
        copies.append(
            pltpu.make_async_remote_copy(
                src_ref=result_ref.at[to], dst_ref=result_came.at[k - 1], send_sem=result_send.at[k - 1],
                recv_sem=result_recv.at[k - 1], device_id=(d, to), device_id_type=MESH,
            )
        )
    for k in range(1, dps):
        to = lax.rem(d + k, dps)
        copies.append(
            pltpu.make_async_remote_copy(
                src_ref=out_ref.at[to], dst_ref=out_came.at[k - 1], send_sem=out_send.at[k - 1],
                recv_sem=out_recv.at[k - 1], device_id=(to, s), device_id_type=MESH,
            )
        )
    return copies


def backward_scan(low, kq, values, gate, mixed, dgated, history, final, weight, bias, skip, result_part, out_part, states):
    length, channels = values.shape
    rank = low.shape[1]
    rows = min(128, length)
    blocks = length // rows
    by_row = lambda width: pl.BlockSpec((rows, width), lambda i: (blocks - 1 - i, 0))
    whole = lambda a: pl.BlockSpec(a.shape, lambda i: (0, 0))
    total = pl.BlockSpec((1, channels), lambda i: (0, 0))
    wide = pltpu.VMEM((rows // 8, 8, channels), jnp.float32)
    spread = pltpu.VMEM((rows * states, LANE), jnp.float32)
    longer = pltpu.VMEM((rows * states + 8 * states, LANE), jnp.float32)
    anywhere = pl.BlockSpec(memory_space=pl.ANY)
    dma = pltpu.SemaphoreType.DMA
    parts, dps = result_part.shape[0], out_part.shape[0]
    links = lambda *refs: exchange(parts, dps, *refs)
    return pl.pallas_call(
        lambda *refs: backward_body(states, links, *refs),
        grid=(blocks,),
        in_specs=[
            by_row(rank), by_row(LANE), by_row(channels), by_row(channels), by_row(channels), by_row(channels),
            pl.BlockSpec((rows * states, channels), lambda i: (blocks - 1 - i, 0)),
            whole(final), whole(weight), whole(bias), whole(skip), anywhere, anywhere,
        ],
        out_specs=[by_row(channels), by_row(channels), by_row(channels), by_row(rank), by_row(LANE), total, total, anywhere, anywhere],
        out_shape=[
            jax.ShapeDtypeStruct((length, channels), jnp.bfloat16),
            jax.ShapeDtypeStruct((length, channels), jnp.bfloat16),
            jax.ShapeDtypeStruct((length, channels), jnp.float32),
            jax.ShapeDtypeStruct((length, rank), jnp.float32),
            jax.ShapeDtypeStruct((length, LANE), jnp.float32),
            jax.ShapeDtypeStruct((1, channels), jnp.float32),
            jax.ShapeDtypeStruct((1, channels), jnp.float32),
            jax.ShapeDtypeStruct((parts - 1,) + result_part.shape[1:], jnp.bfloat16),
            jax.ShapeDtypeStruct((dps - 1,) + out_part.shape[1:], jnp.bfloat16),
        ],
        scratch_shapes=[
            pltpu.VMEM((states, channels), jnp.float32),
            pltpu.VMEM((states, channels), jnp.float32),
            spread, spread, wide, wide, wide, wide, wide, longer, longer,
            pltpu.VMEM((rows // 8, 8, LANE), jnp.float32), pltpu.VMEM((rows // 8, 8, LANE), jnp.float32),
            pltpu.VMEM((rows * states, LANE), jnp.bfloat16),
            pltpu.VMEM((2 * channels // LANE * 64 + 64, LANE), jnp.float32),
            dma((parts - 1,)), dma((parts - 1,)), dma((dps - 1,)), dma((dps - 1,)),
        ],
        compiler_params=pltpu.CompilerParams(collective_id=3, has_side_effects=True, vmem_limit_bytes=56 * 1024 * 1024),
        cost_estimate=pl.CostEstimate(flops=30 * length * states * channels, bytes_accessed=2 * length * states * channels, transcendentals=0),
    )(low, kq, values, gate, mixed, dgated, history, final, weight, bias, skip, result_part, out_part)


MESH = pl.DeviceIdType.MESH
GAIN_ROWS = 16


def plane_mates(d):
    core, x, y = lax.rem(d, 2), lax.rem(d // 2, 2), d // 4
    return d + 1 - 2 * core, d + 2 - 4 * x, d + 4 - 8 * y


def start_body(
    parts, block,
    tokens_ref, in_weight_ref, extra_ref, gain_ref, cot_ref,
    normed_out, weight_out, conv_ref, gate_ref, select_out, beta_out, vector_out, gain_out, cot_early,
    tokens_all, normed_all, weight_all, extra_all,
    near_send, near_recv, plane_send, plane_recv, gain_send, gain_recv, line_send, line_recv, local_sem, early_send, early_recv, spread_ref,
):
    d, s = lax.axis_index("dp"), lax.axis_index("seq")
    sib, xm, ym = plane_mates(d)
    own = spread_ref.shape[1]
    rows, width = tokens_ref.shape
    small = extra_ref.shape[0]
    channels = conv_ref.shape[1]
    chunk = rows // 4

    for j in range(spread_ref.shape[2] // block):
        for q in range(parts):
            first = (j * parts + q) * block
            spread_ref[q, :, j * block : (j + 1) * block] = in_weight_ref[:, first : first + block]

    barrier = pltpu.get_barrier_semaphore()
    for mate in (sib, xm, ym):
        pl.semaphore_signal(barrier, inc=1, device_id=(mate, s), device_id_type=MESH)
    for k in range(1, parts):
        pl.semaphore_signal(barrier, inc=1, device_id=(d, lax.rem(s + k, parts)), device_id_type=MESH)
    pl.semaphore_wait(barrier, 3 + parts - 1)

    def remote(src, dst, send, recv, to):
        return pltpu.make_async_remote_copy(
            src_ref=src, dst_ref=dst, send_sem=send, recv_sem=recv, device_id=to, device_id_type=MESH
        )

    def weight_rows(owner, source):
        return weight_all.at[pl.ds(pl.multiple_of((owner * parts + source) * own, own), own), :]

    def extra_rows(owner):
        return extra_all.at[owner]

    def gain_rows(source):
        return extra_all.at[d, pl.ds(pl.multiple_of(small + source * GAIN_ROWS, GAIN_ROWS), GAIN_ROWS), pl.ds(0, LANE)]

    near = []
    for k in range(1, parts):
        to = (d, lax.rem(s + k, parts))
        near.append(remote(spread_ref.at[to[1]], weight_rows(d, s), near_send.at[k], near_recv.at[k], to))
        near.append(remote(gain_ref, gain_rows(s), gain_send.at[k], gain_recv.at[k], to))
    for copy in near:
        copy.start()
    mine = [
        pltpu.make_async_copy(spread_ref.at[s], weight_rows(d, s), local_sem.at[0]),
        pltpu.make_async_copy(gain_ref, gain_rows(s), local_sem.at[1]),
        pltpu.make_async_copy(extra_ref, extra_all.at[d, pl.ds(0, small), :], local_sem.at[2]),
        pltpu.make_async_copy(tokens_ref, tokens_all.at[pl.ds(pl.multiple_of(s * rows, rows), rows), :], local_sem.at[3]),
    ]
    for copy in mine:
        copy.start()

    def token_rows(part, c):
        return tokens_all.at[pl.ds(pl.multiple_of(part * rows + c * chunk, chunk), chunk), :]

    def token_copy(way, distance, c):
        part = s - way * (distance - 1)
        src = tokens_ref.at[pl.ds(c * chunk, chunk), :] if distance == 1 else token_rows(part, c)
        side = 0 if way == 1 else 1
        return remote(
            src, token_rows(part, c), line_send.at[side, distance, c], line_recv.at[side, distance, c], (d, s + way)
        )

    def can_send(way, distance):
        reach = s + 1 < parts if way == 1 else s >= 1
        came = s - (distance - 1) >= 0 if way == 1 else s + (distance - 1) < parts
        return jnp.logical_and(reach, came)

    def arrives(way, distance):
        return s >= distance if way == 1 else s + distance < parts

    def send_tokens(distance, c):
        for way in (1, -1):
            @pl.when(can_send(way, distance))
            def _():
                token_copy(way, distance, c).start()

    def sent_tokens(distance, c):
        for way in (1, -1):
            @pl.when(can_send(way, distance))
            def _():
                token_copy(way, distance, c).wait_send()

    def take_tokens(distance, c):
        for way in (1, -1):
            @pl.when(arrives(way, distance))
            def _():
                part = s - way * distance
                side = 0 if way == 1 else 1
                remote(
                    token_rows(part, c), token_rows(part, c), line_send.at[side, distance, c],
                    line_recv.at[side, distance, c], (d, s),
                ).wait_recv()

    inner = jnp.logical_and(s >= 1, s + 1 < parts)

    def early_copy(way):
        side = 0 if way == 1 else 1
        return remote(cot_ref, cot_early.at[side], early_send.at[side], early_recv.at[side], (d, s + way))

    def last_copy(way):
        side = 0 if way == 1 else 1
        piece = pl.ds(0, chunk)
        return remote(
            cot_ref.at[piece, :], cot_early.at[side, piece, :], early_send.at[2 + side], early_recv.at[2 + side], (d, s + way)
        )

    def sends_last(way):
        return s == parts - 2 if way == 1 else s == 1

    def takes_last(way):
        return s == parts - 1 if way == 1 else s == 0

    def sends_early(way):
        return s + 2 < parts if way == 1 else s >= 2

    units = parts + 1

    def unit(owner, k):
        return extra_rows(owner) if k == parts else weight_rows(owner, lax.rem(s - k + parts, parts))

    kinds = {"own": (d, 0), "x": (xm, 2), "y": (ym, 4)}

    def plane_copy(owner, k, rel, kind, to):
        return remote(unit(owner, k), unit(owner, k), plane_send.at[kind, k], plane_recv.at[rel, k], (to, s))

    diag = xm + ym - d
    sib_of = lambda mate: mate + sib - d

    def route(k):
        steps = [
            (0, d, 1, 0, sib), (0, d, 2, 1, xm), (0, d, 4, 2, ym),
            (2, xm, 3, 3, sib), (4, ym, 5, 5, sib), (6, diag, 7, 7, sib),
        ]
        steps.append((2, xm, 6, 4, ym) if k % 2 == 0 else (4, ym, 6, 6, xm))
        return steps

    def pass_on(stage, k):
        for at, owner, rel, kind, to in route(k):
            if at == stage:
                plane_copy(owner, k, rel, kind, to).start()

    owners = {1: sib, 2: xm, 3: sib_of(xm), 4: ym, 5: sib_of(ym), 6: diag, 7: sib_of(diag)}

    def take(rel, k):
        plane_copy(owners[rel], k, rel, 0, d).wait_recv()

    for c in range(4):
        send_tokens(1, c)
    mine[0].wait()
    pass_on(0, 0)
    for k in range(1, parts):
        near_wait = remote(
            spread_ref.at[s], weight_rows(d, lax.rem(s - k + parts, parts)), near_send.at[k], near_recv.at[k], (d, s)
        )
        near_wait.wait_recv()
        pass_on(0, k)
    mine[1].wait()
    mine[2].wait()
    for k in range(1, parts):
        remote(gain_ref, gain_rows(lax.rem(s - k + parts, parts)), gain_send.at[k], gain_recv.at[k], (d, s)).wait_recv()
    pass_on(0, parts)
    for k in range(units):
        take(2, k)
        pass_on(2, k)
        take(4, k)
        pass_on(4, k)
        if k < 4:
            take_tokens(1, k)
            send_tokens(2, k)
    for way in (1, -1):
        @pl.when(sends_early(way))
        def _():
            early_copy(way).start()

    for k in range(units):
        take(6, k)
        pass_on(6, k)
        if k < 4:
            take_tokens(2, k)
            send_tokens(3, k)
    for way in (1, -1):
        @pl.when(sends_last(way))
        def _():
            last_copy(way).start()

    for rel in (1, 3, 5, 7):
        for k in range(units):
            take(rel, k)
    mine[3].wait()
    weight_copy = pltpu.make_async_copy(weight_all, weight_out, local_sem.at[4])
    weight_copy.start()
    sel = select_out.shape[1]
    for owner in range(extra_all.shape[0]):
        here = slice(owner * small, (owner + 1) * small)
        select_out[here, :] = extra_all[owner, 0:small, 0:sel]
        beta_out[here, :] = extra_all[owner, 0:small, sel : sel + LANE]
        vectors = extra_all[owner, 0:small, sel + LANE : sel + 2 * LANE].astype(jnp.float32)
        vector_out[:, here] = jnp.transpose(vectors)[: vector_out.shape[0]]

    lane = lax.broadcasted_iota(jnp.int32, (1, LANE), 1)
    pieces = []
    for owner in range(extra_all.shape[0]):
        for source in range(0, parts, 2):
            row = small + source * GAIN_ROWS
            even = extra_all[owner, row : row + GAIN_ROWS, 0:LANE].astype(jnp.float32)[0:1]
            odd = extra_all[owner, row + GAIN_ROWS : row + 2 * GAIN_ROWS, 0:LANE].astype(jnp.float32)[0:1]
            pieces.append(jnp.where(lane < own, even, odd))
    gain = jnp.concatenate(pieces, axis=1)
    gain_out[...] = gain

    tile = min(512, channels)

    def work(part):
        for c in range(4):
            at = pl.ds(pl.multiple_of(part * rows + c * chunk, chunk), chunk)
            flat = tokens_all[at, :].astype(jnp.float32)
            scale = lax.rsqrt(jnp.mean(flat * flat, axis=-1, keepdims=True) + 1e-05)
            normed_all[at, :] = (flat * scale * gain).astype(jnp.bfloat16)
        at = pl.ds(pl.multiple_of(part * rows, rows), rows)

        def columns(n, carry):
            left = pl.multiple_of(n * tile, tile)
            right = pl.multiple_of(channels + n * tile, tile)
            conv_ref[at, pl.ds(left, tile)] = jnp.dot(
                normed_all[at, :], weight_all[:, pl.ds(left, tile)], preferred_element_type=jnp.float32
            ).astype(jnp.bfloat16)
            gate_ref[at, pl.ds(left, tile)] = jnp.dot(
                normed_all[at, :], weight_all[:, pl.ds(right, tile)], preferred_element_type=jnp.float32
            )
            return carry

        lax.fori_loop(0, channels // tile, columns, 0)

    def work_at(low, high):
        def each(part, carry):
            away = jnp.abs(part - s)

            @pl.when(jnp.logical_and(away >= low, away <= high))
            def _():
                work(part)

            return carry

        lax.fori_loop(0, parts, each, 0)

    work_at(0, 2)
    for c in range(4):
        take_tokens(3, c)
    work_at(3, 3)
    normed_copy = pltpu.make_async_copy(normed_all, normed_out, local_sem.at[5])
    normed_copy.start()

    for way in (1, -1):
        @pl.when(inner)
        def _():
            early_copy(way).wait_recv()

        @pl.when(sends_early(way))
        def _():
            early_copy(way).wait_send()

        @pl.when(takes_last(way))
        def _():
            last_copy(way).wait_recv()

        @pl.when(sends_last(way))
        def _():
            last_copy(way).wait_send()

    for copy in near:
        copy.wait_send()
    for k in range(units):
        for at, owner, rel, kind, to in route(k):
            plane_copy(owner, k, rel, kind, to).wait_send()
    for distance in range(1, parts):
        for c in range(4):
            sent_tokens(distance, c)
    weight_copy.wait()
    normed_copy.wait()


def start(tokens, in_weight, extra, gain, cotangent, parts, dps):
    own, both = in_weight.shape[0], in_weight.shape[1] // parts
    rows, width = tokens.shape
    small, lanes = extra.shape
    any_space = pl.BlockSpec(memory_space=pl.ANY)
    vmem = pl.BlockSpec(memory_space=pltpu.VMEM)
    tall = small + parts * GAIN_ROWS
    dma = pltpu.SemaphoreType.DMA
    return pl.pallas_call(
        lambda *refs: start_body(parts, small, *refs),
        out_shape=[
            jax.ShapeDtypeStruct((parts * rows, width), jnp.bfloat16),
            jax.ShapeDtypeStruct((dps * parts * own, both), jnp.bfloat16),
            jax.ShapeDtypeStruct((parts * rows, both // 2), jnp.bfloat16),
            jax.ShapeDtypeStruct((parts * rows, both // 2), jnp.float32),
            jax.ShapeDtypeStruct((dps * small, lanes - 2 * LANE), jnp.bfloat16),
            jax.ShapeDtypeStruct((dps * small, LANE), jnp.bfloat16),
            jax.ShapeDtypeStruct((8, dps * small), jnp.float32),
            jax.ShapeDtypeStruct((1, width), jnp.float32),
            jax.ShapeDtypeStruct((2, rows, width), jnp.bfloat16),
        ],
        in_specs=[vmem, vmem, vmem, vmem, any_space],
        out_specs=[any_space, any_space, vmem, vmem, vmem, vmem, vmem, vmem, any_space],
        scratch_shapes=[
            pltpu.VMEM((parts * rows, width), jnp.bfloat16),
            pltpu.VMEM((parts * rows, width), jnp.bfloat16),
            pltpu.VMEM((dps * parts * own, both), jnp.bfloat16),
            pltpu.VMEM((dps, tall, lanes), jnp.bfloat16),
            dma((parts,)), dma((parts,)),
            dma((8, parts + 1)), dma((8, parts + 1)),
            dma((parts,)), dma((parts,)),
            dma((2, parts, 4)), dma((2, parts, 4)),
            dma((6,)), dma((4,)), dma((4,)), pltpu.VMEM((parts, own, both), jnp.bfloat16),
        ],
        compiler_params=pltpu.CompilerParams(
            collective_id=1, has_side_effects=True, vmem_limit_bytes=56 * 1024 * 1024
        ),
        cost_estimate=pl.CostEstimate(
            flops=2 * parts * rows * width * both, bytes_accessed=40 * 1024 * 1024, transcendentals=0
        ),
    )(tokens, in_weight, extra, gain, cotangent)


def line_sums(parts, rows, terms, came, send, recv, early=None):
    d, s = lax.axis_index("dp"), lax.axis_index("seq")
    chunk = rows // 4

    def own_rows(part, c):
        return pl.ds(pl.multiple_of(part * rows + c * chunk, chunk), chunk)

    def slot(way, left, part, c):
        at = parts if way == -1 and left == 0 else part
        return came.at[at, pl.ds(c * chunk, chunk), :]

    def copy_of(way, steps, c):
        side = 0 if way == 1 else 1
        part = s + way * steps
        return pltpu.make_async_remote_copy(
            src_ref=terms.at[own_rows(part, c), :], dst_ref=slot(way, steps - 1, part, c),
            send_sem=send.at[side, steps, c], recv_sem=recv.at[side, steps - 1, c],
            device_id=(d, s + way), device_id_type=MESH,
        )

    def valid(way, steps):
        if early is not None and steps == 1:
            return jnp.logical_and(s >= 1, s + 1 < parts)
        return s + steps < parts if way == 1 else s >= steps

    def ends_here(way):
        least = 1 if early is None else 2
        return s >= least if way == 1 else s + least < parts

    def upstream(way):
        return s >= 1 if way == 1 else s + 1 < parts

    def taken(way, left, c):
        side = 0 if way == 1 else 1
        place = slot(way, left, s + way * left, c)
        pltpu.make_async_remote_copy(
            src_ref=place, dst_ref=place, send_sem=send.at[side, left, c], recv_sem=recv.at[side, left, c],
            device_id=(d, s), device_id_type=MESH,
        ).wait_recv()

    def pass_on(steps, c):
        for way in (1, -1):
            @pl.when(valid(way, steps))
            def _():
                if steps < parts - 1:
                    @pl.when(upstream(way))
                    def _():
                        taken(way, steps, c)
                        mine = own_rows(s + way * steps, c)
                        more = came[s + way * steps, c * chunk : (c + 1) * chunk, :]
                        terms[mine, :] = (terms[mine, :].astype(jnp.float32) + more.astype(jnp.float32)).astype(jnp.bfloat16)

                copy_of(way, steps, c).start()

    def total(c):
        for way in (1, -1):
            @pl.when(ends_here(way))
            def _():
                taken(way, 0, c)

        at = pl.ds(c * chunk, chunk)
        low = jnp.where(ends_here(1), came[s, at, :].astype(jnp.float32), 0.0)
        high = jnp.where(ends_here(-1), came[parts, at, :].astype(jnp.float32), 0.0)
        total = terms[own_rows(s, c), :].astype(jnp.float32) + low + high
        if early is not None:
            total = total + jnp.where(jnp.logical_or(s == 1, s == parts - 2), early[at, :].astype(jnp.float32), 0.0)
        return total

    def sent():
        for steps in range(1, parts):
            for c in range(4):
                for way in (1, -1):
                    @pl.when(valid(way, steps))
                    def _():
                        copy_of(way, steps, c).wait_send()

    return pass_on, total, sent


def end_body(
    parts, block,
    dmixed_hbm, normed_hbm, weight_hbm, tokens_hbm, cot_hbm, gain_ref, shard_hbm, small_hbm,
    input_grad_ref, in_grad_ref, gain_grad_ref, small_grad_ref,
    dn, dn_recv, sib_send, sib_recv, q_send, q_recv, total, z_send, z_recv,
    small_sib_send, small_sib_recv, small_q_send, small_q_recv,
    line_send, line_recv, pair_send, pair_recv, cross_send, cross_recv, near_send, near_recv,
    dmixed_ref, normed_ref, weight_ref, tokens_ref, cot_ref, shard_ref, small_ref, load_sem,
):
    d, s = lax.axis_index("dp"), lax.axis_index("seq")
    sib, xm, ym = plane_mates(d)
    diag = xm + ym - d
    own, both = shard_ref.shape[0], dmixed_ref.shape[1]
    rows, width = tokens_ref.shape
    chunk = rows // 4
    tall = parts * own
    tile = min(512, both)

    loads = [
        pltpu.make_async_copy(src, dst, load_sem.at[i])
        for i, (src, dst) in enumerate(
            (
                (dmixed_hbm, dmixed_ref), (weight_hbm, weight_ref), (normed_hbm, normed_ref), (small_hbm, small_ref),
                (tokens_hbm, tokens_ref), (cot_hbm, cot_ref), (shard_hbm, shard_ref),
            )
        )
    ]
    for load in loads[:2]:
        load.start()
    barrier = pltpu.get_barrier_semaphore()
    for mate in (sib, xm, ym, diag):
        pl.semaphore_signal(barrier, inc=1, device_id=(mate, s), device_id_type=MESH)
    for k in range(1, parts):
        pl.semaphore_signal(barrier, inc=1, device_id=(d, lax.rem(s + k, parts)), device_id_type=MESH)
    pl.semaphore_wait(barrier, 4 + parts - 1)

    def remote(src, dst, send, recv, to):
        return pltpu.make_async_remote_copy(
            src_ref=src, dst_ref=dst, send_sem=send, recv_sem=recv, device_id=to, device_id_type=MESH
        )

    pass_line, line_total, line_sent = line_sums(parts, rows, dn, dn_recv, line_send, line_recv)

    def dn_part(part):
        at = pl.ds(pl.multiple_of(part * rows, rows), rows)

        def columns(n, carry):
            cols = pl.ds(pl.multiple_of(n * tile, tile), tile)
            dn[at, cols] = lax.dot_general(
                dmixed_ref[at, :], weight_ref[cols, :], (((1,), (1,)), ((), ())), preferred_element_type=jnp.float32
            ).astype(jnp.bfloat16)
            return carry

        lax.fori_loop(0, width // tile, columns, 0)

    far = (parts - 1) * (1 - s // 2)
    next_far = lax.rem(2 - 2 * s + 10, 5)
    nearer = 1 + lax.rem(s, 2)
    for load in loads[:2]:
        load.wait()
    for load in loads[2:]:
        load.start()
    dn_part(far)
    for c in range(4):
        pass_line(parts - 1, c)
    for load in loads[2:4]:
        load.wait()

    def grad_block(owner, store):
        left = pl.ds(pl.multiple_of(owner * tall, tall), tall)

        def columns(n, carry):
            cols = pl.ds(pl.multiple_of(n * tile, tile), tile)
            store(
                cols,
                lax.dot_general(
                    normed_ref[:, left], dmixed_ref[:, cols], (((0,), (0,)), ((), ())),
                    preferred_element_type=jnp.float32,
                ),
            )
            return carry

        lax.fori_loop(0, both // tile, columns, 0)

    mates = (diag, xm, ym, d)
    sib_of = lambda mate: mate + sib - d

    def pair_copy(r):
        return remote(sib_send.at[r], sib_recv.at[r], pair_send.at[0, r], pair_recv.at[0, r], (sib, s))

    def pair_copy_small(r):
        return remote(small_sib_send.at[r], small_sib_recv.at[r], pair_send.at[1, r], pair_recv.at[1, r], (sib, s))

    def cross_copy(r):
        return remote(q_send.at[r], q_recv.at[r], cross_send.at[0, r], cross_recv.at[0, r], (mates[r], s))

    def cross_copy_small(r):
        return remote(small_q_send.at[r], small_q_recv.at[r], cross_send.at[1, r], cross_recv.at[1, r], (mates[r], s))

    for r in range(4):
        def store_pair(cols, value):
            sib_send[r, :, cols] = value.astype(jnp.bfloat16)

        grad_block(sib_of(mates[r]), store_pair)
        pair_copy(r).start()
        small_sib_send[r] = small_ref[sib_of(mates[r])].astype(jnp.bfloat16)
        pair_copy_small(r).start()
    dn_part(next_far)
    for r in range(4):
        pair_copy(r).wait_recv()
        pair_copy_small(r).wait_recv()
        both_small = small_ref[mates[r]] + small_sib_recv[r].astype(jnp.float32)
        if r < 3:
            def store_cross(cols, value):
                q_send[r, :, cols] = (value + sib_recv[r, :, cols].astype(jnp.float32)).astype(jnp.bfloat16)

            grad_block(mates[r], store_cross)
            cross_copy(r).start()
            small_q_send[r] = both_small.astype(jnp.bfloat16)
            cross_copy_small(r).start()
        else:
            def store_total(cols, value):
                total[:, cols] = value + sib_recv[r, :, cols].astype(jnp.float32)

            grad_block(mates[r], store_total)
            small_grad_ref[...] = both_small
        pass_line(parts - 2, r)
        if r == 2:
            dn_part(nearer)
            dn_part(s)
    for c in range(4):
        pass_line(parts - 3, c)
    for load in loads[4:]:
        load.wait()

    for r in range(3):
        cross_copy(r).wait_recv()
        cross_copy_small(r).wait_recv()
        total[...] += q_recv[r].astype(jnp.float32)
        small_grad_ref[...] += small_q_recv[r].astype(jnp.float32)
    z_send[...] = total[...].astype(jnp.bfloat16)

    def near_copy(k):
        to = lax.rem(s + k, parts)
        return remote(
            z_send.at[pl.ds(pl.multiple_of(to * own, own), own), :], z_recv.at[k], near_send.at[k], near_recv.at[k], (d, to)
        )

    for k in range(1, parts):
        near_copy(k).start()

    for c in range(4):
        at = pl.ds(c * chunk, chunk)
        v = line_total(c) * gain_ref[...]
        flat = tokens_ref[at, :].astype(jnp.float32)
        scale = lax.rsqrt(jnp.mean(flat * flat, axis=-1, keepdims=True) + 1e-05)
        du = scale * v - flat * (scale * scale * scale) * jnp.mean(flat * v, axis=-1, keepdims=True)
        input_grad_ref[at, :] = (cot_ref[at, :].astype(jnp.float32) + du).astype(jnp.bfloat16)

    channel_blocks = both // block
    gain_total = jnp.zeros((own, block), jnp.float32)
    for k in range(parts):
        source = lax.rem(s - k + parts, parts)
        if k > 0:
            near_copy(k).wait_recv()
        for j in range(channel_blocks):
            cols = slice(j * block, (j + 1) * block)
            if k == 0:
                piece = z_send[pl.ds(pl.multiple_of(s * own, own), own), cols]
            else:
                piece = z_recv[k, :, cols]
            to = pl.ds(pl.multiple_of((j * parts + source) * block, block), block)
            in_grad_ref[:, to] = piece
            gain_total = gain_total + piece.astype(jnp.float32) * shard_ref[:, to].astype(jnp.float32)
    gain_grad_ref[...] = jnp.broadcast_to(jnp.sum(gain_total, axis=1, keepdims=True), gain_grad_ref.shape)

    for r in range(4):
        pair_copy(r).wait_send()
        pair_copy_small(r).wait_send()
    for r in range(3):
        cross_copy(r).wait_send()
        cross_copy_small(r).wait_send()
    for k in range(1, parts):
        near_copy(k).wait_send()
    line_sent()


def end(dmixed, normed, weight, tokens, cotangent, gain, shard, small, parts, block):
    both = dmixed.shape[1]
    rows, width = tokens.shape
    own = shard.shape[0]
    dps, _, lanes = small.shape
    tall = parts * own
    vmem = pl.BlockSpec(memory_space=pltpu.VMEM)
    anywhere = pl.BlockSpec(memory_space=pl.ANY)
    dma = pltpu.SemaphoreType.DMA
    low = jnp.bfloat16
    return pl.pallas_call(
        lambda *refs: end_body(parts, block, *refs),
        out_shape=[
            jax.ShapeDtypeStruct((rows, width), low),
            jax.ShapeDtypeStruct((own, parts * both), low),
            jax.ShapeDtypeStruct((own, LANE), jnp.float32),
            jax.ShapeDtypeStruct((block, lanes), jnp.float32),
        ],
        in_specs=[anywhere] * 5 + [vmem] + [anywhere] * 2,
        out_specs=[vmem] * 4,
        scratch_shapes=[
            pltpu.VMEM((parts * rows, width), low),
            pltpu.VMEM((parts + 1, rows, width), low),
            pltpu.VMEM((4, tall, both), low), pltpu.VMEM((4, tall, both), low),
            pltpu.VMEM((3, tall, both), low), pltpu.VMEM((3, tall, both), low),
            pltpu.VMEM((tall, both), jnp.float32),
            pltpu.VMEM((tall, both), low), pltpu.VMEM((parts, own, both), low),
            pltpu.VMEM((4, block, lanes), low), pltpu.VMEM((4, block, lanes), low),
            pltpu.VMEM((3, block, lanes), low), pltpu.VMEM((3, block, lanes), low),
            dma((2, parts, 4)), dma((2, parts, 4)),
            dma((2, 4)), dma((2, 4)), dma((2, 3)), dma((2, 3)), dma((parts,)), dma((parts,)),
            *[pltpu.VMEM(a.shape, a.dtype) for a in (dmixed, normed, weight, tokens, cotangent, shard, small)], dma((7,)),
        ],
        compiler_params=pltpu.CompilerParams(
            collective_id=2, has_side_effects=True, vmem_limit_bytes=60 * 1024 * 1024
        ),
        cost_estimate=pl.CostEstimate(
            flops=4 * parts * rows * width * both, bytes_accessed=30 * 1024 * 1024, transcendentals=0
        ),
    )(dmixed, normed, weight, tokens, cotangent, gain, shard, small)


def linked_forward_body(
    states, parts, dps, taps,
    conv_in_ref, gate_ref, select_ref, vector_ref, weight_ref, out_shard, cot_shard, cot_early,
    mixed_ref, history_ref, final_ref, values_out, low_ref, kq_ref, dgated_out, result_out, out_part_ref, early_out, key_ref, query_ref,
    state_ref, rate_ref, input_ref, out_ref, row_ref, pick_ref, half_ref,
    part_low, part_kq, came_low, came_kq, sum_low, sum_kq,
    rs_send, rs_recv, ag_send, ag_recv, out_send, out_recv, line_send, line_recv, local_sem,
    out_all, cot_all, gated_all, out_total, values_ref, dgated_ref, result_ref, leave_sem, early_send, early_recv,
):
    d, s = lax.axis_index("dp"), lax.axis_index("seq")
    step = pl.program_id(0)
    length, channels = values_ref.shape
    rows = gate_ref.shape[0]
    span = length // parts
    block = out_shard.shape[0]
    chunk = span // 4
    packed = LANE // (2 * states)
    conv_w_ref, conv_b_ref = vector_ref, vector_ref[taps : taps + 1, :]
    bias_ref, skip_ref = vector_ref[taps + 1 : taps + 2, :], vector_ref[taps + 2 : taps + 3, :]
    short = span // packed

    def remote(src, dst, send, recv, to):
        return pltpu.make_async_remote_copy(
            src_ref=src, dst_ref=dst, send_sem=send, recv_sem=recv, device_id=to, device_id_type=MESH
        )

    def out_rows(owner):
        return out_all.at[pl.ds(pl.multiple_of(owner * block, block), block), :]

    out_copies = []
    for k in range(1, dps):
        out_copies.append(
            remote(out_shard, out_rows(d), out_send.at[k - 1], out_recv.at[k - 1], (lax.rem(d + k, dps), s))
        )

    inner = jnp.logical_and(s >= 1, s + 1 < parts)

    def cot_rows(part, c):
        return cot_all.at[pl.ds(pl.multiple_of(part * span + c * chunk, chunk), chunk), :]

    def cot_copy(way, distance, c):
        part = s - way * (distance - 1)
        side = 0 if way == 1 else 1
        piece = pl.ds(c * chunk, chunk)
        src = {1: cot_shard.at[piece, :], 2: cot_early.at[side, piece, :]}.get(distance)
        src = cot_rows(part, c) if src is None else src
        return remote(
            src, cot_rows(part, c), line_send.at[side, distance, c], line_recv.at[side, distance, c], (d, s + way)
        )

    def can_send(way, distance):
        if distance == 1:
            return s == parts - 2 if way == 1 else s == 1
        came = s >= distance - 1 if way == 1 else s + distance - 1 < parts
        return jnp.logical_and(inner, came)

    def arrives(way, distance):
        if distance == 1:
            return s == parts - 1 if way == 1 else s == 0
        return s >= distance if way == 1 else s + distance < parts

    def into_end(way):
        return s == parts - 2 if way == 1 else s == 1

    def send_cot(distance, c, which=None):
        for way in (1, -1):
            go = can_send(way, distance)
            if which is not None:
                go = jnp.logical_and(go, into_end(way) if which else jnp.logical_not(into_end(way)))

            @pl.when(go)
            def _():
                cot_copy(way, distance, c).start()

    def sent_cot(distance, c):
        for way in (1, -1):
            @pl.when(can_send(way, distance))
            def _():
                cot_copy(way, distance, c).wait_send()

    def take_cot(distance, c):
        for way in (1, -1):
            @pl.when(arrives(way, distance))
            def _():
                part = s - way * distance
                side = 0 if way == 1 else 1
                remote(
                    cot_rows(part, c), cot_rows(part, c), line_send.at[side, distance, c],
                    line_recv.at[side, distance, c], (d, s),
                ).wait_recv()

    def end_rows(way):
        side = 0 if way == 1 else 1
        return pltpu.make_async_copy(
            cot_early.at[side, pl.ds(0, chunk), :], cot_rows(s - way, 0), local_sem.at[3 + side]
        )

    def early_rows(way):
        side = 0 if way == 1 else 1
        return pltpu.make_async_copy(
            cot_early.at[side], cot_all.at[pl.ds(pl.multiple_of((s - way) * span, span), span), :], local_sem.at[3 + side]
        )

    def early_result(way):
        part = 1 if way == 1 else parts - 2
        side = 0 if way == 1 else 1
        return remote(
            result_ref.at[pl.ds(part * span, span), :], early_out, early_send.at[side], early_recv.at[side], (d, s + way)
        )

    def sends_result(way):
        return s == 0 if way == 1 else s == parts - 1

    def takes_result(way):
        return s == 1 if way == 1 else s == parts - 2

    def own_copy(which):
        if which == 0:
            return pltpu.make_async_copy(out_shard, out_rows(d), local_sem.at[0])
        here = pl.ds(pl.multiple_of(s * span, span), span)
        return pltpu.make_async_copy(cot_shard, cot_all.at[here, :], local_sem.at[1])

    @pl.when(step == 0)
    def _():
        barrier = pltpu.get_barrier_semaphore()
        for k in range(1, parts):
            pl.semaphore_signal(barrier, inc=1, device_id=(d, lax.rem(s + k, parts)), device_id_type=MESH)
        for k in range(1, dps):
            pl.semaphore_signal(barrier, inc=1, device_id=(lax.rem(d + k, dps), s), device_id_type=MESH)
        pl.semaphore_wait(barrier, parts + dps - 2)
        state_ref[...] = jnp.zeros_like(state_ref)
        for copy in out_copies:
            copy.start()
        own_copy(0).start()
        own_copy(1).start()
        for way in (1, -1):
            @pl.when(inner)
            def _():
                early_rows(way).start()

            @pl.when(arrives(way, 1))
            def _():
                end_rows(way).start()

        send_cot(1, 1)
        send_cot(2, 0, False)

    def rs_copies(k):
        at = lax.rem(s + k, parts)
        return (
            remote(part_low.at[at], came_low.at[k - 1], rs_send.at[0, k - 1], rs_recv.at[0, k - 1], (d, at)),
            remote(part_kq.at[at], came_kq.at[k - 1], rs_send.at[1, k - 1], rs_recv.at[1, k - 1], (d, at)),
        )

    def ag_copies(k):
        to = lax.rem(s + k, parts)
        return (
            remote(sum_low.at[s], sum_low.at[s], ag_send.at[0, k - 1], ag_recv.at[0, k - 1], (d, to)),
            remote(sum_kq.at[s], sum_kq.at[s], ag_send.at[1, k - 1], ag_recv.at[1, k - 1], (d, to)),
        )

    def ag_taken(k, part):
        return (
            remote(sum_low.at[part], sum_low.at[part], ag_send.at[0, k - 1], ag_recv.at[0, k - 1], (d, s)),
            remote(sum_kq.at[part], sum_kq.at[part], ag_send.at[1, k - 1], ag_recv.at[1, k - 1], (d, s)),
        )

    def convolve(part):
        start = pl.multiple_of(part * span, span)
        before = pl.multiple_of(jnp.maximum(start - 16, 0), 16)
        wide = min(256, channels)
        for left in range(0, channels, wide):
            cols = slice(left, left + wide)
            head = conv_in_ref[pl.ds(before, 16), cols].astype(jnp.float32)
            head = jnp.where(part == 0, 0.0, head)
            body = jnp.concatenate([head, conv_in_ref[pl.ds(start, span), cols].astype(jnp.float32)], axis=0)
            total = conv_b_ref[:, cols]
            for tap in range(taps):
                by = taps - 1 - tap
                total = total + body[16 - by : 16 - by + span] * conv_w_ref[tap : tap + 1, cols]
            values_ref[pl.ds(start, span), cols] = (total * sigmoid(total)).astype(jnp.bfloat16)
        projected = jnp.dot(values_ref[pl.ds(start, span), :], select_ref[...], preferred_element_type=jnp.float32)
        part_low[part] = projected[:, :LANE].astype(jnp.bfloat16)
        pack = projected[:short, LANE:]
        for g in range(1, packed):
            pack = pack + pltpu.roll(projected[g * short : (g + 1) * short, LANE:], g * 2 * states, 1)
        part_kq[part] = pack

    @pl.when(step < parts - 1)
    def _():
        convolve(lax.rem(s + 1 + step, parts))

    for k in range(1, parts):
        @pl.when(step == k - 1)
        def _():
            for copy in rs_copies(k):
                copy.start()

    @pl.when(step == parts - 2)
    def _():
        send_cot(1, 2)

    @pl.when(step == parts - 1)
    def _():
        convolve(s)
        low = part_low[s].astype(jnp.float32)
        kq = part_kq[s]
        for k in range(1, parts):
            for copy in rs_copies(k):
                copy.wait_recv()
            low = low + came_low[k - 1].astype(jnp.float32)
            kq = kq + came_kq[k - 1]
        sum_low[s] = low.astype(jnp.bfloat16)
        sum_kq[s] = kq
        for k in range(1, parts):
            for copy in ag_copies(k):
                copy.start()
        send_cot(1, 3)
        send_cot(2, 1, False)

    per_part = span // rows
    at_block = step - parts

    def unpack(part):
        start = pl.multiple_of(part * span, span)
        low_ref[pl.ds(start, span), :] = sum_low[part]
        pack = sum_kq[part]
        lane = lax.broadcasted_iota(jnp.int32, pack.shape, 1)
        for g in range(packed):
            turned = pack if g == 0 else pltpu.roll(pack, LANE - g * 2 * states, 1)
            kq_ref[pl.ds(pl.multiple_of(start + g * short, short), short), :] = jnp.where(lane < 2 * states, turned, 0.0)

    for part in range(parts):
        @pl.when(at_block == part * per_part)
        def _():
            for k in range(1, parts):
                @pl.when(lax.rem(s - k + parts, parts) == part)
                def _():
                    for copy in ag_taken(k, part):
                        copy.wait_recv()

            unpack(part)

    plan = (
        (("outer", 0), ("inner", 2)), (("outer", 1), ("inner", 3)), (("outer", 2), ("outer", 3)), (("last", 0),),
        (("last", 1), ("last", 2)), (("last", 3),),
    )
    for at, moves in enumerate(plan):
        @pl.when(at_block == at)
        def _():
            for kind, c in moves:
                if kind == "last":
                    take_cot(2, c)
                    send_cot(3, c)
                else:
                    send_cot(2, c, kind == "outer")

    @pl.when(jnp.logical_and(at_block >= 0, at_block < length // rows))
    def _():
        here = pl.ds(pl.multiple_of(at_block * rows, rows), rows)
        kq = kq_ref[here, :]
        values = values_ref[here, :].astype(jnp.float32)
        beta, inverse = step_sizes(low_ref[here, :], kq, weight_ref, bias_ref, states)
        rates = beta * inverse
        rate_ref[...] = by_eights(rates)
        input_ref[...] = by_eights(rates * values)
        spread_columns(kq, row_ref, pick_ref, key_ref, query_ref, states)
        forward_rows(states, rows, channels, history_ref, state_ref, key_ref, query_ref, rate_ref, input_ref, out_ref, half_ref)
        mixed = as_rows(out_ref[...]) + skip_ref[...] * values
        gate = gate_ref[...]
        mixed_ref[...] = mixed
        gated_all[here, :] = (mixed * gate * sigmoid(gate)).astype(jnp.bfloat16)

    width = cot_all.shape[1]
    tile = min(512, width)

    def leaving(part, which):
        here = pl.ds(pl.multiple_of(part * span, span), span)
        ref, out = ((dgated_ref, dgated_out), (result_ref, result_out))[which]
        return pltpu.make_async_copy(ref.at[here, :], out.at[here, :], leave_sem.at[part, which])

    values_copy = pltpu.make_async_copy(values_ref, values_out, local_sem.at[2])

    @pl.when(step == parts)
    def _():
        values_copy.start()

    def products(part):
        here = pl.ds(pl.multiple_of(part * span, span), span)

        def across(n, carry):
            cols = pl.ds(pl.multiple_of(n * tile, tile), tile)
            out_total[:, cols] += lax.dot_general(
                gated_all[here, :], cot_all[here, cols], (((0,), (0,)), ((), ())), preferred_element_type=jnp.float32
            )
            return carry

        lax.fori_loop(0, width // tile, across, 0)
        deep = min(512, channels)

        def along(n, carry):
            cols = pl.ds(pl.multiple_of(n * deep, deep), deep)
            dgated_ref[here, cols] = lax.dot_general(
                cot_all[here, :], out_all[cols, :], (((1,), (1,)), ((), ())), preferred_element_type=jnp.float32
            )
            return carry

        lax.fori_loop(0, channels // deep, along, 0)
        leaving(part, 0).start()

    def result_terms(part):
        here = pl.ds(part * span, span)

        def across(n, carry):
            cols = pl.ds(pl.multiple_of(n * tile, tile), tile)
            result_ref[here, cols] = jnp.dot(
                gated_all[here, :], out_all[:, cols], preferred_element_type=jnp.float32
            ).astype(jnp.bfloat16)
            return carry

        lax.fori_loop(0, width // tile, across, 0)
        leaving(part, 1).start()

    @pl.when(at_block == length // rows - per_part)
    def _():
        own_copy(0).wait()
        for copy in out_copies:
            copy.wait_recv()
        for part in range(parts - 1):
            result_terms(part)
        for way in (1, -1):
            @pl.when(sends_result(way))
            def _():
                early_result(way).start()

    def products_at(low, high):
        def each(part, carry):
            away = jnp.abs(part - s)

            @pl.when(jnp.logical_and(away >= low, away <= high))
            def _():
                products(part)

            return carry

        lax.fori_loop(0, parts, each, 0)

    @pl.when(step == pl.num_programs(0) - 1)
    def _():
        final_ref[...] = state_ref[...]
        out_total[...] = jnp.zeros_like(out_total)
        own_copy(1).wait()
        for way in (1, -1):
            @pl.when(inner)
            def _():
                early_rows(way).wait()

            @pl.when(arrives(way, 1))
            def _():
                end_rows(way).wait()

        result_terms(parts - 1)
        products_at(0, 0)
        for c in range(1, 4):
            take_cot(1, c)
        products_at(1, 1)
        products_at(2, parts - 2)
        for c in range(4):
            take_cot(parts - 1, c)
        products_at(parts - 1, parts - 1)
        out_part_ref[...] = out_total[...].astype(jnp.bfloat16)
        values_copy.wait()
        for way in (1, -1):
            @pl.when(takes_result(way))
            def _():
                early_result(way).wait_recv()

            @pl.when(sends_result(way))
            def _():
                early_result(way).wait_send()

        for part in range(parts):
            leaving(part, 0).wait()
            leaving(part, 1).wait()
        for copy in out_copies:
            copy.wait_send()
        for distance in range(1, parts):
            for c in range(1 if distance == 1 else 0, 4):
                sent_cot(distance, c)
        for k in range(1, parts):
            for copy in rs_copies(k) + ag_copies(k):
                copy.wait_send()


def linked_forward(
    conv_in, gate, select, vectors, weight, out_shard, cot_shard, cot_early, parts, dps, taps, states
):
    length, channels = conv_in.shape
    block, width = out_shard.shape
    span = length // parts
    rows = min(128, span)
    blocks = length // rows
    short = span // (LANE // (2 * states))
    at = lambda i: jnp.clip(i - parts, 0, blocks - 1)
    by_row = lambda size: pl.BlockSpec((rows, size), lambda i: (at(i), 0))
    whole = lambda a: pl.BlockSpec(a.shape, lambda i: (0, 0))
    kept = lambda *shape: pl.BlockSpec(shape, lambda i: (0, 0))
    anywhere = pl.BlockSpec(memory_space=pl.ANY)
    dma = pltpu.SemaphoreType.DMA
    f32, low = jnp.float32, jnp.bfloat16
    eights = pltpu.VMEM((rows // 8, 8, channels), f32)
    return pl.pallas_call(
        lambda *refs: linked_forward_body(states, parts, dps, taps, *refs),
        grid=(parts + blocks + 1,),
        in_specs=[
            whole(conv_in), by_row(channels), whole(select), whole(vectors), whole(weight), anywhere, anywhere,
            anywhere,
        ],
        out_specs=[
            by_row(channels), pl.BlockSpec((rows * states, channels), lambda i: (at(i), 0)),
            kept(states, channels), anywhere, kept(length, LANE), kept(length, LANE),
            anywhere, anywhere, kept(dps * block, width), anywhere,
            pl.BlockSpec((rows * states, LANE), lambda i: (at(i), 0)), pl.BlockSpec((rows * states, LANE), lambda i: (at(i), 0)),
        ],
        out_shape=[
            jax.ShapeDtypeStruct((length, channels), f32),
            jax.ShapeDtypeStruct((length * states, channels), low),
            jax.ShapeDtypeStruct((states, channels), f32),
            jax.ShapeDtypeStruct((length, channels), low),
            jax.ShapeDtypeStruct((length, LANE), low),
            jax.ShapeDtypeStruct((length, LANE), f32),
            jax.ShapeDtypeStruct((length, channels), f32),
            jax.ShapeDtypeStruct((length, width), low),
            jax.ShapeDtypeStruct((dps * block, width), low),
            jax.ShapeDtypeStruct((span, width), low),
            jax.ShapeDtypeStruct((length * states, LANE), f32),
            jax.ShapeDtypeStruct((length * states, LANE), f32),
        ],
        scratch_shapes=[
            pltpu.VMEM((states, channels), f32),
            eights, eights, eights, pltpu.VMEM((rows // 8, 8, LANE), f32),
            pltpu.VMEM((rows * states, LANE), low), pltpu.VMEM((channels // LANE * 64 + 64, LANE), f32),
            pltpu.VMEM((parts, span, LANE), low), pltpu.VMEM((parts, short, LANE), f32),
            pltpu.VMEM((parts - 1, span, LANE), low), pltpu.VMEM((parts - 1, short, LANE), f32),
            pltpu.VMEM((parts, span, LANE), low), pltpu.VMEM((parts, short, LANE), f32),
            dma((2, parts - 1)), dma((2, parts - 1)), dma((2, parts - 1)), dma((2, parts - 1)),
            dma((dps - 1,)), dma((dps - 1,)), dma((2, parts, 4)), dma((2, parts, 4)), dma((5,)),
            pltpu.VMEM((dps * block, width), low), pltpu.VMEM((length, width), low), pltpu.VMEM((length, channels), low),
            pltpu.VMEM((dps * block, width), f32), pltpu.VMEM((length, channels), low),
            pltpu.VMEM((length, channels), f32), pltpu.VMEM((length, width), low), dma((parts, 2)), dma((2,)), dma((2,)),
        ],
        compiler_params=pltpu.CompilerParams(
            collective_id=4, has_side_effects=True, vmem_limit_bytes=60 * 1024 * 1024
        ),
        cost_estimate=pl.CostEstimate(
            flops=14 * length * states * channels, bytes_accessed=2 * length * states * channels, transcendentals=0
        ),
    )(conv_in, gate, select, vectors, weight, out_shard, cot_shard, cot_early)


def linked_backward_body(
    states, parts, dps, taps,
    low_ref, kq_ref, gate_ref, mixed_ref, dgated_ref, history_ref, final_ref, weight_ref,
    values_ref, conv_in_ref, select_ref, given_ref, tokens_ref, early_ref, key_ref, query_ref, part_hbm, out_ref,
    dmixed_out, small_ref, result_ref, out_grad_ref,
    grad_ref, state_ref, rate_ref, inverse_ref, do_ref, values32_ref, fed_ref, kept_ref, part_key_ref,
    part_query_ref, placed_ref, half_ref,
    dvalues_ref, dproj_ref, next_ref, vector_ref, part_low, part_kq, came_low, came_kq, sum_low, sum_kq,
    rs_send, rs_recv, ag_send, ag_recv, result_came, line_send, line_recv, out_send, out_recv,
    out_came, out_here, local_sem, dmixed_ref, part_ref, leave_sem,
):
    d, s = lax.axis_index("dp"), lax.axis_index("seq")
    step = pl.program_id(0)
    rows, channels = gate_ref.shape
    length = values_ref.shape[0]
    blocks = length // rows
    span = length // parts
    per_part = span // rows
    packed = LANE // (2 * states)
    short = span // packed
    sel = select_ref.shape[1]
    conv_w_ref, conv_b_ref = given_ref, given_ref[taps : taps + 1, :]
    bias_ref, skip_ref = given_ref[taps + 1 : taps + 2, :], given_ref[taps + 2 : taps + 3, :]

    def remote(src, dst, send, recv, to):
        return pltpu.make_async_remote_copy(
            src_ref=src, dst_ref=dst, send_sem=send, recv_sem=recv, device_id=to, device_id_type=MESH
        )

    copies = []
    for k in range(1, dps):
        to = lax.rem(d + k, dps)
        copies.append(remote(out_ref.at[to], out_came.at[k - 1], out_send.at[k - 1], out_recv.at[k - 1], (to, s)))
    out_copy = pltpu.make_async_copy(out_ref.at[d], out_here, local_sem.at[0])
    part_copy = pltpu.make_async_copy(part_hbm, part_ref, local_sem.at[1])
    pass_line, line_total, line_sent = line_sums(parts, span, part_ref, result_came, line_send, line_recv, early_ref)

    @pl.when(step == 0)
    def _():
        part_copy.start()
        barrier = pltpu.get_barrier_semaphore()
        for k in range(1, parts):
            pl.semaphore_signal(barrier, inc=1, device_id=(d, lax.rem(s + k, parts)), device_id_type=MESH)
        for k in range(1, dps):
            pl.semaphore_signal(barrier, inc=1, device_id=(lax.rem(d + k, dps), s), device_id_type=MESH)
        pl.semaphore_wait(barrier, parts + dps - 2)
        grad_ref[...] = jnp.zeros_like(grad_ref)
        state_ref[...] = final_ref[...]
        next_ref[...] = jnp.zeros_like(next_ref)
        vector_ref[...] = jnp.zeros_like(vector_ref)
        small_ref[...] = jnp.zeros_like(small_ref)
        for copy in copies:
            copy.start()
        out_copy.start()
        part_copy.wait()

    def rs_copies(k):
        at = lax.rem(s + k, parts)
        return (
            remote(part_low.at[at], came_low.at[k - 1], rs_send.at[0, k - 1], rs_recv.at[0, k - 1], (d, at)),
            remote(part_kq.at[at], came_kq.at[k - 1], rs_send.at[1, k - 1], rs_recv.at[1, k - 1], (d, at)),
        )

    def ag_copies(k):
        to = lax.rem(s + k, parts)
        return (
            remote(sum_low.at[s], sum_low.at[s], ag_send.at[0, k - 1], ag_recv.at[0, k - 1], (d, to)),
            remote(sum_kq.at[s], sum_kq.at[s], ag_send.at[1, k - 1], ag_recv.at[1, k - 1], (d, to)),
        )

    def ag_taken(k, part):
        return (
            remote(sum_low.at[part], sum_low.at[part], ag_send.at[0, k - 1], ag_recv.at[0, k - 1], (d, s)),
            remote(sum_kq.at[part], sum_kq.at[part], ag_send.at[1, k - 1], ag_recv.at[1, k - 1], (d, s)),
        )

    def add_up():
        low = part_low[s].astype(jnp.float32)
        kq = part_kq[s]
        for k in range(1, parts):
            for copy in rs_copies(k):
                copy.wait_recv()
            low = low + came_low[k - 1].astype(jnp.float32)
            kq = kq + came_kq[k - 1]
        sum_low[s] = low.astype(jnp.bfloat16)
        sum_kq[s] = kq.astype(jnp.bfloat16)
        for k in range(1, parts):
            for copy in ag_copies(k):
                copy.start()

    def leaving(part):
        here = pl.ds(pl.multiple_of(part * span, span), span)
        return pltpu.make_async_copy(dmixed_ref.at[here, :], dmixed_out.at[here, :], leave_sem.at[part])

    def conv_back(part):
        for k in range(1, parts):
            @pl.when(lax.rem(s - k + parts, parts) == part)
            def _():
                for copy in ag_taken(k, part):
                    copy.wait_recv()

        here = pl.ds(pl.multiple_of(part * span, span), span)
        before = pl.multiple_of(jnp.maximum(part * span - 16, 0), 16)
        dproj_ref[:, :LANE] = sum_low[part]
        pack = sum_kq[part].astype(jnp.float32)
        lane = lax.broadcasted_iota(jnp.int32, pack.shape, 1)
        for g in range(packed):
            turned = pack if g == 0 else pltpu.roll(pack, LANE - g * 2 * states, 1)
            dproj_ref[g * short : (g + 1) * short, LANE:] = jnp.where(lane < 2 * states, turned, 0.0).astype(jnp.bfloat16)
        wide = min(256, channels)
        for left in range(0, channels, wide):
            cols = slice(left, left + wide)
            small_ref[cols, :sel] += lax.dot_general(
                values_ref[here, cols], dproj_ref[...], (((0,), (0,)), ((), ())), preferred_element_type=jnp.float32
            )
            head = conv_in_ref[pl.ds(before, 16), cols].astype(jnp.float32)
            head = jnp.where(part == 0, 0.0, head)
            body = jnp.concatenate([head, conv_in_ref[here, cols].astype(jnp.float32)], axis=0)
            total = conv_b_ref[:, cols]
            for tap in range(taps):
                by = taps - 1 - tap
                total = total + body[16 - by : 16 - by + span] * conv_w_ref[tap : tap + 1, cols]
            sg = sigmoid(total)
            dvalues = dvalues_ref[here, cols] + lax.dot_general(
                dproj_ref[...], select_ref[cols, :], (((1,), (1,)), ((), ())), preferred_element_type=jnp.float32
            )
            dconv = dvalues * (sg + total * sg * (1.0 - sg))
            vector_ref[taps : taps + 1, cols] += jnp.sum(dconv, axis=0, keepdims=True)
            after = jnp.concatenate([dconv, next_ref[:, cols]], axis=0)
            dconv_in = jnp.zeros_like(dconv)
            for tap in range(taps):
                by = taps - 1 - tap
                shifted = body[16 - by : 16 - by + span]
                vector_ref[tap : tap + 1, cols] += jnp.sum(dconv * shifted, axis=0, keepdims=True)
                dconv_in = dconv_in + after[by : by + span] * conv_w_ref[tap : tap + 1, cols]
            next_ref[:, cols] = dconv[0:8]
            dmixed_ref[here, cols] = dconv_in.astype(jnp.bfloat16)
        leaving(part).start()

    plan = (
        ((3, 0),), ((3, 1), (2, 0)), ((3, 2), (2, 1)), ((3, 3), (2, 2), (1, 0)), ((2, 3), (1, 1)), ((1, 2),), ((1, 3),),
    )
    for at_step, moves in enumerate(plan):
        @pl.when(step == at_step)
        def _():
            for steps, c in moves:
                pass_line(steps, c)

    for part in range(parts):
        ends = (parts - part) * per_part - 1
        sums = min(ends + 3, blocks - 1 if part > 0 else blocks)

        @pl.when(jnp.logical_and(step == sums, s == part))
        def _():
            add_up()

        @pl.when(step == blocks + 1 - part)
        def _():
            conv_back(part)

    @pl.when(step < blocks)
    def _():
        block = blocks - 1 - step
        here = pl.ds(pl.multiple_of(block * rows, rows), rows)
        low, kq = low_ref[...], kq_ref[...]
        beta, inverse = step_sizes(low, kq, weight_ref, bias_ref, states)
        rate_ref[...] = by_eights(beta * inverse)
        inverse_ref[...] = inverse
        values = values_ref[here, :].astype(jnp.float32)
        values32_ref[...] = by_eights(values)
        gate = gate_ref[...]
        dgated = dgated_ref[...].astype(jnp.float32)
        sg = sigmoid(gate)
        do = dgated * (gate * sg)
        do_ref[...] = by_eights(do)
        dmixed_ref[here, channels:] = (dgated * mixed_ref[...] * (sg + gate * sg * (1.0 - sg))).astype(jnp.bfloat16)
        vector_ref[taps + 2 : taps + 3, :] += jnp.sum(do * values, axis=0, keepdims=True)
        backward_rows(
            states, rows, channels, history_ref, grad_ref, state_ref, key_ref, query_ref, rate_ref, do_ref, values32_ref,
            fed_ref, kept_ref, part_key_ref, part_query_ref, half_ref,
        )
        fed = as_rows(fed_ref[...])
        dvalues_ref[here, :] = fed + skip_ref[...] * as_rows(do_ref[...])
        scaled = as_rows(values32_ref[...]) * fed - as_rows(kept_ref[...])
        rates = as_rows(rate_ref[...])
        dpre = scaled * (inverse_ref[...] - rates)
        vector_ref[taps + 1 : taps + 2, :] += jnp.sum(dpre, axis=0, keepdims=True)
        dpre_low = dpre.astype(jnp.bfloat16)
        small_ref[:, sel : sel + LANE] += lax.dot_general(
            dpre_low, low, (((0,), (0,)), ((), ())), preferred_element_type=jnp.float32
        )
        through = -2.0 * jnp.sum(scaled * rates, axis=1, keepdims=True)
        gather_columns(part_key_ref, part_query_ref, placed_ref, rows, states)
        lanes = lax.broadcasted_iota(jnp.int32, kq.shape, 1)
        dkq = as_rows(placed_ref[...]) + jnp.where(lanes < states, kq * through, 0.0)
        part = block // per_part
        within = lax.rem(block, per_part)
        part_low[part, pl.ds(pl.multiple_of(within * rows, rows), rows), :] = jnp.dot(
            dpre_low, weight_ref[...], preferred_element_type=jnp.float32
        ).astype(jnp.bfloat16)
        for g in range(packed):
            first = g * short - within * rows

            @pl.when(jnp.logical_and(first >= 0, first < rows))
            def _():
                for w in range(per_part):
                    if w * rows <= g * short < (w + 1) * rows:
                        lo = g * short - w * rows
                        piece = dkq[lo : lo + short]
                        piece = piece if g == 0 else pltpu.roll(piece, g * 2 * states, 1)
                        if g == (per_part - 1) * rows // short:
                            part_kq[part] = piece
                        else:
                            part_kq[part] += piece

        @pl.when(within == 0)
        def _():
            for k in range(1, parts):
                @pl.when(lax.rem(s + k, parts) == part)
                def _():
                    for copy in rs_copies(k):
                        copy.start()

    @pl.when(step == pl.num_programs(0) - 1)
    def _():
        small_ref[:, sel + LANE :] = jnp.transpose(vector_ref[...])
        chunk = span // 4
        for c in range(4):
            at = pl.ds(c * chunk, chunk)
            result_ref[at, :] = (tokens_ref[at, :].astype(jnp.float32) + line_total(c)).astype(jnp.bfloat16)
        line_sent()
        for part in range(parts):
            leaving(part).wait()
        out_copy.wait()
        total = out_here[...].astype(jnp.float32)
        for k in range(1, dps):
            copies[k - 1].wait_recv()
            total = total + out_came[k - 1].astype(jnp.float32)
        out_grad_ref[...] = total
        for copy in copies:
            copy.wait_send()
        for k in range(1, parts):
            for copy in rs_copies(k) + ag_copies(k):
                copy.wait_send()


def linked_backward(
    low, kq, gate, mixed, dgated, history, final, weight, values, conv_in, select, vectors, tokens, early,
    key, query, result_part, out_part, parts, taps, states,
):
    length, channels = values.shape
    dps = out_part.shape[0]
    width = tokens.shape[1]
    sel = select.shape[1]
    span = length // parts
    rows = min(128, span)
    blocks = length // rows
    short = span // (LANE // (2 * states))
    at = lambda i: jnp.maximum(blocks - 1 - i, 0)
    by_row = lambda size: pl.BlockSpec((rows, size), lambda i: (at(i), 0))
    whole = lambda a: pl.BlockSpec(a.shape, lambda i: (0, 0))
    kept = lambda *shape: pl.BlockSpec(shape, lambda i: (0, 0))
    anywhere = pl.BlockSpec(memory_space=pl.ANY)
    dma = pltpu.SemaphoreType.DMA
    f32, bf16 = jnp.float32, jnp.bfloat16
    wide = pltpu.VMEM((rows // 8, 8, channels), f32)
    eights = pltpu.VMEM((rows // 8, 8, LANE), f32)
    spread = pltpu.VMEM((rows * states + 8 * states, LANE), f32)
    return pl.pallas_call(
        lambda *refs: linked_backward_body(states, parts, dps, taps, *refs),
        grid=(blocks + 2,),
        in_specs=[
            by_row(LANE), by_row(LANE), by_row(channels), by_row(channels), by_row(channels),
            pl.BlockSpec((rows * states, channels), lambda i: (at(i), 0)),
            whole(final), whole(weight), whole(values), whole(conv_in), whole(select), whole(vectors), whole(tokens),
            whole(early), pl.BlockSpec((rows * states, LANE), lambda i: (at(i), 0)),
            pl.BlockSpec((rows * states, LANE), lambda i: (at(i), 0)), anywhere, anywhere,
        ],
        out_specs=[anywhere, kept(channels, sel + 2 * LANE), kept(span, width), kept(*out_part.shape[1:])],
        out_shape=[
            jax.ShapeDtypeStruct((length, 2 * channels), bf16),
            jax.ShapeDtypeStruct((channels, sel + 2 * LANE), f32),
            jax.ShapeDtypeStruct((span, width), bf16),
            jax.ShapeDtypeStruct(out_part.shape[1:], f32),
        ],
        scratch_shapes=[
            pltpu.VMEM((states, channels), f32), pltpu.VMEM((states, channels), f32),
            wide, pltpu.VMEM((rows, channels), f32), wide, wide, wide, wide, spread, spread, eights,
            pltpu.VMEM((2 * channels // LANE * 64 + 64, LANE), f32),
            pltpu.VMEM((length, channels), f32), pltpu.VMEM((span, sel), bf16), pltpu.VMEM((8, channels), f32),
            pltpu.VMEM((LANE, channels), f32),
            pltpu.VMEM((parts, span, LANE), bf16), pltpu.VMEM((parts, short, LANE), f32),
            pltpu.VMEM((parts - 1, span, LANE), bf16), pltpu.VMEM((parts - 1, short, LANE), f32),
            pltpu.VMEM((parts, span, LANE), bf16), pltpu.VMEM((parts, short, LANE), bf16),
            dma((2, parts - 1)), dma((2, parts - 1)), dma((2, parts - 1)), dma((2, parts - 1)),
            pltpu.VMEM((parts + 1, span, width), bf16), dma((2, parts, 4)), dma((2, parts, 4)),
            dma((dps - 1,)), dma((dps - 1,)), pltpu.VMEM((dps - 1,) + out_part.shape[1:], bf16),
            pltpu.VMEM(out_part.shape[1:], bf16), dma((2,)), pltpu.VMEM((length, 2 * channels), bf16),
            pltpu.VMEM((length, width), bf16), dma((parts,)),
        ],
        compiler_params=pltpu.CompilerParams(
            collective_id=5, has_side_effects=True, vmem_limit_bytes=60 * 1024 * 1024
        ),
        cost_estimate=pl.CostEstimate(
            flops=30 * length * states * channels, bytes_accessed=2 * length * states * channels, transcendentals=0
        ),
    )(low, kq, gate, mixed, dgated, history, final, weight, values, conv_in, select, vectors, tokens, early, key, query, result_part, out_part)


def contract(left, right, left_dim, right_dim):
    return lax.dot_general(
        left, right, (((left_dim,), (right_dim,)), ((), ())), preferred_element_type=jnp.float32
    )


def gathered(shard, axis):
    return lax.all_gather(shard, axis, axis=0, tiled=True)


def scattered(total, axis):
    return lax.psum_scatter(total, axis, scatter_dimension=0, tiled=True)


def summed_rows(partial, axis):
    size = lax.axis_size(axis)
    parts = partial.astype(jnp.bfloat16).reshape((size, partial.shape[0] // size) + partial.shape[1:])
    parts = lax.all_to_all(parts, axis, 0, 0)
    return jnp.sum(parts.astype(jnp.float32), axis=0)


def later(rows, by):
    if by == 0:
        return rows
    return jnp.pad(rows, ((by, 0), (0, 0)))[: rows.shape[0]]


def sooner(rows, by):
    if by == 0:
        return rows
    return jnp.pad(rows, ((0, by), (0, 0)))[by:]


def local(
    tokens,
    cotangent,
    norm_gain,
    in_weight,
    conv_weight,
    conv_bias,
    select_weight,
    beta_weight,
    beta_bias,
    skip_gain,
    out_weight,
):
    parts, dps = lax.axis_size("seq"), lax.axis_size("dp")
    rows, width = tokens.shape[1:]
    block = conv_weight.shape[0]
    channels = block * dps
    taps = conv_weight.shape[1]
    rank = beta_weight.shape[1]
    states = (select_weight.shape[1] - rank) // 2
    own = in_weight.shape[0]

    flat = tokens.reshape(rows, width).astype(jnp.float32)
    scale = lax.rsqrt(jnp.mean(flat * flat, axis=-1, keepdims=True) + 1e-05)
    vectors = jnp.concatenate(
        [conv_weight, conv_bias[:, None], beta_bias[:, None], skip_gain[:, None]], axis=1
    )
    wide = -(-select_weight.shape[1] // LANE) * LANE
    small = jnp.concatenate(
        [
            jnp.pad(select_weight, ((0, 0), (0, wide - select_weight.shape[1]))),
            beta_weight,
            jnp.pad(vectors, ((0, 0), (0, LANE - vectors.shape[1]))),
        ],
        axis=1,
    )
    small_slice = (dps, parts, 2 * own, rank) == (8, 4, LANE, LANE)
    if small_slice:
        doubled = jnp.broadcast_to(jnp.tile(norm_gain.reshape(1, own), (1, 2)), (GAIN_ROWS, LANE))
        normed, in_w, conv_in, gate, select_w, beta_w, vectors, gain, cot_early = start(
            tokens.reshape(rows, width), in_weight, small, doubled, cotangent.reshape(rows, width), parts, dps
        )
    else:
        gain = gathered(norm_gain, ("dp", "seq"))
        normed = gathered((flat * scale * gain.astype(jnp.float32)).astype(jnp.bfloat16), "seq")
        spread = in_weight.reshape(own, 2, dps, parts, block).transpose(3, 0, 1, 2, 4).reshape(parts, own, 2 * channels)
        in_w = gathered(lax.all_to_all(spread, "seq", 0, 0).reshape(parts * own, 2 * channels), "dp")
        smalls = gathered(small, "dp")
        conv_in = jnp.dot(normed, in_w[:, :channels], preferred_element_type=jnp.float32).astype(jnp.bfloat16)
        gate = jnp.dot(normed, in_w[:, channels:], preferred_element_type=jnp.float32)
    cot_here = cotangent.reshape(rows, width)
    if small_slice:
        mixed, history, final, values, low, kq, dgated, result_part, out_part, early, key, query = linked_forward(
            conv_in, gate, select_w, vectors, beta_w, out_weight, cot_here, cot_early, parts, dps, taps, states,
        )
    else:
        gain = gain.astype(jnp.float32)
        select_w = smalls[:, : select_weight.shape[1]]
        beta_w = smalls[:, wide : wide + rank]
        vectors = smalls[:, wide + rank :].astype(jnp.float32)
        conv_w, conv_b = vectors[:, :taps], vectors[:, taps]
        beta_b, skip = vectors[:, taps + 1].reshape(1, channels), vectors[:, taps + 2].reshape(1, channels)
        conv_wide = conv_in.astype(jnp.float32)
        conv_sum = conv_b
        for tap in range(taps):
            conv_sum = conv_sum + later(conv_wide, taps - 1 - tap) * conv_w[:, tap]
        out_w = gathered(out_weight, "dp")
        cot = gathered(cot_here, "seq")
        values = jax.nn.silu(conv_sum).astype(jnp.bfloat16)
        projected = lax.psum(jnp.dot(values, select_w, preferred_element_type=jnp.float32), "seq")
        low = projected[:, :rank].astype(jnp.bfloat16)
        kq = jnp.pad(projected[:, rank:], ((0, 0), (0, LANE - 2 * states)))
        gated, mixed, history, final = forward_scan(low, kq, values, gate, beta_w, beta_b, skip, states)
        result_part = jnp.dot(gated, out_w, preferred_element_type=jnp.float32).astype(jnp.bfloat16)
        out_part = contract(gated, cot, 0, 0).astype(jnp.bfloat16)
        dgated = contract(cot, out_w, 1, 1)
    out_part = out_part.reshape(dps, block, width)
    if small_slice:
        dmixed, small_grads, result, out_grad = linked_backward(
            low, kq, gate, mixed, dgated, history, final, beta_w, values, conv_in, select_w, vectors,
            tokens.reshape(rows, width), early, key, query, result_part, out_part, parts, taps, states,
        )
        small_grads = small_grads.reshape(dps, block, wide + rank + LANE)
    else:
        result_part = result_part.reshape(parts, rows, width)
        dgate, dpre_low, dvalues, dlow, dkq, bias_grad, skip_grad, result_came, out_came = backward_scan(
            low, kq, values, gate, mixed, dgated, history, final, beta_w, beta_b, skip, result_part, out_part, states
        )
        part_here = lax.dynamic_index_in_dim(result_part, lax.axis_index("seq"), 0, False).astype(jnp.float32)
        result = (flat + (part_here + jnp.sum(result_came.astype(jnp.float32), axis=0))).astype(jnp.bfloat16)
        out_here = lax.dynamic_index_in_dim(out_part, lax.axis_index("dp"), 0, False).astype(jnp.float32)
        out_grad = out_here + jnp.sum(out_came.astype(jnp.float32), axis=0)
        dprojected = lax.psum(jnp.concatenate([dlow, dkq[:, : 2 * states]], axis=1), "seq").astype(jnp.bfloat16)
        beta_grad = contract(dpre_low, low, 0, 0)
        select_grad = contract(values, dprojected, 0, 0)
        dvalues = contract(dprojected, select_w, 1, 1) + dvalues
        s = jax.nn.sigmoid(conv_sum)
        dconv = dvalues * (s + conv_sum * s * (1.0 - s))
        conv_w_grad = jnp.stack(
            [jnp.sum(dconv * later(conv_wide, taps - 1 - tap), axis=0) for tap in range(taps)], axis=1
        )
        conv_b_grad = jnp.sum(dconv, axis=0)
        dconv_in = 0.0
        for tap in range(taps):
            dconv_in = dconv_in + sooner(dconv, taps - 1 - tap) * conv_w[:, tap]
        dmixed = jnp.concatenate([dconv_in.astype(jnp.bfloat16), dgate], axis=1)
        vector_grads = jnp.concatenate(
            [conv_w_grad, conv_b_grad[:, None], bias_grad.reshape(channels, 1), skip_grad.reshape(channels, 1)], axis=1
        )
        small_grads = jnp.concatenate(
            [
                jnp.pad(select_grad, ((0, 0), (0, wide - select_grad.shape[1]))),
                beta_grad,
                jnp.pad(vector_grads, ((0, 0), (0, LANE - vector_grads.shape[1]))),
            ],
            axis=1,
        ).reshape(dps, block, wide + rank + LANE)
    if small_slice:
        input_grad, in_grad, gain_sums, small_grads = end(
            dmixed, normed, in_w, tokens.reshape(rows, width), cot_here, gain, in_weight, small_grads,
            parts, block,
        )
        gain_sums = gain_sums[:, 0]
    else:
        in_grad = summed_rows(contract(normed, dmixed, 0, 0), "dp").astype(jnp.bfloat16)
        in_grad = lax.all_to_all(in_grad.reshape(parts, own, 2 * channels), "seq", 0, 0).astype(jnp.float32)
        in_grad = in_grad.reshape(parts, own, 2, dps, block).transpose(1, 2, 3, 0, 4).reshape(own, 2 * parts * channels)
        gain_sums = jnp.sum(in_grad * in_weight.astype(jnp.float32), axis=1)
        v = summed_rows(contract(dmixed, in_w, 1, 1), "seq") * gain
        du = scale * v - flat * (scale * scale * scale) * jnp.mean(flat * v, axis=-1, keepdims=True)
        input_grad = (cot_here.astype(jnp.float32) + du).astype(jnp.bfloat16)
        small_grads = jnp.sum(lax.all_to_all(small_grads, "dp", 0, 0), axis=0)
    rows_grad = small_grads[:, wide + rank :]
    return (
        result.reshape(tokens.shape),
        input_grad.reshape(tokens.shape),
        gain_sums / norm_gain.astype(jnp.float32),
        in_grad.astype(jnp.float32),
        rows_grad[:, :taps],
        rows_grad[:, taps],
        small_grads[:, : select_weight.shape[1]],
        small_grads[:, wide : wide + rank],
        rows_grad[:, taps + 1],
        rows_grad[:, taps + 2],
        out_grad,
    )


def solution(mesh):
    split = P(("dp", "seq"))
    rows = P("dp", "seq", None)
    return jax.shard_map(
        local,
        mesh=mesh,
        in_specs=(rows, rows) + (split,) * 9,
        out_specs=(rows, rows) + (split,) * 9,
        check_vma=False,
    )
```
